32 devices in a mesh: blade: 8 (over z, y), span: 4 (over x, core).
Axes of the slice: x: 2, y: 2, z: 4, core: 2. Of those that a mesh axis runs over, the one named last changes fastest.
Arguments:
- conductance: float32 [8, 32, 32, 512], P('blade', None, 'span'), may hold values from 0.02 to 0.2
- depth_inverse: float32 [8, 32, 32], P('blade')
- surface_residual: float32 [8, 4, 32, 512], P('blade', None, 'span'), may hold values from -6 to 6
- surface_excess: float32 [8, 3, 32, 512], P('blade', None, 'span'), may hold values from 0.3 to 3
- segment_map: int32 [32, 4], P('span'), may hold values from 0 to 2047, as said below
- frame_index: int32 [3], replicated, may hold values from 0 to 3
Outputs:
- adjoint: float32 [8, 32, 32, 512], P('blade', None, 'span')
- gradient: float32 [2048], P(('blade', 'span'))
The draws below stay inside these ranges and needn't reach their ends.
Inputs may be any that keep to these rules, and one draw needn't show every extreme that they name: `segment_map`: every entry is a passage segment number.
All inputs are finite; a program needn't handle non-finite values.
Results may differ from the reference program's by a relative error of at most 0.0003.
Values sent between devices are 32-bit elements; how exact they have to be, the bound alone decides.
No kernel may reach another device: no remote copies, remote signals or barrier semaphores. Data moves between devices by JAX's collectives and lax.ppermute only.
A program may use at most 64 MiB of HBM per device.

```python
import math
import jax
import jax.numpy as jnp
from jax import lax

ND = 32
NC = 512
SP_DEV = 8
STEPS = 3
FRAMES = 4
SEGS = 2048
BLADES = 8
SPAN = 32
NBLK = 4


def draw_depth_inverse(key, part):
    first, second = jax.random.split(jax.random.fold_in(key, 11))
    off = jax.random.uniform(first, (BLADES, ND, ND), jnp.float32, -1.0, 1.0) * (0.6 / ND ** 0.5)
    diag = jax.random.uniform(second, (BLADES, ND), jnp.float32, 0.6, 1.0)
    eye = jnp.eye(ND, dtype=jnp.float32)
    return off * (1.0 - eye) + diag[:, :, None] * eye


def draw_segment_map(key, part):
    n_slabs = SPAN // SP_DEV
    share = SEGS // (BLADES * n_slabs)
    key_span, key_blade, key_offset = jax.random.split(jax.random.fold_in(key, 23), 3)
    row_ids = jnp.arange(SPAN, dtype=jnp.int32)[:, None]
    col_ids = jnp.arange(NBLK, dtype=jnp.int32)[None, :]
    slab = row_ids // SP_DEV
    local = row_ids % SP_DEV * NBLK + col_ids
    random_span = jax.random.randint(key_span, (SPAN, NBLK), 0, n_slabs, dtype=jnp.int32)
    owner_span = jnp.where(local == 0, (slab + n_slabs - 1) % n_slabs, jnp.where(local == 1, slab + 0 * col_ids, random_span))
    owner_blade = jax.random.randint(key_blade, (SPAN, NBLK), 0, BLADES, dtype=jnp.int32)
    offset = jax.random.randint(key_offset, (SPAN, NBLK), 0, share, dtype=jnp.int32)
    values = ((owner_blade * n_slabs + owner_span) * share + offset).astype(jnp.int32)
    lowest = (row_ids == 1) & (col_ids == 0)
    highest = (row_ids == SPAN - 1) & (col_ids == NBLK - 1)
    values = jnp.where(lowest, jnp.int32(0), values)
    values = jnp.where(highest, jnp.int32(SEGS - 1), values)
    return values.astype(jnp.int32)


def block_scale(key, extent, cuts, least, largest):
    def one(position, blocks):
        heights = jax.random.uniform(jax.random.fold_in(jax.random.fold_in(key, 6), position), (blocks,), jnp.float32, least / len(cuts), largest / len(cuts))
        return jnp.repeat(jnp.exp(heights), extent[position] // blocks).reshape((-1,) + (1,) * (len(extent) - position - 1))

    factor_of = one(*cuts[0])
    for cut in cuts[1:]:
        factor_of = factor_of * one(*cut)
    return factor_of


def centred(stream_key, dims, width, reach, shards=(), held_as=jnp.bfloat16):
    factor_of = block_scale(stream_key, dims, shards, -0.22, 0.18) if shards else 1.0
    drawn = jax.random.normal(stream_key, dims, jnp.float32) * width * factor_of
    return jnp.minimum(jnp.maximum(drawn, -reach), reach).astype(held_as)


def setup_inputs(seed: int = 0) -> dict:
    seeds = jax.random.split(jax.random.key(seed), 7)
    return {
        "conductance": jnp.clip(jnp.exp(math.log(0.2) - 2.3025851 * jax.random.uniform(seeds[0], (BLADES, ND, SPAN, NC), jnp.float32) ** block_scale(seeds[0], (BLADES, ND, SPAN, NC), ((0, 8), (2, 4)), -0.2, 0.2)), 0.02, 0.2),
        "depth_inverse": draw_depth_inverse(jax.random.fold_in(seeds[6], 71), 0),
        "surface_residual": centred(seeds[2], (BLADES, FRAMES, SPAN, NC), 1.0, 6.0, ((0, 8), (2, 4)), jnp.float32),
        "surface_excess": jnp.clip(jnp.exp(math.log(3.0) - 2.3025851 * jax.random.uniform(seeds[3], (BLADES, STEPS, SPAN, NC), jnp.float32) ** block_scale(seeds[3], (BLADES, STEPS, SPAN, NC), ((0, 8), (2, 4)), -0.2, 0.2)), 0.3, 3.0),
        "segment_map": draw_segment_map(jax.random.fold_in(seeds[6], 71), 0),
        "frame_index": jax.random.randint(seeds[5], (STEPS,), 0, FRAMES).astype(jnp.int32),
    }


def lateral(lam_pad, kap_pad):
    lp = jnp.pad(lam_pad, ((0, 0), (0, 0), (0, 0), (1, 1)))
    kp = jnp.pad(kap_pad, ((0, 0), (0, 0), (0, 0), (1, 1)))
    rows = lp.shape[2] - 2
    cols = lp.shape[3] - 2
    center = lp[:, :, 1:1 + rows, 1:1 + cols]
    kcen = kp[:, :, 1:1 + rows, 1:1 + cols]
    total = jnp.zeros_like(center)
    for first, second in ((2, 1), (0, 1), (1, 2), (1, 0)):
        near = lp[:, :, first:first + rows, second:second + cols]
        knear = kp[:, :, first:first + rows, second:second + cols]
        total = total + 0.5 * (kcen + knear) * (near - center)
    return total

def reference(conductance, depth_inverse, surface_residual, surface_excess, segment_map, frame_index):
    span_pad = ((0, 0), (0, 0), (1, 1), (0, 0))
    kap_pad = jnp.pad(conductance, span_pad)
    adjoint = jnp.zeros_like(conductance)
    contribution = jnp.zeros(surface_excess[:, 0].shape, jnp.float32)
    for step in range(STEPS - 1, -1, -1):
        source = adjoint + lateral(jnp.pad(adjoint, span_pad), kap_pad)
        frame = jnp.take(surface_residual, frame_index[step], axis=1)
        source = source.at[:, 0].add(frame)
        adjoint = jnp.einsum('bij,bjsc->bisc', depth_inverse, source, precision=lax.Precision.HIGHEST)
        contribution = contribution + adjoint[:, 0] * surface_excess[:, step]
    block_sums = contribution.reshape(BLADES, SPAN, NBLK, 128).sum(axis=3).sum(axis=0)
    gradient = jax.ops.segment_sum(block_sums.reshape(-1), segment_map.reshape(-1), num_segments=SEGS)
    return (adjoint, gradient / math.sqrt(128.0 * STEPS))
```

```python
import math

import jax
import jax.numpy as jnp
from jax import lax
from jax.sharding import PartitionSpec as P

STEPS = 3
SEGS = 2048


def with_halo(cells, sides, width):
    for axis, dim in sides:
        count = lax.axis_size(axis)
        ends = count - 1
        head = lax.slice_in_dim(cells, 0, width, axis=dim)
        tail = lax.slice_in_dim(cells, cells.shape[dim] - width, cells.shape[dim], axis=dim)
        cells = jnp.concatenate(
            [
                lax.ppermute(tail, axis, [(i, (i + 1) % count) for i in range(ends)]),
                cells,
                lax.ppermute(head, axis, [((i + 1) % count, i) for i in range(ends)]),
            ],
            axis=dim,
        )
    return cells


def lateral(lam_pad, kap_pad):
    lp = jnp.pad(lam_pad, ((0, 0), (0, 0), (0, 0), (1, 1)))
    kp = jnp.pad(kap_pad, ((0, 0), (0, 0), (0, 0), (1, 1)))
    rows = lp.shape[2] - 2
    cols = lp.shape[3] - 2
    center = lp[:, :, 1 : 1 + rows, 1 : 1 + cols]
    kcen = kp[:, :, 1 : 1 + rows, 1 : 1 + cols]
    total = jnp.zeros_like(center)
    for first, second in ((2, 1), (0, 1), (1, 2), (1, 0)):
        near = lp[:, :, first : first + rows, second : second + cols]
        knear = kp[:, :, first : first + rows, second : second + cols]
        total = total + 0.5 * (kcen + knear) * (near - center)
    return total


def per_device(
    conductance, depth_inverse, surface_residual, surface_excess, segment_map, frame_index
):
    frames = surface_residual.shape[1]
    rows = conductance.shape[2]
    cols = conductance.shape[3]
    blocks = cols // 128
    segments = SEGS
    frame_ids = jnp.arange(frames, dtype=jnp.int32)
    contribution = jnp.zeros((rows, cols), jnp.float32)
    kap_pad = with_halo(conductance, (("span", 2),), 1)
    adjoint = jnp.zeros_like(conductance)
    for step in range(STEPS - 1, -1, -1):
        if step == STEPS - 1:
            source = adjoint
        else:
            lam_pad = with_halo(adjoint, (("span", 2),), 1)
            source = adjoint + lateral(lam_pad, kap_pad)
        pick = (frame_ids == frame_index[step]).astype(jnp.float32)
        frame = jnp.sum(surface_residual[0] * pick[:, None, None], axis=0)
        source = source.at[0, 0].add(frame)
        adjoint = jnp.einsum(
            "ij,bjsc->bisc", depth_inverse[0], source, precision=lax.Precision.HIGHEST
        )
        contribution = contribution + adjoint[0, 0] * surface_excess[0, step]
    block_sums = contribution.reshape(rows, blocks, 128).sum(axis=2)
    seg_ids = jnp.arange(segments, dtype=jnp.int32)
    scale = 1.0 / math.sqrt(128.0 * STEPS)
    onehot = (segment_map.reshape(-1, 1) == seg_ids[None, :]).astype(jnp.float32)
    partial_sums = jnp.dot(
        block_sums.reshape(1, -1),
        onehot,
        precision=lax.Precision.HIGHEST,
        preferred_element_type=jnp.float32,
    )[0]
    devices = lax.axis_size("blade") * lax.axis_size("span")
    pieces = lax.all_to_all(
        partial_sums.reshape(devices, -1), ("blade", "span"), 0, 0, tiled=True
    )
    return (adjoint, jnp.sum(pieces, axis=0) * scale)


def solution(mesh):
    placed = (
        P("blade", None, "span", None),
        P("blade", None, None),
        P("blade", None, "span", None),
        P("blade", None, "span", None),
        P("span", None),
        P(),
    )
    return jax.shard_map(
        per_device,
        mesh=mesh,
        in_specs=placed,
        out_specs=(P("blade", None, "span", None), P(("blade", "span"))),
        check_vma=False,
    )
```

```python
import functools
import math

import jax
import jax.numpy as jnp
from jax import lax
from jax.experimental import pallas as pl
from jax.experimental.pallas import tpu as pltpu
from jax.sharding import PartitionSpec as P

STEPS = 3
SEGS = 2048
F32 = jnp.float32
BF16 = jnp.bfloat16
VMEM = pl.BlockSpec(memory_space=pltpu.VMEM)
SMEM = pl.BlockSpec(memory_space=pltpu.SMEM)


def split(x):
    high = x.astype(BF16)
    return high, (x - high.astype(F32)).astype(BF16)


def dot(a, b):
    return jnp.dot(a, b, preferred_element_type=F32)


def dot3(a_high, a_low, b):
    b_high, b_low = split(b)
    return dot(a_high, b_high) + dot(a_high, b_low) + dot(a_low, b_high)


def iota(shape, dim):
    return lax.broadcasted_iota(jnp.int32, shape, dim)


def chord_next(x):
    last = x.ndim - 1
    size = x.shape[last]
    moved = pltpu.roll(x, size - 1, last)
    return jnp.where(iota(x.shape, last) == size - 1, 0.0, moved)


def chord_prev(x):
    last = x.ndim - 1
    moved = pltpu.roll(x, 1, last)
    return jnp.where(iota(x.shape, last) == 0, 0.0, moved)


def row_prev(x, edge):
    axis = x.ndim - 2
    return jnp.where(iota(x.shape, axis) == 0, edge, pltpu.roll(x, 1, axis))


def row_next(x, edge):
    axis = x.ndim - 2
    rows = x.shape[axis]
    return jnp.where(iota(x.shape, axis) == rows - 1, edge, pltpu.roll(x, rows - 1, axis))


def pack_kernel(k_ref, res_ref, up_ref, down_ref):
    depth, rows, _ = k_ref.shape
    frames = res_ref.shape[0]
    for out, near, far in ((up_ref, 0, 1), (down_ref, rows - 1, rows - 2)):
        out[0:depth, :] = k_ref[:, near, :]
        out[depth : 2 * depth, :] = k_ref[:, far, :]
        base = 2 * depth
        out[base : base + frames, :] = res_ref[:, near, :]
        out[base + frames : base + 2 * frames, :] = res_ref[:, far, :]


def weights_kernel(k_ref, d_ref, w_ref, mat_ref, edge_ref):
    depth, rows, cols = k_ref.shape
    size = depth * rows

    def body(i, _):
        half = 0.5 * k_ref[i]
        w_next = half + chord_next(half)
        w_prev = half + chord_prev(half)
        w_up = half + row_prev(half, 0.0)
        w_down = half + row_next(half, 0.0)
        w_ref[0, i] = 1.0 - (w_next + w_prev + w_up + w_down)
        w_ref[1, i] = w_next
        w_ref[2, i] = w_prev
        w_ref[3, i] = w_up
        w_ref[4, i] = w_down
        return 0

    lax.fori_loop(0, depth, body, 0, unroll=4)

    d_high, d_low = split(d_ref[...])
    tall = (iota((size, depth), 0) // rows == iota((size, depth), 1)).astype(BF16)
    wide = (iota((depth, size), 0) == iota((depth, size), 1) // rows).astype(BF16)
    same = iota((size, size), 0) % rows == iota((size, size), 1) % rows
    both = (iota((depth, 2 * depth), 0) == iota((depth, 2 * depth), 1) % depth).astype(BF16)
    row = iota((size, 2 * depth), 0) % rows
    left = iota((size, 2 * depth), 1) < depth
    at_edge = jnp.logical_or(
        jnp.logical_and(left, row == 0),
        jnp.logical_and(jnp.logical_not(left), row == rows - 1),
    )
    for n, part in enumerate((d_high, d_low)):
        column = dot(tall, part).astype(BF16)
        mat_ref[n] = jnp.where(same, dot(column, wide), 0.0).astype(BF16)
        edge_ref[n] = jnp.where(at_edge, dot(column, both), 0.0).astype(BF16)


def main_kernel(
    per_device_segments,
    scale,
    frame_ref,
    map_ref,
    d_ref,
    res_ref,
    excess_ref,
    w_ref,
    mat_ref,
    edge_ref,
    own_top_ref,
    own_bottom_ref,
    top_ref,
    bottom_ref,
    adj_ref,
    part_ref,
    halo_ref,
    source_ref,
    first_ref,
):
    depth, rows, cols = adj_ref.shape
    frames = res_ref.shape[0]
    size = depth * rows
    blocks = cols // 128
    span = lax.axis_index("span")
    last = lax.axis_size("span") - 1
    frame2 = frame_ref[2]
    frame1 = frame_ref[1]
    frame0 = frame_ref[0]
    base = 2 * depth
    first = d_ref[:, 0:1]
    is_surface = iota((depth, 1), 0) == 0

    halo_ref[...] = jnp.zeros_like(halo_ref)
    sources = []
    edges = ((top_ref, own_top_ref, 0, span > 0), (bottom_ref, own_bottom_ref, rows - 1, span < last))
    field_edges = []
    for got, own, row, inside in edges:
        half = 0.5 * got[0:depth, :]
        half_far = 0.5 * got[depth : 2 * depth, :]
        half_own = 0.5 * own[0:depth, :]
        f = got[pl.ds(base + frame2, 1), :]
        f_far = got[pl.ds(base + frames + frame2, 1), :]
        f_own = own[pl.ds(base + frame2, 1), :]
        g = got[pl.ds(base + frame1, 1), :]
        halo_ref[:, row, :] = half
        w_next = half + chord_next(half)
        w_prev = half + chord_prev(half)
        w_far = half + half_far
        w_own = half + half_own
        moved = (
            f
            + w_next * (chord_next(f) - f)
            + w_prev * (chord_prev(f) - f)
            + w_far * (f_far - f)
            + w_own * (f_own - f)
        )
        source = first * moved + jnp.where(is_surface, g, 0.0)
        sources.append(jnp.where(inside, source, 0.0))
        field_edges.append(f)
    halo_first = dot3(edge_ref[0], edge_ref[1], jnp.concatenate(sources, axis=0))

    f = res_ref[frame2]
    f_top, f_bottom = field_edges
    f_next = chord_next(f)
    f_prev = chord_prev(f)
    f_up = row_prev(f, f_top)
    f_down = row_next(f, f_bottom)
    row_id = iota((rows, cols), 0)
    f_edge = jnp.where(row_id == 0, f_top, f_bottom) - f

    def first_source(i, _):
        moved = (
            w_ref[0, i] * f
            + w_ref[1, i] * f_next
            + w_ref[2, i] * f_prev
            + w_ref[3, i] * f_up
            + w_ref[4, i] * f_down
            + halo_ref[i] * f_edge
        )
        source_ref[pl.ds(i * rows, rows), :] = d_ref[pl.ds(i, 1), 0:1] * moved
        return 0

    lax.fori_loop(0, depth, first_source, 0, unroll=4)
    source_ref[0:rows, :] += res_ref[frame1]
    first_ref[...] = dot3(mat_ref[0], mat_ref[1], source_ref[...])
    source_ref[...] = halo_first

    def second_source(i, _):
        v = first_ref[pl.ds(i * rows, rows), :]
        edge = source_ref[pl.ds(i * rows, rows), :]
        source_ref[pl.ds(i * rows, rows), :] = (
            w_ref[0, i] * v
            + w_ref[1, i] * chord_next(v)
            + w_ref[2, i] * chord_prev(v)
            + w_ref[3, i] * row_prev(v, edge)
            + w_ref[4, i] * row_next(v, edge)
            + halo_ref[i] * (edge - v)
        )
        return 0

    lax.fori_loop(0, depth, second_source, 0, unroll=4)
    source_ref[0:rows, :] += res_ref[frame0]
    result = dot3(mat_ref[0], mat_ref[1], source_ref[...])
    adj_ref[...] = result.reshape(depth, rows, cols)

    contribution = (
        d_ref[0:1, 0:1] * f * excess_ref[2]
        + first_ref[0:rows, :] * excess_ref[1]
        + result[0:rows, :] * excess_ref[0]
    ) * scale
    owners = part_ref.shape[0]
    lanes = part_ref.shape[-1]
    shape = (owners, 128)
    lane = iota(shape, 1)
    segment = jnp.where(lane < lanes, iota(shape, 0) * lanes + lane, -1)
    total = jnp.zeros(shape, F32)
    for block in range(blocks):
        sums = jnp.sum(contribution[:, block * 128 : (block + 1) * 128], axis=1, keepdims=True)
        for row in range(rows):
            total += jnp.where(segment == map_ref[row, block], sums[row : row + 1, :], 0.0)
    part_ref[...] = total[:, :lanes].reshape(part_ref.shape)


def per_device(
    conductance, depth_inverse, surface_residual, surface_excess, segment_map, frame_index
):
    _, depth, rows, cols = conductance.shape
    frames = surface_residual.shape[1]
    k = conductance[0]
    inverse = depth_inverse[0]
    residual = surface_residual[0]
    excess = surface_excess[0]
    size = depth * rows
    count = lax.axis_size("span")
    devices = count * lax.axis_size("blade")
    lanes = SEGS // devices
    packed = jax.ShapeDtypeStruct((2 * (depth + frames), cols), F32)
    up, down = pl.pallas_call(
        pack_kernel,
        out_shape=(packed, packed),
        in_specs=[VMEM] * 2,
        out_specs=(VMEM,) * 2,
        name="pack_edges",
    )(k, residual)
    top = lax.ppermute(down, "span", [(i, i + 1) for i in range(count - 1)])
    bottom = lax.ppermute(up, "span", [(i + 1, i) for i in range(count - 1)])
    weights, mat, edge = pl.pallas_call(
        weights_kernel,
        out_shape=(
            jax.ShapeDtypeStruct((5, depth, rows, cols), F32),
            jax.ShapeDtypeStruct((2, size, size), BF16),
            jax.ShapeDtypeStruct((2, size, 2 * depth), BF16),
        ),
        in_specs=[VMEM] * 2,
        out_specs=(VMEM,) * 3,
        compiler_params=pltpu.CompilerParams(vmem_limit_bytes=24 * 2**20),
        name="weights",
    )(k, inverse)
    scale = 1.0 / math.sqrt(128.0 * STEPS)
    adjoint, partial = pl.pallas_call(
        functools.partial(main_kernel, lanes, scale),
        out_shape=(
            jax.ShapeDtypeStruct((depth, rows, cols), F32),
            jax.ShapeDtypeStruct((devices, lanes), F32),
        ),
        in_specs=[SMEM, SMEM] + [VMEM] * 10,
        out_specs=(VMEM,) * 2,
        scratch_shapes=[pltpu.VMEM((depth, rows, cols), F32)] + [pltpu.VMEM((size, cols), F32)] * 2,
        compiler_params=pltpu.CompilerParams(vmem_limit_bytes=24 * 2**20),
        name="steps",
    )(
        frame_index,
        segment_map,
        inverse,
        residual,
        excess,
        weights,
        mat,
        edge,
        up,
        down,
        top,
        bottom,
    )
    pieces = lax.all_to_all(partial, ("blade", "span"), 0, 0, tiled=True)
    return (adjoint[None], jnp.sum(pieces, axis=0))


def solution(mesh):
    placed = (
        P("blade", None, "span", None),
        P("blade", None, None),
        P("blade", None, "span", None),
        P("blade", None, "span", None),
        P("span", None),
        P(),
    )
    return jax.shard_map(
        per_device,
        mesh=mesh,
        in_specs=placed,
        out_specs=(P("blade", None, "span", None), P(("blade", "span"))),
        check_vma=False,
    )
```

```python
import functools
import math

import jax
import jax.numpy as jnp
from jax import lax
from jax.experimental import pallas as pl
from jax.experimental.pallas import tpu as pltpu
from jax.sharding import PartitionSpec as P

STEPS = 3
SEGS = 2048
F32 = jnp.float32
BF16 = jnp.bfloat16
VMEM = pl.BlockSpec(memory_space=pltpu.VMEM)
HBM = pl.BlockSpec(memory_space=pltpu.HBM)


def split(x):
    high = x.astype(BF16)
    return high, (x - high.astype(F32)).astype(BF16)


def dot(a, b):
    return jnp.dot(a, b, preferred_element_type=F32)


def dot3(a_high, a_low, b):
    b_high, b_low = split(b)
    return dot(a_high, b_high) + dot(a_high, b_low) + dot(a_low, b_high)


def iota(shape, dim):
    return lax.broadcasted_iota(jnp.int32, shape, dim)


def chord_next(x):
    last = x.ndim - 1
    size = x.shape[last]
    moved = pltpu.roll(x, size - 1, last)
    return jnp.where(iota(x.shape, last) == size - 1, 0.0, moved)


def chord_prev(x):
    last = x.ndim - 1
    moved = pltpu.roll(x, 1, last)
    return jnp.where(iota(x.shape, last) == 0, 0.0, moved)


def row_prev(x, edge):
    axis = x.ndim - 2
    return jnp.where(iota(x.shape, axis) == 0, edge, pltpu.roll(x, 1, axis))


def row_next(x, edge):
    axis = x.ndim - 2
    rows = x.shape[axis]
    return jnp.where(iota(x.shape, axis) == rows - 1, edge, pltpu.roll(x, rows - 1, axis))


def load_kernel(
    frame_hbm,
    k_hbm,
    res_hbm,
    excess_hbm,
    d_hbm,
    map_hbm,
    up_ref,
    down_ref,
    k_ref,
    frames_ref,
    excess_ref,
    d_ref,
    map_ref,
    frame_ref,
    res_ref,
    sems,
):
    pairs = (
        (frame_hbm, frame_ref),
        (res_hbm, res_ref),
        (k_hbm, k_ref),
        (excess_hbm, excess_ref),
        (d_hbm, d_ref),
        (map_hbm, map_ref),
    )
    copies = [pltpu.make_async_copy(a, b, sems.at[n]) for n, (a, b) in enumerate(pairs)]
    for copy in copies:
        copy.start()
    depth, rows, cols = k_ref.shape
    base = 2 * depth
    copies[0].wait()
    copies[1].wait()
    for step in range(STEPS):
        frames_ref[step] = res_ref[frame_ref[step]]
    copies[2].wait()
    for out, near, far in ((up_ref, 0, 1), (down_ref, rows - 1, rows - 2)):
        out[0:depth, :] = k_ref[:, near, :]
        out[depth:base, :] = k_ref[:, far, :]
        out[base : base + 8, :] = jnp.concatenate(
            [
                frames_ref[2, near : near + 1, :],
                frames_ref[1, near : near + 1, :],
                frames_ref[2, far : far + 1, :],
                jnp.zeros((5, cols), F32),
            ],
            axis=0,
        )
    for copy in copies[3:]:
        copy.wait()


def weights_kernel(k_ref, d_ref, w_ref, mat_ref, edge_ref):
    depth, rows, cols = k_ref.shape
    size = depth * rows

    def body(i, _):
        half = 0.5 * k_ref[i]
        w_next = half + chord_next(half)
        w_prev = half + chord_prev(half)
        w_up = half + row_prev(half, 0.0)
        w_down = half + row_next(half, 0.0)
        w_ref[0, i] = 1.0 - (w_next + w_prev + w_up + w_down)
        w_ref[1, i] = w_next
        w_ref[2, i] = w_prev
        w_ref[3, i] = w_up
        w_ref[4, i] = w_down
        return 0

    lax.fori_loop(0, depth, body, 0, unroll=4)

    d_high, d_low = split(d_ref[...])
    tall = (iota((size, depth), 0) // rows == iota((size, depth), 1)).astype(BF16)
    wide = (iota((depth, size), 0) == iota((depth, size), 1) // rows).astype(BF16)
    same = iota((size, size), 0) % rows == iota((size, size), 1) % rows
    both = (iota((depth, 2 * depth), 0) == iota((depth, 2 * depth), 1) % depth).astype(BF16)
    row = iota((size, 2 * depth), 0) % rows
    left = iota((size, 2 * depth), 1) < depth
    at_edge = jnp.logical_or(
        jnp.logical_and(left, row == 0),
        jnp.logical_and(jnp.logical_not(left), row == rows - 1),
    )
    for n, part in enumerate((d_high, d_low)):
        column = dot(tall, part).astype(BF16)
        mat_ref[n] = jnp.where(same, dot(column, wide), 0.0).astype(BF16)
        edge_ref[n] = jnp.where(at_edge, dot(column, both), 0.0).astype(BF16)


def main_kernel(
    lanes,
    scale,
    map_vmem,
    d_ref,
    frames_ref,
    excess_ref,
    w_ref,
    mat_ref,
    edge_ref,
    own_top_ref,
    own_bottom_ref,
    top_ref,
    bottom_ref,
    adj_ref,
    part_ref,
    halo_ref,
    source_ref,
    first_ref,
    map_ref,
    map_sem,
):
    map_copy = pltpu.make_async_copy(map_vmem, map_ref, map_sem)
    map_copy.start()
    depth, rows, cols = adj_ref.shape
    blocks = cols // 128
    span = lax.axis_index("span")
    last = lax.axis_size("span") - 1
    base = 2 * depth
    first = d_ref[:, 0:1]
    is_surface = iota((depth, 1), 0) == 0

    halo_ref[...] = jnp.zeros_like(halo_ref)
    sources = []
    edges = ((top_ref, own_top_ref, 0, span > 0), (bottom_ref, own_bottom_ref, rows - 1, span < last))
    field_edges = []
    for got, own, row, inside in edges:
        half = 0.5 * got[0:depth, :]
        half_far = 0.5 * got[depth : 2 * depth, :]
        half_own = 0.5 * own[0:depth, :]
        f = got[base : base + 1, :]
        g = got[base + 1 : base + 2, :]
        f_far = got[base + 2 : base + 3, :]
        f_own = own[base : base + 1, :]
        halo_ref[:, row, :] = half
        w_next = half + chord_next(half)
        w_prev = half + chord_prev(half)
        w_far = half + half_far
        w_own = half + half_own
        moved = (
            f
            + w_next * (chord_next(f) - f)
            + w_prev * (chord_prev(f) - f)
            + w_far * (f_far - f)
            + w_own * (f_own - f)
        )
        source = first * moved + jnp.where(is_surface, g, 0.0)
        sources.append(jnp.where(inside, source, 0.0))
        field_edges.append(f)
    halo_first = dot3(edge_ref[0], edge_ref[1], jnp.concatenate(sources, axis=0))

    f = frames_ref[2]
    f_top, f_bottom = field_edges
    f_next = chord_next(f)
    f_prev = chord_prev(f)
    f_up = row_prev(f, f_top)
    f_down = row_next(f, f_bottom)
    row_id = iota((rows, cols), 0)
    f_edge = jnp.where(row_id == 0, f_top, f_bottom) - f

    def first_source(i, _):
        moved = (
            w_ref[0, i] * f
            + w_ref[1, i] * f_next
            + w_ref[2, i] * f_prev
            + w_ref[3, i] * f_up
            + w_ref[4, i] * f_down
            + halo_ref[i] * f_edge
        )
        source_ref[pl.ds(i * rows, rows), :] = d_ref[pl.ds(i, 1), 0:1] * moved
        return 0

    lax.fori_loop(0, depth, first_source, 0, unroll=4)
    source_ref[0:rows, :] += frames_ref[1]
    first_ref[...] = dot3(mat_ref[0], mat_ref[1], source_ref[...])
    source_ref[...] = halo_first

    def second_source(i, _):
        v = first_ref[pl.ds(i * rows, rows), :]
        edge = source_ref[pl.ds(i * rows, rows), :]
        source_ref[pl.ds(i * rows, rows), :] = (
            w_ref[0, i] * v
            + w_ref[1, i] * chord_next(v)
            + w_ref[2, i] * chord_prev(v)
            + w_ref[3, i] * row_prev(v, edge)
            + w_ref[4, i] * row_next(v, edge)
            + halo_ref[i] * (edge - v)
        )
        return 0

    lax.fori_loop(0, depth, second_source, 0, unroll=4)
    source_ref[0:rows, :] += frames_ref[0]
    result = dot3(mat_ref[0], mat_ref[1], source_ref[...])
    adj_ref[...] = result.reshape(depth, rows, cols)

    contribution = (
        d_ref[0:1, 0:1] * f * excess_ref[2]
        + first_ref[0:rows, :] * excess_ref[1]
        + result[0:rows, :] * excess_ref[0]
    ) * scale
    shape = part_ref.shape[0], part_ref.shape[2]
    place = iota(shape, 1)
    segment = (place // lanes * shape[0] + iota(shape, 0)) * lanes + place % lanes
    total = jnp.zeros(shape, F32)
    map_copy.wait()
    for block in range(blocks):
        sums = jnp.sum(contribution[:, block * 128 : (block + 1) * 128], axis=1, keepdims=True)
        for row in range(rows):
            total += jnp.where(segment == map_ref[block, row], sums[row : row + 1, :], 0.0)
    part_ref[...] = total[:, None, :]


def regroup_kernel(got_ref, out_ref):
    total = jnp.sum(got_ref[:, 0, :], axis=0, keepdims=True)
    lanes = out_ref.shape[2]
    for n in range(out_ref.shape[0]):
        out_ref[n] = total[:, n * lanes : (n + 1) * lanes]


def per_device(
    conductance, depth_inverse, surface_residual, surface_excess, segment_map, frame_index
):
    _, depth, rows, cols = conductance.shape
    frames = surface_residual.shape[1]
    blocks = segment_map.shape[1]
    size = depth * rows
    spans = lax.axis_size("span")
    blades = lax.axis_size("blade")
    lanes = SEGS // (spans * blades)
    packed = jax.ShapeDtypeStruct((2 * depth + 8, cols), F32)
    up, down, k, picked, excess, inverse, ids = pl.pallas_call(
        load_kernel,
        out_shape=(
            packed,
            packed,
            jax.ShapeDtypeStruct((depth, rows, cols), F32),
            jax.ShapeDtypeStruct((STEPS, rows, cols), F32),
            jax.ShapeDtypeStruct((STEPS, rows, cols), F32),
            jax.ShapeDtypeStruct((depth, depth), F32),
            jax.ShapeDtypeStruct((blocks, rows), jnp.int32),
        ),
        in_specs=[HBM] * 6,
        out_specs=(VMEM,) * 7,
        scratch_shapes=[
            pltpu.SMEM((STEPS,), jnp.int32),
            pltpu.VMEM((frames, rows, cols), F32),
            pltpu.SemaphoreType.DMA((6,)),
        ],
        compiler_params=pltpu.CompilerParams(vmem_limit_bytes=60 * 2**20),
        name="load",
    )(
        frame_index,
        conductance[0],
        surface_residual[0],
        surface_excess[0],
        depth_inverse[0],
        segment_map.T,
    )
    top = lax.ppermute(down, "span", [(i, i + 1) for i in range(spans - 1)])
    bottom = lax.ppermute(up, "span", [(i + 1, i) for i in range(spans - 1)])
    weights, mat, edge = pl.pallas_call(
        weights_kernel,
        out_shape=(
            jax.ShapeDtypeStruct((5, depth, rows, cols), F32),
            jax.ShapeDtypeStruct((2, size, size), BF16),
            jax.ShapeDtypeStruct((2, size, 2 * depth), BF16),
        ),
        in_specs=[VMEM] * 2,
        out_specs=(VMEM,) * 3,
        compiler_params=pltpu.CompilerParams(vmem_limit_bytes=24 * 2**20),
        name="weights",
    )(k, inverse)
    scale = 1.0 / math.sqrt(128.0 * STEPS)
    adjoint, partial = pl.pallas_call(
        functools.partial(main_kernel, lanes, scale),
        out_shape=(
            jax.ShapeDtypeStruct((depth, rows, cols), F32),
            jax.ShapeDtypeStruct((spans, 1, blades * lanes), F32),
        ),
        in_specs=[VMEM] * 11,
        out_specs=(VMEM,) * 2,
        scratch_shapes=[
            pltpu.VMEM((depth, rows, cols), F32),
            pltpu.VMEM((size, cols), F32),
            pltpu.VMEM((size, cols), F32),
            pltpu.SMEM((blocks, rows), jnp.int32),
            pltpu.SemaphoreType.DMA,
        ],
        compiler_params=pltpu.CompilerParams(vmem_limit_bytes=24 * 2**20),
        name="steps",
    )(ids, inverse, picked, excess, weights, mat, edge, up, down, top, bottom)
    pieces = pl.pallas_call(
        regroup_kernel,
        out_shape=jax.ShapeDtypeStruct((blades, 1, lanes), F32),
        in_specs=[VMEM],
        out_specs=VMEM,
        name="regroup",
    )(lax.all_to_all(partial, "span", 0, 0, tiled=True))
    owned = jnp.sum(lax.all_to_all(pieces, "blade", 0, 0, tiled=True), axis=(0, 1))
    return (adjoint[None], owned)


def solution(mesh):
    placed = (
        P("blade", None, "span", None),
        P("blade", None, None),
        P("blade", None, "span", None),
        P("blade", None, "span", None),
        P("span", None),
        P(),
    )
    return jax.shard_map(
        per_device,
        mesh=mesh,
        in_specs=placed,
        out_specs=(P("blade", None, "span", None), P(("blade", "span"))),
        check_vma=False,
    )
```

```python
import functools
import math

import jax
import jax.numpy as jnp
from jax import lax
from jax.experimental import pallas as pl
from jax.experimental.pallas import tpu as pltpu
from jax.sharding import PartitionSpec as P

STEPS = 3
SEGS = 2048
F32 = jnp.float32
BF16 = jnp.bfloat16
VMEM = pl.BlockSpec(memory_space=pltpu.VMEM)
HBM = pl.BlockSpec(memory_space=pltpu.HBM)
GRANT = 16 * 2**20


def split(x):
    high = x.astype(BF16)
    return high, (x - high.astype(F32)).astype(BF16)


def dot(a, b):
    return jnp.dot(a, b, preferred_element_type=F32)


def dot3(a_high, a_low, b):
    b_high, b_low = split(b)
    return dot(a_high, b_high) + dot(a_high, b_low) + dot(a_low, b_high)


def iota(shape, dim):
    return lax.broadcasted_iota(jnp.int32, shape, dim)


def chord_next(x):
    last = x.ndim - 1
    size = x.shape[last]
    moved = pltpu.roll(x, size - 1, last)
    return jnp.where(iota(x.shape, last) == size - 1, 0.0, moved)


def chord_prev(x):
    last = x.ndim - 1
    moved = pltpu.roll(x, 1, last)
    return jnp.where(iota(x.shape, last) == 0, 0.0, moved)


def row_prev(x, edge):
    axis = x.ndim - 2
    return jnp.where(iota(x.shape, axis) == 0, edge, pltpu.roll(x, 1, axis))


def row_next(x, edge):
    axis = x.ndim - 2
    rows = x.shape[axis]
    return jnp.where(iota(x.shape, axis) == rows - 1, edge, pltpu.roll(x, rows - 1, axis))


def load_kernel(
    frame_hbm,
    k_hbm,
    res_hbm,
    excess_hbm,
    d_hbm,
    map_hbm,
    up_ref,
    down_ref,
    k_ref,
    frames_ref,
    excess_ref,
    d_ref,
    map_ref,
    frame_ref,
    res_ref,
    sems,
):
    pairs = (
        (frame_hbm, frame_ref),
        (res_hbm, res_ref),
        (k_hbm, k_ref),
        (excess_hbm, excess_ref),
        (d_hbm, d_ref),
        (map_hbm, map_ref),
    )
    copies = [pltpu.make_async_copy(a, b, sems.at[n]) for n, (a, b) in enumerate(pairs)]
    for copy in copies:
        copy.start()
    depth, rows, cols = k_ref.shape
    base = 2 * depth
    copies[0].wait()
    copies[1].wait()
    for step in range(STEPS):
        frames_ref[step] = res_ref[frame_ref[step]]
    copies[2].wait()
    for out, near, far in ((up_ref, 0, 1), (down_ref, rows - 1, rows - 2)):
        out[0:depth, :] = k_ref[:, near, :]
        out[depth:base, :] = k_ref[:, far, :]
        out[base : base + 8, :] = jnp.concatenate(
            [
                frames_ref[2, near : near + 1, :],
                frames_ref[1, near : near + 1, :],
                frames_ref[2, far : far + 1, :],
                jnp.zeros((5, cols), F32),
            ],
            axis=0,
        )
    for copy in copies[3:]:
        copy.wait()


def weights_kernel(k_ref, d_ref, w_ref, mat_ref, edge_ref):
    depth, rows, cols = k_ref.shape
    size = depth * rows

    def body(i, _):
        half = 0.5 * k_ref[i]
        w_next = half + chord_next(half)
        w_prev = half + chord_prev(half)
        w_up = half + row_prev(half, 0.0)
        w_down = half + row_next(half, 0.0)
        w_ref[0, i] = 1.0 - (w_next + w_prev + w_up + w_down)
        w_ref[1, i] = w_next
        w_ref[2, i] = w_prev
        w_ref[3, i] = w_up
        w_ref[4, i] = w_down
        return 0

    lax.fori_loop(0, depth, body, 0, unroll=4)

    d_high, d_low = split(d_ref[...])
    tall = (iota((size, depth), 0) // rows == iota((size, depth), 1)).astype(BF16)
    wide = (iota((depth, size), 0) == iota((depth, size), 1) // rows).astype(BF16)
    same = iota((size, size), 0) % rows == iota((size, size), 1) % rows
    both = (iota((depth, 2 * depth), 0) == iota((depth, 2 * depth), 1) % depth).astype(BF16)
    row = iota((size, 2 * depth), 0) % rows
    left = iota((size, 2 * depth), 1) < depth
    at_edge = jnp.logical_or(
        jnp.logical_and(left, row == 0),
        jnp.logical_and(jnp.logical_not(left), row == rows - 1),
    )
    for n, part in enumerate((d_high, d_low)):
        column = dot(tall, part).astype(BF16)
        mat_ref[n] = jnp.where(same, dot(column, wide), 0.0).astype(BF16)
        edge_ref[n] = jnp.where(at_edge, dot(column, both), 0.0).astype(BF16)


def main_kernel(
    scale,
    map_vmem,
    d_ref,
    frames_ref,
    excess_ref,
    w_ref,
    mat_ref,
    edge_ref,
    own_top_ref,
    own_bottom_ref,
    top_ref,
    bottom_ref,
    adj_hbm,
    part_ref,
    adj_ref,
    halo_ref,
    source_ref,
    first_ref,
    map_ref,
    sems,
):
    map_copy = pltpu.make_async_copy(map_vmem, map_ref, sems.at[0])
    map_copy.start()
    depth, rows, cols = adj_ref.shape
    blocks = cols // 128
    span = lax.axis_index("span")
    last = lax.axis_size("span") - 1
    base = 2 * depth
    first = d_ref[:, 0:1]
    is_surface = iota((depth, 1), 0) == 0

    halo_ref[...] = jnp.zeros_like(halo_ref)
    sources = []
    edges = ((top_ref, own_top_ref, 0, span > 0), (bottom_ref, own_bottom_ref, rows - 1, span < last))
    field_edges = []
    for got, own, row, inside in edges:
        half = 0.5 * got[0:depth, :]
        half_far = 0.5 * got[depth : 2 * depth, :]
        half_own = 0.5 * own[0:depth, :]
        f = got[base : base + 1, :]
        g = got[base + 1 : base + 2, :]
        f_far = got[base + 2 : base + 3, :]
        f_own = own[base : base + 1, :]
        halo_ref[:, row, :] = half
        w_next = half + chord_next(half)
        w_prev = half + chord_prev(half)
        w_far = half + half_far
        w_own = half + half_own
        moved = (
            f
            + w_next * (chord_next(f) - f)
            + w_prev * (chord_prev(f) - f)
            + w_far * (f_far - f)
            + w_own * (f_own - f)
        )
        source = first * moved + jnp.where(is_surface, g, 0.0)
        sources.append(jnp.where(inside, source, 0.0))
        field_edges.append(f)
    halo_first = dot3(edge_ref[0], edge_ref[1], jnp.concatenate(sources, axis=0))

    f = frames_ref[2]
    f_top, f_bottom = field_edges
    f_next = chord_next(f)
    f_prev = chord_prev(f)
    f_up = row_prev(f, f_top)
    f_down = row_next(f, f_bottom)
    row_id = iota((rows, cols), 0)
    f_edge = jnp.where(row_id == 0, f_top, f_bottom) - f

    def first_source(i, _):
        moved = (
            w_ref[0, i] * f
            + w_ref[1, i] * f_next
            + w_ref[2, i] * f_prev
            + w_ref[3, i] * f_up
            + w_ref[4, i] * f_down
            + halo_ref[i] * f_edge
        )
        source_ref[pl.ds(i * rows, rows), :] = d_ref[pl.ds(i, 1), 0:1] * moved
        return 0

    lax.fori_loop(0, depth, first_source, 0, unroll=4)
    source_ref[0:rows, :] += frames_ref[1]
    first_ref[...] = dot3(mat_ref[0], mat_ref[1], source_ref[...])
    source_ref[...] = halo_first

    def second_source(i, _):
        v = first_ref[pl.ds(i * rows, rows), :]
        edge = source_ref[pl.ds(i * rows, rows), :]
        source_ref[pl.ds(i * rows, rows), :] = (
            w_ref[0, i] * v
            + w_ref[1, i] * chord_next(v)
            + w_ref[2, i] * chord_prev(v)
            + w_ref[3, i] * row_prev(v, edge)
            + w_ref[4, i] * row_next(v, edge)
            + halo_ref[i] * (edge - v)
        )
        return 0

    lax.fori_loop(0, depth, second_source, 0, unroll=4)
    source_ref[0:rows, :] += frames_ref[0]
    result = dot3(mat_ref[0], mat_ref[1], source_ref[...])
    adj_ref[...] = result.reshape(depth, rows, cols)
    adj_copy = pltpu.make_async_copy(adj_ref, adj_hbm, sems.at[1])
    adj_copy.start()

    contribution = (
        d_ref[0:1, 0:1] * f * excess_ref[2]
        + first_ref[0:rows, :] * excess_ref[1]
        + result[0:rows, :] * excess_ref[0]
    ) * scale
    owners, _, lanes = part_ref.shape
    shape = (owners, 128)
    lane = iota(shape, 1)
    segment = jnp.where(lane < lanes, iota(shape, 0) * lanes + lane, -1)
    total = jnp.zeros(shape, F32)
    map_copy.wait()
    for block in range(blocks):
        sums = jnp.sum(contribution[:, block * 128 : (block + 1) * 128], axis=1, keepdims=True)
        for row in range(rows):
            total += jnp.where(segment == map_ref[block, row], sums[row : row + 1, :], 0.0)
    part_ref[...] = total[:, None, :lanes]
    adj_copy.wait()


def per_device(
    conductance, depth_inverse, surface_residual, surface_excess, segment_map, frame_index
):
    _, depth, rows, cols = conductance.shape
    frames = surface_residual.shape[1]
    blocks = segment_map.shape[1]
    size = depth * rows
    spans = lax.axis_size("span")
    blades = lax.axis_size("blade")
    lanes = SEGS // (spans * blades)
    packed = pltpu.VMEM((2 * depth + 8, cols), F32)
    up, down, k, picked, excess, inverse, ids = pl.pallas_call(
        load_kernel,
        out_shape=(
            packed,
            packed,
            pltpu.VMEM((depth, rows, cols), F32),
            pltpu.VMEM((STEPS, rows, cols), F32),
            pltpu.VMEM((STEPS, rows, cols), F32),
            pltpu.VMEM((depth, depth), F32),
            pltpu.VMEM((blocks, rows), jnp.int32),
        ),
        in_specs=[HBM] * 6,
        out_specs=(VMEM,) * 7,
        scratch_shapes=[
            pltpu.SMEM((STEPS,), jnp.int32),
            pltpu.VMEM((frames, rows, cols), F32),
            pltpu.SemaphoreType.DMA((6,)),
        ],
        compiler_params=pltpu.CompilerParams(vmem_limit_bytes=GRANT),
        name="load",
    )(
        *(
            pltpu.with_memory_space_constraint(x, pltpu.HBM)
            for x in (
                frame_index,
                conductance[0],
                surface_residual[0],
                surface_excess[0],
                depth_inverse[0],
                segment_map.T,
            )
        )
    )
    top = lax.ppermute(down, "span", [(i, i + 1) for i in range(spans - 1)])
    bottom = lax.ppermute(up, "span", [(i + 1, i) for i in range(spans - 1)])
    weights, mat, edge = pl.pallas_call(
        weights_kernel,
        out_shape=(
            pltpu.VMEM((5, depth, rows, cols), F32),
            pltpu.VMEM((2, size, size), BF16),
            pltpu.VMEM((2, size, 2 * depth), BF16),
        ),
        in_specs=[VMEM] * 2,
        out_specs=(VMEM,) * 3,
        compiler_params=pltpu.CompilerParams(vmem_limit_bytes=GRANT),
        name="weights",
    )(k, inverse)
    scale = 1.0 / math.sqrt(128.0 * STEPS)
    adjoint, partial = pl.pallas_call(
        functools.partial(main_kernel, scale),
        out_shape=(
            pltpu.HBM((depth, rows, cols), F32),
            pltpu.VMEM((spans * blades, 1, lanes), F32),
        ),
        in_specs=[VMEM] * 11,
        out_specs=(HBM, VMEM),
        scratch_shapes=[
            pltpu.VMEM((depth, rows, cols), F32),
            pltpu.VMEM((depth, rows, cols), F32),
            pltpu.VMEM((size, cols), F32),
            pltpu.VMEM((size, cols), F32),
            pltpu.SMEM((blocks, rows), jnp.int32),
            pltpu.SemaphoreType.DMA((2,)),
        ],
        compiler_params=pltpu.CompilerParams(vmem_limit_bytes=GRANT),
        name="steps",
    )(ids, inverse, picked, excess, weights, mat, edge, up, down, top, bottom)
    pieces = lax.all_to_all(partial, ("blade", "span"), 0, 0, tiled=True)
    owned = jnp.sum(pieces, axis=(0, 1))
    return (adjoint[None], owned)


def solution(mesh):
    placed = (
        P("blade", None, "span", None),
        P("blade", None, None),
        P("blade", None, "span", None),
        P("blade", None, "span", None),
        P("span", None),
        P(),
    )
    return jax.shard_map(
        per_device,
        mesh=mesh,
        in_specs=placed,
        out_specs=(P("blade", None, "span", None), P(("blade", "span"))),
        check_vma=False,
    )
```

```python
import functools
import math

import jax
import jax.numpy as jnp
from jax import lax
from jax.experimental import pallas as pl
from jax.experimental.pallas import tpu as pltpu
from jax.sharding import PartitionSpec as P

STEPS = 3
SEGS = 2048
F32 = jnp.float32
BF16 = jnp.bfloat16
VMEM = pl.BlockSpec(memory_space=pltpu.VMEM)
HBM = pl.BlockSpec(memory_space=pltpu.HBM)
GRANT = pltpu.CompilerParams(vmem_limit_bytes=16 * 2**20)


def split(x):
    high = x.astype(BF16)
    return high, (x - high.astype(F32)).astype(BF16)


def dot(a, b):
    return jnp.dot(a, b, preferred_element_type=F32)


def left_three(matrix):
    high, low = matrix
    return jnp.concatenate([high, low, high], axis=1)


def right_three(x):
    high, low = split(x)
    return jnp.concatenate([high, high, low], axis=0)


def iota(shape, dim):
    return lax.broadcasted_iota(jnp.int32, shape, dim)


def shift_next(x, axis):
    size = x.shape[axis]
    return jnp.where(iota(x.shape, axis) == size - 1, 0.0, pltpu.roll(x, size - 1, axis))


def shift_prev(x, axis, first):
    return jnp.where(iota(x.shape, axis) == 0, first, pltpu.roll(x, 1, axis))


def divergence(v, weight, half, axis):
    flux = weight * (shift_next(v, axis) - v)
    return flux - shift_prev(flux, axis, half * v)


def sides(rows):
    span = lax.axis_index("span")
    count = lax.axis_size("span")
    even = lax.rem(span, 2) == 0
    has_next = span + 1 < count
    has_prev = span > 0
    return (
        (even, jnp.where(even, has_next, has_prev)),
        (jnp.logical_not(even), jnp.where(even, has_prev, has_next)),
    )


def load_kernel(
    frame_hbm,
    k_hbm,
    res_hbm,
    excess_hbm,
    d_hbm,
    map_hbm,
    far_ref,
    near_ref,
    k_ref,
    frames_ref,
    excess_ref,
    d_ref,
    map_ref,
    frame_ref,
    res_ref,
    sems,
):
    pairs = (
        (frame_hbm, frame_ref),
        (res_hbm, res_ref),
        (k_hbm, k_ref),
        (excess_hbm, excess_ref),
        (d_hbm, d_ref),
        (map_hbm, map_ref),
    )
    copies = [pltpu.make_async_copy(a, b, sems.at[n]) for n, (a, b) in enumerate(pairs)]
    for copy in copies:
        copy.start()
    depth, rows, cols = k_ref.shape
    base = 2 * depth
    even = lax.rem(lax.axis_index("span"), 2) == 0
    copies[0].wait()
    copies[1].wait()
    for step in range(STEPS):
        frames_ref[step] = res_ref[frame_ref[step]]
    copies[2].wait()
    edges = []
    for edge, second in ((0, 1), (rows - 1, rows - 2)):
        fields = [
            frames_ref[2, edge : edge + 1, :],
            frames_ref[1, edge : edge + 1, :],
            frames_ref[2, second : second + 1, :],
            jnp.zeros((5, cols), F32),
        ]
        edges.append((k_ref[:, edge, :], k_ref[:, second, :], jnp.concatenate(fields, axis=0)))
    starts = (0, depth, base, base + 8)
    for n in range(3):
        first, last = edges[0][n], edges[1][n]
        near_ref[starts[n] : starts[n + 1], :] = jnp.where(even, last, first)
        far_ref[starts[n] : starts[n + 1], :] = jnp.where(even, first, last)
    for copy in copies[3:]:
        copy.wait()


def base_kernel(
    scale,
    k_ref,
    frames_ref,
    excess_ref,
    d_ref,
    adj_ref,
    edge_ref,
    contribution_ref,
    quad_ref,
    place_ref,
    mat_ref,
    right_ref,
    first_ref,
    chord_ref,
    span_ref,
    factor_ref,
):
    depth, rows, cols = k_ref.shape
    size = depth * rows
    factor_ref[...] = jnp.broadcast_to(d_ref[:, 0:1], factor_ref.shape)

    parts = split(d_ref[...])
    tall = (iota((size, depth), 0) // rows == iota((size, depth), 1)).astype(BF16)
    wide = (iota((depth, size), 0) == iota((depth, size), 1) // rows).astype(BF16)
    four = 4 * depth
    tile = (iota((depth, four), 0) == iota((depth, four), 1) % depth).astype(BF16)
    same = iota((size, size), 0) % rows == iota((size, size), 1) % rows
    quad_same = iota((four, four), 0) // depth == iota((four, four), 1) // depth
    targets = []
    for after, _ in sides(rows):
        targets.append(jnp.where(after, rows - 1, 0))
        targets.append(jnp.where(after, rows - 2, 1))
    which = iota((size, four), 1) // depth
    target = jnp.where(
        which == 0,
        targets[0],
        jnp.where(which == 1, targets[1], jnp.where(which == 2, targets[2], targets[3])),
    )
    placed = iota((size, four), 0) % rows == target
    mats, quads, places = [], [], []
    for part in parts:
        column = dot(tall, part).astype(BF16)
        row = dot(part, tile)
        mats.append(jnp.where(same, dot(column, wide), 0.0).astype(BF16))
        places.append(jnp.where(placed, dot(column, tile), 0.0).astype(BF16))
        stacked = jnp.concatenate([row] * 4, axis=0)
        quads.append(jnp.where(quad_same, stacked, 0.0).astype(BF16))
    mat_ref[...] = left_three(mats)
    quad_ref[...] = left_three(quads)
    place_ref[...] = left_three(places)

    f = frames_ref[2]
    f_chord = shift_next(f, 1) - f
    f_span = shift_next(f, 0) - f

    def put(i, both):
        high, low = split(both)
        span = pl.ds(i * rows, 2 * rows)
        right_ref[0, span, :] = high
        right_ref[1, span, :] = high
        right_ref[2, span, :] = low

    for i in range(0, depth, 2):
        found = []
        for j in (i, i + 1):
            half = 0.5 * k_ref[j]
            w_chord = half + shift_next(half, 1)
            w_span = half + shift_next(half, 0)
            chord_ref[j] = w_chord
            span_ref[j] = w_span
            edge = half * f
            flux_chord = w_chord * f_chord
            flux_span = w_span * f_span
            moved = f + flux_chord - shift_prev(flux_chord, 1, edge)
            moved = moved + flux_span - shift_prev(flux_span, 0, edge)
            factor = jnp.concatenate(
                [jnp.broadcast_to(factor_ref[j : j + 1, :], (rows, 128))] * (cols // 128), axis=1
            )
            source = factor * moved
            found.append(source + frames_ref[1] if j == 0 else source)
        put(i, jnp.concatenate(found, axis=0))
    right = right_ref[...].reshape(3 * size, cols)
    first_ref[...] = dot(mat_ref[...], right).reshape(depth, rows, cols)

    for i in range(0, depth, 2):
        found = []
        for j in (i, i + 1):
            v = first_ref[j]
            half = 0.5 * k_ref[j]
            source = (
                v + divergence(v, chord_ref[j], half, 1) + divergence(v, span_ref[j], half, 0)
            )
            found.append(source + frames_ref[0] if j == 0 else source)
        put(i, jnp.concatenate(found, axis=0))
    right = right_ref[...].reshape(3 * size, cols)
    adj_ref[...] = dot(mat_ref[...], right).reshape(depth, rows, cols)

    top = first_ref[:, 0, :]
    bottom = first_ref[:, rows - 1, :]
    for n, (after, _) in enumerate(sides(rows)):
        edge_ref[n] = jnp.where(after, bottom, top)
    contribution_ref[...] = scale * (
        d_ref[0:1, 0:1] * f * excess_ref[2]
        + first_ref[0] * excess_ref[1]
        + adj_ref[0] * excess_ref[0]
    )


def correct_kernel(
    scale,
    map_vmem,
    d_ref,
    excess_ref,
    base_ref,
    edge_ref,
    contribution_ref,
    quad_ref,
    place_ref,
    own_far_ref,
    own_near_ref,
    far_ref,
    near_ref,
    adj_hbm,
    part_ref,
    adj_ref,
    map_ref,
    sems,
):
    map_copy = pltpu.make_async_copy(map_vmem, map_ref, sems.at[0])
    map_copy.start()
    depth, rows, cols = base_ref.shape
    blocks = cols // 128
    base = 2 * depth
    factor = d_ref[:, 0:1]
    surface = iota((depth, 1), 0) == 0

    kept = []
    sources = []
    pairs = ((near_ref, own_near_ref), (far_ref, own_far_ref))
    for (got, own), (after, inside) in zip(pairs, sides(rows)):
        half = 0.5 * got[0:depth, :]
        half_next = 0.5 * got[depth:base, :]
        half_own = 0.5 * own[0:depth, :]
        half_second = 0.5 * own[depth:base, :]
        f = got[base : base + 1, :]
        frame = got[base + 1 : base + 2, :]
        f_next = got[base + 2 : base + 3, :]
        f_own = own[base : base + 1, :]
        face = half + half_own
        w_chord = half + shift_next(half, 1)
        flux = w_chord * (shift_next(f, 1) - f)
        moved = (
            f
            + flux
            - shift_prev(flux, 1, half * f)
            + (half + half_next) * (f_next - f)
            + face * (f_own - f)
        )
        outer = factor * moved + jnp.where(surface, frame, 0.0)
        sources.append(factor * (face * f - half * f_own))
        sources.append(jnp.where(inside, outer, 0.0))
        kept.append((half, half_own, half_own + half_second, face, after))
    found = dot(quad_ref[...], right_three(jnp.concatenate(sources, axis=0)))

    sources = []
    surfaces = []
    for n, (half, half_own, inner, face, after) in enumerate(kept):
        e = found[2 * n * depth : (2 * n + 1) * depth]
        outer = found[(2 * n + 1) * depth : (2 * n + 2) * depth]
        w_chord = half_own + shift_next(half_own, 1)
        change = (
            e
            + divergence(e, w_chord, half_own, 1)
            - (half + half_own + inner) * e
            + face * outer
            - half * edge_ref[n]
        )
        sources.append(change)
        sources.append(inner * e)
        row = jnp.where(after, rows - 1, 0)
        surfaces.append(jnp.where(iota((rows, cols), 0) == row, e[0:1, :], 0.0))
    found = dot(place_ref[...], right_three(jnp.concatenate(sources, axis=0)))
    adj_ref[...] = base_ref[...] + found.reshape(depth, rows, cols)
    adj_copy = pltpu.make_async_copy(adj_ref, adj_hbm, sems.at[1])
    adj_copy.start()

    contribution = contribution_ref[...] + scale * (
        (surfaces[0] + surfaces[1]) * excess_ref[1] + found[0:rows, :] * excess_ref[0]
    )
    owners, _, lanes = part_ref.shape
    shape = (owners, 128)
    lane = iota(shape, 1)
    segment = jnp.where(lane < lanes, iota(shape, 0) * lanes + lane, -1)
    total = jnp.zeros(shape, F32)
    map_copy.wait()
    for block in range(blocks):
        sums = jnp.sum(contribution[:, block * 128 : (block + 1) * 128], axis=1, keepdims=True)
        for row in range(rows):
            total += jnp.where(segment == map_ref[block, row], sums[row : row + 1, :], 0.0)
    part_ref[...] = total[:, None, :lanes]
    adj_copy.wait()


def per_device(
    conductance, depth_inverse, surface_residual, surface_excess, segment_map, frame_index
):
    _, depth, rows, cols = conductance.shape
    frames = surface_residual.shape[1]
    blocks = segment_map.shape[1]
    size = depth * rows
    four = 4 * depth
    spans = lax.axis_size("span")
    devices = spans * lax.axis_size("blade")
    lanes = SEGS // devices
    field = pltpu.VMEM((depth, rows, cols), F32)
    packed = pltpu.VMEM((2 * depth + 8, cols), F32)
    own_far, own_near, k, picked, excess, inverse, ids = pl.pallas_call(
        load_kernel,
        out_shape=(
            packed,
            packed,
            field,
            pltpu.VMEM((STEPS, rows, cols), F32),
            pltpu.VMEM((STEPS, rows, cols), F32),
            pltpu.VMEM((depth, depth), F32),
            pltpu.VMEM((blocks, rows), jnp.int32),
        ),
        in_specs=[HBM] * 6,
        out_specs=(VMEM,) * 7,
        scratch_shapes=[
            pltpu.SMEM((STEPS,), jnp.int32),
            pltpu.VMEM((frames, rows, cols), F32),
            pltpu.SemaphoreType.DMA((6,)),
        ],
        compiler_params=GRANT,
        name="load",
    )(
        *(
            pltpu.with_memory_space_constraint(x, pltpu.HBM)
            for x in (
                frame_index,
                conductance[0],
                surface_residual[0],
                surface_excess[0],
                depth_inverse[0],
                segment_map.T,
            )
        )
    )
    across = [(i, i + 1) for i in range(1, spans - 1, 2)]
    within = [(i, i + 1) for i in range(0, spans - 1, 2)]
    near = lax.ppermute(own_near, "span", within + [(b, a) for a, b in within])
    far = lax.ppermute(own_far, "span", across + [(b, a) for a, b in across])
    scale = 1.0 / math.sqrt(128.0 * STEPS)
    base, edge, contribution, quad, place = pl.pallas_call(
        functools.partial(base_kernel, scale),
        out_shape=(
            field,
            pltpu.VMEM((2, depth, cols), F32),
            pltpu.VMEM((rows, cols), F32),
            pltpu.VMEM((four, 3 * four), BF16),
            pltpu.VMEM((size, 3 * four), BF16),
        ),
        in_specs=[VMEM] * 4,
        out_specs=(VMEM,) * 5,
        scratch_shapes=[
            pltpu.VMEM((size, 3 * size), BF16),
            pltpu.VMEM((3, size, cols), BF16),
            field,
            field,
            field,
            pltpu.VMEM((depth, 128), F32),
        ],
        compiler_params=GRANT,
        name="base",
    )(k, picked, excess, inverse)
    adjoint, partial = pl.pallas_call(
        functools.partial(correct_kernel, scale),
        out_shape=(
            pltpu.HBM((depth, rows, cols), F32),
            pltpu.VMEM((devices, 1, lanes), F32),
        ),
        in_specs=[VMEM] * 12,
        out_specs=(HBM, VMEM),
        scratch_shapes=[
            field,
            pltpu.SMEM((blocks, rows), jnp.int32),
            pltpu.SemaphoreType.DMA((2,)),
        ],
        compiler_params=GRANT,
        name="correct",
    )(
        ids,
        inverse,
        excess,
        base,
        edge,
        contribution,
        quad,
        place,
        own_far,
        own_near,
        far,
        near,
    )
    pieces = lax.all_to_all(partial, ("blade", "span"), 0, 0, tiled=True)
    return (adjoint[None], jnp.sum(pieces, axis=(0, 1)))


def solution(mesh):
    placed = (
        P("blade", None, "span", None),
        P("blade", None, None),
        P("blade", None, "span", None),
        P("blade", None, "span", None),
        P("span", None),
        P(),
    )
    return jax.shard_map(
        per_device,
        mesh=mesh,
        in_specs=placed,
        out_specs=(P("blade", None, "span", None), P(("blade", "span"))),
        check_vma=False,
    )
```

```python
import functools
import math

import jax
import jax.numpy as jnp
from jax import lax
from jax.experimental import pallas as pl
from jax.experimental.pallas import tpu as pltpu
from jax.sharding import PartitionSpec as P

STEPS = 3
SEGS = 2048
F32 = jnp.float32
BF16 = jnp.bfloat16
VMEM = pl.BlockSpec(memory_space=pltpu.VMEM)
HBM = pl.BlockSpec(memory_space=pltpu.HBM)
GRANT = pltpu.CompilerParams(vmem_limit_bytes=16 * 2**20)


def split(x):
    high = x.astype(BF16)
    return high, (x - high.astype(F32)).astype(BF16)


def dot(a, b):
    return jnp.dot(a, b, preferred_element_type=F32)


def left_three(matrix):
    high, low = matrix
    return jnp.concatenate([high, low, high], axis=1)


def right_three(x):
    high, low = split(x)
    return jnp.concatenate([high, high, low], axis=0)


def iota(shape, dim):
    return lax.broadcasted_iota(jnp.int32, shape, dim)


def shift_next(x, axis):
    size = x.shape[axis]
    return jnp.where(iota(x.shape, axis) == size - 1, 0.0, pltpu.roll(x, size - 1, axis))


def shift_prev(x, axis, first):
    return jnp.where(iota(x.shape, axis) == 0, first, pltpu.roll(x, 1, axis))


def divergence(v, weight, half, axis):
    flux = weight * (shift_next(v, axis) - v)
    return flux - shift_prev(flux, axis, half * v)


def sides(rows):
    span = lax.axis_index("span")
    count = lax.axis_size("span")
    even = lax.rem(span, 2) == 0
    has_next = span + 1 < count
    has_prev = span > 0
    return (
        (even, jnp.where(even, has_next, has_prev)),
        (jnp.logical_not(even), jnp.where(even, has_prev, has_next)),
    )


def load_kernel(
    frame_hbm,
    k_hbm,
    res_hbm,
    excess_hbm,
    d_hbm,
    map_hbm,
    far_ref,
    near_ref,
    k_ref,
    frames_ref,
    excess_ref,
    d_ref,
    map_ref,
    frame_ref,
    res_ref,
    sems,
):
    pairs = (
        (frame_hbm, frame_ref),
        (res_hbm, res_ref),
        (k_hbm, k_ref),
        (excess_hbm, excess_ref),
        (d_hbm, d_ref),
        (map_hbm, map_ref),
    )
    copies = [pltpu.make_async_copy(a, b, sems.at[n]) for n, (a, b) in enumerate(pairs)]
    for copy in copies:
        copy.start()
    depth, rows, cols = k_ref.shape
    base = 2 * depth
    even = lax.rem(lax.axis_index("span"), 2) == 0
    copies[0].wait()
    copies[1].wait()
    for step in range(STEPS):
        frames_ref[step] = res_ref[frame_ref[step]]
    copies[2].wait()
    edges = []
    for edge, second in ((0, 1), (rows - 1, rows - 2)):
        fields = [
            frames_ref[2, edge : edge + 1, :],
            frames_ref[1, edge : edge + 1, :],
            frames_ref[2, second : second + 1, :],
            jnp.zeros((5, cols), F32),
        ]
        edges.append((k_ref[:, edge, :], k_ref[:, second, :], jnp.concatenate(fields, axis=0)))
    starts = (0, depth, base, base + 8)
    for n in range(3):
        first, last = edges[0][n], edges[1][n]
        near_ref[starts[n] : starts[n + 1], :] = jnp.where(even, last, first)
        far_ref[starts[n] : starts[n + 1], :] = jnp.where(even, first, last)
    for copy in copies[3:]:
        copy.wait()


def base_kernel(
    scale,
    k_ref,
    frames_ref,
    excess_ref,
    d_ref,
    adj_ref,
    edge_ref,
    contribution_ref,
    quad_ref,
    place_ref,
    mat_ref,
    right_ref,
    first_ref,
    chord_ref,
    span_ref,
    factor_ref,
):
    depth, rows, cols = k_ref.shape
    size = depth * rows
    factor_ref[...] = jnp.broadcast_to(d_ref[:, 0:1], factor_ref.shape)

    parts = split(d_ref[...])
    tall = (iota((size, depth), 0) // rows == iota((size, depth), 1)).astype(BF16)
    wide = (iota((depth, size), 0) == iota((depth, size), 1) // rows).astype(BF16)
    four = 4 * depth
    tile = (iota((depth, four), 0) == iota((depth, four), 1) % depth).astype(BF16)
    same = iota((size, size), 0) % rows == iota((size, size), 1) % rows
    quad_same = iota((four, four), 0) // depth == iota((four, four), 1) // depth
    targets = []
    for after, _ in sides(rows):
        targets.append(jnp.where(after, rows - 1, 0))
        targets.append(jnp.where(after, rows - 2, 1))
    which = iota((size, four), 1) // depth
    target = jnp.where(
        which == 0,
        targets[0],
        jnp.where(which == 1, targets[1], jnp.where(which == 2, targets[2], targets[3])),
    )
    placed = iota((size, four), 0) % rows == target
    mats, quads, places = [], [], []
    for part in parts:
        column = dot(tall, part).astype(BF16)
        row = dot(part, tile)
        mats.append(jnp.where(same, dot(column, wide), 0.0).astype(BF16))
        places.append(jnp.where(placed, dot(column, tile), 0.0).astype(BF16))
        stacked = jnp.concatenate([row] * 4, axis=0)
        quads.append(jnp.where(quad_same, stacked, 0.0).astype(BF16))
    mat_ref[...] = left_three(mats)
    quad_ref[...] = left_three(quads)
    place_ref[...] = left_three(places)

    f = frames_ref[2]
    f_chord = shift_next(f, 1) - f
    f_span = shift_next(f, 0) - f

    def put(i, both):
        high, low = split(both)
        span = pl.ds(i * rows, 2 * rows)
        right_ref[0, span, :] = high
        right_ref[1, span, :] = high
        right_ref[2, span, :] = low

    for i in range(0, depth, 2):
        found = []
        for j in (i, i + 1):
            half = 0.5 * k_ref[j]
            w_chord = half + shift_next(half, 1)
            w_span = half + shift_next(half, 0)
            chord_ref[j] = w_chord
            span_ref[j] = w_span
            edge = half * f
            flux_chord = w_chord * f_chord
            flux_span = w_span * f_span
            moved = f + flux_chord - shift_prev(flux_chord, 1, edge)
            moved = moved + flux_span - shift_prev(flux_span, 0, edge)
            factor = jnp.concatenate(
                [jnp.broadcast_to(factor_ref[j : j + 1, :], (rows, 128))] * (cols // 128), axis=1
            )
            source = factor * moved
            found.append(source + frames_ref[1] if j == 0 else source)
        put(i, jnp.concatenate(found, axis=0))
    right = right_ref[...].reshape(3 * size, cols)
    first_ref[...] = dot(mat_ref[...], right).reshape(depth, rows, cols)

    for i in range(0, depth, 2):
        found = []
        for j in (i, i + 1):
            v = first_ref[j]
            half = 0.5 * k_ref[j]
            source = (
                v + divergence(v, chord_ref[j], half, 1) + divergence(v, span_ref[j], half, 0)
            )
            found.append(source + frames_ref[0] if j == 0 else source)
        put(i, jnp.concatenate(found, axis=0))
    right = right_ref[...].reshape(3 * size, cols)
    adj_ref[...] = dot(mat_ref[...], right).reshape(depth, rows, cols)

    top = first_ref[:, 0, :]
    bottom = first_ref[:, rows - 1, :]
    for n, (after, _) in enumerate(sides(rows)):
        edge_ref[n] = jnp.where(after, bottom, top)
    contribution_ref[...] = scale * (
        d_ref[0:1, 0:1] * f * excess_ref[2]
        + first_ref[0] * excess_ref[1]
        + adj_ref[0] * excess_ref[0]
    )


def correct_kernel(
    scale,
    map_vmem,
    d_ref,
    excess_ref,
    base_ref,
    edge_ref,
    contribution_ref,
    quad_ref,
    place_ref,
    own_far_ref,
    own_near_ref,
    far_ref,
    near_ref,
    adj_hbm,
    part_ref,
    adj_ref,
    map_ref,
    sems,
):
    map_copy = pltpu.make_async_copy(map_vmem, map_ref, sems.at[0])
    map_copy.start()
    depth, rows, cols = base_ref.shape
    blocks = cols // 128
    base = 2 * depth
    factor = d_ref[:, 0:1]
    surface = iota((depth, 1), 0) == 0

    kept = []
    sources = []
    pairs = ((near_ref, own_near_ref), (far_ref, own_far_ref))
    for (got, own), (after, inside) in zip(pairs, sides(rows)):
        half = 0.5 * got[0:depth, :]
        half_next = 0.5 * got[depth:base, :]
        half_own = 0.5 * own[0:depth, :]
        half_second = 0.5 * own[depth:base, :]
        f = got[base : base + 1, :]
        frame = got[base + 1 : base + 2, :]
        f_next = got[base + 2 : base + 3, :]
        f_own = own[base : base + 1, :]
        face = half + half_own
        w_chord = half + shift_next(half, 1)
        flux = w_chord * (shift_next(f, 1) - f)
        moved = (
            f
            + flux
            - shift_prev(flux, 1, half * f)
            + (half + half_next) * (f_next - f)
            + face * (f_own - f)
        )
        outer = factor * moved + jnp.where(surface, frame, 0.0)
        sources.append(factor * (face * f - half * f_own))
        sources.append(jnp.where(inside, outer, 0.0))
        kept.append((half, half_own, half_own + half_second, face, after))
    found = dot(quad_ref[...], right_three(jnp.concatenate(sources, axis=0)))

    sources = []
    surfaces = []
    for n, (half, half_own, inner, face, after) in enumerate(kept):
        e = found[2 * n * depth : (2 * n + 1) * depth]
        outer = found[(2 * n + 1) * depth : (2 * n + 2) * depth]
        w_chord = half_own + shift_next(half_own, 1)
        change = (
            e
            + divergence(e, w_chord, half_own, 1)
            - (half + half_own + inner) * e
            + face * outer
            - half * edge_ref[n]
        )
        sources.append(change)
        sources.append(inner * e)
        row = jnp.where(after, rows - 1, 0)
        surfaces.append(jnp.where(iota((rows, cols), 0) == row, e[0:1, :], 0.0))
    found = dot(place_ref[...], right_three(jnp.concatenate(sources, axis=0)))
    adj_ref[...] = base_ref[...] + found.reshape(depth, rows, cols)
    adj_copy = pltpu.make_async_copy(adj_ref, adj_hbm, sems.at[1])
    adj_copy.start()

    contribution = contribution_ref[...] + scale * (
        (surfaces[0] + surfaces[1]) * excess_ref[1] + found[0:rows, :] * excess_ref[0]
    )
    shape = (rows, 128)
    lane = iota(shape, 1)
    held = jnp.zeros(shape, F32)
    for block in range(blocks):
        sums = jnp.sum(contribution[:, block * 128 : (block + 1) * 128], axis=1, keepdims=True)
        held += jnp.where(lane == block * rows + iota(shape, 0), sums, 0.0)
    line = jnp.sum(held, axis=0, keepdims=True)
    place = iota((1, 128), 1)
    map_copy.wait()
    for block in range(blocks):
        for row in range(rows):
            spot = (blocks + block) * rows + row
            line = jnp.where(place == spot, map_ref[block, row].astype(F32), line)
    part_ref[...] = line
    adj_copy.wait()


def pick_kernel(spans, lanes, entries, got_ref, out_ref):
    devices = got_ref.shape[0]
    mine = lax.axis_index("blade") * spans + lax.axis_index("span")
    segment = (iota((lanes, entries), 0) + mine * lanes).astype(F32)
    sums = jnp.sum(got_ref[...].reshape(devices // spans, spans, 128), axis=0)
    total = jnp.zeros((8, lanes), F32)
    for n in range(spans):
        hit = (got_ref[n : n + 1, entries : 2 * entries] == segment).astype(BF16)
        value = sums[n : n + 1, 0:entries]
        high, rest = split(value)
        low = (value - high.astype(F32) - rest.astype(F32)).astype(BF16)
        rows = jnp.concatenate([high, rest, low, jnp.zeros((5, entries), BF16)], axis=0)
        total += lax.dot_general(
            rows, hit, (((1,), (1,)), ((), ())), preferred_element_type=F32
        )
    out_ref[...] = jnp.sum(total, axis=0)


def per_device(
    conductance, depth_inverse, surface_residual, surface_excess, segment_map, frame_index
):
    _, depth, rows, cols = conductance.shape
    frames = surface_residual.shape[1]
    blocks = segment_map.shape[1]
    size = depth * rows
    four = 4 * depth
    spans = lax.axis_size("span")
    devices = spans * lax.axis_size("blade")
    lanes = SEGS // devices
    field = pltpu.VMEM((depth, rows, cols), F32)
    packed = pltpu.VMEM((2 * depth + 8, cols), F32)
    own_far, own_near, k, picked, excess, inverse, ids = pl.pallas_call(
        load_kernel,
        out_shape=(
            packed,
            packed,
            field,
            pltpu.VMEM((STEPS, rows, cols), F32),
            pltpu.VMEM((STEPS, rows, cols), F32),
            pltpu.VMEM((depth, depth), F32),
            pltpu.VMEM((blocks, rows), jnp.int32),
        ),
        in_specs=[HBM] * 6,
        out_specs=(VMEM,) * 7,
        scratch_shapes=[
            pltpu.SMEM((STEPS,), jnp.int32),
            pltpu.VMEM((frames, rows, cols), F32),
            pltpu.SemaphoreType.DMA((6,)),
        ],
        compiler_params=GRANT,
        name="load",
    )(
        *(
            pltpu.with_memory_space_constraint(x, pltpu.HBM)
            for x in (
                frame_index,
                conductance[0],
                surface_residual[0],
                surface_excess[0],
                depth_inverse[0],
                segment_map.T,
            )
        )
    )
    across = [(i, i + 1) for i in range(1, spans - 1, 2)]
    within = [(i, i + 1) for i in range(0, spans - 1, 2)]
    near = lax.ppermute(own_near, "span", within + [(b, a) for a, b in within])
    far = lax.ppermute(own_far, "span", across + [(b, a) for a, b in across])
    scale = 1.0 / math.sqrt(128.0 * STEPS)
    base, edge, contribution, quad, place = pl.pallas_call(
        functools.partial(base_kernel, scale),
        out_shape=(
            field,
            pltpu.VMEM((2, depth, cols), F32),
            pltpu.VMEM((rows, cols), F32),
            pltpu.VMEM((four, 3 * four), BF16),
            pltpu.VMEM((size, 3 * four), BF16),
        ),
        in_specs=[VMEM] * 4,
        out_specs=(VMEM,) * 5,
        scratch_shapes=[
            pltpu.VMEM((size, 3 * size), BF16),
            pltpu.VMEM((3, size, cols), BF16),
            field,
            field,
            field,
            pltpu.VMEM((depth, 128), F32),
        ],
        compiler_params=GRANT,
        name="base",
    )(k, picked, excess, inverse)
    adjoint, partial = pl.pallas_call(
        functools.partial(correct_kernel, scale),
        out_shape=(
            pltpu.HBM((depth, rows, cols), F32),
            pltpu.VMEM((1, 128), F32),
        ),
        in_specs=[VMEM] * 12,
        out_specs=(HBM, VMEM),
        scratch_shapes=[
            field,
            pltpu.SMEM((blocks, rows), jnp.int32),
            pltpu.SemaphoreType.DMA((2,)),
        ],
        compiler_params=GRANT,
        name="correct",
    )(
        ids,
        inverse,
        excess,
        base,
        edge,
        contribution,
        quad,
        place,
        own_far,
        own_near,
        far,
        near,
    )
    pieces = lax.all_gather(partial, ("blade", "span"), axis=0, tiled=True)
    owned = pl.pallas_call(
        functools.partial(pick_kernel, spans, lanes, blocks * rows),
        out_shape=pltpu.HBM((lanes,), F32),
        in_specs=[VMEM],
        out_specs=VMEM,
        compiler_params=GRANT,
        name="pick",
    )(pieces)
    return (adjoint[None], owned)


def solution(mesh):
    placed = (
        P("blade", None, "span", None),
        P("blade", None, None),
        P("blade", None, "span", None),
        P("blade", None, "span", None),
        P("span", None),
        P(),
    )
    return jax.shard_map(
        per_device,
        mesh=mesh,
        in_specs=placed,
        out_specs=(P("blade", None, "span", None), P(("blade", "span"))),
        check_vma=False,
    )
```

```python
import functools
import math

import jax
import jax.numpy as jnp
from jax import lax
from jax.experimental import pallas as pl
from jax.experimental.pallas import tpu as pltpu
from jax.sharding import PartitionSpec as P

STEPS = 3
SEGS = 2048
CHUNKS = 4
F32 = jnp.float32
BF16 = jnp.bfloat16
VMEM = pl.BlockSpec(memory_space=pltpu.VMEM)
HBM = pl.BlockSpec(memory_space=pltpu.HBM)
GRANT = pltpu.CompilerParams(vmem_limit_bytes=16 * 2**20)


def split(x):
    high = x.astype(BF16)
    return high, (x - high.astype(F32)).astype(BF16)


def dot(a, b):
    return jnp.dot(a, b, preferred_element_type=F32)


def left_three(matrix):
    high, low = matrix
    return jnp.concatenate([high, low, high], axis=1)


def right_three(x):
    high, low = split(x)
    return jnp.concatenate([high, high, low], axis=0)


def iota(shape, dim):
    return lax.broadcasted_iota(jnp.int32, shape, dim)


def shift_next(x, axis):
    size = x.shape[axis]
    return jnp.where(iota(x.shape, axis) == size - 1, 0.0, pltpu.roll(x, size - 1, axis))


def shift_prev(x, axis, first):
    return jnp.where(iota(x.shape, axis) == 0, first, pltpu.roll(x, 1, axis))


def divergence(v, weight, half, axis):
    flux = weight * (shift_next(v, axis) - v)
    return flux - shift_prev(flux, axis, half * v)


def sides():
    span = lax.axis_index("span")
    count = lax.axis_size("span")
    even = lax.rem(span, 2) == 0
    has_next = span + 1 < count
    has_prev = span > 0
    return (
        (even, jnp.where(even, has_next, has_prev)),
        (jnp.logical_not(even), jnp.where(even, has_prev, has_next)),
    )


def load_kernel(
    frame_hbm,
    k_hbm,
    res_hbm,
    excess_hbm,
    d_hbm,
    map_hbm,
    far_ref,
    near_ref,
    k_ref,
    frames_ref,
    excess_ref,
    d_ref,
    map_ref,
    frame_ref,
    res_ref,
    line_ref,
    sems,
):
    depth, rows, cols = k_ref.shape
    base = 2 * depth
    pairs = []
    sent = (near_ref, far_ref)
    for n, (after, _) in enumerate(sides()):
        edge = jnp.where(after, rows - 1, 0)
        second = jnp.where(after, rows - 2, 1)
        pairs += [
            (k_hbm.at[:, edge, :], sent[n].at[0:depth, :]),
            (k_hbm.at[:, second, :], sent[n].at[depth:base, :]),
            (res_hbm.at[:, edge, :], line_ref.at[2 * n]),
            (res_hbm.at[:, second, :], line_ref.at[2 * n + 1]),
        ]
    pairs += [
        (frame_hbm, frame_ref),
        (res_hbm, res_ref),
        (k_hbm, k_ref),
        (excess_hbm, excess_ref),
        (d_hbm, d_ref),
        (map_hbm, map_ref),
    ]
    copies = [pltpu.make_async_copy(a, b, sems.at[n]) for n, (a, b) in enumerate(pairs)]
    for copy in copies:
        copy.start()
    for copy in copies:
        copy.wait()
    for step in range(STEPS):
        frames_ref[step] = res_ref[frame_ref[step]]
    for n, ref in enumerate(sent):
        lines = [
            line_ref[2 * n, pl.ds(frame_ref[2], 1), :],
            line_ref[2 * n, pl.ds(frame_ref[1], 1), :],
            line_ref[2 * n + 1, pl.ds(frame_ref[2], 1), :],
        ]
        rest = ref.shape[0] - base - len(lines)
        if rest:
            lines.append(jnp.zeros((rest, cols), F32))
        ref[base:, :] = jnp.concatenate(lines, axis=0)


def base_kernel(
    scale,
    k_ref,
    frames_ref,
    excess_ref,
    d_ref,
    adj_ref,
    edge_ref,
    contribution_ref,
    pair_ref,
    place_ref,
    mat_ref,
    right_ref,
    first_ref,
    chord_ref,
    span_ref,
    factor_ref,
):
    depth, rows, cols = k_ref.shape
    size = depth * rows
    factor_ref[...] = jnp.broadcast_to(d_ref[:, 0:1], factor_ref.shape)

    parts = split(d_ref[...])
    tall = (iota((size, depth), 0) // rows == iota((size, depth), 1)).astype(BF16)
    wide = (iota((depth, size), 0) == iota((depth, size), 1) // rows).astype(BF16)
    two = 2 * depth
    tile = (iota((depth, two), 0) == iota((depth, two), 1) % depth).astype(BF16)
    same = iota((size, size), 0) % rows == iota((size, size), 1) % rows
    pair_same = iota((two, two), 0) // depth == iota((two, two), 1) // depth
    row_of = iota((size, two), 0) % rows
    first_half = iota((size, two), 1) < depth
    placed = []
    for after, _ in sides():
        edge = jnp.where(after, rows - 1, 0)
        second = jnp.where(after, rows - 2, 1)
        placed.append(row_of == jnp.where(first_half, edge, second))
    mats, pairs, places = [], [], ([], [])
    for part in parts:
        column = dot(tall, part).astype(BF16)
        row = dot(part, tile)
        mats.append(jnp.where(same, dot(column, wide), 0.0).astype(BF16))
        columns = dot(column, tile)
        for found, target in zip(places, placed):
            found.append(jnp.where(target, columns, 0.0).astype(BF16))
        pairs.append(
            jnp.where(pair_same, jnp.concatenate([row] * 2, axis=0), 0.0).astype(BF16)
        )
    mat_ref[...] = left_three(mats)
    pair_ref[...] = left_three(pairs)
    for n in range(2):
        place_ref[n] = left_three(places[n])

    f = frames_ref[2]
    f_chord = shift_next(f, 1) - f
    f_span = shift_next(f, 0) - f

    def put(i, both):
        high, low = split(both)
        span = pl.ds(i * rows, 2 * rows)
        right_ref[0, span, :] = high
        right_ref[1, span, :] = high
        right_ref[2, span, :] = low

    for i in range(0, depth, 2):
        found = []
        for j in (i, i + 1):
            half = 0.5 * k_ref[j]
            w_chord = half + shift_next(half, 1)
            w_span = half + shift_next(half, 0)
            chord_ref[j] = w_chord
            span_ref[j] = w_span
            edge = half * f
            flux_chord = w_chord * f_chord
            flux_span = w_span * f_span
            moved = f + flux_chord - shift_prev(flux_chord, 1, edge)
            moved = moved + flux_span - shift_prev(flux_span, 0, edge)
            factor = jnp.concatenate(
                [jnp.broadcast_to(factor_ref[j : j + 1, :], (rows, 128))] * (cols // 128), axis=1
            )
            source = factor * moved
            found.append(source + frames_ref[1] if j == 0 else source)
        put(i, jnp.concatenate(found, axis=0))
    right = right_ref[...].reshape(3 * size, cols)
    first_ref[...] = dot(mat_ref[...], right).reshape(depth, rows, cols)

    for i in range(0, depth, 2):
        found = []
        for j in (i, i + 1):
            v = first_ref[j]
            half = 0.5 * k_ref[j]
            source = (
                v + divergence(v, chord_ref[j], half, 1) + divergence(v, span_ref[j], half, 0)
            )
            found.append(source + frames_ref[0] if j == 0 else source)
        put(i, jnp.concatenate(found, axis=0))
    right = right_ref[...].reshape(3 * size, cols)
    adj_ref[...] = dot(mat_ref[...], right).reshape(depth, rows, cols)

    top = first_ref[:, 0, :]
    bottom = first_ref[:, rows - 1, :]
    for n, (after, _) in enumerate(sides()):
        edge_ref[n] = jnp.where(after, bottom, top)
    contribution_ref[...] = scale * (
        d_ref[0:1, 0:1] * f * excess_ref[2]
        + first_ref[0] * excess_ref[1]
        + adj_ref[0] * excess_ref[0]
    )


def correction(n, got, own, d_ref, edge_ref, pair_ref, place_ref):
    _, depth, cols = edge_ref.shape
    rows = place_ref.shape[1] // depth
    base = 2 * depth
    after, inside = sides()[n]
    factor = d_ref[:, 0:1]
    half = 0.5 * got[0:depth, :]
    half_next = 0.5 * got[depth:base, :]
    half_own = 0.5 * own[0:depth, :]
    inner = half_own + 0.5 * own[depth:base, :]
    f = got[base : base + 1, :]
    frame = got[base + 1 : base + 2, :]
    f_next = got[base + 2 : base + 3, :]
    f_own = own[base : base + 1, :]
    face = half + half_own
    flux = (half + shift_next(half, 1)) * (shift_next(f, 1) - f)
    moved = (
        f
        + flux
        - shift_prev(flux, 1, half * f)
        + (half + half_next) * (f_next - f)
        + face * (f_own - f)
    )
    outer = factor * moved + jnp.where(iota((depth, 1), 0) == 0, frame, 0.0)
    sources = [factor * (face * f - half * f_own), jnp.where(inside, outer, 0.0)]
    found = dot(pair_ref[...], right_three(jnp.concatenate(sources, axis=0)))
    e = found[0:depth]
    outer = found[depth:base]
    w_chord = half_own + shift_next(half_own, 1)
    change = (
        e
        + divergence(e, w_chord, half_own, 1)
        - (half + half_own + inner) * e
        + face * outer
        - half * edge_ref[n]
    )
    found = dot(place_ref[n], right_three(jnp.concatenate([change, inner * e], axis=0)))
    row = jnp.where(after, rows - 1, 0)
    return found, jnp.where(iota((rows, cols), 0) == row, e[0:1, :], 0.0)


def near_kernel(
    scale,
    d_ref,
    excess_ref,
    edge_ref,
    pair_ref,
    place_ref,
    base_ref,
    contribution_ref,
    own_ref,
    got_ref,
    adj_ref,
    out_ref,
):
    rows = base_ref.shape[1]
    found, surface = correction(0, got_ref, own_ref, d_ref, edge_ref, pair_ref, place_ref)
    adj_ref[...] = base_ref[...] + found.reshape(base_ref.shape)
    out_ref[...] = contribution_ref[...] + scale * (
        surface * excess_ref[1] + found[0:rows, :] * excess_ref[0]
    )


def far_kernel(
    scale,
    own_ref,
    got_ref,
    d_ref,
    excess_ref,
    edge_ref,
    pair_ref,
    place_ref,
    base_ref,
    contribution_ref,
    map_vmem,
    adj_hbm,
    part_ref,
    adj_ref,
    map_ref,
    map_sem,
    sems,
):
    map_copy = pltpu.make_async_copy(map_vmem, map_ref, map_sem)
    map_copy.start()
    depth, rows, cols = base_ref.shape
    blocks = cols // 128
    found, surface = correction(1, got_ref, own_ref, d_ref, edge_ref, pair_ref, place_ref)
    step = depth // CHUNKS
    copies = []
    for n in range(CHUNKS):
        part = pl.ds(n * step, step)
        new = found[n * step * rows : (n + 1) * step * rows].reshape(step, rows, cols)
        adj_ref[part] = base_ref[part] + new
        copies.append(pltpu.make_async_copy(adj_ref.at[part], adj_hbm.at[part], sems.at[n]))
        copies[-1].start()

    contribution = contribution_ref[...] + scale * (
        surface * excess_ref[1] + found[0:rows, :] * excess_ref[0]
    )
    owners, _, lanes = part_ref.shape
    shape = (owners, 128)
    lane = iota(shape, 1)
    segment = jnp.where(lane < lanes, iota(shape, 0) * lanes + lane, -1)
    total = jnp.zeros(shape, F32)
    map_copy.wait()
    for block in range(blocks):
        sums = jnp.sum(contribution[:, block * 128 : (block + 1) * 128], axis=1, keepdims=True)
        for row in range(rows):
            total += jnp.where(segment == map_ref[block, row], sums[row : row + 1, :], 0.0)
    part_ref[...] = total[:, None, :lanes]
    for copy in copies:
        copy.wait()


def per_device(
    conductance, depth_inverse, surface_residual, surface_excess, segment_map, frame_index
):
    _, depth, rows, cols = conductance.shape
    frames = surface_residual.shape[1]
    blocks = segment_map.shape[1]
    size = depth * rows
    spans = lax.axis_size("span")
    devices = spans * lax.axis_size("blade")
    lanes = SEGS // devices
    field = pltpu.VMEM((depth, rows, cols), F32)
    packed_far = pltpu.VMEM((2 * depth + 8, cols), F32)
    packed_near = pltpu.VMEM((2 * depth + 3, cols), F32)
    own_far, own_near, k, picked, excess, inverse, ids = pl.pallas_call(
        load_kernel,
        out_shape=(
            packed_far,
            packed_near,
            field,
            pltpu.VMEM((STEPS, rows, cols), F32),
            pltpu.VMEM((STEPS, rows, cols), F32),
            pltpu.VMEM((depth, depth), F32),
            pltpu.VMEM((blocks, rows), jnp.int32),
        ),
        in_specs=[HBM] * 6,
        out_specs=(VMEM,) * 7,
        scratch_shapes=[
            pltpu.SMEM((STEPS,), jnp.int32),
            pltpu.VMEM((frames, rows, cols), F32),
            pltpu.VMEM((4, frames, cols), F32),
            pltpu.SemaphoreType.DMA((14,)),
        ],
        compiler_params=GRANT,
        name="load",
    )(
        *(
            pltpu.with_memory_space_constraint(x, pltpu.HBM)
            for x in (
                frame_index,
                conductance[0],
                surface_residual[0],
                surface_excess[0],
                depth_inverse[0],
                segment_map.T,
            )
        )
    )
    across = [(i, i + 1) for i in range(1, spans - 1, 2)]
    within = [(i, i + 1) for i in range(0, spans - 1, 2)]
    near = lax.ppermute(own_near, "span", within + [(b, a) for a, b in within])
    far = lax.ppermute(own_far, "span", across + [(b, a) for a, b in across])
    scale = 1.0 / math.sqrt(128.0 * STEPS)
    line = pltpu.VMEM((rows, cols), F32)
    base, edge, contribution, pair, place = pl.pallas_call(
        functools.partial(base_kernel, scale),
        out_shape=(
            field,
            pltpu.VMEM((2, depth, cols), F32),
            line,
            pltpu.VMEM((2 * depth, 6 * depth), BF16),
            pltpu.VMEM((2, size, 6 * depth), BF16),
        ),
        in_specs=[VMEM] * 4,
        out_specs=(VMEM,) * 5,
        scratch_shapes=[
            pltpu.VMEM((size, 3 * size), BF16),
            pltpu.VMEM((3, size, cols), BF16),
            field,
            field,
            field,
            pltpu.VMEM((depth, 128), F32),
        ],
        compiler_params=GRANT,
        name="base",
    )(k, picked, excess, inverse)
    fixed = (inverse, excess, edge, pair, place)
    base, contribution = pl.pallas_call(
        functools.partial(near_kernel, scale),
        out_shape=(field, line),
        in_specs=[VMEM] * 9,
        out_specs=(VMEM,) * 2,
        compiler_params=GRANT,
        name="near",
    )(*fixed, base, contribution, own_near, near)
    adjoint, partial = pl.pallas_call(
        functools.partial(far_kernel, scale),
        out_shape=(
            pltpu.HBM((depth, rows, cols), F32),
            pltpu.VMEM((devices, 1, lanes), F32),
        ),
        in_specs=[VMEM] * 10,
        out_specs=(HBM, VMEM),
        scratch_shapes=[
            field,
            pltpu.SMEM((blocks, rows), jnp.int32),
            pltpu.SemaphoreType.DMA,
            pltpu.SemaphoreType.DMA((CHUNKS,)),
        ],
        compiler_params=GRANT,
        name="far",
    )(own_far, far, *fixed, base, contribution, ids)
    pieces = lax.all_to_all(partial, ("blade", "span"), 0, 0, tiled=True)
    return (adjoint[None], jnp.sum(pieces, axis=(0, 1)))


def solution(mesh):
    placed = (
        P("blade", None, "span", None),
        P("blade", None, None),
        P("blade", None, "span", None),
        P("blade", None, "span", None),
        P("span", None),
        P(),
    )
    return jax.shard_map(
        per_device,
        mesh=mesh,
        in_specs=placed,
        out_specs=(P("blade", None, "span", None), P(("blade", "span"))),
        check_vma=False,
    )
```

```python
import functools
import math

import jax
import jax.numpy as jnp
from jax import lax
from jax.experimental import pallas as pl
from jax.experimental.pallas import tpu as pltpu
from jax.sharding import PartitionSpec as P

STEPS = 3
SEGS = 2048
F32 = jnp.float32
BF16 = jnp.bfloat16
VMEM = pl.BlockSpec(memory_space=pltpu.VMEM)
HBM = pl.BlockSpec(memory_space=pltpu.HBM)
GRANT = pltpu.CompilerParams(vmem_limit_bytes=16 * 2**20)


def split(x):
    high = x.astype(BF16)
    return high, (x - high.astype(F32)).astype(BF16)


def dot(a, b):
    return jnp.dot(a, b, preferred_element_type=F32)


def left_three(matrix):
    high, low = matrix
    return jnp.concatenate([high, low, high], axis=1)


def right_three(x):
    high, low = split(x)
    return jnp.concatenate([high, high, low], axis=0)


def iota(shape, dim):
    return lax.broadcasted_iota(jnp.int32, shape, dim)


def shift_next(x, axis):
    size = x.shape[axis]
    return jnp.where(iota(x.shape, axis) == size - 1, 0.0, pltpu.roll(x, size - 1, axis))


def shift_prev(x, axis, first):
    return jnp.where(iota(x.shape, axis) == 0, first, pltpu.roll(x, 1, axis))


def divergence(v, weight, half, axis):
    flux = weight * (shift_next(v, axis) - v)
    return flux - shift_prev(flux, axis, half * v)


def sides():
    span = lax.axis_index("span")
    count = lax.axis_size("span")
    even = lax.rem(span, 2) == 0
    has_next = span + 1 < count
    has_prev = span > 0
    return (
        (even, jnp.where(even, has_next, has_prev)),
        (jnp.logical_not(even), jnp.where(even, has_prev, has_next)),
    )


def chunked(ref, start, count, step):
    chunks = ref.shape[0] // step
    return jnp.concatenate(
        [ref[c * step + start : c * step + start + count, :] for c in range(chunks)], axis=1
    )


def packed_field(ref, depth, cols, n):
    chunks = cols // 128
    return chunked(ref.at[n * chunks * depth : (n + 1) * chunks * depth], 0, depth, depth)


def packed_line(ref, depth, cols, n):
    chunks = cols // 128
    base = (2 * depth + n) * chunks
    return chunked(ref.at[base : base + chunks], 0, 1, 1)


def row_of_each(ref, chunk, depth, rows, row):
    return ref[pl.ds(chunk * depth * rows + row, depth, stride=rows), :]


def load_kernel(
    rows,
    frame_hbm,
    k_hbm,
    res_hbm,
    excess_hbm,
    d_hbm,
    map_hbm,
    far_ref,
    near_ref,
    k_ref,
    frames_ref,
    excess_ref,
    d_ref,
    map_ref,
    frame_ref,
    res_ref,
    sems,
):
    size, cols = k_hbm.shape
    depth = size // rows
    chunks = cols // 128
    pairs = [(frame_hbm, frame_ref), (res_hbm, res_ref)]
    for c in range(chunks):
        pairs.append((k_hbm.at[:, pl.ds(c * 128, 128)], k_ref.at[pl.ds(c * size, size)]))
    pairs += [(excess_hbm, excess_ref), (d_hbm, d_ref), (map_hbm, map_ref)]
    copies = [pltpu.make_async_copy(a, b, sems.at[n]) for n, (a, b) in enumerate(pairs)]
    for copy in copies:
        copy.start()
    sent = (near_ref, far_ref)
    picks = []
    for after, _ in sides():
        picks.append((jnp.where(after, rows - 1, 0), jnp.where(after, rows - 2, 1)))
    copies[0].wait()
    copies[1].wait()
    for step in range(STEPS):
        frames_ref[step] = res_ref[frame_ref[step]]
    base = 2 * chunks * depth
    for ref, (edge, second) in zip(sent, picks):
        for n, (step, row) in enumerate(((2, edge), (1, edge), (2, second))):
            line = frames_ref[step, pl.ds(row, 1), :]
            for c in range(chunks):
                spot = base + n * chunks + c
                ref[spot : spot + 1, :] = line[:, c * 128 : (c + 1) * 128]
        if ref.shape[0] > base + 3 * chunks:
            ref[base + 3 * chunks :, :] = jnp.zeros((ref.shape[0] - base - 3 * chunks, 128), F32)
    for c in range(chunks):
        copies[2 + c].wait()
        for ref, row_pair in zip(sent, picks):
            for n, row in enumerate(row_pair):
                spot = (n * chunks + c) * depth
                ref[spot : spot + depth, :] = row_of_each(k_ref, c, depth, rows, row)
    for copy in copies[2 + chunks :]:
        copy.wait()


def base_kernel(
    scale,
    k_ref,
    frames_ref,
    excess_ref,
    d_ref,
    adj_ref,
    edge_ref,
    contribution_ref,
    pair_ref,
    place_ref,
    mat_ref,
    right_ref,
    first_ref,
    chord_ref,
    span_ref,
    factor_ref,
):
    depth, rows, cols = adj_ref.shape
    size = depth * rows
    factor_ref[...] = jnp.broadcast_to(d_ref[:, 0:1], factor_ref.shape)

    parts = split(d_ref[...])
    tall = (iota((size, depth), 0) // rows == iota((size, depth), 1)).astype(BF16)
    wide = (iota((depth, size), 0) == iota((depth, size), 1) // rows).astype(BF16)
    two = 2 * depth
    tile = (iota((depth, two), 0) == iota((depth, two), 1) % depth).astype(BF16)
    same = iota((size, size), 0) % rows == iota((size, size), 1) % rows
    pair_same = iota((two, two), 0) // depth == iota((two, two), 1) // depth
    row_of = iota((size, two), 0) % rows
    first_half = iota((size, two), 1) < depth
    placed = []
    for after, _ in sides():
        edge = jnp.where(after, rows - 1, 0)
        second = jnp.where(after, rows - 2, 1)
        placed.append(row_of == jnp.where(first_half, edge, second))
    mats, pairs, places = [], [], ([], [])
    for part in parts:
        column = dot(tall, part).astype(BF16)
        row = dot(part, tile)
        mats.append(jnp.where(same, dot(column, wide), 0.0).astype(BF16))
        columns = dot(column, tile)
        for found, target in zip(places, placed):
            found.append(jnp.where(target, columns, 0.0).astype(BF16))
        pairs.append(
            jnp.where(pair_same, jnp.concatenate([row] * 2, axis=0), 0.0).astype(BF16)
        )
    mat_ref[...] = left_three(mats)
    pair_ref[...] = left_three(pairs)
    for n in range(2):
        place_ref[n] = left_three(places[n])

    f = frames_ref[2]
    f_chord = shift_next(f, 1) - f
    f_span = shift_next(f, 0) - f

    def put(i, both):
        high, low = split(both)
        span = pl.ds(i * rows, 2 * rows)
        right_ref[0, span, :] = high
        right_ref[1, span, :] = high
        right_ref[2, span, :] = low

    for i in range(0, depth, 2):
        found = []
        for j in (i, i + 1):
            half = 0.5 * chunked(k_ref, j * rows, rows, size)
            w_chord = half + shift_next(half, 1)
            w_span = half + shift_next(half, 0)
            chord_ref[j] = w_chord
            span_ref[j] = w_span
            edge = half * f
            flux_chord = w_chord * f_chord
            flux_span = w_span * f_span
            moved = f + flux_chord - shift_prev(flux_chord, 1, edge)
            moved = moved + flux_span - shift_prev(flux_span, 0, edge)
            factor = jnp.concatenate(
                [jnp.broadcast_to(factor_ref[j : j + 1, :], (rows, 128))] * (cols // 128), axis=1
            )
            source = factor * moved
            found.append(source + frames_ref[1] if j == 0 else source)
        put(i, jnp.concatenate(found, axis=0))
    right = right_ref[...].reshape(3 * size, cols)
    first = dot(mat_ref[...], right)
    for c in range(cols // 128):
        first_ref[c * size : (c + 1) * size, :] = first[:, c * 128 : (c + 1) * 128]

    for i in range(0, depth, 2):
        found = []
        for j in (i, i + 1):
            v = chunked(first_ref, j * rows, rows, size)
            half = 0.5 * chunked(k_ref, j * rows, rows, size)
            source = (
                v + divergence(v, chord_ref[j], half, 1) + divergence(v, span_ref[j], half, 0)
            )
            found.append(source + frames_ref[0] if j == 0 else source)
        put(i, jnp.concatenate(found, axis=0))
    right = right_ref[...].reshape(3 * size, cols)
    adj_ref[...] = dot(mat_ref[...], right).reshape(depth, rows, cols)

    for n, (after, _) in enumerate(sides()):
        row = jnp.where(after, rows - 1, 0)
        for c in range(cols // 128):
            edge_ref[n, :, c * 128 : (c + 1) * 128] = row_of_each(first_ref, c, depth, rows, row)
    contribution_ref[...] = scale * (
        d_ref[0:1, 0:1] * f * excess_ref[2]
        + chunked(first_ref, 0, rows, size) * excess_ref[1]
        + adj_ref[0] * excess_ref[0]
    )


def correction(n, got, own, d_ref, edge_ref, pair_ref, place_ref):
    _, depth, cols = edge_ref.shape
    rows = place_ref.shape[1] // depth
    after, inside = sides()[n]
    factor = d_ref[:, 0:1]
    half = 0.5 * packed_field(got, depth, cols, 0)
    half_next = 0.5 * packed_field(got, depth, cols, 1)
    half_own = 0.5 * packed_field(own, depth, cols, 0)
    inner = half_own + 0.5 * packed_field(own, depth, cols, 1)
    f = packed_line(got, depth, cols, 0)
    frame = packed_line(got, depth, cols, 1)
    f_next = packed_line(got, depth, cols, 2)
    f_own = packed_line(own, depth, cols, 0)
    face = half + half_own
    flux = (half + shift_next(half, 1)) * (shift_next(f, 1) - f)
    moved = (
        f
        + flux
        - shift_prev(flux, 1, half * f)
        + (half + half_next) * (f_next - f)
        + face * (f_own - f)
    )
    outer = factor * moved + jnp.where(iota((depth, 1), 0) == 0, frame, 0.0)
    sources = [factor * (face * f - half * f_own), jnp.where(inside, outer, 0.0)]
    found = dot(pair_ref[...], right_three(jnp.concatenate(sources, axis=0)))
    e = found[0:depth]
    outer = found[depth:]
    w_chord = half_own + shift_next(half_own, 1)
    change = (
        e
        + divergence(e, w_chord, half_own, 1)
        - (half + half_own + inner) * e
        + face * outer
        - half * edge_ref[n]
    )
    found = dot(place_ref[n], right_three(jnp.concatenate([change, inner * e], axis=0)))
    row = jnp.where(after, rows - 1, 0)
    return found, jnp.where(iota((rows, cols), 0) == row, e[0:1, :], 0.0)


def near_kernel(
    scale,
    d_ref,
    excess_ref,
    edge_ref,
    pair_ref,
    place_ref,
    base_ref,
    contribution_ref,
    own_ref,
    got_ref,
    adj_ref,
    out_ref,
):
    rows = base_ref.shape[1]
    found, surface = correction(0, got_ref, own_ref, d_ref, edge_ref, pair_ref, place_ref)
    adj_ref[...] = base_ref[...] + found.reshape(base_ref.shape)
    out_ref[...] = contribution_ref[...] + scale * (
        surface * excess_ref[1] + found[0:rows, :] * excess_ref[0]
    )


def far_kernel(
    scale,
    own_ref,
    got_ref,
    d_ref,
    excess_ref,
    edge_ref,
    pair_ref,
    place_ref,
    base_ref,
    contribution_ref,
    map_vmem,
    adj_ref,
    part_ref,
    map_ref,
    map_sem,
):
    map_copy = pltpu.make_async_copy(map_vmem, map_ref, map_sem)
    map_copy.start()
    depth, rows, cols = base_ref.shape
    blocks = cols // 128
    found, surface = correction(1, got_ref, own_ref, d_ref, edge_ref, pair_ref, place_ref)
    adj_ref[...] = base_ref[...] + found.reshape(depth, rows, cols)
    contribution = contribution_ref[...] + scale * (
        surface * excess_ref[1] + found[0:rows, :] * excess_ref[0]
    )
    owners, _, lanes = part_ref.shape
    shape = (owners, 128)
    lane = iota(shape, 1)
    segment = jnp.where(lane < lanes, iota(shape, 0) * lanes + lane, -1)
    total = jnp.zeros(shape, F32)
    map_copy.wait()
    for block in range(blocks):
        sums = jnp.sum(contribution[:, block * 128 : (block + 1) * 128], axis=1, keepdims=True)
        for row in range(rows):
            total += jnp.where(segment == map_ref[block, row], sums[row : row + 1, :], 0.0)
    part_ref[...] = total[:, None, :lanes]


def finish_kernel(adj_vmem, got_ref, adj_hbm, out_hbm, out_ref, sems):
    adj_copy = pltpu.make_async_copy(adj_vmem, adj_hbm, sems.at[0])
    adj_copy.start()
    out_ref[...] = jnp.sum(got_ref[:, 0, :], axis=0)
    out_copy = pltpu.make_async_copy(out_ref, out_hbm, sems.at[1])
    out_copy.start()
    adj_copy.wait()
    out_copy.wait()


def per_device(
    conductance, depth_inverse, surface_residual, surface_excess, segment_map, frame_index
):
    _, depth, rows, cols = conductance.shape
    frames = surface_residual.shape[1]
    blocks = segment_map.shape[1]
    size = depth * rows
    spans = lax.axis_size("span")
    devices = spans * lax.axis_size("blade")
    lanes = SEGS // devices
    field = pltpu.VMEM((depth, rows, cols), F32)
    chunks = cols // 128
    packed_far = pltpu.VMEM(((2 * depth + 4) * chunks, 128), F32)
    packed_near = pltpu.VMEM(((2 * depth + 3) * chunks, 128), F32)
    own_far, own_near, k, picked, excess, inverse, ids = pl.pallas_call(
        functools.partial(load_kernel, rows),
        out_shape=(
            packed_far,
            packed_near,
            pltpu.VMEM((chunks * size, 128), F32),
            pltpu.VMEM((STEPS, rows, cols), F32),
            pltpu.VMEM((STEPS, rows, cols), F32),
            pltpu.VMEM((depth, depth), F32),
            pltpu.VMEM((blocks, rows), jnp.int32),
        ),
        in_specs=[HBM] * 6,
        out_specs=(VMEM,) * 7,
        scratch_shapes=[
            pltpu.SMEM((STEPS,), jnp.int32),
            pltpu.VMEM((frames, rows, cols), F32),
            pltpu.SemaphoreType.DMA((5 + chunks,)),
        ],
        compiler_params=GRANT,
        name="load",
    )(
        *(
            pltpu.with_memory_space_constraint(x, pltpu.HBM)
            for x in (
                frame_index,
                conductance.reshape(size, cols),
                surface_residual[0],
                surface_excess[0],
                depth_inverse[0],
                segment_map.T,
            )
        )
    )
    across = [(i, i + 1) for i in range(1, spans - 1, 2)]
    within = [(i, i + 1) for i in range(0, spans - 1, 2)]
    near = lax.ppermute(own_near, "span", within + [(b, a) for a, b in within])
    far = lax.ppermute(own_far, "span", across + [(b, a) for a, b in across])
    scale = 1.0 / math.sqrt(128.0 * STEPS)
    line = pltpu.VMEM((rows, cols), F32)
    base, edge, contribution, pair, place = pl.pallas_call(
        functools.partial(base_kernel, scale),
        out_shape=(
            field,
            pltpu.VMEM((2, depth, cols), F32),
            line,
            pltpu.VMEM((2 * depth, 6 * depth), BF16),
            pltpu.VMEM((2, size, 6 * depth), BF16),
        ),
        in_specs=[VMEM] * 4,
        out_specs=(VMEM,) * 5,
        scratch_shapes=[
            pltpu.VMEM((size, 3 * size), BF16),
            pltpu.VMEM((3, size, cols), BF16),
            pltpu.VMEM((chunks * size, 128), F32),
            field,
            field,
            pltpu.VMEM((depth, 128), F32),
        ],
        compiler_params=GRANT,
        name="base",
    )(k, picked, excess, inverse)
    fixed = (inverse, excess, edge, pair, place)
    base, contribution = pl.pallas_call(
        functools.partial(near_kernel, scale),
        out_shape=(field, line),
        in_specs=[VMEM] * 9,
        out_specs=(VMEM,) * 2,
        compiler_params=GRANT,
        name="near",
    )(*fixed, base, contribution, own_near, near)
    adjoint, partial = pl.pallas_call(
        functools.partial(far_kernel, scale),
        out_shape=(
            field,
            pltpu.VMEM((devices, 1, lanes), F32),
        ),
        in_specs=[VMEM] * 10,
        out_specs=(VMEM,) * 2,
        scratch_shapes=[
            pltpu.SMEM((blocks, rows), jnp.int32),
            pltpu.SemaphoreType.DMA,
        ],
        compiler_params=GRANT,
        name="far",
    )(own_far, far, *fixed, base, contribution, ids)
    pieces = lax.all_to_all(partial, ("blade", "span"), 0, 0, tiled=True)
    adjoint, owned = pl.pallas_call(
        finish_kernel,
        out_shape=(pltpu.HBM((depth, rows, cols), F32), pltpu.HBM((lanes,), F32)),
        in_specs=[VMEM] * 2,
        out_specs=(HBM,) * 2,
        scratch_shapes=[pltpu.VMEM((lanes,), F32), pltpu.SemaphoreType.DMA((2,))],
        compiler_params=GRANT,
        name="finish",
    )(adjoint, pltpu.with_memory_space_constraint(pieces, pltpu.VMEM))
    return (adjoint[None], owned)


def solution(mesh):
    placed = (
        P("blade", None, "span", None),
        P("blade", None, None),
        P("blade", None, "span", None),
        P("blade", None, "span", None),
        P("span", None),
        P(),
    )
    return jax.shard_map(
        per_device,
        mesh=mesh,
        in_specs=placed,
        out_specs=(P("blade", None, "span", None), P(("blade", "span"))),
        check_vma=False,
    )
```

```python
import functools
import math

import jax
import jax.numpy as jnp
from jax import lax
from jax.experimental import pallas as pl
from jax.experimental.pallas import tpu as pltpu
from jax.sharding import PartitionSpec as P

STEPS = 3
SEGS = 2048
PIECES = 4
F32 = jnp.float32
BF16 = jnp.bfloat16
VMEM = pl.BlockSpec(memory_space=pltpu.VMEM)
HBM = pl.BlockSpec(memory_space=pltpu.HBM)
GRANT = pltpu.CompilerParams(vmem_limit_bytes=16 * 2**20)


def split(x):
    high = x.astype(BF16)
    return high, (x - high.astype(F32)).astype(BF16)


def dot(a, b):
    return jnp.dot(a, b, preferred_element_type=F32)


def left_three(matrix):
    high, low = matrix
    return jnp.concatenate([high, low, high], axis=1)


def right_three(x):
    high, low = split(x)
    return jnp.concatenate([high, high, low], axis=0)


def iota(shape, dim):
    return lax.broadcasted_iota(jnp.int32, shape, dim)


def shift_next(x, axis):
    size = x.shape[axis]
    return jnp.where(iota(x.shape, axis) == size - 1, 0.0, pltpu.roll(x, size - 1, axis))


def shift_prev(x, axis, first):
    return jnp.where(iota(x.shape, axis) == 0, first, pltpu.roll(x, 1, axis))


def divergence(v, weight, half, axis):
    flux = weight * (shift_next(v, axis) - v)
    return flux - shift_prev(flux, axis, half * v)


def sides():
    span = lax.axis_index("span")
    count = lax.axis_size("span")
    even = lax.rem(span, 2) == 0
    has_next = span + 1 < count
    has_prev = span > 0
    return (
        (even, jnp.where(even, has_next, has_prev)),
        (jnp.logical_not(even), jnp.where(even, has_prev, has_next)),
    )


def chunked(ref, start, count, step):
    chunks = ref.shape[0] // step
    return jnp.concatenate(
        [ref[c * step + start : c * step + start + count, :] for c in range(chunks)], axis=1
    )


def packed_field(ref, depth, cols, n):
    chunks = cols // 128
    return chunked(ref.at[n * chunks * depth : (n + 1) * chunks * depth], 0, depth, depth)


def packed_line(ref, depth, cols, n):
    chunks = cols // 128
    base = (2 * depth + n) * chunks
    return chunked(ref.at[base : base + chunks], 0, 1, 1)


def row_of_each(ref, chunk, depth, rows, row):
    return ref[pl.ds(chunk * depth * rows + row, depth, stride=rows), :]


def load_kernel(
    rows,
    frame_hbm,
    k_hbm,
    res_hbm,
    excess_hbm,
    d_hbm,
    map_hbm,
    far_ref,
    near_ref,
    k_ref,
    frames_ref,
    excess_ref,
    d_ref,
    map_ref,
    frame_ref,
    res_ref,
    sems,
):
    size, cols = k_hbm.shape
    depth = size // rows
    chunks = cols // 128
    pairs = [(frame_hbm, frame_ref), (res_hbm, res_ref)]
    for c in range(chunks):
        pairs.append((k_hbm.at[:, pl.ds(c * 128, 128)], k_ref.at[pl.ds(c * size, size)]))
    pairs += [(excess_hbm, excess_ref), (d_hbm, d_ref), (map_hbm, map_ref)]
    copies = [pltpu.make_async_copy(a, b, sems.at[n]) for n, (a, b) in enumerate(pairs)]
    for copy in copies:
        copy.start()
    sent = (near_ref, far_ref)
    picks = []
    for after, _ in sides():
        picks.append((jnp.where(after, rows - 1, 0), jnp.where(after, rows - 2, 1)))
    copies[0].wait()
    copies[1].wait()
    for step in range(STEPS):
        frames_ref[step] = res_ref[frame_ref[step]]
    base = 2 * chunks * depth
    for ref, (edge, second) in zip(sent, picks):
        for n, (step, row) in enumerate(((2, edge), (1, edge), (2, second))):
            line = frames_ref[step, pl.ds(row, 1), :]
            for c in range(chunks):
                spot = base + n * chunks + c
                ref[spot : spot + 1, :] = line[:, c * 128 : (c + 1) * 128]
        if ref.shape[0] > base + 3 * chunks:
            ref[base + 3 * chunks :, :] = jnp.zeros((ref.shape[0] - base - 3 * chunks, 128), F32)
    for c in range(chunks):
        copies[2 + c].wait()
        for ref, row_pair in zip(sent, picks):
            for n, row in enumerate(row_pair):
                spot = (n * chunks + c) * depth
                ref[spot : spot + depth, :] = row_of_each(k_ref, c, depth, rows, row)
    for copy in copies[2 + chunks :]:
        copy.wait()


def base_kernel(
    scale,
    k_ref,
    frames_ref,
    excess_ref,
    d_ref,
    adj_ref,
    edge_ref,
    contribution_ref,
    pair_ref,
    place_ref,
    mat_ref,
    right_ref,
    first_ref,
    chord_ref,
    span_ref,
    factor_ref,
):
    depth, rows, cols = adj_ref.shape
    size = depth * rows
    factor_ref[...] = jnp.broadcast_to(d_ref[:, 0:1], factor_ref.shape)

    parts = split(d_ref[...])
    tall = (iota((size, depth), 0) // rows == iota((size, depth), 1)).astype(BF16)
    wide = (iota((depth, size), 0) == iota((depth, size), 1) // rows).astype(BF16)
    two = 2 * depth
    tile = (iota((depth, two), 0) == iota((depth, two), 1) % depth).astype(BF16)
    same = iota((size, size), 0) % rows == iota((size, size), 1) % rows
    pair_same = iota((two, two), 0) // depth == iota((two, two), 1) // depth
    row_of = iota((size, two), 0) % rows
    first_half = iota((size, two), 1) < depth
    placed = []
    for after, _ in sides():
        edge = jnp.where(after, rows - 1, 0)
        second = jnp.where(after, rows - 2, 1)
        placed.append(row_of == jnp.where(first_half, edge, second))
    mats, pairs, places = [], [], ([], [])
    for part in parts:
        column = dot(tall, part).astype(BF16)
        row = dot(part, tile)
        mats.append(jnp.where(same, dot(column, wide), 0.0).astype(BF16))
        columns = dot(column, tile)
        for found, target in zip(places, placed):
            found.append(jnp.where(target, columns, 0.0).astype(BF16))
        pairs.append(
            jnp.where(pair_same, jnp.concatenate([row] * 2, axis=0), 0.0).astype(BF16)
        )
    mat_ref[...] = left_three(mats)
    pair_ref[...] = left_three(pairs)
    for n in range(2):
        place_ref[n] = left_three(places[n])

    f = frames_ref[2]
    f_chord = shift_next(f, 1) - f
    f_span = shift_next(f, 0) - f

    def put(i, both):
        high, low = split(both)
        span = pl.ds(i * rows, 2 * rows)
        right_ref[0, span, :] = high
        right_ref[1, span, :] = high
        right_ref[2, span, :] = low

    for i in range(0, depth, 2):
        found = []
        for j in (i, i + 1):
            half = 0.5 * chunked(k_ref, j * rows, rows, size)
            w_chord = half + shift_next(half, 1)
            w_span = half + shift_next(half, 0)
            chord_ref[j] = w_chord
            span_ref[j] = w_span
            edge = half * f
            flux_chord = w_chord * f_chord
            flux_span = w_span * f_span
            moved = f + flux_chord - shift_prev(flux_chord, 1, edge)
            moved = moved + flux_span - shift_prev(flux_span, 0, edge)
            factor = jnp.concatenate(
                [jnp.broadcast_to(factor_ref[j : j + 1, :], (rows, 128))] * (cols // 128), axis=1
            )
            source = factor * moved
            found.append(source + frames_ref[1] if j == 0 else source)
        put(i, jnp.concatenate(found, axis=0))
    right = right_ref[...].reshape(3 * size, cols)
    first = dot(mat_ref[...], right)
    for c in range(cols // 128):
        first_ref[c * size : (c + 1) * size, :] = first[:, c * 128 : (c + 1) * 128]

    for i in range(0, depth, 2):
        found = []
        for j in (i, i + 1):
            v = chunked(first_ref, j * rows, rows, size)
            half = 0.5 * chunked(k_ref, j * rows, rows, size)
            source = (
                v + divergence(v, chord_ref[j], half, 1) + divergence(v, span_ref[j], half, 0)
            )
            found.append(source + frames_ref[0] if j == 0 else source)
        put(i, jnp.concatenate(found, axis=0))
    right = right_ref[...].reshape(3 * size, cols)
    adj_ref[...] = dot(mat_ref[...], right).reshape(depth, rows, cols)

    for n, (after, _) in enumerate(sides()):
        row = jnp.where(after, rows - 1, 0)
        for c in range(cols // 128):
            edge_ref[n, :, c * 128 : (c + 1) * 128] = row_of_each(first_ref, c, depth, rows, row)
    contribution_ref[...] = scale * (
        d_ref[0:1, 0:1] * f * excess_ref[2]
        + chunked(first_ref, 0, rows, size) * excess_ref[1]
        + adj_ref[0] * excess_ref[0]
    )


def correction(n, got, own, d_ref, edge_ref, pair_ref, place_ref):
    _, depth, cols = edge_ref.shape
    rows = place_ref.shape[1] // depth
    after, inside = sides()[n]
    factor = d_ref[:, 0:1]
    half = 0.5 * packed_field(got, depth, cols, 0)
    half_next = 0.5 * packed_field(got, depth, cols, 1)
    half_own = 0.5 * packed_field(own, depth, cols, 0)
    inner = half_own + 0.5 * packed_field(own, depth, cols, 1)
    f = packed_line(got, depth, cols, 0)
    frame = packed_line(got, depth, cols, 1)
    f_next = packed_line(got, depth, cols, 2)
    f_own = packed_line(own, depth, cols, 0)
    face = half + half_own
    flux = (half + shift_next(half, 1)) * (shift_next(f, 1) - f)
    moved = (
        f
        + flux
        - shift_prev(flux, 1, half * f)
        + (half + half_next) * (f_next - f)
        + face * (f_own - f)
    )
    outer = factor * moved + jnp.where(iota((depth, 1), 0) == 0, frame, 0.0)
    sources = [factor * (face * f - half * f_own), jnp.where(inside, outer, 0.0)]
    found = dot(pair_ref[...], right_three(jnp.concatenate(sources, axis=0)))
    e = found[0:depth]
    outer = found[depth:]
    w_chord = half_own + shift_next(half_own, 1)
    change = (
        e
        + divergence(e, w_chord, half_own, 1)
        - (half + half_own + inner) * e
        + face * outer
        - half * edge_ref[n]
    )
    found = dot(place_ref[n], right_three(jnp.concatenate([change, inner * e], axis=0)))
    row = jnp.where(after, rows - 1, 0)
    return found, jnp.where(iota((rows, cols), 0) == row, e[0:1, :], 0.0)


def add_segments(total, contribution, picked_rows, map_ref):
    owners, _, lanes = total.shape
    shape = (owners, 128)
    lane = iota(shape, 1)
    segment = jnp.where(lane < lanes, iota(shape, 0) * lanes + lane, -1)
    found = jnp.zeros(shape, F32)
    for block in range(contribution.shape[1] // 128):
        part = contribution[:, block * 128 : (block + 1) * 128]
        sums = jnp.sum(part, axis=1, keepdims=True)
        for n, row in enumerate(picked_rows):
            found += jnp.where(segment == map_ref[block, row], sums[n : n + 1, :], 0.0)
    return total + found[:, None, :lanes]


def near_kernel(
    scale,
    d_ref,
    excess_ref,
    edge_ref,
    pair_ref,
    place_ref,
    map_vmem,
    base_ref,
    contribution_ref,
    own_ref,
    got_ref,
    adj_ref,
    part_ref,
    map_ref,
    map_sem,
):
    map_copy = pltpu.make_async_copy(map_vmem, map_ref, map_sem)
    map_copy.start()
    rows = base_ref.shape[1]
    found, surface = correction(0, got_ref, own_ref, d_ref, edge_ref, pair_ref, place_ref)
    adj_ref[...] = base_ref[...] + found.reshape(base_ref.shape)
    contribution = contribution_ref[...] + scale * (
        surface * excess_ref[1] + found[0:rows, :] * excess_ref[0]
    )
    map_copy.wait()
    part_ref[...] = add_segments(
        jnp.zeros(part_ref.shape, F32), contribution, range(rows), map_ref
    )


def far_kernel(
    scale,
    own_ref,
    got_ref,
    d_ref,
    excess_ref,
    edge_ref,
    pair_ref,
    place_ref,
    map_vmem,
    base_ref,
    part_in_ref,
    adj_ref,
    part_ref,
    map_ref,
    map_sem,
):
    map_copy = pltpu.make_async_copy(map_vmem, map_ref, map_sem)
    map_copy.start()
    rows = base_ref.shape[1]
    found, surface = correction(1, got_ref, own_ref, d_ref, edge_ref, pair_ref, place_ref)
    contribution = scale * (surface * excess_ref[1] + found[0:rows, :] * excess_ref[0])
    after = sides()[1][0]
    two = jnp.where(
        after,
        jnp.concatenate([contribution[rows - 1 :], contribution[rows - 2 : rows - 1]], axis=0),
        contribution[0:2],
    )
    picked_rows = (jnp.where(after, rows - 1, 0), jnp.where(after, rows - 2, 1))
    map_copy.wait()
    part_ref[...] = add_segments(part_in_ref[...], two, picked_rows, map_ref)
    adj_ref[...] = base_ref[...] + found.reshape(base_ref.shape)


def finish_kernel(adj_vmem, got_ref, adj_hbm, out_hbm, out_ref, sems):
    step = adj_vmem.shape[0] // PIECES
    copies = []
    for n in range(PIECES):
        piece = pl.ds(n * step, step)
        copies.append(
            pltpu.make_async_copy(adj_vmem.at[piece], adj_hbm.at[piece], sems.at[n])
        )
        copies[-1].start()
    out_ref[...] = jnp.sum(got_ref[:, 0, :], axis=0)
    copies.append(pltpu.make_async_copy(out_ref, out_hbm, sems.at[PIECES]))
    copies[-1].start()
    for copy in copies:
        copy.wait()


def per_device(
    conductance, depth_inverse, surface_residual, surface_excess, segment_map, frame_index
):
    _, depth, rows, cols = conductance.shape
    frames = surface_residual.shape[1]
    blocks = segment_map.shape[1]
    size = depth * rows
    spans = lax.axis_size("span")
    devices = spans * lax.axis_size("blade")
    lanes = SEGS // devices
    field = pltpu.VMEM((depth, rows, cols), F32)
    chunks = cols // 128
    packed_far = pltpu.VMEM(((2 * depth + 4) * chunks, 128), F32)
    packed_near = pltpu.VMEM(((2 * depth + 3) * chunks, 128), F32)
    own_far, own_near, k, picked, excess, inverse, ids = pl.pallas_call(
        functools.partial(load_kernel, rows),
        out_shape=(
            packed_far,
            packed_near,
            pltpu.VMEM((chunks * size, 128), F32),
            pltpu.VMEM((STEPS, rows, cols), F32),
            pltpu.VMEM((STEPS, rows, cols), F32),
            pltpu.VMEM((depth, depth), F32),
            pltpu.VMEM((blocks, rows), jnp.int32),
        ),
        in_specs=[HBM] * 6,
        out_specs=(VMEM,) * 7,
        scratch_shapes=[
            pltpu.SMEM((STEPS,), jnp.int32),
            pltpu.VMEM((frames, rows, cols), F32),
            pltpu.SemaphoreType.DMA((5 + chunks,)),
        ],
        compiler_params=GRANT,
        name="load",
    )(
        *(
            pltpu.with_memory_space_constraint(x, pltpu.HBM)
            for x in (
                frame_index,
                conductance.reshape(size, cols),
                surface_residual[0],
                surface_excess[0],
                depth_inverse[0],
                segment_map.T,
            )
        )
    )
    across = [(i, i + 1) for i in range(1, spans - 1, 2)]
    within = [(i, i + 1) for i in range(0, spans - 1, 2)]
    near = lax.ppermute(own_near, "span", within + [(b, a) for a, b in within])
    far = lax.ppermute(own_far, "span", across + [(b, a) for a, b in across])
    scale = 1.0 / math.sqrt(128.0 * STEPS)
    line = pltpu.VMEM((rows, cols), F32)
    base, edge, contribution, pair, place = pl.pallas_call(
        functools.partial(base_kernel, scale),
        out_shape=(
            field,
            pltpu.VMEM((2, depth, cols), F32),
            line,
            pltpu.VMEM((2 * depth, 6 * depth), BF16),
            pltpu.VMEM((2, size, 6 * depth), BF16),
        ),
        in_specs=[VMEM] * 4,
        out_specs=(VMEM,) * 5,
        scratch_shapes=[
            pltpu.VMEM((size, 3 * size), BF16),
            pltpu.VMEM((3, size, cols), BF16),
            pltpu.VMEM((chunks * size, 128), F32),
            field,
            field,
            pltpu.VMEM((depth, 128), F32),
        ],
        compiler_params=GRANT,
        name="base",
    )(k, picked, excess, inverse)
    fixed = (inverse, excess, edge, pair, place, ids)
    sums = pltpu.VMEM((devices, 1, lanes), F32)
    map_scratch = [pltpu.SMEM((blocks, rows), jnp.int32), pltpu.SemaphoreType.DMA]
    base, partial = pl.pallas_call(
        functools.partial(near_kernel, scale),
        out_shape=(field, sums),
        in_specs=[VMEM] * 10,
        out_specs=(VMEM,) * 2,
        scratch_shapes=map_scratch,
        compiler_params=GRANT,
        name="near",
    )(*fixed, base, contribution, own_near, near)
    adjoint, partial = pl.pallas_call(
        functools.partial(far_kernel, scale),
        out_shape=(field, sums),
        in_specs=[VMEM] * 10,
        out_specs=(VMEM,) * 2,
        scratch_shapes=map_scratch,
        compiler_params=GRANT,
        name="far",
    )(own_far, far, *fixed, base, partial)
    pieces = lax.all_to_all(partial, ("blade", "span"), 0, 0, tiled=True)
    adjoint, owned = pl.pallas_call(
        finish_kernel,
        out_shape=(pltpu.HBM((depth, rows, cols), F32), pltpu.HBM((lanes,), F32)),
        in_specs=[VMEM] * 2,
        out_specs=(HBM,) * 2,
        scratch_shapes=[pltpu.VMEM((lanes,), F32), pltpu.SemaphoreType.DMA((PIECES + 1,))],
        compiler_params=GRANT,
        name="finish",
    )(adjoint, pltpu.with_memory_space_constraint(pieces, pltpu.VMEM))
    return (adjoint[None], owned)


def solution(mesh):
    placed = (
        P("blade", None, "span", None),
        P("blade", None, None),
        P("blade", None, "span", None),
        P("blade", None, "span", None),
        P("span", None),
        P(),
    )
    return jax.shard_map(
        per_device,
        mesh=mesh,
        in_specs=placed,
        out_specs=(P("blade", None, "span", None), P(("blade", "span"))),
        check_vma=False,
    )
```

```python
import functools
import math

import jax
import jax.numpy as jnp
from jax import lax
from jax.experimental import pallas as pl
from jax.experimental.pallas import tpu as pltpu
from jax.sharding import PartitionSpec as P

STEPS = 3
SEGS = 2048
PIECES = 4
F32 = jnp.float32
BF16 = jnp.bfloat16
VMEM = pl.BlockSpec(memory_space=pltpu.VMEM)
HBM = pl.BlockSpec(memory_space=pltpu.HBM)
GRANT = pltpu.CompilerParams(vmem_limit_bytes=16 * 2**20)


def split(x):
    high = x.astype(BF16)
    return high, (x - high.astype(F32)).astype(BF16)


def dot(a, b):
    return jnp.dot(a, b, preferred_element_type=F32)


def left_three(matrix):
    high, low = matrix
    return jnp.concatenate([high, low, high], axis=1)


def right_three(x):
    high, low = split(x)
    return jnp.concatenate([high, high, low], axis=0)


def iota(shape, dim):
    return lax.broadcasted_iota(jnp.int32, shape, dim)


def shift_next(x, axis):
    size = x.shape[axis]
    return jnp.where(iota(x.shape, axis) == size - 1, 0.0, pltpu.roll(x, size - 1, axis))


def shift_prev(x, axis, first):
    return jnp.where(iota(x.shape, axis) == 0, first, pltpu.roll(x, 1, axis))


def divergence(v, weight, half, axis):
    flux = weight * (shift_next(v, axis) - v)
    return flux - shift_prev(flux, axis, half * v)


def sides():
    span = lax.axis_index("span")
    count = lax.axis_size("span")
    even = lax.rem(span, 2) == 0
    has_next = span + 1 < count
    has_prev = span > 0
    return (
        (even, jnp.where(even, has_next, has_prev)),
        (jnp.logical_not(even), jnp.where(even, has_prev, has_next)),
    )


def chunked(ref, start, count, step):
    chunks = ref.shape[0] // step
    return jnp.concatenate(
        [ref[c * step + start : c * step + start + count, :] for c in range(chunks)], axis=1
    )


def packed_field(ref, depth, cols, n):
    chunks = cols // 128
    return chunked(ref.at[n * chunks * depth : (n + 1) * chunks * depth], 0, depth, depth)


def packed_line(ref, depth, cols, n):
    chunks = cols // 128
    base = (2 * depth + n) * chunks
    return chunked(ref.at[base : base + chunks], 0, 1, 1)


def row_of_each(ref, chunk, depth, rows, row):
    return ref[pl.ds(chunk * depth * rows + row, depth, stride=rows), :]


def load_kernel(
    rows,
    frame_hbm,
    k_hbm,
    res_hbm,
    excess_hbm,
    d_hbm,
    map_hbm,
    far_ref,
    near_ref,
    k_ref,
    frames_ref,
    excess_ref,
    d_ref,
    map_ref,
    frame_ref,
    res_ref,
    sems,
):
    size, cols = k_hbm.shape
    depth = size // rows
    chunks = cols // 128
    pairs = [
        (k_hbm.at[:, pl.ds(c * 128, 128)], k_ref.at[pl.ds(c * size, size)]) for c in range(chunks)
    ]
    pairs += [(frame_hbm, frame_ref), (res_hbm, res_ref)]
    pairs += [(excess_hbm, excess_ref), (d_hbm, d_ref), (map_hbm, map_ref)]
    copies = [pltpu.make_async_copy(a, b, sems.at[n]) for n, (a, b) in enumerate(pairs)]
    for n, copy in enumerate(copies):
        copy.start(priority=n % 2)
    sent = (near_ref, far_ref)
    picks = []
    for after, _ in sides():
        picks.append((jnp.where(after, rows - 1, 0), jnp.where(after, rows - 2, 1)))
    copies[chunks].wait()
    copies[chunks + 1].wait()
    for step in range(STEPS):
        frames_ref[step] = res_ref[frame_ref[step]]
    base = 2 * chunks * depth
    for ref, (edge, second) in zip(sent, picks):
        for n, (step, row) in enumerate(((2, edge), (1, edge), (2, second))):
            line = frames_ref[step, pl.ds(row, 1), :]
            for c in range(chunks):
                spot = base + n * chunks + c
                ref[spot : spot + 1, :] = line[:, c * 128 : (c + 1) * 128]
        if ref.shape[0] > base + 3 * chunks:
            ref[base + 3 * chunks :, :] = jnp.zeros((ref.shape[0] - base - 3 * chunks, 128), F32)
    for c in range(chunks):
        copies[c].wait()
        for ref, row_pair in zip(sent, picks):
            for n, row in enumerate(row_pair):
                spot = (n * chunks + c) * depth
                ref[spot : spot + depth, :] = row_of_each(k_ref, c, depth, rows, row)
    for copy in copies[2 + chunks :]:
        copy.wait()


def base_kernel(
    scale,
    k_ref,
    frames_ref,
    excess_ref,
    d_ref,
    adj_ref,
    edge_ref,
    contribution_ref,
    pair_ref,
    place_ref,
    mat_ref,
    right_ref,
    first_ref,
    chord_ref,
    span_ref,
    factor_ref,
):
    depth, rows, cols = adj_ref.shape
    size = depth * rows
    factor_ref[...] = jnp.broadcast_to(d_ref[:, 0:1], factor_ref.shape)

    parts = split(d_ref[...])
    tall = (iota((size, depth), 0) // rows == iota((size, depth), 1)).astype(BF16)
    wide = (iota((depth, size), 0) == iota((depth, size), 1) // rows).astype(BF16)
    two = 2 * depth
    tile = (iota((depth, two), 0) == iota((depth, two), 1) % depth).astype(BF16)
    same = iota((size, size), 0) % rows == iota((size, size), 1) % rows
    pair_same = iota((two, two), 0) // depth == iota((two, two), 1) // depth
    row_of = iota((size, two), 0) % rows
    first_half = iota((size, two), 1) < depth
    placed = []
    for after, _ in sides():
        edge = jnp.where(after, rows - 1, 0)
        second = jnp.where(after, rows - 2, 1)
        placed.append(row_of == jnp.where(first_half, edge, second))
    mats, pairs, places = [], [], ([], [])
    for part in parts:
        column = dot(tall, part).astype(BF16)
        row = dot(part, tile)
        mats.append(jnp.where(same, dot(column, wide), 0.0).astype(BF16))
        columns = dot(column, tile)
        for found, target in zip(places, placed):
            found.append(jnp.where(target, columns, 0.0).astype(BF16))
        pairs.append(
            jnp.where(pair_same, jnp.concatenate([row] * 2, axis=0), 0.0).astype(BF16)
        )
    mat_ref[...] = left_three(mats)
    pair_ref[...] = left_three(pairs)
    for n in range(2):
        place_ref[n] = left_three(places[n])

    f = frames_ref[2]
    f_chord = shift_next(f, 1) - f
    f_span = shift_next(f, 0) - f

    def put(i, both):
        high, low = split(both)
        span = pl.ds(i * rows, 2 * rows)
        right_ref[0, span, :] = high
        right_ref[1, span, :] = high
        right_ref[2, span, :] = low

    for i in range(0, depth, 2):
        found = []
        for j in (i, i + 1):
            half = 0.5 * chunked(k_ref, j * rows, rows, size)
            w_chord = half + shift_next(half, 1)
            w_span = half + shift_next(half, 0)
            chord_ref[j] = w_chord
            span_ref[j] = w_span
            edge = half * f
            flux_chord = w_chord * f_chord
            flux_span = w_span * f_span
            moved = f + flux_chord - shift_prev(flux_chord, 1, edge)
            moved = moved + flux_span - shift_prev(flux_span, 0, edge)
            factor = jnp.concatenate(
                [jnp.broadcast_to(factor_ref[j : j + 1, :], (rows, 128))] * (cols // 128), axis=1
            )
            source = factor * moved
            found.append(source + frames_ref[1] if j == 0 else source)
        put(i, jnp.concatenate(found, axis=0))
    right = right_ref[...].reshape(3 * size, cols)
    first = dot(mat_ref[...], right)
    for c in range(cols // 128):
        first_ref[c * size : (c + 1) * size, :] = first[:, c * 128 : (c + 1) * 128]

    for i in range(0, depth, 2):
        found = []
        for j in (i, i + 1):
            v = chunked(first_ref, j * rows, rows, size)
            half = 0.5 * chunked(k_ref, j * rows, rows, size)
            source = (
                v + divergence(v, chord_ref[j], half, 1) + divergence(v, span_ref[j], half, 0)
            )
            found.append(source + frames_ref[0] if j == 0 else source)
        put(i, jnp.concatenate(found, axis=0))
    right = right_ref[...].reshape(3 * size, cols)
    adj_ref[...] = dot(mat_ref[...], right).reshape(depth, rows, cols)

    for n, (after, _) in enumerate(sides()):
        row = jnp.where(after, rows - 1, 0)
        for c in range(cols // 128):
            edge_ref[n, :, c * 128 : (c + 1) * 128] = row_of_each(first_ref, c, depth, rows, row)
    contribution_ref[...] = scale * (
        d_ref[0:1, 0:1] * f * excess_ref[2]
        + chunked(first_ref, 0, rows, size) * excess_ref[1]
        + adj_ref[0] * excess_ref[0]
    )


def correction(n, got, own, d_ref, edge_ref, pair_ref, place_ref):
    _, depth, cols = edge_ref.shape
    rows = place_ref.shape[1] // depth
    after, inside = sides()[n]
    factor = d_ref[:, 0:1]
    half = 0.5 * packed_field(got, depth, cols, 0)
    half_next = 0.5 * packed_field(got, depth, cols, 1)
    half_own = 0.5 * packed_field(own, depth, cols, 0)
    inner = half_own + 0.5 * packed_field(own, depth, cols, 1)
    f = packed_line(got, depth, cols, 0)
    frame = packed_line(got, depth, cols, 1)
    f_next = packed_line(got, depth, cols, 2)
    f_own = packed_line(own, depth, cols, 0)
    face = half + half_own
    flux = (half + shift_next(half, 1)) * (shift_next(f, 1) - f)
    moved = (
        f
        + flux
        - shift_prev(flux, 1, half * f)
        + (half + half_next) * (f_next - f)
        + face * (f_own - f)
    )
    outer = factor * moved + jnp.where(iota((depth, 1), 0) == 0, frame, 0.0)
    sources = [factor * (face * f - half * f_own), jnp.where(inside, outer, 0.0)]
    found = dot(pair_ref[...], right_three(jnp.concatenate(sources, axis=0)))
    e = found[0:depth]
    outer = found[depth:]
    w_chord = half_own + shift_next(half_own, 1)
    change = (
        e
        + divergence(e, w_chord, half_own, 1)
        - (half + half_own + inner) * e
        + face * outer
        - half * edge_ref[n]
    )
    found = dot(place_ref[n], right_three(jnp.concatenate([change, inner * e], axis=0)))
    row = jnp.where(after, rows - 1, 0)
    return found, jnp.where(iota((rows, cols), 0) == row, e[0:1, :], 0.0)


def add_segments(total, contribution, picked_rows, map_ref):
    owners, _, lanes = total.shape
    shape = (owners, 128)
    lane = iota(shape, 1)
    segment = jnp.where(lane < lanes, iota(shape, 0) * lanes + lane, -1)
    found = jnp.zeros(shape, F32)
    for block in range(contribution.shape[1] // 128):
        part = contribution[:, block * 128 : (block + 1) * 128]
        sums = jnp.sum(part, axis=1, keepdims=True)
        for n, row in enumerate(picked_rows):
            found += jnp.where(segment == map_ref[block, row], sums[n : n + 1, :], 0.0)
    return total + found[:, None, :lanes]


def near_kernel(
    scale,
    d_ref,
    excess_ref,
    edge_ref,
    pair_ref,
    place_ref,
    map_vmem,
    base_ref,
    contribution_ref,
    own_ref,
    got_ref,
    adj_ref,
    part_ref,
    map_ref,
    map_sem,
):
    map_copy = pltpu.make_async_copy(map_vmem, map_ref, map_sem)
    map_copy.start()
    rows = base_ref.shape[1]
    found, surface = correction(0, got_ref, own_ref, d_ref, edge_ref, pair_ref, place_ref)
    adj_ref[...] = base_ref[...] + found.reshape(base_ref.shape)
    contribution = contribution_ref[...] + scale * (
        surface * excess_ref[1] + found[0:rows, :] * excess_ref[0]
    )
    map_copy.wait()
    part_ref[...] = add_segments(
        jnp.zeros(part_ref.shape, F32), contribution, range(rows), map_ref
    )


def far_kernel(
    scale,
    own_ref,
    got_ref,
    d_ref,
    excess_ref,
    edge_ref,
    pair_ref,
    place_ref,
    map_vmem,
    base_ref,
    part_in_ref,
    adj_ref,
    part_ref,
    map_ref,
    map_sem,
):
    map_copy = pltpu.make_async_copy(map_vmem, map_ref, map_sem)
    map_copy.start()
    rows = base_ref.shape[1]
    found, surface = correction(1, got_ref, own_ref, d_ref, edge_ref, pair_ref, place_ref)
    contribution = scale * (surface * excess_ref[1] + found[0:rows, :] * excess_ref[0])
    after = sides()[1][0]
    two = jnp.where(
        after,
        jnp.concatenate([contribution[rows - 1 :], contribution[rows - 2 : rows - 1]], axis=0),
        contribution[0:2],
    )
    picked_rows = (jnp.where(after, rows - 1, 0), jnp.where(after, rows - 2, 1))
    map_copy.wait()
    part_ref[...] = add_segments(part_in_ref[...], two, picked_rows, map_ref)
    adj_ref[...] = base_ref[...] + found.reshape(base_ref.shape)


def finish_kernel(adj_vmem, got_ref, adj_hbm, out_hbm, out_ref, sems):
    step = adj_vmem.shape[0] // PIECES
    copies = []
    for n in range(PIECES):
        piece = pl.ds(n * step, step)
        copies.append(
            pltpu.make_async_copy(adj_vmem.at[piece], adj_hbm.at[piece], sems.at[n])
        )
        copies[-1].start(priority=n % 2)
    out_ref[...] = jnp.sum(got_ref[:, 0, :], axis=0)
    copies.append(pltpu.make_async_copy(out_ref, out_hbm, sems.at[PIECES]))
    copies[-1].start()
    for copy in copies:
        copy.wait()


def per_device(
    conductance, depth_inverse, surface_residual, surface_excess, segment_map, frame_index
):
    _, depth, rows, cols = conductance.shape
    frames = surface_residual.shape[1]
    blocks = segment_map.shape[1]
    size = depth * rows
    spans = lax.axis_size("span")
    devices = spans * lax.axis_size("blade")
    lanes = SEGS // devices
    field = pltpu.VMEM((depth, rows, cols), F32)
    chunks = cols // 128
    packed_far = pltpu.VMEM(((2 * depth + 4) * chunks, 128), F32)
    packed_near = pltpu.VMEM(((2 * depth + 3) * chunks, 128), F32)
    own_far, own_near, k, picked, excess, inverse, ids = pl.pallas_call(
        functools.partial(load_kernel, rows),
        out_shape=(
            packed_far,
            packed_near,
            pltpu.VMEM((chunks * size, 128), F32),
            pltpu.VMEM((STEPS, rows, cols), F32),
            pltpu.VMEM((STEPS, rows, cols), F32),
            pltpu.VMEM((depth, depth), F32),
            pltpu.VMEM((blocks, rows), jnp.int32),
        ),
        in_specs=[HBM] * 6,
        out_specs=(VMEM,) * 7,
        scratch_shapes=[
            pltpu.SMEM((STEPS,), jnp.int32),
            pltpu.VMEM((frames, rows, cols), F32),
            pltpu.SemaphoreType.DMA((5 + chunks,)),
        ],
        compiler_params=GRANT,
        name="load",
    )(
        *(
            pltpu.with_memory_space_constraint(x, pltpu.HBM)
            for x in (
                frame_index,
                conductance.reshape(size, cols),
                surface_residual[0],
                surface_excess[0],
                depth_inverse[0],
                segment_map.T,
            )
        )
    )
    across = [(i, i + 1) for i in range(1, spans - 1, 2)]
    within = [(i, i + 1) for i in range(0, spans - 1, 2)]
    near = lax.ppermute(own_near, "span", within + [(b, a) for a, b in within])
    far = lax.ppermute(own_far, "span", across + [(b, a) for a, b in across])
    scale = 1.0 / math.sqrt(128.0 * STEPS)
    line = pltpu.VMEM((rows, cols), F32)
    base, edge, contribution, pair, place = pl.pallas_call(
        functools.partial(base_kernel, scale),
        out_shape=(
            field,
            pltpu.VMEM((2, depth, cols), F32),
            line,
            pltpu.VMEM((2 * depth, 6 * depth), BF16),
            pltpu.VMEM((2, size, 6 * depth), BF16),
        ),
        in_specs=[VMEM] * 4,
        out_specs=(VMEM,) * 5,
        scratch_shapes=[
            pltpu.VMEM((size, 3 * size), BF16),
            pltpu.VMEM((3, size, cols), BF16),
            pltpu.VMEM((chunks * size, 128), F32),
            field,
            field,
            pltpu.VMEM((depth, 128), F32),
        ],
        compiler_params=GRANT,
        name="base",
    )(k, picked, excess, inverse)
    fixed = (inverse, excess, edge, pair, place, ids)
    sums = pltpu.VMEM((devices, 1, lanes), F32)
    map_scratch = [pltpu.SMEM((blocks, rows), jnp.int32), pltpu.SemaphoreType.DMA]
    base, partial = pl.pallas_call(
        functools.partial(near_kernel, scale),
        out_shape=(field, sums),
        in_specs=[VMEM] * 10,
        out_specs=(VMEM,) * 2,
        scratch_shapes=map_scratch,
        compiler_params=GRANT,
        name="near",
    )(*fixed, base, contribution, own_near, near)
    adjoint, partial = pl.pallas_call(
        functools.partial(far_kernel, scale),
        out_shape=(field, sums),
        in_specs=[VMEM] * 10,
        out_specs=(VMEM,) * 2,
        scratch_shapes=map_scratch,
        compiler_params=GRANT,
        name="far",
    )(own_far, far, *fixed, base, partial)
    pieces = lax.all_to_all(partial, ("blade", "span"), 0, 0, tiled=True)
    adjoint, owned = pl.pallas_call(
        finish_kernel,
        out_shape=(pltpu.HBM((depth, rows, cols), F32), pltpu.HBM((lanes,), F32)),
        in_specs=[VMEM] * 2,
        out_specs=(HBM,) * 2,
        scratch_shapes=[pltpu.VMEM((lanes,), F32), pltpu.SemaphoreType.DMA((PIECES + 1,))],
        compiler_params=GRANT,
        name="finish",
    )(adjoint, pltpu.with_memory_space_constraint(pieces, pltpu.VMEM))
    return (adjoint[None], owned)


def solution(mesh):
    placed = (
        P("blade", None, "span", None),
        P("blade", None, None),
        P("blade", None, "span", None),
        P("blade", None, "span", None),
        P("span", None),
        P(),
    )
    return jax.shard_map(
        per_device,
        mesh=mesh,
        in_specs=placed,
        out_specs=(P("blade", None, "span", None), P(("blade", "span"))),
        check_vma=False,
    )
```

```python
import functools
import math

import jax
import jax.numpy as jnp
from jax import lax
from jax.experimental import pallas as pl
from jax.experimental.pallas import tpu as pltpu
from jax.sharding import PartitionSpec as P

STEPS = 3
SEGS = 2048
F32 = jnp.float32
BF16 = jnp.bfloat16
VMEM = pl.BlockSpec(memory_space=pltpu.VMEM)
HBM = pl.BlockSpec(memory_space=pltpu.HBM)
GRANT = pltpu.CompilerParams(vmem_limit_bytes=16 * 2**20)


def split(x):
    high = x.astype(BF16)
    return high, (x - high.astype(F32)).astype(BF16)


def dot(a, b):
    return jnp.dot(a, b, preferred_element_type=F32)


def left_three(matrix):
    high, low = matrix
    return jnp.concatenate([high, low, high], axis=1)


def right_three(x):
    high, low = split(x)
    return jnp.concatenate([high, high, low], axis=0)


def iota(shape, dim):
    return lax.broadcasted_iota(jnp.int32, shape, dim)


def shift_next(x, axis):
    size = x.shape[axis]
    return jnp.where(iota(x.shape, axis) == size - 1, 0.0, pltpu.roll(x, size - 1, axis))


def shift_prev(x, axis, first):
    return jnp.where(iota(x.shape, axis) == 0, first, pltpu.roll(x, 1, axis))


def divergence(v, weight, half, axis):
    flux = weight * (shift_next(v, axis) - v)
    return flux - shift_prev(flux, axis, half * v)


def sides():
    span = lax.axis_index("span")
    count = lax.axis_size("span")
    even = lax.rem(span, 2) == 0
    has_next = span + 1 < count
    has_prev = span > 0
    return (
        (even, jnp.where(even, has_next, has_prev)),
        (jnp.logical_not(even), jnp.where(even, has_prev, has_next)),
    )


def chunked(ref, start, count, step):
    chunks = ref.shape[0] // step
    return jnp.concatenate(
        [ref[c * step + start : c * step + start + count, :] for c in range(chunks)], axis=1
    )


def packed_field(ref, depth, cols, n):
    chunks = cols // 128
    return chunked(ref.at[n * chunks * depth : (n + 1) * chunks * depth], 0, depth, depth)


def packed_line(ref, depth, cols, n):
    chunks = cols // 128
    base = (2 * depth + n) * chunks
    return chunked(ref.at[base : base + chunks], 0, 1, 1)


def row_of_each(ref, chunk, depth, rows, row):
    return ref[pl.ds(chunk * depth * rows + row, depth, stride=rows), :]


def far_rows(rows):
    after = sides()[1][0]
    return jnp.where(after, rows - 1, 0), jnp.where(after, rows - 2, 1)


def load_kernel(
    rows,
    frame_hbm,
    k_hbm,
    res_hbm,
    d_hbm,
    far_ref,
    near_ref,
    k_ref,
    frames_ref,
    d_ref,
    frame_ref,
    res_ref,
    sems,
):
    size, cols = k_hbm.shape
    depth = size // rows
    chunks = cols // 128
    pairs = [(frame_hbm, frame_ref), (res_hbm, res_ref)]
    for c in range(chunks):
        pairs.append((k_hbm.at[:, pl.ds(c * 128, 128)], k_ref.at[pl.ds(c * size, size)]))
    pairs.append((d_hbm, d_ref))
    copies = [pltpu.make_async_copy(a, b, sems.at[n]) for n, (a, b) in enumerate(pairs)]
    for copy in copies:
        copy.start()
    sent = (near_ref, far_ref)
    picks = []
    for after, _ in sides():
        picks.append((jnp.where(after, rows - 1, 0), jnp.where(after, rows - 2, 1)))
    copies[0].wait()
    copies[1].wait()
    for step in range(STEPS):
        frames_ref[step] = res_ref[frame_ref[step]]
    base = 2 * chunks * depth
    for ref, (edge, second) in zip(sent, picks):
        for n, (step, row) in enumerate(((2, edge), (1, edge), (2, second))):
            line = frames_ref[step, pl.ds(row, 1), :]
            for c in range(chunks):
                spot = base + n * chunks + c
                ref[spot : spot + 1, :] = line[:, c * 128 : (c + 1) * 128]
        if ref.shape[0] > base + 3 * chunks:
            ref[base + 3 * chunks :, :] = jnp.zeros((ref.shape[0] - base - 3 * chunks, 128), F32)
    for c in range(chunks):
        copies[2 + c].wait()
        for ref, row_pair in zip(sent, picks):
            for n, row in enumerate(row_pair):
                spot = (n * chunks + c) * depth
                ref[spot : spot + depth, :] = row_of_each(k_ref, c, depth, rows, row)
    for copy in copies[2 + chunks :]:
        copy.wait()


def base_kernel(
    scale,
    k_ref,
    frames_ref,
    d_ref,
    excess_hbm,
    map_hbm,
    adj_ref,
    two_ref,
    excess_ref,
    map_ref,
    edge_ref,
    contribution_ref,
    pair_ref,
    place_ref,
    mat_ref,
    right_ref,
    first_ref,
    chord_ref,
    span_ref,
    factor_ref,
    sems,
):
    copies = [
        pltpu.make_async_copy(excess_hbm, excess_ref, sems.at[0]),
        pltpu.make_async_copy(map_hbm, map_ref, sems.at[1]),
    ]
    for copy in copies:
        copy.start()
    depth, rows, cols = chord_ref.shape
    size = depth * rows
    factor_ref[...] = jnp.broadcast_to(d_ref[:, 0:1], factor_ref.shape)

    parts = split(d_ref[...])
    tall = (iota((size, depth), 0) // rows == iota((size, depth), 1)).astype(BF16)
    wide = (iota((depth, size), 0) == iota((depth, size), 1) // rows).astype(BF16)
    two = 2 * depth
    tile = (iota((depth, two), 0) == iota((depth, two), 1) % depth).astype(BF16)
    same = iota((size, size), 0) % rows == iota((size, size), 1) % rows
    pair_same = iota((two, two), 0) // depth == iota((two, two), 1) // depth
    row_of = iota((size, two), 0) % rows
    first_half = iota((size, two), 1) < depth
    after = sides()[0][0]
    edge = jnp.where(after, rows - 1, 0)
    second = jnp.where(after, rows - 2, 1)
    placed = row_of == jnp.where(first_half, edge, second)
    mats, pairs, places = [], [], []
    for part in parts:
        column = dot(tall, part).astype(BF16)
        row = dot(part, tile)
        mats.append(jnp.where(same, dot(column, wide), 0.0).astype(BF16))
        places.append(jnp.where(placed, dot(column, tile), 0.0).astype(BF16))
        pairs.append(
            jnp.where(pair_same, jnp.concatenate([row] * 2, axis=0), 0.0).astype(BF16)
        )
    mat_ref[...] = left_three(mats)
    pair_ref[...] = left_three(pairs)
    place_ref[...] = left_three(places)

    f = frames_ref[2]
    f_chord = shift_next(f, 1) - f
    f_span = shift_next(f, 0) - f

    def put(i, both):
        high, low = split(both)
        span = pl.ds(i * rows, 2 * rows)
        right_ref[0, span, :] = high
        right_ref[1, span, :] = high
        right_ref[2, span, :] = low

    for i in range(0, depth, 2):
        found = []
        for j in (i, i + 1):
            half = 0.5 * chunked(k_ref, j * rows, rows, size)
            w_chord = half + shift_next(half, 1)
            w_span = half + shift_next(half, 0)
            chord_ref[j] = w_chord
            span_ref[j] = w_span
            edge = half * f
            flux_chord = w_chord * f_chord
            flux_span = w_span * f_span
            moved = f + flux_chord - shift_prev(flux_chord, 1, edge)
            moved = moved + flux_span - shift_prev(flux_span, 0, edge)
            factor = jnp.concatenate(
                [jnp.broadcast_to(factor_ref[j : j + 1, :], (rows, 128))] * (cols // 128), axis=1
            )
            source = factor * moved
            found.append(source + frames_ref[1] if j == 0 else source)
        put(i, jnp.concatenate(found, axis=0))
    right = right_ref[...].reshape(3 * size, cols)
    first = dot(mat_ref[...], right)
    for c in range(cols // 128):
        first_ref[c * size : (c + 1) * size, :] = first[:, c * 128 : (c + 1) * 128]

    for i in range(0, depth, 2):
        found = []
        for j in (i, i + 1):
            v = chunked(first_ref, j * rows, rows, size)
            half = 0.5 * chunked(k_ref, j * rows, rows, size)
            source = (
                v + divergence(v, chord_ref[j], half, 1) + divergence(v, span_ref[j], half, 0)
            )
            found.append(source + frames_ref[0] if j == 0 else source)
        put(i, jnp.concatenate(found, axis=0))
    right = right_ref[...].reshape(3 * size, cols)
    adj = dot(mat_ref[...], right)
    for c in range(cols // 128):
        adj_ref[c * size : (c + 1) * size, :] = adj[:, c * 128 : (c + 1) * 128]

    for n, (after, _) in enumerate(sides()):
        row = jnp.where(after, rows - 1, 0)
        for c in range(cols // 128):
            edge_ref[n, :, c * 128 : (c + 1) * 128] = row_of_each(first_ref, c, depth, rows, row)
    for n, row in enumerate(far_rows(rows)):
        for c in range(cols // 128):
            two_ref[n, :, c * 128 : (c + 1) * 128] = row_of_each(adj_ref, c, depth, rows, row)
    for copy in copies:
        copy.wait()
    contribution_ref[...] = scale * (
        d_ref[0:1, 0:1] * f * excess_ref[2]
        + chunked(first_ref, 0, rows, size) * excess_ref[1]
        + chunked(adj_ref, 0, rows, size) * excess_ref[0]
    )


def correction(n, got, own, d_ref, edge_ref, pair_ref):
    _, depth, cols = edge_ref.shape
    _, inside = sides()[n]
    factor = d_ref[:, 0:1]
    half = 0.5 * packed_field(got, depth, cols, 0)
    half_next = 0.5 * packed_field(got, depth, cols, 1)
    half_own = 0.5 * packed_field(own, depth, cols, 0)
    inner = half_own + 0.5 * packed_field(own, depth, cols, 1)
    f = packed_line(got, depth, cols, 0)
    frame = packed_line(got, depth, cols, 1)
    f_next = packed_line(got, depth, cols, 2)
    f_own = packed_line(own, depth, cols, 0)
    face = half + half_own
    flux = (half + shift_next(half, 1)) * (shift_next(f, 1) - f)
    moved = (
        f
        + flux
        - shift_prev(flux, 1, half * f)
        + (half + half_next) * (f_next - f)
        + face * (f_own - f)
    )
    outer = factor * moved + jnp.where(iota((depth, 1), 0) == 0, frame, 0.0)
    sources = [factor * (face * f - half * f_own), jnp.where(inside, outer, 0.0)]
    found = dot(pair_ref[...], right_three(jnp.concatenate(sources, axis=0)))
    e = found[0:depth]
    outer = found[depth:]
    w_chord = half_own + shift_next(half_own, 1)
    change = (
        e
        + divergence(e, w_chord, half_own, 1)
        - (half + half_own + inner) * e
        + face * outer
        - half * edge_ref[n]
    )
    return right_three(jnp.concatenate([change, inner * e], axis=0)), e[0:1, :]


def add_segments(total, contribution, picked_rows, map_ref):
    owners, _, lanes = total.shape
    shape = (owners, 128)
    lane = iota(shape, 1)
    segment = jnp.where(lane < lanes, iota(shape, 0) * lanes + lane, -1)
    found = jnp.zeros(shape, F32)
    for block in range(contribution.shape[1] // 128):
        part = contribution[:, block * 128 : (block + 1) * 128]
        sums = jnp.sum(part, axis=1, keepdims=True)
        for n, row in enumerate(picked_rows):
            found += jnp.where(segment == map_ref[block, row], sums[n : n + 1, :], 0.0)
    return total + found[:, None, :lanes]


def near_kernel(
    scale,
    d_ref,
    excess_ref,
    edge_ref,
    pair_ref,
    map_vmem,
    place_ref,
    base_ref,
    contribution_ref,
    own_ref,
    got_ref,
    adj_hbm,
    part_ref,
    adj_ref,
    map_ref,
    sems,
):
    map_copy = pltpu.make_async_copy(map_vmem, map_ref, sems.at[0])
    map_copy.start()
    depth, rows, cols = adj_ref.shape
    size = depth * rows
    sources, surface = correction(0, got_ref, own_ref, d_ref, edge_ref, pair_ref)
    found = dot(place_ref[...], sources)
    adj_ref[...] = (chunked(base_ref, 0, size, size) + found).reshape(depth, rows, cols)
    adj_copy = pltpu.make_async_copy(adj_ref, adj_hbm, sems.at[1])
    adj_copy.start()
    row = jnp.where(sides()[0][0], rows - 1, 0)
    surface = jnp.where(iota((rows, cols), 0) == row, surface, 0.0)
    contribution = contribution_ref[...] + scale * (
        surface * excess_ref[1] + found[0:rows, :] * excess_ref[0]
    )
    map_copy.wait()
    part_ref[...] = add_segments(
        jnp.zeros(part_ref.shape, F32), contribution, range(rows), map_ref
    )
    adj_copy.wait()


def far_kernel(
    scale,
    own_ref,
    got_ref,
    d_ref,
    excess_ref,
    edge_ref,
    pair_ref,
    map_vmem,
    two_ref,
    part_in_ref,
    out_ref,
    part_ref,
    map_ref,
    map_sem,
):
    map_copy = pltpu.make_async_copy(map_vmem, map_ref, map_sem)
    map_copy.start()
    depth = two_ref.shape[1]
    rows = excess_ref.shape[1]
    sources, surface = correction(1, got_ref, own_ref, d_ref, edge_ref, pair_ref)
    found = dot(pair_ref[...], sources)
    edge, second = far_rows(rows)
    contribution = scale * jnp.concatenate(
        [
            surface * excess_ref[1, pl.ds(edge, 1), :]
            + found[0:1] * excess_ref[0, pl.ds(edge, 1), :],
            found[depth : depth + 1] * excess_ref[0, pl.ds(second, 1), :],
        ],
        axis=0,
    )
    map_copy.wait()
    part_ref[...] = add_segments(part_in_ref[...], contribution, (edge, second), map_ref)
    out_ref[...] = two_ref[...] + found.reshape(two_ref.shape)


def finish_kernel(_, two_ref, got_ref, adj_hbm, out_hbm, out_ref, sems):
    copies = []
    for n, row in enumerate(far_rows(adj_hbm.shape[1])):
        copies.append(pltpu.make_async_copy(two_ref.at[n], adj_hbm.at[:, row, :], sems.at[n]))
        copies[-1].start()
    out_ref[...] = jnp.sum(got_ref[:, 0, :], axis=0)
    copies.append(pltpu.make_async_copy(out_ref, out_hbm, sems.at[2]))
    copies[-1].start()
    for copy in copies:
        copy.wait()


def in_hbm(x):
    return pltpu.with_memory_space_constraint(x, pltpu.HBM)


def per_device(
    conductance, depth_inverse, surface_residual, surface_excess, segment_map, frame_index
):
    _, depth, rows, cols = conductance.shape
    frames = surface_residual.shape[1]
    blocks = segment_map.shape[1]
    size = depth * rows
    spans = lax.axis_size("span")
    devices = spans * lax.axis_size("blade")
    lanes = SEGS // devices
    field = pltpu.VMEM((depth, rows, cols), F32)
    chunks = cols // 128
    packed_far = pltpu.VMEM(((2 * depth + 4) * chunks, 128), F32)
    packed_near = pltpu.VMEM(((2 * depth + 3) * chunks, 128), F32)
    own_far, own_near, k, picked, inverse = pl.pallas_call(
        functools.partial(load_kernel, rows),
        out_shape=(
            packed_far,
            packed_near,
            pltpu.VMEM((chunks * size, 128), F32),
            pltpu.VMEM((STEPS, rows, cols), F32),
            pltpu.VMEM((depth, depth), F32),
        ),
        in_specs=[HBM] * 4,
        out_specs=(VMEM,) * 5,
        scratch_shapes=[
            pltpu.SMEM((STEPS,), jnp.int32),
            pltpu.VMEM((frames, rows, cols), F32),
            pltpu.SemaphoreType.DMA((3 + chunks,)),
        ],
        compiler_params=GRANT,
        name="load",
    )(
        in_hbm(frame_index),
        in_hbm(conductance.reshape(size, cols)),
        in_hbm(surface_residual[0]),
        in_hbm(depth_inverse[0]),
    )
    across = [(i, i + 1) for i in range(1, spans - 1, 2)]
    within = [(i, i + 1) for i in range(0, spans - 1, 2)]
    near = lax.ppermute(own_near, "span", within + [(b, a) for a, b in within])
    far = lax.ppermute(own_far, "span", across + [(b, a) for a, b in across])
    scale = 1.0 / math.sqrt(128.0 * STEPS)
    line = pltpu.VMEM((rows, cols), F32)
    base, two, excess, ids, edge, contribution, pair, place = pl.pallas_call(
        functools.partial(base_kernel, scale),
        out_shape=(
            pltpu.VMEM((chunks * size, 128), F32),
            pltpu.VMEM((2, depth, cols), F32),
            pltpu.VMEM((STEPS, rows, cols), F32),
            pltpu.VMEM((blocks, rows), jnp.int32),
            pltpu.VMEM((2, depth, cols), F32),
            line,
            pltpu.VMEM((2 * depth, 6 * depth), BF16),
            pltpu.VMEM((size, 6 * depth), BF16),
        ),
        in_specs=[VMEM] * 3 + [HBM] * 2,
        out_specs=(VMEM,) * 8,
        scratch_shapes=[
            pltpu.VMEM((size, 3 * size), BF16),
            pltpu.VMEM((3, size, cols), BF16),
            pltpu.VMEM((chunks * size, 128), F32),
            field,
            field,
            pltpu.VMEM((depth, 128), F32),
            pltpu.SemaphoreType.DMA((2,)),
        ],
        compiler_params=GRANT,
        name="base",
    )(k, picked, inverse, in_hbm(surface_excess[0]), in_hbm(segment_map.T))
    fixed = (inverse, excess, edge, pair, ids)
    sums = pltpu.VMEM((devices, 1, lanes), F32)
    adjoint, partial = pl.pallas_call(
        functools.partial(near_kernel, scale),
        out_shape=(pltpu.HBM((depth, rows, cols), F32), sums),
        in_specs=[VMEM] * 10,
        out_specs=(HBM, VMEM),
        scratch_shapes=[
            field,
            pltpu.SMEM((blocks, rows), jnp.int32),
            pltpu.SemaphoreType.DMA((2,)),
        ],
        compiler_params=GRANT,
        name="near",
    )(*fixed, place, base, contribution, own_near, near)
    two, partial = pl.pallas_call(
        functools.partial(far_kernel, scale),
        out_shape=(pltpu.VMEM((2, depth, cols), F32), sums),
        in_specs=[VMEM] * 9,
        out_specs=(VMEM,) * 2,
        scratch_shapes=[pltpu.SMEM((blocks, rows), jnp.int32), pltpu.SemaphoreType.DMA],
        compiler_params=GRANT,
        name="far",
    )(own_far, far, *fixed, two, partial)
    pieces = lax.all_to_all(partial, ("blade", "span"), 0, 0, tiled=True)
    adjoint, owned = pl.pallas_call(
        finish_kernel,
        out_shape=(pltpu.HBM((depth, rows, cols), F32), pltpu.HBM((lanes,), F32)),
        in_specs=[HBM, VMEM, VMEM],
        out_specs=(HBM,) * 2,
        scratch_shapes=[pltpu.VMEM((lanes,), F32), pltpu.SemaphoreType.DMA((3,))],
        input_output_aliases={0: 0},
        compiler_params=GRANT,
        name="finish",
    )(in_hbm(adjoint), two, pltpu.with_memory_space_constraint(pieces, pltpu.VMEM))
    return (adjoint[None], owned)


def solution(mesh):
    placed = (
        P("blade", None, "span", None),
        P("blade", None, None),
        P("blade", None, "span", None),
        P("blade", None, "span", None),
        P("span", None),
        P(),
    )
    return jax.shard_map(
        per_device,
        mesh=mesh,
        in_specs=placed,
        out_specs=(P("blade", None, "span", None), P(("blade", "span"))),
        check_vma=False,
    )
```

```python
import functools
import math

import jax
import jax.numpy as jnp
from jax import lax
from jax.experimental import pallas as pl
from jax.experimental.pallas import tpu as pltpu
from jax.sharding import PartitionSpec as P

STEPS = 3
SEGS = 2048
F32 = jnp.float32
BF16 = jnp.bfloat16
VMEM = pl.BlockSpec(memory_space=pltpu.VMEM)
HBM = pl.BlockSpec(memory_space=pltpu.HBM)
GRANT = pltpu.CompilerParams(vmem_limit_bytes=16 * 2**20)


def split(x):
    high = x.astype(BF16)
    return high, (x - high.astype(F32)).astype(BF16)


def dot(a, b):
    return jnp.dot(a, b, preferred_element_type=F32)


def left_three(matrix):
    high, low = matrix
    return jnp.concatenate([high, low, high], axis=1)


def right_three(x):
    high, low = split(x)
    return jnp.concatenate([high, high, low], axis=0)


def iota(shape, dim):
    return lax.broadcasted_iota(jnp.int32, shape, dim)


def shift_next(x, axis):
    size = x.shape[axis]
    return jnp.where(iota(x.shape, axis) == size - 1, 0.0, pltpu.roll(x, size - 1, axis))


def shift_prev(x, axis, first):
    return jnp.where(iota(x.shape, axis) == 0, first, pltpu.roll(x, 1, axis))


def divergence(v, weight, half, axis):
    flux = weight * (shift_next(v, axis) - v)
    return flux - shift_prev(flux, axis, half * v)


def sides():
    span = lax.axis_index("span")
    count = lax.axis_size("span")
    even = lax.rem(span, 2) == 0
    has_next = span + 1 < count
    has_prev = span > 0
    return (
        (even, jnp.where(even, has_next, has_prev)),
        (jnp.logical_not(even), jnp.where(even, has_prev, has_next)),
    )


def chunked(ref, start, count, step):
    chunks = ref.shape[0] // step
    return jnp.concatenate(
        [ref[c * step + start : c * step + start + count, :] for c in range(chunks)], axis=1
    )


def packed_field(ref, depth, cols, n):
    chunks = cols // 128
    return chunked(ref.at[n * chunks * depth : (n + 1) * chunks * depth], 0, depth, depth)


def packed_line(ref, depth, cols, n):
    chunks = cols // 128
    base = (2 * depth + n) * chunks
    return chunked(ref.at[base : base + chunks], 0, 1, 1)


def row_of_each(ref, chunk, depth, rows, row):
    return ref[pl.ds(chunk * depth * rows + row, depth, stride=rows), :]


def far_rows(rows):
    after = sides()[1][0]
    return jnp.where(after, rows - 1, 0), jnp.where(after, rows - 2, 1)


def load_kernel(
    rows,
    frame_hbm,
    k_hbm,
    res_hbm,
    d_hbm,
    far_ref,
    near_ref,
    k_ref,
    frames_ref,
    d_ref,
    frame_ref,
    res_ref,
    sems,
):
    size, cols = k_hbm.shape
    depth = size // rows
    chunks = cols // 128
    pairs = [(frame_hbm, frame_ref), (res_hbm, res_ref)]
    for c in range(chunks):
        pairs.append((k_hbm.at[:, pl.ds(c * 128, 128)], k_ref.at[pl.ds(c * size, size)]))
    pairs.append((d_hbm, d_ref))
    copies = [pltpu.make_async_copy(a, b, sems.at[n]) for n, (a, b) in enumerate(pairs)]
    for copy in copies:
        copy.start()
    sent = (near_ref, far_ref)
    picks = []
    for after, _ in sides():
        picks.append((jnp.where(after, rows - 1, 0), jnp.where(after, rows - 2, 1)))
    copies[0].wait()
    copies[1].wait()
    for step in range(STEPS):
        frames_ref[step] = res_ref[frame_ref[step]]
    base = 2 * chunks * depth
    for ref, (edge, second) in zip(sent, picks):
        for n, (step, row) in enumerate(((2, edge), (1, edge), (2, second))):
            line = frames_ref[step, pl.ds(row, 1), :]
            for c in range(chunks):
                spot = base + n * chunks + c
                ref[spot : spot + 1, :] = line[:, c * 128 : (c + 1) * 128]
        if ref.shape[0] > base + 3 * chunks:
            ref[base + 3 * chunks :, :] = jnp.zeros((ref.shape[0] - base - 3 * chunks, 128), F32)
    for c in range(chunks):
        copies[2 + c].wait()
        for ref, row_pair in zip(sent, picks):
            for n, row in enumerate(row_pair):
                spot = (n * chunks + c) * depth
                ref[spot : spot + depth, :] = row_of_each(k_ref, c, depth, rows, row)
    for copy in copies[2 + chunks :]:
        copy.wait()


def base_kernel(
    scale,
    k_ref,
    frames_ref,
    d_ref,
    excess_hbm,
    map_hbm,
    adj_ref,
    two_ref,
    excess_ref,
    map_ref,
    edge_ref,
    contribution_ref,
    pair_ref,
    place_ref,
    mat_ref,
    right_ref,
    first_ref,
    chord_ref,
    span_ref,
    factor_ref,
    sems,
):
    copies = [
        pltpu.make_async_copy(excess_hbm, excess_ref, sems.at[0]),
        pltpu.make_async_copy(map_hbm, map_ref, sems.at[1]),
    ]
    for copy in copies:
        copy.start()
    depth, rows, cols = chord_ref.shape
    size = depth * rows
    factor_ref[...] = jnp.broadcast_to(d_ref[:, 0:1], factor_ref.shape)

    parts = split(d_ref[...])
    tall = (iota((size, depth), 0) // rows == iota((size, depth), 1)).astype(BF16)
    wide = (iota((depth, size), 0) == iota((depth, size), 1) // rows).astype(BF16)
    two = 2 * depth
    tile = (iota((depth, two), 0) == iota((depth, two), 1) % depth).astype(BF16)
    same = iota((size, size), 0) % rows == iota((size, size), 1) % rows
    pair_same = iota((two, two), 0) // depth == iota((two, two), 1) // depth
    row_of = iota((size, two), 0) % rows
    first_half = iota((size, two), 1) < depth
    after = sides()[0][0]
    edge = jnp.where(after, rows - 1, 0)
    second = jnp.where(after, rows - 2, 1)
    placed = row_of == jnp.where(first_half, edge, second)
    mats, pairs, places = [], [], []
    for part in parts:
        column = dot(tall, part).astype(BF16)
        row = dot(part, tile)
        mats.append(jnp.where(same, dot(column, wide), 0.0).astype(BF16))
        places.append(jnp.where(placed, dot(column, tile), 0.0).astype(BF16))
        pairs.append(
            jnp.where(pair_same, jnp.concatenate([row] * 2, axis=0), 0.0).astype(BF16)
        )
    mat_ref[...] = left_three(mats)
    pair_ref[...] = left_three(pairs)
    place_ref[...] = left_three(places)

    f = frames_ref[2]
    f_chord = shift_next(f, 1) - f
    f_span = shift_next(f, 0) - f

    def put(i, both):
        high, low = split(both)
        span = pl.ds(i * rows, 2 * rows)
        right_ref[0, span, :] = high
        right_ref[1, span, :] = high
        right_ref[2, span, :] = low

    for i in range(0, depth, 2):
        found = []
        for j in (i, i + 1):
            half = 0.5 * chunked(k_ref, j * rows, rows, size)
            w_chord = half + shift_next(half, 1)
            w_span = half + shift_next(half, 0)
            chord_ref[j] = w_chord
            span_ref[j] = w_span
            edge = half * f
            flux_chord = w_chord * f_chord
            flux_span = w_span * f_span
            moved = f + flux_chord - shift_prev(flux_chord, 1, edge)
            moved = moved + flux_span - shift_prev(flux_span, 0, edge)
            factor = jnp.concatenate(
                [jnp.broadcast_to(factor_ref[j : j + 1, :], (rows, 128))] * (cols // 128), axis=1
            )
            source = factor * moved
            found.append(source + frames_ref[1] if j == 0 else source)
        put(i, jnp.concatenate(found, axis=0))
    right = right_ref[...].reshape(3 * size, cols)
    first = dot(mat_ref[...], right)
    for c in range(cols // 128):
        first_ref[c * size : (c + 1) * size, :] = first[:, c * 128 : (c + 1) * 128]

    for i in range(0, depth, 2):
        found = []
        for j in (i, i + 1):
            v = chunked(first_ref, j * rows, rows, size)
            half = 0.5 * chunked(k_ref, j * rows, rows, size)
            source = (
                v + divergence(v, chord_ref[j], half, 1) + divergence(v, span_ref[j], half, 0)
            )
            found.append(source + frames_ref[0] if j == 0 else source)
        put(i, jnp.concatenate(found, axis=0))
    right = right_ref[...].reshape(3 * size, cols)
    adj = dot(mat_ref[...], right)
    for c in range(cols // 128):
        adj_ref[c * size : (c + 1) * size, :] = adj[:, c * 128 : (c + 1) * 128]

    for n, (after, _) in enumerate(sides()):
        row = jnp.where(after, rows - 1, 0)
        for c in range(cols // 128):
            edge_ref[n, :, c * 128 : (c + 1) * 128] = row_of_each(first_ref, c, depth, rows, row)
    for n, row in enumerate(far_rows(rows)):
        for c in range(cols // 128):
            two_ref[n, :, c * 128 : (c + 1) * 128] = row_of_each(adj_ref, c, depth, rows, row)
    for copy in copies:
        copy.wait()
    contribution_ref[...] = scale * (
        d_ref[0:1, 0:1] * f * excess_ref[2]
        + chunked(first_ref, 0, rows, size) * excess_ref[1]
        + chunked(adj_ref, 0, rows, size) * excess_ref[0]
    )


def correction(n, got, own, d_ref, edge_ref, pair_ref):
    _, depth, cols = edge_ref.shape
    _, inside = sides()[n]
    factor = d_ref[:, 0:1]
    half = 0.5 * packed_field(got, depth, cols, 0)
    half_next = 0.5 * packed_field(got, depth, cols, 1)
    half_own = 0.5 * packed_field(own, depth, cols, 0)
    inner = half_own + 0.5 * packed_field(own, depth, cols, 1)
    f = packed_line(got, depth, cols, 0)
    frame = packed_line(got, depth, cols, 1)
    f_next = packed_line(got, depth, cols, 2)
    f_own = packed_line(own, depth, cols, 0)
    face = half + half_own
    flux = (half + shift_next(half, 1)) * (shift_next(f, 1) - f)
    moved = (
        f
        + flux
        - shift_prev(flux, 1, half * f)
        + (half + half_next) * (f_next - f)
        + face * (f_own - f)
    )
    outer = factor * moved + jnp.where(iota((depth, 1), 0) == 0, frame, 0.0)
    sources = [factor * (face * f - half * f_own), jnp.where(inside, outer, 0.0)]
    found = dot(pair_ref[...], right_three(jnp.concatenate(sources, axis=0)))
    e = found[0:depth]
    outer = found[depth:]
    w_chord = half_own + shift_next(half_own, 1)
    change = (
        e
        + divergence(e, w_chord, half_own, 1)
        - (half + half_own + inner) * e
        + face * outer
        - half * edge_ref[n]
    )
    return right_three(jnp.concatenate([change, inner * e], axis=0)), e[0:1, :]


def add_segments(total, contribution, picked_rows, map_ref):
    owners, _, lanes = total.shape
    shape = (owners, 128)
    lane = iota(shape, 1)
    segment = jnp.where(lane < lanes, iota(shape, 0) * lanes + lane, -1)
    found = jnp.zeros(shape, F32)
    for block in range(contribution.shape[1] // 128):
        part = contribution[:, block * 128 : (block + 1) * 128]
        sums = jnp.sum(part, axis=1, keepdims=True)
        for n, row in enumerate(picked_rows):
            found += jnp.where(segment == map_ref[block, row], sums[n : n + 1, :], 0.0)
    return total + found[:, None, :lanes]


def near_kernel(
    scale,
    d_ref,
    excess_ref,
    edge_ref,
    pair_ref,
    map_vmem,
    place_ref,
    base_ref,
    contribution_ref,
    own_ref,
    got_ref,
    adj_ref,
    part_ref,
    map_ref,
    map_sem,
):
    map_copy = pltpu.make_async_copy(map_vmem, map_ref, map_sem)
    map_copy.start()
    depth, rows, cols = adj_ref.shape
    size = depth * rows
    sources, surface = correction(0, got_ref, own_ref, d_ref, edge_ref, pair_ref)
    found = dot(place_ref[...], sources)
    adj_ref[...] = (chunked(base_ref, 0, size, size) + found).reshape(depth, rows, cols)
    row = jnp.where(sides()[0][0], rows - 1, 0)
    surface = jnp.where(iota((rows, cols), 0) == row, surface, 0.0)
    contribution = contribution_ref[...] + scale * (
        surface * excess_ref[1] + found[0:rows, :] * excess_ref[0]
    )
    map_copy.wait()
    part_ref[...] = add_segments(
        jnp.zeros(part_ref.shape, F32), contribution, range(rows), map_ref
    )


def far_kernel(
    scale,
    own_ref,
    got_ref,
    d_ref,
    excess_ref,
    edge_ref,
    pair_ref,
    map_vmem,
    two_ref,
    part_in_ref,
    out_ref,
    part_ref,
    map_ref,
    map_sem,
):
    map_copy = pltpu.make_async_copy(map_vmem, map_ref, map_sem)
    map_copy.start()
    depth = two_ref.shape[1]
    rows = excess_ref.shape[1]
    sources, surface = correction(1, got_ref, own_ref, d_ref, edge_ref, pair_ref)
    found = dot(pair_ref[...], sources)
    edge, second = far_rows(rows)
    contribution = scale * jnp.concatenate(
        [
            surface * excess_ref[1, pl.ds(edge, 1), :]
            + found[0:1] * excess_ref[0, pl.ds(edge, 1), :],
            found[depth : depth + 1] * excess_ref[0, pl.ds(second, 1), :],
        ],
        axis=0,
    )
    map_copy.wait()
    part_ref[...] = add_segments(part_in_ref[...], contribution, (edge, second), map_ref)
    out_ref[...] = two_ref[...] + found.reshape(two_ref.shape)


def store_kernel(adj_ref, two_ref, adj_hbm, sems):
    copy = pltpu.make_async_copy(adj_ref, adj_hbm, sems.at[2])
    copy.start()
    copy.wait()
    copies = []
    for n, row in enumerate(far_rows(adj_hbm.shape[1])):
        copies.append(pltpu.make_async_copy(two_ref.at[n], adj_hbm.at[:, row, :], sems.at[n]))
        copies[-1].start()
    for copy in copies:
        copy.wait()


def in_hbm(x):
    return pltpu.with_memory_space_constraint(x, pltpu.HBM)


def per_device(
    conductance, depth_inverse, surface_residual, surface_excess, segment_map, frame_index
):
    _, depth, rows, cols = conductance.shape
    frames = surface_residual.shape[1]
    blocks = segment_map.shape[1]
    size = depth * rows
    spans = lax.axis_size("span")
    devices = spans * lax.axis_size("blade")
    lanes = SEGS // devices
    field = pltpu.VMEM((depth, rows, cols), F32)
    chunks = cols // 128
    packed_far = pltpu.VMEM(((2 * depth + 4) * chunks, 128), F32)
    packed_near = pltpu.VMEM(((2 * depth + 3) * chunks, 128), F32)
    own_far, own_near, k, picked, inverse = pl.pallas_call(
        functools.partial(load_kernel, rows),
        out_shape=(
            packed_far,
            packed_near,
            pltpu.VMEM((chunks * size, 128), F32),
            pltpu.VMEM((STEPS, rows, cols), F32),
            pltpu.VMEM((depth, depth), F32),
        ),
        in_specs=[HBM] * 4,
        out_specs=(VMEM,) * 5,
        scratch_shapes=[
            pltpu.SMEM((STEPS,), jnp.int32),
            pltpu.VMEM((frames, rows, cols), F32),
            pltpu.SemaphoreType.DMA((3 + chunks,)),
        ],
        compiler_params=GRANT,
        name="load",
    )(
        in_hbm(frame_index),
        in_hbm(conductance.reshape(size, cols)),
        in_hbm(surface_residual[0]),
        in_hbm(depth_inverse[0]),
    )
    across = [(i, i + 1) for i in range(1, spans - 1, 2)]
    within = [(i, i + 1) for i in range(0, spans - 1, 2)]
    near = lax.ppermute(own_near, "span", within + [(b, a) for a, b in within])
    far = lax.ppermute(own_far, "span", across + [(b, a) for a, b in across])
    scale = 1.0 / math.sqrt(128.0 * STEPS)
    line = pltpu.VMEM((rows, cols), F32)
    base, two, excess, ids, edge, contribution, pair, place = pl.pallas_call(
        functools.partial(base_kernel, scale),
        out_shape=(
            pltpu.VMEM((chunks * size, 128), F32),
            pltpu.VMEM((2, depth, cols), F32),
            pltpu.VMEM((STEPS, rows, cols), F32),
            pltpu.VMEM((blocks, rows), jnp.int32),
            pltpu.VMEM((2, depth, cols), F32),
            line,
            pltpu.VMEM((2 * depth, 6 * depth), BF16),
            pltpu.VMEM((size, 6 * depth), BF16),
        ),
        in_specs=[VMEM] * 3 + [HBM] * 2,
        out_specs=(VMEM,) * 8,
        scratch_shapes=[
            pltpu.VMEM((size, 3 * size), BF16),
            pltpu.VMEM((3, size, cols), BF16),
            pltpu.VMEM((chunks * size, 128), F32),
            field,
            field,
            pltpu.VMEM((depth, 128), F32),
            pltpu.SemaphoreType.DMA((2,)),
        ],
        compiler_params=GRANT,
        name="base",
    )(k, picked, inverse, in_hbm(surface_excess[0]), in_hbm(segment_map.T))
    fixed = (inverse, excess, edge, pair, ids)
    sums = pltpu.VMEM((devices, 1, lanes), F32)
    map_scratch = [pltpu.SMEM((blocks, rows), jnp.int32), pltpu.SemaphoreType.DMA]
    adjoint, partial = pl.pallas_call(
        functools.partial(near_kernel, scale),
        out_shape=(field, sums),
        in_specs=[VMEM] * 10,
        out_specs=(VMEM,) * 2,
        scratch_shapes=map_scratch,
        compiler_params=GRANT,
        name="near",
    )(*fixed, place, base, contribution, own_near, near)
    two, partial = pl.pallas_call(
        functools.partial(far_kernel, scale),
        out_shape=(pltpu.VMEM((2, depth, cols), F32), sums),
        in_specs=[VMEM] * 9,
        out_specs=(VMEM,) * 2,
        scratch_shapes=map_scratch,
        compiler_params=GRANT,
        name="far",
    )(own_far, far, *fixed, two, partial)
    pieces = lax.all_to_all(partial, ("blade", "span"), 0, 0, tiled=True)
    adjoint = pl.pallas_call(
        store_kernel,
        out_shape=pltpu.HBM((depth, rows, cols), F32),
        in_specs=[VMEM] * 2,
        out_specs=HBM,
        scratch_shapes=[pltpu.SemaphoreType.DMA((3,))],
        cost_estimate=pl.CostEstimate(
            flops=0, bytes_accessed=4 * size * cols * 2, transcendentals=0
        ),
        compiler_params=GRANT,
        name="store",
    )(adjoint, two)
    return (adjoint[None], jnp.sum(pieces, axis=(0, 1)))


def solution(mesh):
    placed = (
        P("blade", None, "span", None),
        P("blade", None, None),
        P("blade", None, "span", None),
        P("blade", None, "span", None),
        P("span", None),
        P(),
    )
    return jax.shard_map(
        per_device,
        mesh=mesh,
        in_specs=placed,
        out_specs=(P("blade", None, "span", None), P(("blade", "span"))),
        check_vma=False,
    )
```

```python
import functools
import math

import jax
import jax.numpy as jnp
from jax import lax
from jax.experimental import pallas as pl
from jax.experimental.pallas import tpu as pltpu
from jax.sharding import PartitionSpec as P

STEPS = 3
SEGS = 2048
F32 = jnp.float32
BF16 = jnp.bfloat16
VMEM = pl.BlockSpec(memory_space=pltpu.VMEM)
HBM = pl.BlockSpec(memory_space=pltpu.HBM)
GRANT = pltpu.CompilerParams(vmem_limit_bytes=16 * 2**20)


def split(x):
    high = x.astype(BF16)
    return high, (x - high.astype(F32)).astype(BF16)


def dot(a, b):
    return jnp.dot(a, b, preferred_element_type=F32)


def left_three(matrix):
    high, low = matrix
    return jnp.concatenate([high, low, high], axis=1)


def right_three(chunks):
    columns = []
    for x in chunks:
        high, low = split(x)
        columns.append(jnp.concatenate([high, high, low], axis=0))
    return jnp.concatenate(columns, axis=1)


def iota(shape, dim):
    return lax.broadcasted_iota(jnp.int32, shape, dim)


def pieces_of(x):
    return [x[:, c : c + 128] for c in range(0, x.shape[1], 128)]


def chord_next(chunks):
    last = iota(chunks[0].shape, 1) == 127
    moved = [pltpu.roll(x, 127, 1) for x in chunks] + [0.0]
    return [jnp.where(last, moved[c + 1], moved[c]) for c in range(len(chunks))]


def chord_prev(chunks, first):
    start = iota(chunks[0].shape, 1) == 0
    moved = [first] + [pltpu.roll(x, 1, 1) for x in chunks]
    return [jnp.where(start, moved[c], moved[c + 1]) for c in range(len(chunks))]


def row_next(x):
    rows = x.shape[0]
    return jnp.where(iota(x.shape, 0) == rows - 1, 0.0, pltpu.roll(x, rows - 1, 0))


def row_prev(x, first):
    return jnp.where(iota(x.shape, 0) == 0, first, pltpu.roll(x, 1, 0))


def both(fn, *lists):
    return [fn(*items) for items in zip(*lists)]


def chord_faces(half):
    return both(lambda h, n: h + n, half, chord_next(half))


def chord_flow(v, faces, half):
    flux = both(lambda w, n, x: w * (n - x), faces, chord_next(v), v)
    return both(lambda f, p: f - p, flux, chord_prev(flux, half[0] * v[0]))


def span_flow(v, face, half):
    flux = face * (row_next(v) - v)
    return flux - row_prev(flux, half * v)


def sides():
    span = lax.axis_index("span")
    count = lax.axis_size("span")
    even = lax.rem(span, 2) == 0
    has_next = span + 1 < count
    has_prev = span > 0
    return (
        (even, jnp.where(even, has_next, has_prev)),
        (jnp.logical_not(even), jnp.where(even, has_prev, has_next)),
    )


def chunked(ref, start, count, step):
    chunks = ref.shape[0] // step
    return [ref[c * step + start : c * step + start + count, :] for c in range(chunks)]


def packed_field(ref, depth, chunks, n):
    base = n * chunks * depth
    return [ref[base + c * depth : base + (c + 1) * depth, :] for c in range(chunks)]


def packed_line(ref, depth, chunks, n):
    base = (2 * depth + n) * chunks
    return [ref[base + c : base + c + 1, :] for c in range(chunks)]


def row_of_each(ref, chunk, depth, rows, row):
    return ref[pl.ds(chunk * depth * rows + row, depth, stride=rows), :]


def far_rows(rows):
    after = sides()[1][0]
    return jnp.where(after, rows - 1, 0), jnp.where(after, rows - 2, 1)


def load_kernel(
    rows,
    frame_hbm,
    k_hbm,
    res_hbm,
    d_hbm,
    far_ref,
    near_ref,
    k_ref,
    frames_ref,
    d_ref,
    frame_ref,
    res_ref,
    sems,
):
    size, cols = k_hbm.shape
    depth = size // rows
    chunks = cols // 128
    pairs = [(frame_hbm, frame_ref), (res_hbm, res_ref)]
    for c in range(chunks):
        pairs.append((k_hbm.at[:, pl.ds(c * 128, 128)], k_ref.at[pl.ds(c * size, size)]))
    pairs.append((d_hbm, d_ref))
    copies = [pltpu.make_async_copy(a, b, sems.at[n]) for n, (a, b) in enumerate(pairs)]
    for copy in copies:
        copy.start()
    sent = (near_ref, far_ref)
    picks = []
    for after, _ in sides():
        picks.append((jnp.where(after, rows - 1, 0), jnp.where(after, rows - 2, 1)))
    copies[0].wait()
    copies[1].wait()
    for step in range(STEPS):
        frames_ref[step] = res_ref[frame_ref[step]]
    base = 2 * chunks * depth
    for ref, (edge, second) in zip(sent, picks):
        for n, (step, row) in enumerate(((2, edge), (1, edge), (2, second))):
            line = frames_ref[step, pl.ds(row, 1), :]
            for c in range(chunks):
                spot = base + n * chunks + c
                ref[spot : spot + 1, :] = line[:, c * 128 : (c + 1) * 128]
        if ref.shape[0] > base + 3 * chunks:
            ref[base + 3 * chunks :, :] = jnp.zeros((ref.shape[0] - base - 3 * chunks, 128), F32)
    for c in range(chunks):
        copies[2 + c].wait()
        for ref, row_pair in zip(sent, picks):
            for n, row in enumerate(row_pair):
                spot = (n * chunks + c) * depth
                ref[spot : spot + depth, :] = row_of_each(k_ref, c, depth, rows, row)
    for copy in copies[2 + chunks :]:
        copy.wait()


def base_kernel(
    scale,
    k_ref,
    frames_ref,
    d_ref,
    excess_hbm,
    map_hbm,
    adj_ref,
    two_ref,
    excess_ref,
    map_ref,
    edge_ref,
    contribution_ref,
    surface_ref,
    pair_ref,
    place_ref,
    mat_ref,
    right_ref,
    first_ref,
    chord_ref,
    span_ref,
    factor_ref,
    sems,
):
    copies = [
        pltpu.make_async_copy(excess_hbm, excess_ref, sems.at[0]),
        pltpu.make_async_copy(map_hbm, map_ref, sems.at[1]),
    ]
    for copy in copies:
        copy.start()
    depth = d_ref.shape[0]
    _, rows, cols = frames_ref.shape
    chunks = cols // 128
    size = depth * rows
    factor_ref[...] = jnp.broadcast_to(d_ref[:, 0:1], factor_ref.shape)

    parts = split(d_ref[...])
    tall = (iota((size, depth), 0) // rows == iota((size, depth), 1)).astype(BF16)
    wide = (iota((depth, size), 0) == iota((depth, size), 1) // rows).astype(BF16)
    two = 2 * depth
    tile = (iota((depth, two), 0) == iota((depth, two), 1) % depth).astype(BF16)
    same = iota((size, size), 0) % rows == iota((size, size), 1) % rows
    pair_same = iota((two, two), 0) // depth == iota((two, two), 1) // depth
    row_of = iota((size, two), 0) % rows
    first_half = iota((size, two), 1) < depth
    after = sides()[0][0]
    edge = jnp.where(after, rows - 1, 0)
    second = jnp.where(after, rows - 2, 1)
    placed = row_of == jnp.where(first_half, edge, second)
    mats, pairs, places = [], [], []
    for part in parts:
        column = dot(tall, part).astype(BF16)
        row = dot(part, tile)
        mats.append(jnp.where(same, dot(column, wide), 0.0).astype(BF16))
        places.append(jnp.where(placed, dot(column, tile), 0.0).astype(BF16))
        pairs.append(
            jnp.where(pair_same, jnp.concatenate([row] * 2, axis=0), 0.0).astype(BF16)
        )
    mat_ref[...] = left_three(mats)
    pair_ref[...] = left_three(pairs)
    place_ref[...] = left_three(places)

    f = pieces_of(frames_ref[2])
    f_chord = both(lambda n, x: n - x, chord_next(f), f)
    f_span = both(lambda x: row_next(x) - x, f)

    def put(i, first, second):
        span = pl.ds(i * rows, 2 * rows)
        for c in range(chunks):
            lanes = slice(c * 128, (c + 1) * 128)
            high, low = split(jnp.concatenate([first[c], second[c]], axis=0))
            right_ref[0, span, lanes] = high
            right_ref[1, span, lanes] = high
            right_ref[2, span, lanes] = low

    def write(ref, j, items):
        for c in range(chunks):
            ref[c * size + j * rows : c * size + (j + 1) * rows, :] = items[c]

    def read(ref, j):
        return chunked(ref, j * rows, rows, size)

    for i in range(0, depth, 2):
        found = []
        for j in (i, i + 1):
            half = both(lambda x: 0.5 * x, read(k_ref, j))
            w_chord = chord_faces(half)
            w_span = both(lambda h: h + row_next(h), half)
            write(chord_ref, j, w_chord)
            write(span_ref, j, w_span)
            edge = both(lambda h, x: h * x, half, f)
            flux = both(lambda w, x: w * x, w_chord, f_chord)
            before = chord_prev(flux, edge[0])
            factor = jnp.broadcast_to(factor_ref[j : j + 1, :], (rows, 128))
            source = []
            for c in range(chunks):
                flux_span = w_span[c] * f_span[c]
                moved = f[c] + flux[c] - before[c] + flux_span - row_prev(flux_span, edge[c])
                source.append(factor * moved)
            if j == 0:
                source = both(lambda x, g: x + g, source, pieces_of(frames_ref[1]))
            found.append(source)
        put(i, *found)
    right = right_ref[...].reshape(3 * size, cols)
    first = dot(mat_ref[...], right)
    for c in range(chunks):
        first_ref[c * size : (c + 1) * size, :] = first[:, c * 128 : (c + 1) * 128]

    for i in range(0, depth, 2):
        found = []
        for j in (i, i + 1):
            v = read(first_ref, j)
            half = both(lambda x: 0.5 * x, read(k_ref, j))
            chord = chord_flow(v, read(chord_ref, j), half)
            source = both(
                lambda x, a, w, h: x + a + span_flow(x, w, h), v, chord, read(span_ref, j), half
            )
            if j == 0:
                source = both(lambda x, g: x + g, source, pieces_of(frames_ref[0]))
            found.append(source)
        put(i, *found)
    right = right_ref[...].reshape(3 * size, cols)
    adj = dot(mat_ref[...], right)
    for c in range(chunks):
        adj_ref[c * size : (c + 1) * size, :] = adj[:, c * 128 : (c + 1) * 128]

    for n, (after, _) in enumerate(sides()):
        row = jnp.where(after, rows - 1, 0)
        for c in range(cols // 128):
            edge_ref[n, :, c * 128 : (c + 1) * 128] = row_of_each(first_ref, c, depth, rows, row)
    for n, row in enumerate(far_rows(rows)):
        for c in range(cols // 128):
            two_ref[n, :, c * 128 : (c + 1) * 128] = row_of_each(adj_ref, c, depth, rows, row)
    for copy in copies:
        copy.wait()
    row = jnp.where(iota((depth, depth), 0) == iota((depth, depth), 1), d_ref[0:1, :], 0.0)
    surface_ref[...] = jnp.broadcast_to(jnp.sum(row, axis=1, keepdims=True), surface_ref.shape)
    parts = (d_ref[0:1, 0:1] * f[c] for c in range(chunks))
    for c, (own, mid, end) in enumerate(zip(parts, read(first_ref, 0), read(adj_ref, 0))):
        lanes = slice(c * 128, (c + 1) * 128)
        contribution_ref[:, lanes] = scale * (
            own * excess_ref[2, :, lanes]
            + mid * excess_ref[1, :, lanes]
            + end * excess_ref[0, :, lanes]
        )


def correction(n, got, own, d_ref, edge_ref, pair_ref):
    _, depth, cols = edge_ref.shape
    chunks = cols // 128
    _, inside = sides()[n]
    factor = jnp.broadcast_to(d_ref[:, 0:1], (depth, 128))
    at_surface = iota((depth, 128), 0) == 0

    def halved(ref, which):
        return both(lambda x: 0.5 * x, packed_field(ref, depth, chunks, which))

    half = halved(got, 0)
    half_next = halved(got, 1)
    half_own = halved(own, 0)
    inner = both(lambda a, b: a + b, half_own, halved(own, 1))
    f = packed_line(got, depth, chunks, 0)
    frame = packed_line(got, depth, chunks, 1)
    f_next = packed_line(got, depth, chunks, 2)
    f_own = packed_line(own, depth, chunks, 0)
    face = both(lambda a, b: a + b, half, half_own)
    step = both(lambda a, b: a - b, chord_next(f), f)
    flux = both(lambda w, x: w * x, chord_faces(half), step)
    before = chord_prev(flux, half[0] * f[0])
    sources = []
    for c in range(chunks):
        moved = (
            f[c]
            + flux[c]
            - before[c]
            + (half[c] + half_next[c]) * (f_next[c] - f[c])
            + face[c] * (f_own[c] - f[c])
        )
        outer = factor * moved + jnp.where(at_surface, frame[c], 0.0)
        within = factor * (face[c] * f[c] - half[c] * f_own[c])
        sources.append(jnp.concatenate([within, jnp.where(inside, outer, 0.0)], axis=0))
    found = pieces_of(dot(pair_ref[...], right_three(sources)))
    e = both(lambda x: x[0:depth], found)
    chord = chord_flow(e, chord_faces(half_own), half_own)
    change = []
    for c in range(chunks):
        change.append(
            e[c]
            + chord[c]
            - (half[c] + half_own[c] + inner[c]) * e[c]
            + face[c] * found[c][depth:]
            - half[c] * edge_ref[n, :, c * 128 : (c + 1) * 128]
        )
    second = both(lambda a, b: a * b, inner, e)
    return change, second, both(lambda x: x[0:1, :], e)


def stacked(change, second):
    return right_three(both(lambda a, b: jnp.concatenate([a, b], axis=0), change, second))


def add_segments(total, contribution, picked_rows, map_ref):
    owners, _, lanes = total.shape
    shape = (owners, 128)
    lane = iota(shape, 1)
    segment = jnp.where(lane < lanes, iota(shape, 0) * lanes + lane, -1)
    found = jnp.zeros(shape, F32)
    for block, part in enumerate(contribution):
        sums = jnp.sum(part, axis=1, keepdims=True)
        for n, row in enumerate(picked_rows):
            found += jnp.where(segment == map_ref[block, row], sums[n : n + 1, :], 0.0)
    return total + found[:, None, :lanes]


def near_kernel(
    scale,
    d_ref,
    excess_ref,
    edge_ref,
    pair_ref,
    map_vmem,
    place_ref,
    base_ref,
    contribution_ref,
    own_ref,
    got_ref,
    adj_hbm,
    part_ref,
    adj_ref,
    map_ref,
    sems,
):
    map_copy = pltpu.make_async_copy(map_vmem, map_ref, sems.at[0])
    map_copy.start()
    depth, rows, cols = adj_ref.shape
    size = depth * rows
    change, second, surface = correction(0, got_ref, own_ref, d_ref, edge_ref, pair_ref)
    found = pieces_of(dot(place_ref[...], stacked(change, second)))
    for c, old in enumerate(chunked(base_ref, 0, size, size)):
        adj_ref[:, :, c * 128 : (c + 1) * 128] = (old + found[c]).reshape(depth, rows, 128)
    adj_copy = pltpu.make_async_copy(adj_ref, adj_hbm, sems.at[1])
    adj_copy.start()
    at_edge = iota((rows, 128), 0) == jnp.where(sides()[0][0], rows - 1, 0)
    contribution = []
    for c in range(cols // 128):
        lanes = slice(c * 128, (c + 1) * 128)
        contribution.append(
            contribution_ref[:, lanes]
            + scale
            * (
                jnp.where(at_edge, surface[c], 0.0) * excess_ref[1, :, lanes]
                + found[c][0:rows] * excess_ref[0, :, lanes]
            )
        )
    map_copy.wait()
    part_ref[...] = add_segments(
        jnp.zeros(part_ref.shape, F32), contribution, range(rows), map_ref
    )
    adj_copy.wait()


def far_kernel(
    scale,
    own_ref,
    got_ref,
    d_ref,
    excess_ref,
    edge_ref,
    pair_ref,
    map_vmem,
    surface_ref,
    two_ref,
    part_in_ref,
    out_ref,
    part_ref,
    map_ref,
    map_sem,
):
    map_copy = pltpu.make_async_copy(map_vmem, map_ref, map_sem)
    map_copy.start()
    depth, cols = two_ref.shape[1:]
    rows = excess_ref.shape[1]
    change, second, surface = correction(1, got_ref, own_ref, d_ref, edge_ref, pair_ref)
    found = dot(pair_ref[...], stacked(change, second))
    edge_row, second_row = far_rows(rows)
    weight = surface_ref[...]
    middle = pieces_of(excess_ref[1, pl.ds(edge_row, 1), :])
    last = pieces_of(excess_ref[0, pl.ds(edge_row, 1), :])
    last_second = pieces_of(excess_ref[0, pl.ds(second_row, 1), :])
    contribution = []
    for c in range(cols // 128):
        at_edge = jnp.sum(weight * change[c], axis=0, keepdims=True)
        at_second = jnp.sum(weight * second[c], axis=0, keepdims=True)
        lines = [surface[c] * middle[c] + at_edge * last[c], at_second * last_second[c]]
        contribution.append(scale * jnp.concatenate(lines, axis=0))
    map_copy.wait()
    part_ref[...] = add_segments(
        part_in_ref[...], contribution, (edge_row, second_row), map_ref
    )
    out_ref[...] = two_ref[...] + found.reshape(two_ref.shape)


def finish_kernel(_, two_ref, got_ref, adj_hbm, out_hbm, out_ref, sems):
    copies = []
    for n, row in enumerate(far_rows(adj_hbm.shape[1])):
        copies.append(pltpu.make_async_copy(two_ref.at[n], adj_hbm.at[:, row, :], sems.at[n]))
        copies[-1].start()
    out_ref[...] = jnp.sum(got_ref[:, 0, :], axis=0)
    copies.append(pltpu.make_async_copy(out_ref, out_hbm, sems.at[2]))
    copies[-1].start()
    for copy in copies:
        copy.wait()


def in_hbm(x):
    return pltpu.with_memory_space_constraint(x, pltpu.HBM)


def per_device(
    conductance, depth_inverse, surface_residual, surface_excess, segment_map, frame_index
):
    _, depth, rows, cols = conductance.shape
    frames = surface_residual.shape[1]
    blocks = segment_map.shape[1]
    size = depth * rows
    spans = lax.axis_size("span")
    devices = spans * lax.axis_size("blade")
    lanes = SEGS // devices
    field = pltpu.VMEM((depth, rows, cols), F32)
    chunks = cols // 128
    packed_far = pltpu.VMEM(((2 * depth + 4) * chunks, 128), F32)
    packed_near = pltpu.VMEM(((2 * depth + 3) * chunks, 128), F32)
    own_far, own_near, k, picked, inverse = pl.pallas_call(
        functools.partial(load_kernel, rows),
        out_shape=(
            packed_far,
            packed_near,
            pltpu.VMEM((chunks * size, 128), F32),
            pltpu.VMEM((STEPS, rows, cols), F32),
            pltpu.VMEM((depth, depth), F32),
        ),
        in_specs=[HBM] * 4,
        out_specs=(VMEM,) * 5,
        scratch_shapes=[
            pltpu.SMEM((STEPS,), jnp.int32),
            pltpu.VMEM((frames, rows, cols), F32),
            pltpu.SemaphoreType.DMA((3 + chunks,)),
        ],
        compiler_params=GRANT,
        name="load",
    )(
        in_hbm(frame_index),
        in_hbm(conductance.reshape(size, cols)),
        in_hbm(surface_residual[0]),
        in_hbm(depth_inverse[0]),
    )
    across = [(i, i + 1) for i in range(1, spans - 1, 2)]
    within = [(i, i + 1) for i in range(0, spans - 1, 2)]
    near = lax.ppermute(own_near, "span", within + [(b, a) for a, b in within])
    far = lax.ppermute(own_far, "span", across + [(b, a) for a, b in across])
    scale = 1.0 / math.sqrt(128.0 * STEPS)
    line = pltpu.VMEM((rows, cols), F32)
    base, two, excess, ids, edge, contribution, surface, pair, place = pl.pallas_call(
        functools.partial(base_kernel, scale),
        out_shape=(
            pltpu.VMEM((chunks * size, 128), F32),
            pltpu.VMEM((2, depth, cols), F32),
            pltpu.VMEM((STEPS, rows, cols), F32),
            pltpu.VMEM((blocks, rows), jnp.int32),
            pltpu.VMEM((2, depth, cols), F32),
            line,
            pltpu.VMEM((depth, 128), F32),
            pltpu.VMEM((2 * depth, 6 * depth), BF16),
            pltpu.VMEM((size, 6 * depth), BF16),
        ),
        in_specs=[VMEM] * 3 + [HBM] * 2,
        out_specs=(VMEM,) * 9,
        scratch_shapes=[
            pltpu.VMEM((size, 3 * size), BF16),
            pltpu.VMEM((3, size, cols), BF16),
            pltpu.VMEM((chunks * size, 128), F32),
            pltpu.VMEM((chunks * size, 128), F32),
            pltpu.VMEM((chunks * size, 128), F32),
            pltpu.VMEM((depth, 128), F32),
            pltpu.SemaphoreType.DMA((2,)),
        ],
        compiler_params=GRANT,
        name="base",
    )(k, picked, inverse, in_hbm(surface_excess[0]), in_hbm(segment_map.T))
    fixed = (inverse, excess, edge, pair, ids)
    sums = pltpu.VMEM((devices, 1, lanes), F32)
    adjoint, partial = pl.pallas_call(
        functools.partial(near_kernel, scale),
        out_shape=(pltpu.HBM((depth, rows, cols), F32), sums),
        in_specs=[VMEM] * 10,
        out_specs=(HBM, VMEM),
        scratch_shapes=[
            field,
            pltpu.SMEM((blocks, rows), jnp.int32),
            pltpu.SemaphoreType.DMA((2,)),
        ],
        compiler_params=GRANT,
        name="near",
    )(*fixed, place, base, contribution, own_near, near)
    two, partial = pl.pallas_call(
        functools.partial(far_kernel, scale),
        out_shape=(pltpu.VMEM((2, depth, cols), F32), sums),
        in_specs=[VMEM] * 10,
        out_specs=(VMEM,) * 2,
        scratch_shapes=[pltpu.SMEM((blocks, rows), jnp.int32), pltpu.SemaphoreType.DMA],
        compiler_params=GRANT,
        name="far",
    )(own_far, far, *fixed, surface, two, partial)
    pieces = lax.all_to_all(partial, ("blade", "span"), 0, 0, tiled=True)
    adjoint, owned = pl.pallas_call(
        finish_kernel,
        out_shape=(pltpu.HBM((depth, rows, cols), F32), pltpu.HBM((lanes,), F32)),
        in_specs=[HBM, VMEM, VMEM],
        out_specs=(HBM,) * 2,
        scratch_shapes=[pltpu.VMEM((lanes,), F32), pltpu.SemaphoreType.DMA((3,))],
        input_output_aliases={0: 0},
        compiler_params=GRANT,
        name="finish",
    )(in_hbm(adjoint), two, pltpu.with_memory_space_constraint(pieces, pltpu.VMEM))
    return (adjoint[None], owned)


def solution(mesh):
    placed = (
        P("blade", None, "span", None),
        P("blade", None, None),
        P("blade", None, "span", None),
        P("blade", None, "span", None),
        P("span", None),
        P(),
    )
    return jax.shard_map(
        per_device,
        mesh=mesh,
        in_specs=placed,
        out_specs=(P("blade", None, "span", None), P(("blade", "span"))),
        check_vma=False,
    )
```

```python
import functools
import math

import jax
import jax.numpy as jnp
from jax import lax
from jax.experimental import pallas as pl
from jax.experimental.pallas import tpu as pltpu
from jax.sharding import PartitionSpec as P

STEPS = 3
SEGS = 2048
F32 = jnp.float32
BF16 = jnp.bfloat16
VMEM = pl.BlockSpec(memory_space=pltpu.VMEM)
HBM = pl.BlockSpec(memory_space=pltpu.HBM)
GRANT = pltpu.CompilerParams(vmem_limit_bytes=16 * 2**20)


def split(x):
    high = x.astype(BF16)
    return high, (x - high.astype(F32)).astype(BF16)


def dot(a, b):
    return jnp.dot(a, b, preferred_element_type=F32)


def left_three(matrix):
    high, low = matrix
    return jnp.concatenate([high, low, high], axis=1)


def right_three(x):
    high, low = split(x)
    return jnp.concatenate([high, high, low], axis=0)


def iota(shape, dim):
    return lax.broadcasted_iota(jnp.int32, shape, dim)


def shift_next(x, axis):
    size = x.shape[axis]
    return jnp.where(iota(x.shape, axis) == size - 1, 0.0, pltpu.roll(x, size - 1, axis))


def shift_prev(x, axis, first):
    return jnp.where(iota(x.shape, axis) == 0, first, pltpu.roll(x, 1, axis))


def divergence(v, weight, half, axis):
    flux = weight * (shift_next(v, axis) - v)
    return flux - shift_prev(flux, axis, half * v)


def sides():
    span = lax.axis_index("span")
    count = lax.axis_size("span")
    even = lax.rem(span, 2) == 0
    has_next = span + 1 < count
    has_prev = span > 0
    return (
        (even, jnp.where(even, has_next, has_prev)),
        (jnp.logical_not(even), jnp.where(even, has_prev, has_next)),
    )


def chunked(ref, start, count, step):
    chunks = ref.shape[0] // step
    return jnp.concatenate(
        [ref[c * step + start : c * step + start + count, :] for c in range(chunks)], axis=1
    )


def packed_field(ref, depth, cols, n):
    chunks = cols // 128
    return chunked(ref.at[n * chunks * depth : (n + 1) * chunks * depth], 0, depth, depth)


def packed_line(ref, depth, cols, n):
    chunks = cols // 128
    base = (2 * depth + n) * chunks
    return chunked(ref.at[base : base + chunks], 0, 1, 1)


def row_of_each(ref, chunk, depth, rows, row):
    return ref[pl.ds(chunk * depth * rows + row, depth, stride=rows), :]


def far_rows(rows):
    after = sides()[1][0]
    return jnp.where(after, rows - 1, 0), jnp.where(after, rows - 2, 1)


def load_kernel(
    rows,
    frame_hbm,
    k_hbm,
    res_hbm,
    d_hbm,
    far_ref,
    near_ref,
    k_ref,
    frames_ref,
    d_ref,
    frame_ref,
    res_ref,
    sems,
):
    size, cols = k_hbm.shape
    depth = size // rows
    chunks = cols // 128
    pairs = [(frame_hbm, frame_ref), (res_hbm, res_ref)]
    for c in range(chunks):
        pairs.append((k_hbm.at[:, pl.ds(c * 128, 128)], k_ref.at[pl.ds(c * size, size)]))
    pairs.append((d_hbm, d_ref))
    copies = [pltpu.make_async_copy(a, b, sems.at[n]) for n, (a, b) in enumerate(pairs)]
    for copy in copies:
        copy.start()
    sent = (near_ref, far_ref)
    picks = []
    for after, _ in sides():
        picks.append((jnp.where(after, rows - 1, 0), jnp.where(after, rows - 2, 1)))
    for c in range(chunks):
        copies[2 + c].wait()
        for ref, row_pair in zip(sent, picks):
            for n, row in enumerate(row_pair):
                spot = (n * chunks + c) * depth
                ref[spot : spot + depth, :] = row_of_each(k_ref, c, depth, rows, row)
    copies[0].wait()
    copies[1].wait()
    for step in range(STEPS):
        frames_ref[step] = res_ref[frame_ref[step]]
    base = 2 * chunks * depth
    for ref, (edge, second) in zip(sent, picks):
        for n, (step, row) in enumerate(((2, edge), (1, edge), (2, second))):
            line = frames_ref[step, pl.ds(row, 1), :]
            for c in range(chunks):
                spot = base + n * chunks + c
                ref[spot : spot + 1, :] = line[:, c * 128 : (c + 1) * 128]
        if ref.shape[0] > base + 3 * chunks:
            ref[base + 3 * chunks :, :] = jnp.zeros((ref.shape[0] - base - 3 * chunks, 128), F32)
    for copy in copies[2 + chunks :]:
        copy.wait()


def base_kernel(
    scale,
    k_ref,
    frames_ref,
    d_ref,
    own_near_ref,
    own_far_ref,
    excess_hbm,
    map_hbm,
    own_ref,
    adj_ref,
    two_ref,
    excess_ref,
    map_ref,
    edge_ref,
    contribution_ref,
    pair_ref,
    place_ref,
    mat_ref,
    right_ref,
    first_ref,
    chord_ref,
    span_ref,
    factor_ref,
    sems,
):
    copies = [
        pltpu.make_async_copy(excess_hbm, excess_ref, sems.at[0]),
        pltpu.make_async_copy(map_hbm, map_ref, sems.at[1]),
    ]
    for copy in copies:
        copy.start()
    depth, rows, cols = chord_ref.shape
    size = depth * rows
    factor_ref[...] = jnp.broadcast_to(d_ref[:, 0:1], factor_ref.shape)

    parts = split(d_ref[...])
    tall = (iota((size, depth), 0) // rows == iota((size, depth), 1)).astype(BF16)
    wide = (iota((depth, size), 0) == iota((depth, size), 1) // rows).astype(BF16)
    two = 2 * depth
    tile = (iota((depth, two), 0) == iota((depth, two), 1) % depth).astype(BF16)
    same = iota((size, size), 0) % rows == iota((size, size), 1) % rows
    pair_same = iota((two, two), 0) // depth == iota((two, two), 1) // depth
    row_of = iota((size, two), 0) % rows
    first_half = iota((size, two), 1) < depth
    after = sides()[0][0]
    edge = jnp.where(after, rows - 1, 0)
    second = jnp.where(after, rows - 2, 1)
    placed = row_of == jnp.where(first_half, edge, second)
    mats, pairs, places = [], [], []
    for part in parts:
        column = dot(tall, part).astype(BF16)
        row = dot(part, tile)
        mats.append(jnp.where(same, dot(column, wide), 0.0).astype(BF16))
        places.append(jnp.where(placed, dot(column, tile), 0.0).astype(BF16))
        pairs.append(
            jnp.where(pair_same, jnp.concatenate([row] * 2, axis=0), 0.0).astype(BF16)
        )
    mat_ref[...] = left_three(mats)
    pair_ref[...] = left_three(pairs)
    place_ref[...] = left_three(places)

    for n, ref in enumerate((own_near_ref, own_far_ref)):
        half = 0.5 * packed_field(ref, depth, cols, 0)
        inner = half + 0.5 * packed_field(ref, depth, cols, 1)
        w_next = half + shift_next(half, 1)
        w_prev = half + shift_prev(half, 1, 0.0)
        for which, x in enumerate((half, inner, w_next, w_prev)):
            own_ref[n, which] = x
        own_ref[n, 4] = 1.0 - (w_next + w_prev) - (half + inner)

    f = frames_ref[2]
    f_chord = shift_next(f, 1) - f
    f_span = shift_next(f, 0) - f

    def put(i, both):
        high, low = split(both)
        span = pl.ds(i * rows, 2 * rows)
        right_ref[0, span, :] = high
        right_ref[1, span, :] = high
        right_ref[2, span, :] = low

    for i in range(0, depth, 2):
        found = []
        for j in (i, i + 1):
            half = 0.5 * chunked(k_ref, j * rows, rows, size)
            w_chord = half + shift_next(half, 1)
            w_span = half + shift_next(half, 0)
            chord_ref[j] = w_chord
            span_ref[j] = w_span
            edge = half * f
            flux_chord = w_chord * f_chord
            flux_span = w_span * f_span
            moved = f + flux_chord - shift_prev(flux_chord, 1, edge)
            moved = moved + flux_span - shift_prev(flux_span, 0, edge)
            factor = jnp.concatenate(
                [jnp.broadcast_to(factor_ref[j : j + 1, :], (rows, 128))] * (cols // 128), axis=1
            )
            source = factor * moved
            found.append(source + frames_ref[1] if j == 0 else source)
        put(i, jnp.concatenate(found, axis=0))
    right = right_ref[...].reshape(3 * size, cols)
    first = dot(mat_ref[...], right)
    for c in range(cols // 128):
        first_ref[c * size : (c + 1) * size, :] = first[:, c * 128 : (c + 1) * 128]

    for i in range(0, depth, 2):
        found = []
        for j in (i, i + 1):
            v = chunked(first_ref, j * rows, rows, size)
            half = 0.5 * chunked(k_ref, j * rows, rows, size)
            source = (
                v + divergence(v, chord_ref[j], half, 1) + divergence(v, span_ref[j], half, 0)
            )
            found.append(source + frames_ref[0] if j == 0 else source)
        put(i, jnp.concatenate(found, axis=0))
    right = right_ref[...].reshape(3 * size, cols)
    adj = dot(mat_ref[...], right)
    for c in range(cols // 128):
        adj_ref[c * size : (c + 1) * size, :] = adj[:, c * 128 : (c + 1) * 128]

    for n, (after, _) in enumerate(sides()):
        row = jnp.where(after, rows - 1, 0)
        for c in range(cols // 128):
            edge_ref[n, :, c * 128 : (c + 1) * 128] = row_of_each(first_ref, c, depth, rows, row)
    for n, row in enumerate(far_rows(rows)):
        for c in range(cols // 128):
            two_ref[n, :, c * 128 : (c + 1) * 128] = row_of_each(adj_ref, c, depth, rows, row)
    for copy in copies:
        copy.wait()
    contribution_ref[...] = scale * (
        d_ref[0:1, 0:1] * f * excess_ref[2]
        + chunked(first_ref, 0, rows, size) * excess_ref[1]
        + chunked(adj_ref, 0, rows, size) * excess_ref[0]
    )


def correction(n, got, sent, d_ref, own_ref, edge_ref, pair_ref):
    _, depth, cols = edge_ref.shape
    _, inside = sides()[n]
    factor = d_ref[:, 0:1]
    half = 0.5 * packed_field(got, depth, cols, 0)
    half_next = 0.5 * packed_field(got, depth, cols, 1)
    f = packed_line(got, depth, cols, 0)
    frame = packed_line(got, depth, cols, 1)
    f_next = packed_line(got, depth, cols, 2)
    f_own = packed_line(sent, depth, cols, 0)
    face = half + own_ref[n, 0]
    moved = (
        f
        + (half + shift_next(half, 1)) * (shift_next(f, 1) - f)
        + (half + shift_prev(half, 1, 0.0)) * (shift_prev(f, 1, 0.0) - f)
        + (half + half_next) * (f_next - f)
        + face * (f_own - f)
    )
    outer = factor * moved + jnp.where(iota((depth, 1), 0) == 0, frame, 0.0)
    sources = [factor * (face * f - half * f_own), jnp.where(inside, outer, 0.0)]
    found = dot(pair_ref[...], right_three(jnp.concatenate(sources, axis=0)))
    e = found[0:depth]
    outer = found[depth:]
    change = (
        own_ref[n, 4] * e
        + own_ref[n, 2] * shift_next(e, 1)
        + own_ref[n, 3] * shift_prev(e, 1, 0.0)
        + face * outer
        - half * (e + edge_ref[n])
    )
    return right_three(jnp.concatenate([change, own_ref[n, 1] * e], axis=0)), e[0:1, :]


def add_segments(total, contribution, picked_rows, map_ref):
    owners, _, lanes = total.shape
    shape = (owners, 128)
    lane = iota(shape, 1)
    segment = jnp.where(lane < lanes, iota(shape, 0) * lanes + lane, -1)
    found = jnp.zeros(shape, F32)
    for block in range(contribution.shape[1] // 128):
        part = contribution[:, block * 128 : (block + 1) * 128]
        sums = jnp.sum(part, axis=1, keepdims=True)
        for n, row in enumerate(picked_rows):
            found += jnp.where(segment == map_ref[block, row], sums[n : n + 1, :], 0.0)
    return total + found[:, None, :lanes]


def near_kernel(
    scale,
    d_ref,
    own_ref,
    excess_ref,
    edge_ref,
    pair_ref,
    map_vmem,
    place_ref,
    base_ref,
    contribution_ref,
    sent_ref,
    got_ref,
    adj_hbm,
    part_ref,
    adj_ref,
    map_ref,
    sems,
):
    map_copy = pltpu.make_async_copy(map_vmem, map_ref, sems.at[0])
    map_copy.start()
    depth, rows, cols = adj_ref.shape
    size = depth * rows
    sources, surface = correction(0, got_ref, sent_ref, d_ref, own_ref, edge_ref, pair_ref)
    found = dot(place_ref[...], sources)
    adj_ref[...] = (chunked(base_ref, 0, size, size) + found).reshape(depth, rows, cols)
    adj_copy = pltpu.make_async_copy(adj_ref, adj_hbm, sems.at[1])
    adj_copy.start()
    row = jnp.where(sides()[0][0], rows - 1, 0)
    surface = jnp.where(iota((rows, cols), 0) == row, surface, 0.0)
    contribution = contribution_ref[...] + scale * (
        surface * excess_ref[1] + found[0:rows, :] * excess_ref[0]
    )
    map_copy.wait()
    part_ref[...] = add_segments(
        jnp.zeros(part_ref.shape, F32), contribution, range(rows), map_ref
    )
    adj_copy.wait()


def far_kernel(
    scale,
    sent_ref,
    got_ref,
    d_ref,
    own_ref,
    excess_ref,
    edge_ref,
    pair_ref,
    map_vmem,
    two_ref,
    part_in_ref,
    out_ref,
    part_ref,
    map_ref,
    map_sem,
):
    map_copy = pltpu.make_async_copy(map_vmem, map_ref, map_sem)
    map_copy.start()
    depth = two_ref.shape[1]
    rows = excess_ref.shape[1]
    sources, surface = correction(1, got_ref, sent_ref, d_ref, own_ref, edge_ref, pair_ref)
    found = dot(pair_ref[...], sources)
    edge, second = far_rows(rows)
    contribution = scale * jnp.concatenate(
        [
            surface * excess_ref[1, pl.ds(edge, 1), :]
            + found[0:1] * excess_ref[0, pl.ds(edge, 1), :],
            found[depth : depth + 1] * excess_ref[0, pl.ds(second, 1), :],
        ],
        axis=0,
    )
    map_copy.wait()
    part_ref[...] = add_segments(part_in_ref[...], contribution, (edge, second), map_ref)
    out_ref[...] = two_ref[...] + found.reshape(two_ref.shape)


def finish_kernel(_, two_ref, got_ref, adj_hbm, out_hbm, out_ref, sems):
    copies = []
    for n, row in enumerate(far_rows(adj_hbm.shape[1])):
        copies.append(pltpu.make_async_copy(two_ref.at[n], adj_hbm.at[:, row, :], sems.at[n]))
        copies[-1].start()
    out_ref[...] = jnp.sum(got_ref[:, 0, :], axis=0)
    copies.append(pltpu.make_async_copy(out_ref, out_hbm, sems.at[2]))
    copies[-1].start()
    for copy in copies:
        copy.wait()


def in_hbm(x):
    return pltpu.with_memory_space_constraint(x, pltpu.HBM)


def per_device(
    conductance, depth_inverse, surface_residual, surface_excess, segment_map, frame_index
):
    _, depth, rows, cols = conductance.shape
    frames = surface_residual.shape[1]
    blocks = segment_map.shape[1]
    size = depth * rows
    spans = lax.axis_size("span")
    devices = spans * lax.axis_size("blade")
    lanes = SEGS // devices
    field = pltpu.VMEM((depth, rows, cols), F32)
    chunks = cols // 128
    packed_far = pltpu.VMEM(((2 * depth + 4) * chunks, 128), F32)
    packed_near = pltpu.VMEM(((2 * depth + 3) * chunks, 128), F32)
    own_far, own_near, k, picked, inverse = pl.pallas_call(
        functools.partial(load_kernel, rows),
        out_shape=(
            packed_far,
            packed_near,
            pltpu.VMEM((chunks * size, 128), F32),
            pltpu.VMEM((STEPS, rows, cols), F32),
            pltpu.VMEM((depth, depth), F32),
        ),
        in_specs=[HBM] * 4,
        out_specs=(VMEM,) * 5,
        scratch_shapes=[
            pltpu.SMEM((STEPS,), jnp.int32),
            pltpu.VMEM((frames, rows, cols), F32),
            pltpu.SemaphoreType.DMA((3 + chunks,)),
        ],
        compiler_params=GRANT,
        name="load",
    )(
        in_hbm(frame_index),
        in_hbm(conductance.reshape(size, cols)),
        in_hbm(surface_residual[0]),
        in_hbm(depth_inverse[0]),
    )
    across = [(i, i + 1) for i in range(1, spans - 1, 2)]
    within = [(i, i + 1) for i in range(0, spans - 1, 2)]
    near = lax.ppermute(own_near, "span", within + [(b, a) for a, b in within])
    far = lax.ppermute(own_far, "span", across + [(b, a) for a, b in across])
    scale = 1.0 / math.sqrt(128.0 * STEPS)
    line = pltpu.VMEM((rows, cols), F32)
    own, base, two, excess, ids, edge, contribution, pair, place = pl.pallas_call(
        functools.partial(base_kernel, scale),
        out_shape=(
            pltpu.VMEM((2, 5, depth, cols), F32),
            pltpu.VMEM((chunks * size, 128), F32),
            pltpu.VMEM((2, depth, cols), F32),
            pltpu.VMEM((STEPS, rows, cols), F32),
            pltpu.VMEM((blocks, rows), jnp.int32),
            pltpu.VMEM((2, depth, cols), F32),
            line,
            pltpu.VMEM((2 * depth, 6 * depth), BF16),
            pltpu.VMEM((size, 6 * depth), BF16),
        ),
        in_specs=[VMEM] * 5 + [HBM] * 2,
        out_specs=(VMEM,) * 9,
        scratch_shapes=[
            pltpu.VMEM((size, 3 * size), BF16),
            pltpu.VMEM((3, size, cols), BF16),
            pltpu.VMEM((chunks * size, 128), F32),
            field,
            field,
            pltpu.VMEM((depth, 128), F32),
            pltpu.SemaphoreType.DMA((2,)),
        ],
        compiler_params=GRANT,
        name="base",
    )(k, picked, inverse, own_near, own_far, in_hbm(surface_excess[0]), in_hbm(segment_map.T))
    fixed = (inverse, own, excess, edge, pair, ids)
    sums = pltpu.VMEM((devices, 1, lanes), F32)
    adjoint, partial = pl.pallas_call(
        functools.partial(near_kernel, scale),
        out_shape=(pltpu.HBM((depth, rows, cols), F32), sums),
        in_specs=[VMEM] * 11,
        out_specs=(HBM, VMEM),
        scratch_shapes=[
            field,
            pltpu.SMEM((blocks, rows), jnp.int32),
            pltpu.SemaphoreType.DMA((2,)),
        ],
        compiler_params=GRANT,
        name="near",
    )(*fixed, place, base, contribution, own_near, near)
    two, partial = pl.pallas_call(
        functools.partial(far_kernel, scale),
        out_shape=(pltpu.VMEM((2, depth, cols), F32), sums),
        in_specs=[VMEM] * 10,
        out_specs=(VMEM,) * 2,
        scratch_shapes=[pltpu.SMEM((blocks, rows), jnp.int32), pltpu.SemaphoreType.DMA],
        compiler_params=GRANT,
        name="far",
    )(own_far, far, *fixed, two, partial)
    pieces = lax.all_to_all(partial, ("blade", "span"), 0, 0, tiled=True)
    adjoint, owned = pl.pallas_call(
        finish_kernel,
        out_shape=(pltpu.HBM((depth, rows, cols), F32), pltpu.HBM((lanes,), F32)),
        in_specs=[HBM, VMEM, VMEM],
        out_specs=(HBM,) * 2,
        scratch_shapes=[pltpu.VMEM((lanes,), F32), pltpu.SemaphoreType.DMA((3,))],
        input_output_aliases={0: 0},
        compiler_params=GRANT,
        name="finish",
    )(in_hbm(adjoint), two, pltpu.with_memory_space_constraint(pieces, pltpu.VMEM))
    return (adjoint[None], owned)


def solution(mesh):
    placed = (
        P("blade", None, "span", None),
        P("blade", None, None),
        P("blade", None, "span", None),
        P("blade", None, "span", None),
        P("span", None),
        P(),
    )
    return jax.shard_map(
        per_device,
        mesh=mesh,
        in_specs=placed,
        out_specs=(P("blade", None, "span", None), P(("blade", "span"))),
        check_vma=False,
    )
```

```python
import functools
import math

import jax
import jax.numpy as jnp
from jax import lax
from jax.experimental import pallas as pl
from jax.experimental.pallas import tpu as pltpu
from jax.sharding import PartitionSpec as P

STEPS = 3
SEGS = 2048
F32 = jnp.float32
BF16 = jnp.bfloat16
VMEM = pl.BlockSpec(memory_space=pltpu.VMEM)
HBM = pl.BlockSpec(memory_space=pltpu.HBM)
GRANT = pltpu.CompilerParams(vmem_limit_bytes=16 * 2**20)


def split(x):
    high = x.astype(BF16)
    return high, (x - high.astype(F32)).astype(BF16)


def dot(a, b):
    return jnp.dot(a, b, preferred_element_type=F32)


def left_three(matrix):
    high, low = matrix
    return jnp.concatenate([high, low, high], axis=1)


def right_three(x):
    high, low = split(x)
    return jnp.concatenate([high, high, low], axis=0)


def iota(shape, dim):
    return lax.broadcasted_iota(jnp.int32, shape, dim)


def shift_next(x, axis):
    size = x.shape[axis]
    return jnp.where(iota(x.shape, axis) == size - 1, 0.0, pltpu.roll(x, size - 1, axis))


def shift_prev(x, axis, first):
    return jnp.where(iota(x.shape, axis) == 0, first, pltpu.roll(x, 1, axis))


def divergence(v, weight, half, axis):
    flux = weight * (shift_next(v, axis) - v)
    return flux - shift_prev(flux, axis, half * v)


def sides():
    span = lax.axis_index("span")
    count = lax.axis_size("span")
    even = lax.rem(span, 2) == 0
    has_next = span + 1 < count
    has_prev = span > 0
    return (
        (even, jnp.where(even, has_next, has_prev)),
        (jnp.logical_not(even), jnp.where(even, has_prev, has_next)),
    )


def chunked(ref, start, count, step):
    chunks = ref.shape[0] // step
    return jnp.concatenate(
        [ref[c * step + start : c * step + start + count, :] for c in range(chunks)], axis=1
    )


def packed_field(ref, depth, cols, n):
    chunks = cols // 128
    return chunked(ref.at[n * chunks * depth : (n + 1) * chunks * depth], 0, depth, depth)


def packed_line(ref, depth, cols, n):
    chunks = cols // 128
    base = (2 * depth + n) * chunks
    return chunked(ref.at[base : base + chunks], 0, 1, 1)


def row_of_each(ref, chunk, depth, rows, row):
    return ref[pl.ds(chunk * depth * rows + row, depth, stride=rows), :]


def far_rows(rows):
    after = sides()[1][0]
    return jnp.where(after, rows - 1, 0), jnp.where(after, rows - 2, 1)


def load_kernel(
    rows,
    frame_hbm,
    k_hbm,
    res_hbm,
    d_hbm,
    far_ref,
    near_ref,
    k_ref,
    frames_ref,
    d_ref,
    frame_ref,
    res_ref,
    sems,
):
    size, cols = k_hbm.shape
    depth = size // rows
    chunks = cols // 128
    pairs = [(frame_hbm, frame_ref), (res_hbm, res_ref)]
    for c in range(chunks):
        pairs.append((k_hbm.at[:, pl.ds(c * 128, 128)], k_ref.at[pl.ds(c * size, size)]))
    pairs.append((d_hbm, d_ref))
    copies = [pltpu.make_async_copy(a, b, sems.at[n]) for n, (a, b) in enumerate(pairs)]
    for copy in copies:
        copy.start()
    sent = (near_ref, far_ref)
    picks = []
    for after, _ in sides():
        picks.append((jnp.where(after, rows - 1, 0), jnp.where(after, rows - 2, 1)))
    copies[0].wait()
    copies[1].wait()
    for step in range(STEPS):
        frames_ref[step] = res_ref[frame_ref[step]]
    base = 2 * chunks * depth
    for ref, (edge, second) in zip(sent, picks):
        for n, (step, row) in enumerate(((2, edge), (1, edge), (2, second))):
            line = frames_ref[step, pl.ds(row, 1), :]
            for c in range(chunks):
                spot = base + n * chunks + c
                ref[spot : spot + 1, :] = line[:, c * 128 : (c + 1) * 128]
        if ref.shape[0] > base + 3 * chunks:
            ref[base + 3 * chunks :, :] = jnp.zeros((ref.shape[0] - base - 3 * chunks, 128), F32)
    for c in range(chunks):
        copies[2 + c].wait()
        for ref, row_pair in zip(sent, picks):
            for n, row in enumerate(row_pair):
                spot = (n * chunks + c) * depth
                ref[spot : spot + depth, :] = row_of_each(k_ref, c, depth, rows, row)
    for copy in copies[2 + chunks :]:
        copy.wait()


def base_kernel(
    scale,
    k_ref,
    frames_ref,
    d_ref,
    excess_hbm,
    map_hbm,
    adj_ref,
    two_ref,
    excess_ref,
    map_ref,
    edge_ref,
    contribution_ref,
    pair_ref,
    place_ref,
    mat_ref,
    right_ref,
    first_ref,
    chord_ref,
    span_ref,
    factor_ref,
    sems,
):
    copies = [
        pltpu.make_async_copy(excess_hbm, excess_ref, sems.at[0]),
        pltpu.make_async_copy(map_hbm, map_ref, sems.at[1]),
    ]
    for copy in copies:
        copy.start()
    depth, rows, cols = chord_ref.shape
    size = depth * rows
    factor_ref[...] = jnp.broadcast_to(d_ref[:, 0:1], factor_ref.shape)

    parts = split(d_ref[...])
    tall = (iota((size, depth), 0) // rows == iota((size, depth), 1)).astype(BF16)
    wide = (iota((depth, size), 0) == iota((depth, size), 1) // rows).astype(BF16)
    two = 2 * depth
    tile = (iota((depth, two), 0) == iota((depth, two), 1) % depth).astype(BF16)
    same = iota((size, size), 0) % rows == iota((size, size), 1) % rows
    pair_same = iota((two, two), 0) // depth == iota((two, two), 1) // depth
    row_of = iota((size, two), 0) % rows
    first_half = iota((size, two), 1) < depth
    after = sides()[0][0]
    edge = jnp.where(after, rows - 1, 0)
    second = jnp.where(after, rows - 2, 1)
    placed = row_of == jnp.where(first_half, edge, second)
    mats, pairs, places = [], [], []
    for part in parts:
        column = dot(tall, part).astype(BF16)
        row = dot(part, tile)
        mats.append(jnp.where(same, dot(column, wide), 0.0).astype(BF16))
        places.append(jnp.where(placed, dot(column, tile), 0.0).astype(BF16))
        pairs.append(
            jnp.where(pair_same, jnp.concatenate([row] * 2, axis=0), 0.0).astype(BF16)
        )
    mat_ref[...] = left_three(mats)
    pair_ref[...] = left_three(pairs)
    place_ref[...] = left_three(places)

    f = frames_ref[2]
    f_chord = shift_next(f, 1) - f
    f_span = shift_next(f, 0) - f

    def put(i, both):
        high, low = split(both)
        span = pl.ds(pl.multiple_of(i * rows, 2 * rows), 2 * rows)
        right_ref[0, span, :] = high
        right_ref[1, span, :] = high
        right_ref[2, span, :] = low

    def at(ref, j):
        return jnp.concatenate(
            [
                ref[pl.ds(pl.multiple_of(c * size + j * rows, rows), rows), :]
                for c in range(cols // 128)
            ],
            axis=1,
        )

    def first_sweep(n, _):
        found = []
        for j in (2 * n, 2 * n + 1):
            half = 0.5 * at(k_ref, j)
            w_chord = half + shift_next(half, 1)
            w_span = half + shift_next(half, 0)
            chord_ref[j] = w_chord
            span_ref[j] = w_span
            edge = half * f
            flux_chord = w_chord * f_chord
            flux_span = w_span * f_span
            moved = f + flux_chord - shift_prev(flux_chord, 1, edge)
            moved = moved + flux_span - shift_prev(flux_span, 0, edge)
            factor = jnp.concatenate(
                [jnp.broadcast_to(factor_ref[pl.ds(j, 1), :], (rows, 128))] * (cols // 128),
                axis=1,
            )
            found.append(factor * moved + jnp.where(j == 0, frames_ref[1], 0.0))
        put(2 * n, jnp.concatenate(found, axis=0))
        return 0

    lax.fori_loop(0, depth // 2, first_sweep, 0, unroll=2)
    right = right_ref[...].reshape(3 * size, cols)
    first = dot(mat_ref[...], right)
    for c in range(cols // 128):
        first_ref[c * size : (c + 1) * size, :] = first[:, c * 128 : (c + 1) * 128]

    def second_sweep(n, _):
        found = []
        for j in (2 * n, 2 * n + 1):
            v = at(first_ref, j)
            half = 0.5 * at(k_ref, j)
            source = (
                v + divergence(v, chord_ref[j], half, 1) + divergence(v, span_ref[j], half, 0)
            )
            found.append(source + jnp.where(j == 0, frames_ref[0], 0.0))
        put(2 * n, jnp.concatenate(found, axis=0))
        return 0

    lax.fori_loop(0, depth // 2, second_sweep, 0, unroll=2)
    right = right_ref[...].reshape(3 * size, cols)
    adj = dot(mat_ref[...], right)
    for c in range(cols // 128):
        adj_ref[c * size : (c + 1) * size, :] = adj[:, c * 128 : (c + 1) * 128]

    for n, (after, _) in enumerate(sides()):
        row = jnp.where(after, rows - 1, 0)
        for c in range(cols // 128):
            edge_ref[n, :, c * 128 : (c + 1) * 128] = row_of_each(first_ref, c, depth, rows, row)
    for n, row in enumerate(far_rows(rows)):
        for c in range(cols // 128):
            two_ref[n, :, c * 128 : (c + 1) * 128] = row_of_each(adj_ref, c, depth, rows, row)
    for copy in copies:
        copy.wait()
    contribution_ref[...] = scale * (
        d_ref[0:1, 0:1] * f * excess_ref[2]
        + chunked(first_ref, 0, rows, size) * excess_ref[1]
        + chunked(adj_ref, 0, rows, size) * excess_ref[0]
    )


def correction(n, got, own, d_ref, edge_ref, pair_ref):
    _, depth, cols = edge_ref.shape
    _, inside = sides()[n]
    factor = d_ref[:, 0:1]
    half = 0.5 * packed_field(got, depth, cols, 0)
    half_next = 0.5 * packed_field(got, depth, cols, 1)
    f = packed_line(got, depth, cols, 0)
    frame = packed_line(got, depth, cols, 1)
    f_next = packed_line(got, depth, cols, 2)
    f_own = packed_line(own, depth, cols, 0)
    half_own = 0.5 * packed_field(own, depth, cols, 0)
    inner = half_own + 0.5 * packed_field(own, depth, cols, 1)
    w_next = half_own + shift_next(half_own, 1)
    w_prev = half_own + shift_prev(half_own, 1, 0.0)
    face = half + half_own
    moved = (
        f
        + (half + shift_next(half, 1)) * (shift_next(f, 1) - f)
        + (half + shift_prev(half, 1, 0.0)) * (shift_prev(f, 1, 0.0) - f)
        + (half + half_next) * (f_next - f)
        + face * (f_own - f)
    )
    outer = factor * moved + jnp.where(iota((depth, 1), 0) == 0, frame, 0.0)
    sources = [factor * (face * f - half * f_own), jnp.where(inside, outer, 0.0)]
    found = dot(pair_ref[...], right_three(jnp.concatenate(sources, axis=0)))
    e = found[0:depth]
    outer = found[depth:]
    change = (
        (1.0 - (w_next + w_prev) - (half_own + inner)) * e
        + w_next * shift_next(e, 1)
        + w_prev * shift_prev(e, 1, 0.0)
        + face * outer
        - half * (e + edge_ref[n])
    )
    return right_three(jnp.concatenate([change, inner * e], axis=0)), e[0:1, :]


def add_segments(total, contribution, picked_rows, map_ref):
    owners, _, lanes = total.shape
    shape = (owners, 128)
    lane = iota(shape, 1)
    segment = jnp.where(lane < lanes, iota(shape, 0) * lanes + lane, -1)
    found = jnp.zeros(shape, F32)
    for block in range(contribution.shape[1] // 128):
        part = contribution[:, block * 128 : (block + 1) * 128]
        sums = jnp.sum(part, axis=1, keepdims=True)
        for n, row in enumerate(picked_rows):
            found += jnp.where(segment == map_ref[block, row], sums[n : n + 1, :], 0.0)
    return total + found[:, None, :lanes]


def near_kernel(
    scale,
    d_ref,
    excess_ref,
    edge_ref,
    pair_ref,
    map_vmem,
    place_ref,
    base_ref,
    contribution_ref,
    own_ref,
    got_ref,
    adj_hbm,
    part_ref,
    adj_ref,
    map_ref,
    sems,
):
    map_copy = pltpu.make_async_copy(map_vmem, map_ref, sems.at[0])
    map_copy.start()
    depth, rows, cols = adj_ref.shape
    size = depth * rows
    sources, surface = correction(0, got_ref, own_ref, d_ref, edge_ref, pair_ref)
    found = dot(place_ref[...], sources)
    adj_ref[...] = (chunked(base_ref, 0, size, size) + found).reshape(depth, rows, cols)
    adj_copy = pltpu.make_async_copy(adj_ref, adj_hbm, sems.at[1])
    adj_copy.start()
    row = jnp.where(sides()[0][0], rows - 1, 0)
    surface = jnp.where(iota((rows, cols), 0) == row, surface, 0.0)
    contribution = contribution_ref[...] + scale * (
        surface * excess_ref[1] + found[0:rows, :] * excess_ref[0]
    )
    map_copy.wait()
    part_ref[...] = add_segments(
        jnp.zeros(part_ref.shape, F32), contribution, range(rows), map_ref
    )
    adj_copy.wait()


def far_kernel(
    scale,
    own_ref,
    got_ref,
    d_ref,
    excess_ref,
    edge_ref,
    pair_ref,
    map_vmem,
    two_ref,
    part_in_ref,
    out_ref,
    part_ref,
    map_ref,
    map_sem,
):
    map_copy = pltpu.make_async_copy(map_vmem, map_ref, map_sem)
    map_copy.start()
    depth = two_ref.shape[1]
    rows = excess_ref.shape[1]
    sources, surface = correction(1, got_ref, own_ref, d_ref, edge_ref, pair_ref)
    found = dot(pair_ref[...], sources)
    edge, second = far_rows(rows)
    contribution = scale * jnp.concatenate(
        [
            surface * excess_ref[1, pl.ds(edge, 1), :]
            + found[0:1] * excess_ref[0, pl.ds(edge, 1), :],
            found[depth : depth + 1] * excess_ref[0, pl.ds(second, 1), :],
        ],
        axis=0,
    )
    map_copy.wait()
    part_ref[...] = add_segments(part_in_ref[...], contribution, (edge, second), map_ref)
    out_ref[...] = two_ref[...] + found.reshape(two_ref.shape)


def finish_kernel(_, two_ref, got_ref, adj_hbm, out_hbm, out_ref, sems):
    copies = []
    for n, row in enumerate(far_rows(adj_hbm.shape[1])):
        copies.append(pltpu.make_async_copy(two_ref.at[n], adj_hbm.at[:, row, :], sems.at[n]))
        copies[-1].start()
    out_ref[...] = jnp.sum(got_ref[:, 0, :], axis=0)
    copies.append(pltpu.make_async_copy(out_ref, out_hbm, sems.at[2]))
    copies[-1].start()
    for copy in copies:
        copy.wait()


def in_hbm(x):
    return pltpu.with_memory_space_constraint(x, pltpu.HBM)


def per_device(
    conductance, depth_inverse, surface_residual, surface_excess, segment_map, frame_index
):
    _, depth, rows, cols = conductance.shape
    frames = surface_residual.shape[1]
    blocks = segment_map.shape[1]
    size = depth * rows
    spans = lax.axis_size("span")
    devices = spans * lax.axis_size("blade")
    lanes = SEGS // devices
    field = pltpu.VMEM((depth, rows, cols), F32)
    chunks = cols // 128
    packed_far = pltpu.VMEM(((2 * depth + 4) * chunks, 128), F32)
    packed_near = pltpu.VMEM(((2 * depth + 3) * chunks, 128), F32)
    own_far, own_near, k, picked, inverse = pl.pallas_call(
        functools.partial(load_kernel, rows),
        out_shape=(
            packed_far,
            packed_near,
            pltpu.VMEM((chunks * size, 128), F32),
            pltpu.VMEM((STEPS, rows, cols), F32),
            pltpu.VMEM((depth, depth), F32),
        ),
        in_specs=[HBM] * 4,
        out_specs=(VMEM,) * 5,
        scratch_shapes=[
            pltpu.SMEM((STEPS,), jnp.int32),
            pltpu.VMEM((frames, rows, cols), F32),
            pltpu.SemaphoreType.DMA((3 + chunks,)),
        ],
        compiler_params=GRANT,
        name="load",
    )(
        in_hbm(frame_index),
        in_hbm(conductance.reshape(size, cols)),
        in_hbm(surface_residual[0]),
        in_hbm(depth_inverse[0]),
    )
    across = [(i, i + 1) for i in range(1, spans - 1, 2)]
    within = [(i, i + 1) for i in range(0, spans - 1, 2)]
    near = lax.ppermute(own_near, "span", within + [(b, a) for a, b in within])
    far = lax.ppermute(own_far, "span", across + [(b, a) for a, b in across])
    scale = 1.0 / math.sqrt(128.0 * STEPS)
    line = pltpu.VMEM((rows, cols), F32)
    base, two, excess, ids, edge, contribution, pair, place = pl.pallas_call(
        functools.partial(base_kernel, scale),
        out_shape=(
            pltpu.VMEM((chunks * size, 128), F32),
            pltpu.VMEM((2, depth, cols), F32),
            pltpu.VMEM((STEPS, rows, cols), F32),
            pltpu.VMEM((blocks, rows), jnp.int32),
            pltpu.VMEM((2, depth, cols), F32),
            line,
            pltpu.VMEM((2 * depth, 6 * depth), BF16),
            pltpu.VMEM((size, 6 * depth), BF16),
        ),
        in_specs=[VMEM] * 3 + [HBM] * 2,
        out_specs=(VMEM,) * 8,
        scratch_shapes=[
            pltpu.VMEM((size, 3 * size), BF16),
            pltpu.VMEM((3, size, cols), BF16),
            pltpu.VMEM((chunks * size, 128), F32),
            field,
            field,
            pltpu.VMEM((depth, 128), F32),
            pltpu.SemaphoreType.DMA((2,)),
        ],
        compiler_params=GRANT,
        name="base",
    )(k, picked, inverse, in_hbm(surface_excess[0]), in_hbm(segment_map.T))
    fixed = (inverse, excess, edge, pair, ids)
    sums = pltpu.VMEM((devices, 1, lanes), F32)
    adjoint, partial = pl.pallas_call(
        functools.partial(near_kernel, scale),
        out_shape=(pltpu.HBM((depth, rows, cols), F32), sums),
        in_specs=[VMEM] * 10,
        out_specs=(HBM, VMEM),
        scratch_shapes=[
            field,
            pltpu.SMEM((blocks, rows), jnp.int32),
            pltpu.SemaphoreType.DMA((2,)),
        ],
        compiler_params=GRANT,
        name="near",
    )(*fixed, place, base, contribution, own_near, near)
    two, partial = pl.pallas_call(
        functools.partial(far_kernel, scale),
        out_shape=(pltpu.VMEM((2, depth, cols), F32), sums),
        in_specs=[VMEM] * 9,
        out_specs=(VMEM,) * 2,
        scratch_shapes=[pltpu.SMEM((blocks, rows), jnp.int32), pltpu.SemaphoreType.DMA],
        compiler_params=GRANT,
        name="far",
    )(own_far, far, *fixed, two, partial)
    pieces = lax.all_to_all(partial, ("blade", "span"), 0, 0, tiled=True)
    adjoint, owned = pl.pallas_call(
        finish_kernel,
        out_shape=(pltpu.HBM((depth, rows, cols), F32), pltpu.HBM((lanes,), F32)),
        in_specs=[HBM, VMEM, VMEM],
        out_specs=(HBM,) * 2,
        scratch_shapes=[pltpu.VMEM((lanes,), F32), pltpu.SemaphoreType.DMA((3,))],
        input_output_aliases={0: 0},
        compiler_params=GRANT,
        name="finish",
    )(in_hbm(adjoint), two, pltpu.with_memory_space_constraint(pieces, pltpu.VMEM))
    return (adjoint[None], owned)


def solution(mesh):
    placed = (
        P("blade", None, "span", None),
        P("blade", None, None),
        P("blade", None, "span", None),
        P("blade", None, "span", None),
        P("span", None),
        P(),
    )
    return jax.shard_map(
        per_device,
        mesh=mesh,
        in_specs=placed,
        out_specs=(P("blade", None, "span", None), P(("blade", "span"))),
        check_vma=False,
    )
```

```python
import functools
import math

import jax
import jax.numpy as jnp
from jax import lax
from jax.experimental import pallas as pl
from jax.experimental.pallas import tpu as pltpu
from jax.sharding import PartitionSpec as P

STEPS = 3
SEGS = 2048
GROUP = 2
F32 = jnp.float32
BF16 = jnp.bfloat16
VMEM = pl.BlockSpec(memory_space=pltpu.VMEM)
HBM = pl.BlockSpec(memory_space=pltpu.HBM)
GRANT = pltpu.CompilerParams(vmem_limit_bytes=16 * 2**20)


def split(x):
    high = x.astype(BF16)
    return high, (x - high.astype(F32)).astype(BF16)


def dot(a, b):
    return jnp.dot(a, b, preferred_element_type=F32)


def left_three(matrix):
    high, low = matrix
    return jnp.concatenate([high, low, high], axis=1)


def right_three(x):
    high, low = split(x)
    return jnp.concatenate([high, high, low], axis=0)


def iota(shape, dim):
    return lax.broadcasted_iota(jnp.int32, shape, dim)


def shift_next(x, axis):
    size = x.shape[axis]
    return jnp.where(iota(x.shape, axis) == size - 1, 0.0, pltpu.roll(x, size - 1, axis))


def shift_prev(x, axis, first):
    return jnp.where(iota(x.shape, axis) == 0, first, pltpu.roll(x, 1, axis))


def divergence(v, weight, half, axis):
    flux = weight * (shift_next(v, axis) - v)
    return flux - shift_prev(flux, axis, half * v)


def sides():
    span = lax.axis_index("span")
    count = lax.axis_size("span")
    even = lax.rem(span, 2) == 0
    has_next = span + 1 < count
    has_prev = span > 0
    return (
        (even, jnp.where(even, has_next, has_prev)),
        (jnp.logical_not(even), jnp.where(even, has_prev, has_next)),
    )


def chunked(ref, start, count, step):
    chunks = ref.shape[0] // step
    return jnp.concatenate(
        [ref[c * step + start : c * step + start + count, :] for c in range(chunks)], axis=1
    )


def packed_field(ref, depth, cols, n):
    chunks = cols // 128
    return chunked(ref.at[n * chunks * depth : (n + 1) * chunks * depth], 0, depth, depth)


def packed_line(ref, depth, cols, n):
    chunks = cols // 128
    base = (2 * depth + n) * chunks
    return chunked(ref.at[base : base + chunks], 0, 1, 1)


def row_of_each(ref, chunk, depth, rows, row):
    return ref[pl.ds(chunk * depth * rows + row, depth, stride=rows), :]


def far_rows(rows):
    after = sides()[1][0]
    return jnp.where(after, rows - 1, 0), jnp.where(after, rows - 2, 1)


def load_kernel(
    rows,
    frame_hbm,
    k_hbm,
    res_hbm,
    d_hbm,
    far_ref,
    near_ref,
    k_ref,
    frames_ref,
    d_ref,
    frame_ref,
    res_ref,
    sems,
):
    size, cols = k_hbm.shape
    depth = size // rows
    chunks = cols // 128
    pairs = [(frame_hbm, frame_ref), (res_hbm, res_ref)]
    for c in range(chunks):
        pairs.append((k_hbm.at[:, pl.ds(c * 128, 128)], k_ref.at[pl.ds(c * size, size)]))
    pairs.append((d_hbm, d_ref))
    copies = [pltpu.make_async_copy(a, b, sems.at[n]) for n, (a, b) in enumerate(pairs)]
    for copy in copies:
        copy.start()
    sent = (near_ref, far_ref)
    picks = []
    for after, _ in sides():
        picks.append((jnp.where(after, rows - 1, 0), jnp.where(after, rows - 2, 1)))
    copies[0].wait()
    copies[1].wait()
    for step in range(STEPS):
        frames_ref[step] = res_ref[frame_ref[step]]
    base = 2 * chunks * depth
    for ref, (edge, second) in zip(sent, picks):
        for n, (step, row) in enumerate(((2, edge), (1, edge), (2, second))):
            line = frames_ref[step, pl.ds(row, 1), :]
            for c in range(chunks):
                spot = base + n * chunks + c
                ref[spot : spot + 1, :] = line[:, c * 128 : (c + 1) * 128]
        if ref.shape[0] > base + 3 * chunks:
            ref[base + 3 * chunks :, :] = jnp.zeros((ref.shape[0] - base - 3 * chunks, 128), F32)
    for c in range(chunks):
        copies[2 + c].wait()
        for ref, row_pair in zip(sent, picks):
            for n, row in enumerate(row_pair):
                spot = (n * chunks + c) * depth
                ref[spot : spot + depth, :] = row_of_each(k_ref, c, depth, rows, row)
    for copy in copies[2 + chunks :]:
        copy.wait()


def base_kernel(
    scale,
    k_ref,
    frames_ref,
    d_ref,
    excess_hbm,
    map_hbm,
    adj_ref,
    two_ref,
    excess_ref,
    map_ref,
    edge_ref,
    contribution_ref,
    pair_ref,
    place_ref,
    mat_ref,
    right_ref,
    first_ref,
    chord_ref,
    span_ref,
    factor_ref,
    sems,
):
    copies = [
        pltpu.make_async_copy(excess_hbm, excess_ref, sems.at[0]),
        pltpu.make_async_copy(map_hbm, map_ref, sems.at[1]),
    ]
    for copy in copies:
        copy.start()
    depth, rows, cols = chord_ref.shape
    size = depth * rows
    factor_ref[...] = jnp.broadcast_to(d_ref[:, 0:1], factor_ref.shape)

    parts = split(d_ref[...])
    tall = (iota((size, depth), 0) // rows == iota((size, depth), 1)).astype(BF16)
    wide = (iota((depth, size), 0) == iota((depth, size), 1) // rows).astype(BF16)
    two = 2 * depth
    tile = (iota((depth, two), 0) == iota((depth, two), 1) % depth).astype(BF16)
    same = iota((size, size), 0) % rows == iota((size, size), 1) % rows
    pair_same = iota((two, two), 0) // depth == iota((two, two), 1) // depth
    row_of = iota((size, two), 0) % rows
    first_half = iota((size, two), 1) < depth
    after = sides()[0][0]
    edge = jnp.where(after, rows - 1, 0)
    second = jnp.where(after, rows - 2, 1)
    placed = row_of == jnp.where(first_half, edge, second)
    mats, pairs, places = [], [], []
    for part in parts:
        column = dot(tall, part).astype(BF16)
        row = dot(part, tile)
        mats.append(jnp.where(same, dot(column, wide), 0.0).astype(BF16))
        places.append(jnp.where(placed, dot(column, tile), 0.0).astype(BF16))
        pairs.append(
            jnp.where(pair_same, jnp.concatenate([row] * 2, axis=0), 0.0).astype(BF16)
        )
    mat_ref[...] = left_three(mats)
    pair_ref[...] = left_three(pairs)
    place_ref[...] = left_three(places)

    f = frames_ref[2]
    f_chord = shift_next(f, 1) - f
    f_span = shift_next(f, 0) - f

    def put(i, both):
        high, low = split(both)
        span = pl.ds(i * rows, 2 * rows)
        right_ref[0, span, :] = high
        right_ref[1, span, :] = high
        right_ref[2, span, :] = low

    def lines_of(ref, i):
        return [chunked(ref, j * rows, rows, size) for j in range(i, i + GROUP)]

    for i in range(0, depth, GROUP):
        halves = [0.5 * x for x in lines_of(k_ref, i)]
        factors = [jnp.broadcast_to(factor_ref[j : j + 1, :], (rows, 128)) for j in range(i, i + GROUP)]
        chords = [half + shift_next(half, 1) for half in halves]
        spans = [half + shift_next(half, 0) for half in halves]
        found = []
        for half, factor, w_chord, w_span in zip(halves, factors, chords, spans):
            edge = half * f
            flux_chord = w_chord * f_chord
            flux_span = w_span * f_span
            moved = f + flux_chord - shift_prev(flux_chord, 1, edge)
            moved = moved + flux_span - shift_prev(flux_span, 0, edge)
            found.append(jnp.concatenate([factor] * (cols // 128), axis=1) * moved)
        if i == 0:
            found[0] = found[0] + frames_ref[1]
        for n in range(GROUP):
            chord_ref[i + n] = chords[n]
            span_ref[i + n] = spans[n]
        for n in range(0, GROUP, 2):
            put(i + n, jnp.concatenate(found[n : n + 2], axis=0))
    right = right_ref[...].reshape(3 * size, cols)
    first = dot(mat_ref[...], right)
    for c in range(cols // 128):
        first_ref[c * size : (c + 1) * size, :] = first[:, c * 128 : (c + 1) * 128]

    for i in range(0, depth, GROUP):
        halves = [0.5 * x for x in lines_of(k_ref, i)]
        values = lines_of(first_ref, i)
        chords = [chord_ref[i + n] for n in range(GROUP)]
        spans = [span_ref[i + n] for n in range(GROUP)]
        found = [
            v + divergence(v, w_chord, half, 1) + divergence(v, w_span, half, 0)
            for v, w_chord, w_span, half in zip(values, chords, spans, halves)
        ]
        if i == 0:
            found[0] = found[0] + frames_ref[0]
        for n in range(0, GROUP, 2):
            put(i + n, jnp.concatenate(found[n : n + 2], axis=0))
    right = right_ref[...].reshape(3 * size, cols)
    adj = dot(mat_ref[...], right)
    for c in range(cols // 128):
        adj_ref[c * size : (c + 1) * size, :] = adj[:, c * 128 : (c + 1) * 128]

    for n, (after, _) in enumerate(sides()):
        row = jnp.where(after, rows - 1, 0)
        for c in range(cols // 128):
            edge_ref[n, :, c * 128 : (c + 1) * 128] = row_of_each(first_ref, c, depth, rows, row)
    for n, row in enumerate(far_rows(rows)):
        for c in range(cols // 128):
            two_ref[n, :, c * 128 : (c + 1) * 128] = row_of_each(adj_ref, c, depth, rows, row)
    for copy in copies:
        copy.wait()
    contribution_ref[...] = scale * (
        d_ref[0:1, 0:1] * f * excess_ref[2]
        + chunked(first_ref, 0, rows, size) * excess_ref[1]
        + chunked(adj_ref, 0, rows, size) * excess_ref[0]
    )


def correction(n, got, own, d_ref, edge_ref, pair_ref):
    _, depth, cols = edge_ref.shape
    _, inside = sides()[n]
    factor = d_ref[:, 0:1]
    half = 0.5 * packed_field(got, depth, cols, 0)
    half_next = 0.5 * packed_field(got, depth, cols, 1)
    f = packed_line(got, depth, cols, 0)
    frame = packed_line(got, depth, cols, 1)
    f_next = packed_line(got, depth, cols, 2)
    f_own = packed_line(own, depth, cols, 0)
    half_own = 0.5 * packed_field(own, depth, cols, 0)
    inner = half_own + 0.5 * packed_field(own, depth, cols, 1)
    w_next = half_own + shift_next(half_own, 1)
    w_prev = half_own + shift_prev(half_own, 1, 0.0)
    face = half + half_own
    moved = (
        f
        + (half + shift_next(half, 1)) * (shift_next(f, 1) - f)
        + (half + shift_prev(half, 1, 0.0)) * (shift_prev(f, 1, 0.0) - f)
        + (half + half_next) * (f_next - f)
        + face * (f_own - f)
    )
    outer = factor * moved + jnp.where(iota((depth, 1), 0) == 0, frame, 0.0)
    sources = [factor * (face * f - half * f_own), jnp.where(inside, outer, 0.0)]
    found = dot(pair_ref[...], right_three(jnp.concatenate(sources, axis=0)))
    e = found[0:depth]
    outer = found[depth:]
    change = (
        (1.0 - (w_next + w_prev) - (half_own + inner)) * e
        + w_next * shift_next(e, 1)
        + w_prev * shift_prev(e, 1, 0.0)
        + face * outer
        - half * (e + edge_ref[n])
    )
    return right_three(jnp.concatenate([change, inner * e], axis=0)), e[0:1, :]


def add_segments(total, contribution, picked_rows, map_ref):
    owners, _, lanes = total.shape
    shape = (owners, 128)
    lane = iota(shape, 1)
    segment = jnp.where(lane < lanes, iota(shape, 0) * lanes + lane, -1)
    found = jnp.zeros(shape, F32)
    for block in range(contribution.shape[1] // 128):
        part = contribution[:, block * 128 : (block + 1) * 128]
        sums = jnp.sum(part, axis=1, keepdims=True)
        for n, row in enumerate(picked_rows):
            found += jnp.where(segment == map_ref[block, row], sums[n : n + 1, :], 0.0)
    return total + found[:, None, :lanes]


def near_kernel(
    scale,
    d_ref,
    excess_ref,
    edge_ref,
    pair_ref,
    map_vmem,
    place_ref,
    base_ref,
    contribution_ref,
    own_ref,
    got_ref,
    adj_hbm,
    part_ref,
    adj_ref,
    map_ref,
    sems,
):
    map_copy = pltpu.make_async_copy(map_vmem, map_ref, sems.at[0])
    map_copy.start()
    depth, rows, cols = adj_ref.shape
    size = depth * rows
    sources, surface = correction(0, got_ref, own_ref, d_ref, edge_ref, pair_ref)
    found = dot(place_ref[...], sources)
    adj_ref[...] = (chunked(base_ref, 0, size, size) + found).reshape(depth, rows, cols)
    adj_copy = pltpu.make_async_copy(adj_ref, adj_hbm, sems.at[1])
    adj_copy.start()
    row = jnp.where(sides()[0][0], rows - 1, 0)
    surface = jnp.where(iota((rows, cols), 0) == row, surface, 0.0)
    contribution = contribution_ref[...] + scale * (
        surface * excess_ref[1] + found[0:rows, :] * excess_ref[0]
    )
    map_copy.wait()
    part_ref[...] = add_segments(
        jnp.zeros(part_ref.shape, F32), contribution, range(rows), map_ref
    )
    adj_copy.wait()


def far_kernel(
    scale,
    own_ref,
    got_ref,
    d_ref,
    excess_ref,
    edge_ref,
    pair_ref,
    map_vmem,
    two_ref,
    part_in_ref,
    out_ref,
    part_ref,
    map_ref,
    map_sem,
):
    map_copy = pltpu.make_async_copy(map_vmem, map_ref, map_sem)
    map_copy.start()
    depth = two_ref.shape[1]
    rows = excess_ref.shape[1]
    sources, surface = correction(1, got_ref, own_ref, d_ref, edge_ref, pair_ref)
    found = dot(pair_ref[...], sources)
    edge, second = far_rows(rows)
    contribution = scale * jnp.concatenate(
        [
            surface * excess_ref[1, pl.ds(edge, 1), :]
            + found[0:1] * excess_ref[0, pl.ds(edge, 1), :],
            found[depth : depth + 1] * excess_ref[0, pl.ds(second, 1), :],
        ],
        axis=0,
    )
    map_copy.wait()
    part_ref[...] = add_segments(part_in_ref[...], contribution, (edge, second), map_ref)
    out_ref[...] = two_ref[...] + found.reshape(two_ref.shape)


def finish_kernel(_, two_ref, got_ref, adj_hbm, out_hbm, out_ref, sems):
    copies = []
    for n, row in enumerate(far_rows(adj_hbm.shape[1])):
        copies.append(pltpu.make_async_copy(two_ref.at[n], adj_hbm.at[:, row, :], sems.at[n]))
        copies[-1].start()
    out_ref[...] = jnp.sum(got_ref[:, 0, :], axis=0)
    copies.append(pltpu.make_async_copy(out_ref, out_hbm, sems.at[2]))
    copies[-1].start()
    for copy in copies:
        copy.wait()


def in_hbm(x):
    return pltpu.with_memory_space_constraint(x, pltpu.HBM)


def per_device(
    conductance, depth_inverse, surface_residual, surface_excess, segment_map, frame_index
):
    _, depth, rows, cols = conductance.shape
    frames = surface_residual.shape[1]
    blocks = segment_map.shape[1]
    size = depth * rows
    spans = lax.axis_size("span")
    devices = spans * lax.axis_size("blade")
    lanes = SEGS // devices
    field = pltpu.VMEM((depth, rows, cols), F32)
    chunks = cols // 128
    packed_far = pltpu.VMEM(((2 * depth + 4) * chunks, 128), F32)
    packed_near = pltpu.VMEM(((2 * depth + 3) * chunks, 128), F32)
    own_far, own_near, k, picked, inverse = pl.pallas_call(
        functools.partial(load_kernel, rows),
        out_shape=(
            packed_far,
            packed_near,
            pltpu.VMEM((chunks * size, 128), F32),
            pltpu.VMEM((STEPS, rows, cols), F32),
            pltpu.VMEM((depth, depth), F32),
        ),
        in_specs=[HBM] * 4,
        out_specs=(VMEM,) * 5,
        scratch_shapes=[
            pltpu.SMEM((STEPS,), jnp.int32),
            pltpu.VMEM((frames, rows, cols), F32),
            pltpu.SemaphoreType.DMA((3 + chunks,)),
        ],
        compiler_params=GRANT,
        name="load",
    )(
        in_hbm(frame_index),
        in_hbm(conductance.reshape(size, cols)),
        in_hbm(surface_residual[0]),
        in_hbm(depth_inverse[0]),
    )
    across = [(i, i + 1) for i in range(1, spans - 1, 2)]
    within = [(i, i + 1) for i in range(0, spans - 1, 2)]
    near = lax.ppermute(own_near, "span", within + [(b, a) for a, b in within])
    far = lax.ppermute(own_far, "span", across + [(b, a) for a, b in across])
    scale = 1.0 / math.sqrt(128.0 * STEPS)
    line = pltpu.VMEM((rows, cols), F32)
    base, two, excess, ids, edge, contribution, pair, place = pl.pallas_call(
        functools.partial(base_kernel, scale),
        out_shape=(
            pltpu.VMEM((chunks * size, 128), F32),
            pltpu.VMEM((2, depth, cols), F32),
            pltpu.VMEM((STEPS, rows, cols), F32),
            pltpu.VMEM((blocks, rows), jnp.int32),
            pltpu.VMEM((2, depth, cols), F32),
            line,
            pltpu.VMEM((2 * depth, 6 * depth), BF16),
            pltpu.VMEM((size, 6 * depth), BF16),
        ),
        in_specs=[VMEM] * 3 + [HBM] * 2,
        out_specs=(VMEM,) * 8,
        scratch_shapes=[
            pltpu.VMEM((size, 3 * size), BF16),
            pltpu.VMEM((3, size, cols), BF16),
            pltpu.VMEM((chunks * size, 128), F32),
            field,
            field,
            pltpu.VMEM((depth, 128), F32),
            pltpu.SemaphoreType.DMA((2,)),
        ],
        compiler_params=GRANT,
        name="base",
    )(k, picked, inverse, in_hbm(surface_excess[0]), in_hbm(segment_map.T))
    fixed = (inverse, excess, edge, pair, ids)
    sums = pltpu.VMEM((devices, 1, lanes), F32)
    adjoint, partial = pl.pallas_call(
        functools.partial(near_kernel, scale),
        out_shape=(pltpu.HBM((depth, rows, cols), F32), sums),
        in_specs=[VMEM] * 10,
        out_specs=(HBM, VMEM),
        scratch_shapes=[
            field,
            pltpu.SMEM((blocks, rows), jnp.int32),
            pltpu.SemaphoreType.DMA((2,)),
        ],
        compiler_params=GRANT,
        name="near",
    )(*fixed, place, base, contribution, own_near, near)
    two, partial = pl.pallas_call(
        functools.partial(far_kernel, scale),
        out_shape=(pltpu.VMEM((2, depth, cols), F32), sums),
        in_specs=[VMEM] * 9,
        out_specs=(VMEM,) * 2,
        scratch_shapes=[pltpu.SMEM((blocks, rows), jnp.int32), pltpu.SemaphoreType.DMA],
        compiler_params=GRANT,
        name="far",
    )(own_far, far, *fixed, two, partial)
    pieces = lax.all_to_all(partial, ("blade", "span"), 0, 0, tiled=True)
    adjoint, owned = pl.pallas_call(
        finish_kernel,
        out_shape=(pltpu.HBM((depth, rows, cols), F32), pltpu.HBM((lanes,), F32)),
        in_specs=[HBM, VMEM, VMEM],
        out_specs=(HBM,) * 2,
        scratch_shapes=[pltpu.VMEM((lanes,), F32), pltpu.SemaphoreType.DMA((3,))],
        input_output_aliases={0: 0},
        compiler_params=GRANT,
        name="finish",
    )(in_hbm(adjoint), two, pltpu.with_memory_space_constraint(pieces, pltpu.VMEM))
    return (adjoint[None], owned)


def solution(mesh):
    placed = (
        P("blade", None, "span", None),
        P("blade", None, None),
        P("blade", None, "span", None),
        P("blade", None, "span", None),
        P("span", None),
        P(),
    )
    return jax.shard_map(
        per_device,
        mesh=mesh,
        in_specs=placed,
        out_specs=(P("blade", None, "span", None), P(("blade", "span"))),
        check_vma=False,
    )
```

```python
import functools
import math

import jax
import jax.numpy as jnp
from jax import lax
from jax.experimental import pallas as pl
from jax.experimental.pallas import tpu as pltpu
from jax.sharding import PartitionSpec as P

STEPS = 3
SEGS = 2048
GROUP = 2
PARTS = 4
F32 = jnp.float32
BF16 = jnp.bfloat16
VMEM = pl.BlockSpec(memory_space=pltpu.VMEM)
HBM = pl.BlockSpec(memory_space=pltpu.HBM)
GRANT = pltpu.CompilerParams(vmem_limit_bytes=16 * 2**20)


def split(x):
    high = x.astype(BF16)
    return high, (x - high.astype(F32)).astype(BF16)


def dot(a, b):
    return jnp.dot(a, b, preferred_element_type=F32)


def left_three(matrix):
    high, low = matrix
    return jnp.concatenate([high, low, high], axis=1)


def right_three(x):
    high, low = split(x)
    return jnp.concatenate([high, high, low], axis=0)


def iota(shape, dim):
    return lax.broadcasted_iota(jnp.int32, shape, dim)


def shift_next(x, axis):
    size = x.shape[axis]
    return jnp.where(iota(x.shape, axis) == size - 1, 0.0, pltpu.roll(x, size - 1, axis))


def shift_prev(x, axis, first):
    return jnp.where(iota(x.shape, axis) == 0, first, pltpu.roll(x, 1, axis))


def divergence(v, weight, half, axis):
    flux = weight * (shift_next(v, axis) - v)
    return flux - shift_prev(flux, axis, half * v)


def sides():
    span = lax.axis_index("span")
    count = lax.axis_size("span")
    even = lax.rem(span, 2) == 0
    has_next = span + 1 < count
    has_prev = span > 0
    return (
        (even, jnp.where(even, has_next, has_prev)),
        (jnp.logical_not(even), jnp.where(even, has_prev, has_next)),
    )


def chunked(ref, start, count, step):
    chunks = ref.shape[0] // step
    return jnp.concatenate(
        [ref[c * step + start : c * step + start + count, :] for c in range(chunks)], axis=1
    )


def packed_field(ref, depth, cols, n):
    chunks = cols // 128
    return chunked(ref.at[n * chunks * depth : (n + 1) * chunks * depth], 0, depth, depth)


def packed_line(ref, depth, cols, n):
    chunks = cols // 128
    base = (2 * depth + n) * chunks
    return chunked(ref.at[base : base + chunks], 0, 1, 1)


def row_of_each(ref, chunk, depth, rows, row):
    return ref[pl.ds(chunk * depth * rows + row, depth, stride=rows), :]


def far_rows(rows):
    after = sides()[1][0]
    return jnp.where(after, rows - 1, 0), jnp.where(after, rows - 2, 1)


def load_kernel(
    frame_hbm,
    k_hbm,
    res_hbm,
    d_hbm,
    far_ref,
    near_ref,
    k_ref,
    frames_ref,
    d_ref,
    frame_ref,
    res_ref,
    sems,
):
    depth, rows, cols = k_ref.shape
    chunks = cols // 128
    step = depth // PARTS
    pairs = [(frame_hbm, frame_ref), (res_hbm, res_ref)]
    for n in range(PARTS):
        part = pl.ds(n * step, step)
        pairs.append((k_hbm.at[part], k_ref.at[part]))
    pairs.append((d_hbm, d_ref))
    copies = [pltpu.make_async_copy(a, b, sems.at[n]) for n, (a, b) in enumerate(pairs)]
    for copy in copies:
        copy.start()
    sent = (near_ref, far_ref)
    picks = []
    for after, _ in sides():
        picks.append((jnp.where(after, rows - 1, 0), jnp.where(after, rows - 2, 1)))
    copies[0].wait()
    copies[1].wait()
    for n in range(STEPS):
        frames_ref[n] = res_ref[frame_ref[n]]
    base = 2 * chunks * depth
    for ref, (edge, second) in zip(sent, picks):
        for n, (frame, row) in enumerate(((2, edge), (1, edge), (2, second))):
            line = frames_ref[frame, pl.ds(row, 1), :]
            for c in range(chunks):
                spot = base + n * chunks + c
                ref[spot : spot + 1, :] = line[:, c * 128 : (c + 1) * 128]
        if ref.shape[0] > base + 3 * chunks:
            ref[base + 3 * chunks :, :] = jnp.zeros((ref.shape[0] - base - 3 * chunks, 128), F32)
    near_after = sides()[0][0]
    for part in range(PARTS):
        copies[2 + part].wait()
        here = slice(part * step, (part + 1) * step)
        for n, (first, last) in enumerate(((0, rows - 1), (1, rows - 2))):
            first, last = k_ref[here, first, :], k_ref[here, last, :]
            for ref, x in (
                (near_ref, jnp.where(near_after, last, first)),
                (far_ref, jnp.where(near_after, first, last)),
            ):
                for c in range(chunks):
                    spot = (n * chunks + c) * depth + part * step
                    ref[spot : spot + step, :] = x[:, c * 128 : (c + 1) * 128]
    for copy in copies[2 + PARTS :]:
        copy.wait()


def base_kernel(
    scale,
    k_ref,
    frames_ref,
    d_ref,
    excess_hbm,
    map_hbm,
    adj_ref,
    two_ref,
    excess_ref,
    map_ref,
    edge_ref,
    contribution_ref,
    pair_ref,
    place_ref,
    mat_ref,
    right_ref,
    first_ref,
    chord_ref,
    span_ref,
    factor_ref,
    sems,
):
    copies = [
        pltpu.make_async_copy(excess_hbm, excess_ref, sems.at[0]),
        pltpu.make_async_copy(map_hbm, map_ref, sems.at[1]),
    ]
    for copy in copies:
        copy.start()
    depth, rows, cols = chord_ref.shape
    size = depth * rows
    factor_ref[...] = jnp.broadcast_to(d_ref[:, 0:1], factor_ref.shape)

    parts = split(d_ref[...])
    tall = (iota((size, depth), 0) // rows == iota((size, depth), 1)).astype(BF16)
    wide = (iota((depth, size), 0) == iota((depth, size), 1) // rows).astype(BF16)
    two = 2 * depth
    tile = (iota((depth, two), 0) == iota((depth, two), 1) % depth).astype(BF16)
    same = iota((size, size), 0) % rows == iota((size, size), 1) % rows
    pair_same = iota((two, two), 0) // depth == iota((two, two), 1) // depth
    row_of = iota((size, two), 0) % rows
    first_half = iota((size, two), 1) < depth
    after = sides()[0][0]
    edge = jnp.where(after, rows - 1, 0)
    second = jnp.where(after, rows - 2, 1)
    placed = row_of == jnp.where(first_half, edge, second)
    mats, pairs, places = [], [], []
    for part in parts:
        column = dot(tall, part).astype(BF16)
        row = dot(part, tile)
        mats.append(jnp.where(same, dot(column, wide), 0.0).astype(BF16))
        places.append(jnp.where(placed, dot(column, tile), 0.0).astype(BF16))
        pairs.append(
            jnp.where(pair_same, jnp.concatenate([row] * 2, axis=0), 0.0).astype(BF16)
        )
    mat_ref[...] = left_three(mats)
    pair_ref[...] = left_three(pairs)
    place_ref[...] = left_three(places)

    f = frames_ref[2]
    f_chord = shift_next(f, 1) - f
    f_span = shift_next(f, 0) - f

    def put(i, both):
        high, low = split(both)
        span = pl.ds(i * rows, 2 * rows)
        right_ref[0, span, :] = high
        right_ref[1, span, :] = high
        right_ref[2, span, :] = low

    def lines_of(ref, i):
        return [chunked(ref, j * rows, rows, size) for j in range(i, i + GROUP)]

    for i in range(0, depth, GROUP):
        halves = [0.5 * k_ref[i + n] for n in range(GROUP)]
        factors = [jnp.broadcast_to(factor_ref[j : j + 1, :], (rows, 128)) for j in range(i, i + GROUP)]
        chords = [half + shift_next(half, 1) for half in halves]
        spans = [half + shift_next(half, 0) for half in halves]
        found = []
        for half, factor, w_chord, w_span in zip(halves, factors, chords, spans):
            edge = half * f
            flux_chord = w_chord * f_chord
            flux_span = w_span * f_span
            moved = f + flux_chord - shift_prev(flux_chord, 1, edge)
            moved = moved + flux_span - shift_prev(flux_span, 0, edge)
            found.append(jnp.concatenate([factor] * (cols // 128), axis=1) * moved)
        if i == 0:
            found[0] = found[0] + frames_ref[1]
        for n in range(GROUP):
            chord_ref[i + n] = chords[n]
            span_ref[i + n] = spans[n]
        for n in range(0, GROUP, 2):
            put(i + n, jnp.concatenate(found[n : n + 2], axis=0))
    right = right_ref[...].reshape(3 * size, cols)
    first = dot(mat_ref[...], right)
    for c in range(cols // 128):
        first_ref[c * size : (c + 1) * size, :] = first[:, c * 128 : (c + 1) * 128]

    for i in range(0, depth, GROUP):
        halves = [0.5 * k_ref[i + n] for n in range(GROUP)]
        values = lines_of(first_ref, i)
        chords = [chord_ref[i + n] for n in range(GROUP)]
        spans = [span_ref[i + n] for n in range(GROUP)]
        found = [
            v + divergence(v, w_chord, half, 1) + divergence(v, w_span, half, 0)
            for v, w_chord, w_span, half in zip(values, chords, spans, halves)
        ]
        if i == 0:
            found[0] = found[0] + frames_ref[0]
        for n in range(0, GROUP, 2):
            put(i + n, jnp.concatenate(found[n : n + 2], axis=0))
    right = right_ref[...].reshape(3 * size, cols)
    adj = dot(mat_ref[...], right)
    for c in range(cols // 128):
        adj_ref[c * size : (c + 1) * size, :] = adj[:, c * 128 : (c + 1) * 128]

    for n, (after, _) in enumerate(sides()):
        row = jnp.where(after, rows - 1, 0)
        for c in range(cols // 128):
            edge_ref[n, :, c * 128 : (c + 1) * 128] = row_of_each(first_ref, c, depth, rows, row)
    for n, row in enumerate(far_rows(rows)):
        for c in range(cols // 128):
            two_ref[n, :, c * 128 : (c + 1) * 128] = row_of_each(adj_ref, c, depth, rows, row)
    for copy in copies:
        copy.wait()
    contribution_ref[...] = scale * (
        d_ref[0:1, 0:1] * f * excess_ref[2]
        + chunked(first_ref, 0, rows, size) * excess_ref[1]
        + chunked(adj_ref, 0, rows, size) * excess_ref[0]
    )


def correction(n, got, own, d_ref, edge_ref, pair_ref):
    _, depth, cols = edge_ref.shape
    _, inside = sides()[n]
    factor = d_ref[:, 0:1]
    half = 0.5 * packed_field(got, depth, cols, 0)
    half_next = 0.5 * packed_field(got, depth, cols, 1)
    f = packed_line(got, depth, cols, 0)
    frame = packed_line(got, depth, cols, 1)
    f_next = packed_line(got, depth, cols, 2)
    f_own = packed_line(own, depth, cols, 0)
    half_own = 0.5 * packed_field(own, depth, cols, 0)
    inner = half_own + 0.5 * packed_field(own, depth, cols, 1)
    w_next = half_own + shift_next(half_own, 1)
    w_prev = half_own + shift_prev(half_own, 1, 0.0)
    face = half + half_own
    moved = (
        f
        + (half + shift_next(half, 1)) * (shift_next(f, 1) - f)
        + (half + shift_prev(half, 1, 0.0)) * (shift_prev(f, 1, 0.0) - f)
        + (half + half_next) * (f_next - f)
        + face * (f_own - f)
    )
    outer = factor * moved + jnp.where(iota((depth, 1), 0) == 0, frame, 0.0)
    sources = [factor * (face * f - half * f_own), jnp.where(inside, outer, 0.0)]
    found = dot(pair_ref[...], right_three(jnp.concatenate(sources, axis=0)))
    e = found[0:depth]
    outer = found[depth:]
    change = (
        (1.0 - (w_next + w_prev) - (half_own + inner)) * e
        + w_next * shift_next(e, 1)
        + w_prev * shift_prev(e, 1, 0.0)
        + face * outer
        - half * (e + edge_ref[n])
    )
    return right_three(jnp.concatenate([change, inner * e], axis=0)), e[0:1, :]


def add_segments(total, contribution, picked_rows, map_ref):
    owners, _, lanes = total.shape
    shape = (owners, 128)
    lane = iota(shape, 1)
    segment = jnp.where(lane < lanes, iota(shape, 0) * lanes + lane, -1)
    found = jnp.zeros(shape, F32)
    for block in range(contribution.shape[1] // 128):
        part = contribution[:, block * 128 : (block + 1) * 128]
        sums = jnp.sum(part, axis=1, keepdims=True)
        for n, row in enumerate(picked_rows):
            found += jnp.where(segment == map_ref[block, row], sums[n : n + 1, :], 0.0)
    return total + found[:, None, :lanes]


def near_kernel(
    scale,
    d_ref,
    excess_ref,
    edge_ref,
    pair_ref,
    map_vmem,
    place_ref,
    base_ref,
    contribution_ref,
    own_ref,
    got_ref,
    adj_hbm,
    part_ref,
    adj_ref,
    map_ref,
    sems,
):
    map_copy = pltpu.make_async_copy(map_vmem, map_ref, sems.at[0])
    map_copy.start()
    depth, rows, cols = adj_ref.shape
    size = depth * rows
    sources, surface = correction(0, got_ref, own_ref, d_ref, edge_ref, pair_ref)
    found = dot(place_ref[...], sources)
    adj_ref[...] = (chunked(base_ref, 0, size, size) + found).reshape(depth, rows, cols)
    adj_copy = pltpu.make_async_copy(adj_ref, adj_hbm, sems.at[1])
    adj_copy.start()
    row = jnp.where(sides()[0][0], rows - 1, 0)
    surface = jnp.where(iota((rows, cols), 0) == row, surface, 0.0)
    contribution = contribution_ref[...] + scale * (
        surface * excess_ref[1] + found[0:rows, :] * excess_ref[0]
    )
    map_copy.wait()
    part_ref[...] = add_segments(
        jnp.zeros(part_ref.shape, F32), contribution, range(rows), map_ref
    )
    adj_copy.wait()


def far_kernel(
    scale,
    own_ref,
    got_ref,
    d_ref,
    excess_ref,
    edge_ref,
    pair_ref,
    map_vmem,
    two_ref,
    part_in_ref,
    out_ref,
    part_ref,
    map_ref,
    map_sem,
):
    map_copy = pltpu.make_async_copy(map_vmem, map_ref, map_sem)
    map_copy.start()
    depth = two_ref.shape[1]
    rows = excess_ref.shape[1]
    sources, surface = correction(1, got_ref, own_ref, d_ref, edge_ref, pair_ref)
    found = dot(pair_ref[...], sources)
    edge, second = far_rows(rows)
    contribution = scale * jnp.concatenate(
        [
            surface * excess_ref[1, pl.ds(edge, 1), :]
            + found[0:1] * excess_ref[0, pl.ds(edge, 1), :],
            found[depth : depth + 1] * excess_ref[0, pl.ds(second, 1), :],
        ],
        axis=0,
    )
    map_copy.wait()
    part_ref[...] = add_segments(part_in_ref[...], contribution, (edge, second), map_ref)
    out_ref[...] = two_ref[...] + found.reshape(two_ref.shape)


def finish_kernel(_, two_ref, got_ref, adj_hbm, out_hbm, out_ref, sems):
    copies = []
    for n, row in enumerate(far_rows(adj_hbm.shape[1])):
        copies.append(pltpu.make_async_copy(two_ref.at[n], adj_hbm.at[:, row, :], sems.at[n]))
        copies[-1].start()
    out_ref[...] = jnp.sum(got_ref[:, 0, :], axis=0)
    copies.append(pltpu.make_async_copy(out_ref, out_hbm, sems.at[2]))
    copies[-1].start()
    for copy in copies:
        copy.wait()


def in_hbm(x):
    return pltpu.with_memory_space_constraint(x, pltpu.HBM)


def per_device(
    conductance, depth_inverse, surface_residual, surface_excess, segment_map, frame_index
):
    _, depth, rows, cols = conductance.shape
    frames = surface_residual.shape[1]
    blocks = segment_map.shape[1]
    size = depth * rows
    spans = lax.axis_size("span")
    devices = spans * lax.axis_size("blade")
    lanes = SEGS // devices
    field = pltpu.VMEM((depth, rows, cols), F32)
    chunks = cols // 128
    packed_far = pltpu.VMEM(((2 * depth + 4) * chunks, 128), F32)
    packed_near = pltpu.VMEM(((2 * depth + 3) * chunks, 128), F32)
    own_far, own_near, k, picked, inverse = pl.pallas_call(
        load_kernel,
        out_shape=(
            packed_far,
            packed_near,
            field,
            pltpu.VMEM((STEPS, rows, cols), F32),
            pltpu.VMEM((depth, depth), F32),
        ),
        in_specs=[HBM] * 4,
        out_specs=(VMEM,) * 5,
        scratch_shapes=[
            pltpu.SMEM((STEPS,), jnp.int32),
            pltpu.VMEM((frames, rows, cols), F32),
            pltpu.SemaphoreType.DMA((3 + PARTS,)),
        ],
        compiler_params=GRANT,
        name="load",
    )(
        in_hbm(frame_index),
        in_hbm(conductance[0]),
        in_hbm(surface_residual[0]),
        in_hbm(depth_inverse[0]),
    )
    across = [(i, i + 1) for i in range(1, spans - 1, 2)]
    within = [(i, i + 1) for i in range(0, spans - 1, 2)]
    near = lax.ppermute(own_near, "span", within + [(b, a) for a, b in within])
    far = lax.ppermute(own_far, "span", across + [(b, a) for a, b in across])
    scale = 1.0 / math.sqrt(128.0 * STEPS)
    line = pltpu.VMEM((rows, cols), F32)
    base, two, excess, ids, edge, contribution, pair, place = pl.pallas_call(
        functools.partial(base_kernel, scale),
        out_shape=(
            pltpu.VMEM((chunks * size, 128), F32),
            pltpu.VMEM((2, depth, cols), F32),
            pltpu.VMEM((STEPS, rows, cols), F32),
            pltpu.VMEM((blocks, rows), jnp.int32),
            pltpu.VMEM((2, depth, cols), F32),
            line,
            pltpu.VMEM((2 * depth, 6 * depth), BF16),
            pltpu.VMEM((size, 6 * depth), BF16),
        ),
        in_specs=[VMEM] * 3 + [HBM] * 2,
        out_specs=(VMEM,) * 8,
        scratch_shapes=[
            pltpu.VMEM((size, 3 * size), BF16),
            pltpu.VMEM((3, size, cols), BF16),
            pltpu.VMEM((chunks * size, 128), F32),
            field,
            field,
            pltpu.VMEM((depth, 128), F32),
            pltpu.SemaphoreType.DMA((2,)),
        ],
        compiler_params=GRANT,
        name="base",
    )(k, picked, inverse, in_hbm(surface_excess[0]), in_hbm(segment_map.T))
    fixed = (inverse, excess, edge, pair, ids)
    sums = pltpu.VMEM((devices, 1, lanes), F32)
    adjoint, partial = pl.pallas_call(
        functools.partial(near_kernel, scale),
        out_shape=(pltpu.HBM((depth, rows, cols), F32), sums),
        in_specs=[VMEM] * 10,
        out_specs=(HBM, VMEM),
        scratch_shapes=[
            field,
            pltpu.SMEM((blocks, rows), jnp.int32),
            pltpu.SemaphoreType.DMA((2,)),
        ],
        compiler_params=GRANT,
        name="near",
    )(*fixed, place, base, contribution, own_near, near)
    two, partial = pl.pallas_call(
        functools.partial(far_kernel, scale),
        out_shape=(pltpu.VMEM((2, depth, cols), F32), sums),
        in_specs=[VMEM] * 9,
        out_specs=(VMEM,) * 2,
        scratch_shapes=[pltpu.SMEM((blocks, rows), jnp.int32), pltpu.SemaphoreType.DMA],
        compiler_params=GRANT,
        name="far",
    )(own_far, far, *fixed, two, partial)
    pieces = lax.all_to_all(partial, ("blade", "span"), 0, 0, tiled=True)
    adjoint, owned = pl.pallas_call(
        finish_kernel,
        out_shape=(pltpu.HBM((depth, rows, cols), F32), pltpu.HBM((lanes,), F32)),
        in_specs=[HBM, VMEM, VMEM],
        out_specs=(HBM,) * 2,
        scratch_shapes=[pltpu.VMEM((lanes,), F32), pltpu.SemaphoreType.DMA((3,))],
        input_output_aliases={0: 0},
        compiler_params=GRANT,
        name="finish",
    )(in_hbm(adjoint), two, pltpu.with_memory_space_constraint(pieces, pltpu.VMEM))
    return (adjoint[None], owned)


def solution(mesh):
    placed = (
        P("blade", None, "span", None),
        P("blade", None, None),
        P("blade", None, "span", None),
        P("blade", None, "span", None),
        P("span", None),
        P(),
    )
    return jax.shard_map(
        per_device,
        mesh=mesh,
        in_specs=placed,
        out_specs=(P("blade", None, "span", None), P(("blade", "span"))),
        check_vma=False,
    )
```

```python
import functools
import math

import jax
import jax.numpy as jnp
from jax import lax
from jax.experimental import pallas as pl
from jax.experimental.pallas import tpu as pltpu
from jax.sharding import PartitionSpec as P

STEPS = 3
SEGS = 2048
GROUP = 2
PARTS = 4
F32 = jnp.float32
BF16 = jnp.bfloat16
VMEM = pl.BlockSpec(memory_space=pltpu.VMEM)
HBM = pl.BlockSpec(memory_space=pltpu.HBM)
GRANT = pltpu.CompilerParams(vmem_limit_bytes=16 * 2**20)


def split(x):
    high = x.astype(BF16)
    return high, (x - high.astype(F32)).astype(BF16)


def dot(a, b):
    return jnp.dot(a, b, preferred_element_type=F32)


def left_three(matrix):
    high, low = matrix
    return jnp.concatenate([high, low, high], axis=1)


def right_three(x):
    high, low = split(x)
    return jnp.concatenate([high, high, low], axis=0)


def iota(shape, dim):
    return lax.broadcasted_iota(jnp.int32, shape, dim)


def shift_next(x, axis):
    size = x.shape[axis]
    return jnp.where(iota(x.shape, axis) == size - 1, 0.0, pltpu.roll(x, size - 1, axis))


def shift_prev(x, axis, first):
    return jnp.where(iota(x.shape, axis) == 0, first, pltpu.roll(x, 1, axis))


def divergence(v, weight, half, axis):
    flux = weight * (shift_next(v, axis) - v)
    return flux - shift_prev(flux, axis, half * v)


def sides():
    span = lax.axis_index("span")
    count = lax.axis_size("span")
    even = lax.rem(span, 2) == 0
    has_next = span + 1 < count
    has_prev = span > 0
    return (
        (even, jnp.where(even, has_next, has_prev)),
        (jnp.logical_not(even), jnp.where(even, has_prev, has_next)),
    )


def chunked(ref, start, count, step):
    chunks = ref.shape[0] // step
    return jnp.concatenate(
        [ref[c * step + start : c * step + start + count, :] for c in range(chunks)], axis=1
    )


def packed_field(ref, depth, cols, n):
    chunks = cols // 128
    return chunked(ref.at[n * chunks * depth : (n + 1) * chunks * depth], 0, depth, depth)


def packed_line(ref, depth, cols, n):
    chunks = cols // 128
    base = (2 * depth + n) * chunks
    return chunked(ref.at[base : base + chunks], 0, 1, 1)


def row_of_each(ref, chunk, depth, rows, row):
    return ref[pl.ds(chunk * depth * rows + row, depth, stride=rows), :]


def far_rows(rows):
    after = sides()[1][0]
    return jnp.where(after, rows - 1, 0), jnp.where(after, rows - 2, 1)


def load_kernel(
    frame_hbm,
    k_hbm,
    res_hbm,
    d_hbm,
    far_ref,
    near_ref,
    k_ref,
    frames_ref,
    d_ref,
    frame_ref,
    res_ref,
    sems,
):
    depth, rows, cols = k_ref.shape
    chunks = cols // 128
    step = depth // PARTS
    pairs = [(frame_hbm, frame_ref), (res_hbm, res_ref)]
    for n in range(PARTS):
        part = pl.ds(n * step, step)
        pairs.append((k_hbm.at[part], k_ref.at[part]))
    pairs.append((d_hbm, d_ref))
    copies = [pltpu.make_async_copy(a, b, sems.at[n]) for n, (a, b) in enumerate(pairs)]
    for copy in copies:
        copy.start()
    sent = (near_ref, far_ref)
    picks = []
    for after, _ in sides():
        picks.append((jnp.where(after, rows - 1, 0), jnp.where(after, rows - 2, 1)))
    copies[0].wait()
    copies[1].wait()
    for n in range(STEPS):
        wanted = jnp.broadcast_to(frame_ref[0:1, n : n + 1], (rows, cols))
        total = jnp.zeros((rows, cols), F32)
        for frame in range(res_ref.shape[0]):
            total = jnp.where(wanted == frame, res_ref[frame], total)
        frames_ref[n] = total
    base = 2 * chunks * depth
    for ref, (edge, second) in zip(sent, picks):
        for n, (frame, row) in enumerate(((2, edge), (1, edge), (2, second))):
            line = frames_ref[frame, pl.ds(row, 1), :]
            for c in range(chunks):
                spot = base + n * chunks + c
                ref[spot : spot + 1, :] = line[:, c * 128 : (c + 1) * 128]
        if ref.shape[0] > base + 3 * chunks:
            ref[base + 3 * chunks :, :] = jnp.zeros((ref.shape[0] - base - 3 * chunks, 128), F32)
    near_after = sides()[0][0]
    for part in range(PARTS):
        copies[2 + part].wait()
        here = slice(part * step, (part + 1) * step)
        for n, (first, last) in enumerate(((0, rows - 1), (1, rows - 2))):
            first, last = k_ref[here, first, :], k_ref[here, last, :]
            for ref, x in (
                (near_ref, jnp.where(near_after, last, first)),
                (far_ref, jnp.where(near_after, first, last)),
            ):
                for c in range(chunks):
                    spot = (n * chunks + c) * depth + part * step
                    ref[spot : spot + step, :] = x[:, c * 128 : (c + 1) * 128]
    for copy in copies[2 + PARTS :]:
        copy.wait()


def base_kernel(
    scale,
    k_ref,
    frames_ref,
    d_ref,
    excess_hbm,
    map_hbm,
    adj_ref,
    two_ref,
    excess_ref,
    map_ref,
    edge_ref,
    contribution_ref,
    pair_ref,
    place_ref,
    mat_ref,
    right_ref,
    first_ref,
    chord_ref,
    span_ref,
    factor_ref,
    sems,
):
    copies = [
        pltpu.make_async_copy(excess_hbm, excess_ref, sems.at[0]),
        pltpu.make_async_copy(map_hbm, map_ref, sems.at[1]),
    ]
    for copy in copies:
        copy.start()
    depth, rows, cols = chord_ref.shape
    size = depth * rows
    factor_ref[...] = jnp.broadcast_to(d_ref[:, 0:1], factor_ref.shape)

    parts = split(d_ref[...])
    tall = (iota((size, depth), 0) // rows == iota((size, depth), 1)).astype(BF16)
    wide = (iota((depth, size), 0) == iota((depth, size), 1) // rows).astype(BF16)
    two = 2 * depth
    tile = (iota((depth, two), 0) == iota((depth, two), 1) % depth).astype(BF16)
    same = iota((size, size), 0) % rows == iota((size, size), 1) % rows
    pair_same = iota((two, two), 0) // depth == iota((two, two), 1) // depth
    row_of = iota((size, two), 0) % rows
    first_half = iota((size, two), 1) < depth
    after = sides()[0][0]
    edge = jnp.where(after, rows - 1, 0)
    second = jnp.where(after, rows - 2, 1)
    placed = row_of == jnp.where(first_half, edge, second)
    mats, pairs, places = [], [], []
    for part in parts:
        column = dot(tall, part).astype(BF16)
        row = dot(part, tile)
        mats.append(jnp.where(same, dot(column, wide), 0.0).astype(BF16))
        places.append(jnp.where(placed, dot(column, tile), 0.0).astype(BF16))
        pairs.append(
            jnp.where(pair_same, jnp.concatenate([row] * 2, axis=0), 0.0).astype(BF16)
        )
    mat_ref[...] = left_three(mats)
    pair_ref[...] = left_three(pairs)
    place_ref[...] = left_three(places)

    f = frames_ref[2]
    f_chord = shift_next(f, 1) - f
    f_span = shift_next(f, 0) - f

    def put(i, both):
        high, low = split(both)
        span = pl.ds(i * rows, 2 * rows)
        right_ref[0, span, :] = high
        right_ref[1, span, :] = high
        right_ref[2, span, :] = low

    def lines_of(ref, i):
        return [chunked(ref, j * rows, rows, size) for j in range(i, i + GROUP)]

    for i in range(0, depth, GROUP):
        halves = [0.5 * k_ref[i + n] for n in range(GROUP)]
        factors = [jnp.broadcast_to(factor_ref[j : j + 1, :], (rows, 128)) for j in range(i, i + GROUP)]
        chords = [half + shift_next(half, 1) for half in halves]
        spans = [half + shift_next(half, 0) for half in halves]
        found = []
        for half, factor, w_chord, w_span in zip(halves, factors, chords, spans):
            edge = half * f
            flux_chord = w_chord * f_chord
            flux_span = w_span * f_span
            moved = f + flux_chord - shift_prev(flux_chord, 1, edge)
            moved = moved + flux_span - shift_prev(flux_span, 0, edge)
            found.append(jnp.concatenate([factor] * (cols // 128), axis=1) * moved)
        if i == 0:
            found[0] = found[0] + frames_ref[1]
        for n in range(GROUP):
            chord_ref[i + n] = chords[n]
            span_ref[i + n] = spans[n]
        for n in range(0, GROUP, 2):
            put(i + n, jnp.concatenate(found[n : n + 2], axis=0))
    right = right_ref[...].reshape(3 * size, cols)
    first = dot(mat_ref[...], right)
    for c in range(cols // 128):
        first_ref[c * size : (c + 1) * size, :] = first[:, c * 128 : (c + 1) * 128]

    for i in range(0, depth, GROUP):
        halves = [0.5 * k_ref[i + n] for n in range(GROUP)]
        values = lines_of(first_ref, i)
        chords = [chord_ref[i + n] for n in range(GROUP)]
        spans = [span_ref[i + n] for n in range(GROUP)]
        found = [
            v + divergence(v, w_chord, half, 1) + divergence(v, w_span, half, 0)
            for v, w_chord, w_span, half in zip(values, chords, spans, halves)
        ]
        if i == 0:
            found[0] = found[0] + frames_ref[0]
        for n in range(0, GROUP, 2):
            put(i + n, jnp.concatenate(found[n : n + 2], axis=0))
    right = right_ref[...].reshape(3 * size, cols)
    adj = dot(mat_ref[...], right)
    for c in range(cols // 128):
        adj_ref[c * size : (c + 1) * size, :] = adj[:, c * 128 : (c + 1) * 128]

    for n, (after, _) in enumerate(sides()):
        row = jnp.where(after, rows - 1, 0)
        for c in range(cols // 128):
            edge_ref[n, :, c * 128 : (c + 1) * 128] = row_of_each(first_ref, c, depth, rows, row)
    for n, row in enumerate(far_rows(rows)):
        for c in range(cols // 128):
            two_ref[n, :, c * 128 : (c + 1) * 128] = row_of_each(adj_ref, c, depth, rows, row)
    for copy in copies:
        copy.wait()
    contribution_ref[...] = scale * (
        d_ref[0:1, 0:1] * f * excess_ref[2]
        + chunked(first_ref, 0, rows, size) * excess_ref[1]
        + chunked(adj_ref, 0, rows, size) * excess_ref[0]
    )


def correction(n, got, own, d_ref, edge_ref, pair_ref):
    _, depth, cols = edge_ref.shape
    _, inside = sides()[n]
    factor = d_ref[:, 0:1]
    half = 0.5 * packed_field(got, depth, cols, 0)
    half_next = 0.5 * packed_field(got, depth, cols, 1)
    f = packed_line(got, depth, cols, 0)
    frame = packed_line(got, depth, cols, 1)
    f_next = packed_line(got, depth, cols, 2)
    f_own = packed_line(own, depth, cols, 0)
    half_own = 0.5 * packed_field(own, depth, cols, 0)
    inner = half_own + 0.5 * packed_field(own, depth, cols, 1)
    w_next = half_own + shift_next(half_own, 1)
    w_prev = half_own + shift_prev(half_own, 1, 0.0)
    face = half + half_own
    moved = (
        f
        + (half + shift_next(half, 1)) * (shift_next(f, 1) - f)
        + (half + shift_prev(half, 1, 0.0)) * (shift_prev(f, 1, 0.0) - f)
        + (half + half_next) * (f_next - f)
        + face * (f_own - f)
    )
    outer = factor * moved + jnp.where(iota((depth, 1), 0) == 0, frame, 0.0)
    sources = [factor * (face * f - half * f_own), jnp.where(inside, outer, 0.0)]
    found = dot(pair_ref[...], right_three(jnp.concatenate(sources, axis=0)))
    e = found[0:depth]
    outer = found[depth:]
    change = (
        (1.0 - (w_next + w_prev) - (half_own + inner)) * e
        + w_next * shift_next(e, 1)
        + w_prev * shift_prev(e, 1, 0.0)
        + face * outer
        - half * (e + edge_ref[n])
    )
    return right_three(jnp.concatenate([change, inner * e], axis=0)), e[0:1, :]


def add_segments(total, contribution, picked_rows, map_ref):
    owners, _, lanes = total.shape
    shape = (owners, 128)
    lane = iota(shape, 1)
    segment = jnp.where(lane < lanes, iota(shape, 0) * lanes + lane, -1)
    found = jnp.zeros(shape, F32)
    for block in range(contribution.shape[1] // 128):
        part = contribution[:, block * 128 : (block + 1) * 128]
        sums = jnp.sum(part, axis=1, keepdims=True)
        for n, row in enumerate(picked_rows):
            found += jnp.where(segment == map_ref[block, row], sums[n : n + 1, :], 0.0)
    return total + found[:, None, :lanes]


def near_kernel(
    scale,
    d_ref,
    excess_ref,
    edge_ref,
    pair_ref,
    map_vmem,
    place_ref,
    base_ref,
    contribution_ref,
    own_ref,
    got_ref,
    adj_hbm,
    part_ref,
    adj_ref,
    map_ref,
    sems,
):
    map_copy = pltpu.make_async_copy(map_vmem, map_ref, sems.at[0])
    map_copy.start()
    depth, rows, cols = adj_ref.shape
    size = depth * rows
    sources, surface = correction(0, got_ref, own_ref, d_ref, edge_ref, pair_ref)
    found = dot(place_ref[...], sources)
    adj_ref[...] = (chunked(base_ref, 0, size, size) + found).reshape(depth, rows, cols)
    adj_copy = pltpu.make_async_copy(adj_ref, adj_hbm, sems.at[1])
    adj_copy.start()
    row = jnp.where(sides()[0][0], rows - 1, 0)
    surface = jnp.where(iota((rows, cols), 0) == row, surface, 0.0)
    contribution = contribution_ref[...] + scale * (
        surface * excess_ref[1] + found[0:rows, :] * excess_ref[0]
    )
    map_copy.wait()
    part_ref[...] = add_segments(
        jnp.zeros(part_ref.shape, F32), contribution, range(rows), map_ref
    )
    adj_copy.wait()


def far_kernel(
    scale,
    own_ref,
    got_ref,
    d_ref,
    excess_ref,
    edge_ref,
    pair_ref,
    map_vmem,
    two_ref,
    part_in_ref,
    out_ref,
    part_ref,
    map_ref,
    map_sem,
):
    map_copy = pltpu.make_async_copy(map_vmem, map_ref, map_sem)
    map_copy.start()
    depth = two_ref.shape[1]
    rows = excess_ref.shape[1]
    sources, surface = correction(1, got_ref, own_ref, d_ref, edge_ref, pair_ref)
    found = dot(pair_ref[...], sources)
    edge, second = far_rows(rows)
    contribution = scale * jnp.concatenate(
        [
            surface * excess_ref[1, pl.ds(edge, 1), :]
            + found[0:1] * excess_ref[0, pl.ds(edge, 1), :],
            found[depth : depth + 1] * excess_ref[0, pl.ds(second, 1), :],
        ],
        axis=0,
    )
    map_copy.wait()
    part_ref[...] = add_segments(part_in_ref[...], contribution, (edge, second), map_ref)
    out_ref[...] = two_ref[...] + found.reshape(two_ref.shape)


def finish_kernel(_, two_ref, got_ref, adj_hbm, out_hbm, out_ref, sems):
    copies = []
    for n, row in enumerate(far_rows(adj_hbm.shape[1])):
        copies.append(pltpu.make_async_copy(two_ref.at[n], adj_hbm.at[:, row, :], sems.at[n]))
        copies[-1].start()
    out_ref[...] = jnp.sum(got_ref[:, 0, :], axis=0)
    copies.append(pltpu.make_async_copy(out_ref, out_hbm, sems.at[2]))
    copies[-1].start()
    for copy in copies:
        copy.wait()


def in_hbm(x):
    return pltpu.with_memory_space_constraint(x, pltpu.HBM)


def per_device(
    conductance, depth_inverse, surface_residual, surface_excess, segment_map, frame_index
):
    _, depth, rows, cols = conductance.shape
    frames = surface_residual.shape[1]
    blocks = segment_map.shape[1]
    size = depth * rows
    spans = lax.axis_size("span")
    devices = spans * lax.axis_size("blade")
    lanes = SEGS // devices
    field = pltpu.VMEM((depth, rows, cols), F32)
    chunks = cols // 128
    packed_far = pltpu.VMEM(((2 * depth + 4) * chunks, 128), F32)
    packed_near = pltpu.VMEM(((2 * depth + 3) * chunks, 128), F32)
    own_far, own_near, k, picked, inverse = pl.pallas_call(
        load_kernel,
        out_shape=(
            packed_far,
            packed_near,
            field,
            pltpu.VMEM((STEPS, rows, cols), F32),
            pltpu.VMEM((depth, depth), F32),
        ),
        in_specs=[HBM] * 4,
        out_specs=(VMEM,) * 5,
        scratch_shapes=[
            pltpu.VMEM((1, STEPS), jnp.int32),
            pltpu.VMEM((frames, rows, cols), F32),
            pltpu.SemaphoreType.DMA((3 + PARTS,)),
        ],
        compiler_params=GRANT,
        name="load",
    )(
        in_hbm(frame_index.reshape(1, STEPS)),
        in_hbm(conductance[0]),
        in_hbm(surface_residual[0]),
        in_hbm(depth_inverse[0]),
    )
    across = [(i, i + 1) for i in range(1, spans - 1, 2)]
    within = [(i, i + 1) for i in range(0, spans - 1, 2)]
    near = lax.ppermute(own_near, "span", within + [(b, a) for a, b in within])
    far = lax.ppermute(own_far, "span", across + [(b, a) for a, b in across])
    scale = 1.0 / math.sqrt(128.0 * STEPS)
    line = pltpu.VMEM((rows, cols), F32)
    base, two, excess, ids, edge, contribution, pair, place = pl.pallas_call(
        functools.partial(base_kernel, scale),
        out_shape=(
            pltpu.VMEM((chunks * size, 128), F32),
            pltpu.VMEM((2, depth, cols), F32),
            pltpu.VMEM((STEPS, rows, cols), F32),
            pltpu.VMEM((blocks, rows), jnp.int32),
            pltpu.VMEM((2, depth, cols), F32),
            line,
            pltpu.VMEM((2 * depth, 6 * depth), BF16),
            pltpu.VMEM((size, 6 * depth), BF16),
        ),
        in_specs=[VMEM] * 3 + [HBM] * 2,
        out_specs=(VMEM,) * 8,
        scratch_shapes=[
            pltpu.VMEM((size, 3 * size), BF16),
            pltpu.VMEM((3, size, cols), BF16),
            pltpu.VMEM((chunks * size, 128), F32),
            field,
            field,
            pltpu.VMEM((depth, 128), F32),
            pltpu.SemaphoreType.DMA((2,)),
        ],
        compiler_params=GRANT,
        name="base",
    )(k, picked, inverse, in_hbm(surface_excess[0]), in_hbm(segment_map.T))
    fixed = (inverse, excess, edge, pair, ids)
    sums = pltpu.VMEM((devices, 1, lanes), F32)
    adjoint, partial = pl.pallas_call(
        functools.partial(near_kernel, scale),
        out_shape=(pltpu.HBM((depth, rows, cols), F32), sums),
        in_specs=[VMEM] * 10,
        out_specs=(HBM, VMEM),
        scratch_shapes=[
            field,
            pltpu.SMEM((blocks, rows), jnp.int32),
            pltpu.SemaphoreType.DMA((2,)),
        ],
        compiler_params=GRANT,
        name="near",
    )(*fixed, place, base, contribution, own_near, near)
    two, partial = pl.pallas_call(
        functools.partial(far_kernel, scale),
        out_shape=(pltpu.VMEM((2, depth, cols), F32), sums),
        in_specs=[VMEM] * 9,
        out_specs=(VMEM,) * 2,
        scratch_shapes=[pltpu.SMEM((blocks, rows), jnp.int32), pltpu.SemaphoreType.DMA],
        compiler_params=GRANT,
        name="far",
    )(own_far, far, *fixed, two, partial)
    pieces = lax.all_to_all(partial, ("blade", "span"), 0, 0, tiled=True)
    adjoint, owned = pl.pallas_call(
        finish_kernel,
        out_shape=(pltpu.HBM((depth, rows, cols), F32), pltpu.HBM((lanes,), F32)),
        in_specs=[HBM, VMEM, VMEM],
        out_specs=(HBM,) * 2,
        scratch_shapes=[pltpu.VMEM((lanes,), F32), pltpu.SemaphoreType.DMA((3,))],
        input_output_aliases={0: 0},
        compiler_params=GRANT,
        name="finish",
    )(in_hbm(adjoint), two, pltpu.with_memory_space_constraint(pieces, pltpu.VMEM))
    return (adjoint[None], owned)


def solution(mesh):
    placed = (
        P("blade", None, "span", None),
        P("blade", None, None),
        P("blade", None, "span", None),
        P("blade", None, "span", None),
        P("span", None),
        P(),
    )
    return jax.shard_map(
        per_device,
        mesh=mesh,
        in_specs=placed,
        out_specs=(P("blade", None, "span", None), P(("blade", "span"))),
        check_vma=False,
    )
```

```python
import functools
import math

import jax
import jax.numpy as jnp
from jax import lax
from jax.experimental import pallas as pl
from jax.experimental.pallas import tpu as pltpu
from jax.sharding import PartitionSpec as P

STEPS = 3
SEGS = 2048
GROUP = 2
F32 = jnp.float32
BF16 = jnp.bfloat16
VMEM = pl.BlockSpec(memory_space=pltpu.VMEM)
HBM = pl.BlockSpec(memory_space=pltpu.HBM)
GRANT = pltpu.CompilerParams(vmem_limit_bytes=16 * 2**20)


def split(x):
    high = x.astype(BF16)
    return high, (x - high.astype(F32)).astype(BF16)


def dot(a, b):
    return jnp.dot(a, b, preferred_element_type=F32)


def left_three(matrix):
    high, low = matrix
    return jnp.concatenate([high, low, high], axis=1)


def right_three(x):
    high, low = split(x)
    return jnp.concatenate([high, high, low], axis=0)


def iota(shape, dim):
    return lax.broadcasted_iota(jnp.int32, shape, dim)


def shift_next(x, axis):
    size = x.shape[axis]
    return jnp.where(iota(x.shape, axis) == size - 1, 0.0, pltpu.roll(x, size - 1, axis))


def shift_prev(x, axis, first):
    return jnp.where(iota(x.shape, axis) == 0, first, pltpu.roll(x, 1, axis))


def divergence(v, weight, half, axis):
    flux = weight * (shift_next(v, axis) - v)
    return flux - shift_prev(flux, axis, half * v)


def sides():
    span = lax.axis_index("span")
    count = lax.axis_size("span")
    even = lax.rem(span, 2) == 0
    has_next = span + 1 < count
    has_prev = span > 0
    return (
        (even, jnp.where(even, has_next, has_prev)),
        (jnp.logical_not(even), jnp.where(even, has_prev, has_next)),
    )


def chunked(ref, start, count, step):
    chunks = ref.shape[0] // step
    return jnp.concatenate(
        [ref[c * step + start : c * step + start + count, :] for c in range(chunks)], axis=1
    )


def packed_field(ref, depth, cols, n):
    chunks = cols // 128
    return chunked(ref.at[n * chunks * depth : (n + 1) * chunks * depth], 0, depth, depth)


def packed_line(ref, depth, cols, n):
    chunks = cols // 128
    base = (2 * depth + n) * chunks
    return chunked(ref.at[base : base + chunks], 0, 1, 1)


def row_of_each(ref, chunk, depth, rows, row):
    return ref[pl.ds(chunk * depth * rows + row, depth, stride=rows), :]


def far_rows(rows):
    after = sides()[1][0]
    return jnp.where(after, rows - 1, 0), jnp.where(after, rows - 2, 1)


def load_kernel(
    frame_hbm,
    k_hbm,
    res_hbm,
    d_hbm,
    far_ref,
    near_ref,
    frames_ref,
    d_ref,
    frame_ref,
    res_ref,
    edge_ref,
    sems,
):
    depth, rows, cols = k_hbm.shape
    chunks = cols // 128
    sent = (near_ref, far_ref)
    afters = [after for after, _ in sides()]
    pairs = []
    for n, after in enumerate(afters):
        first = jnp.where(after, rows - 2, 0)
        pairs.append((k_hbm.at[:, pl.ds(first, 2), :], edge_ref.at[n, :, 0:2, :]))
    pairs += [(frame_hbm, frame_ref), (res_hbm, res_ref), (d_hbm, d_ref)]
    copies = [pltpu.make_async_copy(a, b, sems.at[n]) for n, (a, b) in enumerate(pairs)]
    for copy in copies:
        copy.start()
    copies[2].wait()
    copies[3].wait()
    for n in range(STEPS):
        frames_ref[n] = res_ref[frame_ref[n]]
    base = 2 * chunks * depth
    for ref, after in zip(sent, afters):
        edge, second = jnp.where(after, rows - 1, 0), jnp.where(after, rows - 2, 1)
        for n, (frame, row) in enumerate(((2, edge), (1, edge), (2, second))):
            line = frames_ref[frame, pl.ds(row, 1), :]
            for c in range(chunks):
                spot = base + n * chunks + c
                ref[spot : spot + 1, :] = line[:, c * 128 : (c + 1) * 128]
        if ref.shape[0] > base + 3 * chunks:
            ref[base + 3 * chunks :, :] = jnp.zeros((ref.shape[0] - base - 3 * chunks, 128), F32)
    for n, after in enumerate(afters):
        copies[n].wait()
        low, high = edge_ref[n, :, 0, :], edge_ref[n, :, 1, :]
        for which, x in enumerate((jnp.where(after, high, low), jnp.where(after, low, high))):
            for c in range(chunks):
                spot = (which * chunks + c) * depth
                sent[n][spot : spot + depth, :] = x[:, c * 128 : (c + 1) * 128]
    copies[4].wait()


def base_kernel(
    scale,
    k_ref,
    frames_ref,
    d_ref,
    excess_hbm,
    map_hbm,
    adj_ref,
    two_ref,
    excess_ref,
    map_ref,
    edge_ref,
    contribution_ref,
    pair_ref,
    place_ref,
    mat_ref,
    right_ref,
    first_ref,
    chord_ref,
    span_ref,
    factor_ref,
    sems,
):
    copies = [
        pltpu.make_async_copy(excess_hbm, excess_ref, sems.at[0]),
        pltpu.make_async_copy(map_hbm, map_ref, sems.at[1]),
    ]
    for copy in copies:
        copy.start()
    depth, rows, cols = chord_ref.shape
    size = depth * rows
    factor_ref[...] = jnp.broadcast_to(d_ref[:, 0:1], factor_ref.shape)

    parts = split(d_ref[...])
    tall = (iota((size, depth), 0) // rows == iota((size, depth), 1)).astype(BF16)
    wide = (iota((depth, size), 0) == iota((depth, size), 1) // rows).astype(BF16)
    two = 2 * depth
    tile = (iota((depth, two), 0) == iota((depth, two), 1) % depth).astype(BF16)
    same = iota((size, size), 0) % rows == iota((size, size), 1) % rows
    pair_same = iota((two, two), 0) // depth == iota((two, two), 1) // depth
    row_of = iota((size, two), 0) % rows
    first_half = iota((size, two), 1) < depth
    after = sides()[0][0]
    edge = jnp.where(after, rows - 1, 0)
    second = jnp.where(after, rows - 2, 1)
    placed = row_of == jnp.where(first_half, edge, second)
    mats, pairs, places = [], [], []
    for part in parts:
        column = dot(tall, part).astype(BF16)
        row = dot(part, tile)
        mats.append(jnp.where(same, dot(column, wide), 0.0).astype(BF16))
        places.append(jnp.where(placed, dot(column, tile), 0.0).astype(BF16))
        pairs.append(
            jnp.where(pair_same, jnp.concatenate([row] * 2, axis=0), 0.0).astype(BF16)
        )
    mat_ref[...] = left_three(mats)
    pair_ref[...] = left_three(pairs)
    place_ref[...] = left_three(places)

    f = frames_ref[2]
    f_chord = shift_next(f, 1) - f
    f_span = shift_next(f, 0) - f

    def put(i, both):
        high, low = split(both)
        span = pl.ds(i * rows, 2 * rows)
        right_ref[0, span, :] = high
        right_ref[1, span, :] = high
        right_ref[2, span, :] = low

    def lines_of(ref, i):
        return [chunked(ref, j * rows, rows, size) for j in range(i, i + GROUP)]

    for i in range(0, depth, GROUP):
        halves = [0.5 * k_ref[i + n] for n in range(GROUP)]
        factors = [jnp.broadcast_to(factor_ref[j : j + 1, :], (rows, 128)) for j in range(i, i + GROUP)]
        chords = [half + shift_next(half, 1) for half in halves]
        spans = [half + shift_next(half, 0) for half in halves]
        found = []
        for half, factor, w_chord, w_span in zip(halves, factors, chords, spans):
            edge = half * f
            flux_chord = w_chord * f_chord
            flux_span = w_span * f_span
            moved = f + flux_chord - shift_prev(flux_chord, 1, edge)
            moved = moved + flux_span - shift_prev(flux_span, 0, edge)
            found.append(jnp.concatenate([factor] * (cols // 128), axis=1) * moved)
        if i == 0:
            found[0] = found[0] + frames_ref[1]
        for n in range(GROUP):
            chord_ref[i + n] = chords[n]
            span_ref[i + n] = spans[n]
        for n in range(0, GROUP, 2):
            put(i + n, jnp.concatenate(found[n : n + 2], axis=0))
    right = right_ref[...].reshape(3 * size, cols)
    first = dot(mat_ref[...], right)
    for c in range(cols // 128):
        first_ref[c * size : (c + 1) * size, :] = first[:, c * 128 : (c + 1) * 128]

    for i in range(0, depth, GROUP):
        halves = [0.5 * k_ref[i + n] for n in range(GROUP)]
        values = lines_of(first_ref, i)
        chords = [chord_ref[i + n] for n in range(GROUP)]
        spans = [span_ref[i + n] for n in range(GROUP)]
        found = [
            v + divergence(v, w_chord, half, 1) + divergence(v, w_span, half, 0)
            for v, w_chord, w_span, half in zip(values, chords, spans, halves)
        ]
        if i == 0:
            found[0] = found[0] + frames_ref[0]
        for n in range(0, GROUP, 2):
            put(i + n, jnp.concatenate(found[n : n + 2], axis=0))
    right = right_ref[...].reshape(3 * size, cols)
    adj = dot(mat_ref[...], right)
    for c in range(cols // 128):
        adj_ref[c * size : (c + 1) * size, :] = adj[:, c * 128 : (c + 1) * 128]

    for n, (after, _) in enumerate(sides()):
        row = jnp.where(after, rows - 1, 0)
        for c in range(cols // 128):
            edge_ref[n, :, c * 128 : (c + 1) * 128] = row_of_each(first_ref, c, depth, rows, row)
    for n, row in enumerate(far_rows(rows)):
        for c in range(cols // 128):
            two_ref[n, :, c * 128 : (c + 1) * 128] = row_of_each(adj_ref, c, depth, rows, row)
    for copy in copies:
        copy.wait()
    contribution_ref[...] = scale * (
        d_ref[0:1, 0:1] * f * excess_ref[2]
        + chunked(first_ref, 0, rows, size) * excess_ref[1]
        + chunked(adj_ref, 0, rows, size) * excess_ref[0]
    )


def correction(n, got, own, d_ref, edge_ref, pair_ref):
    _, depth, cols = edge_ref.shape
    _, inside = sides()[n]
    factor = d_ref[:, 0:1]
    half = 0.5 * packed_field(got, depth, cols, 0)
    half_next = 0.5 * packed_field(got, depth, cols, 1)
    f = packed_line(got, depth, cols, 0)
    frame = packed_line(got, depth, cols, 1)
    f_next = packed_line(got, depth, cols, 2)
    f_own = packed_line(own, depth, cols, 0)
    half_own = 0.5 * packed_field(own, depth, cols, 0)
    inner = half_own + 0.5 * packed_field(own, depth, cols, 1)
    w_next = half_own + shift_next(half_own, 1)
    w_prev = half_own + shift_prev(half_own, 1, 0.0)
    face = half + half_own
    moved = (
        f
        + (half + shift_next(half, 1)) * (shift_next(f, 1) - f)
        + (half + shift_prev(half, 1, 0.0)) * (shift_prev(f, 1, 0.0) - f)
        + (half + half_next) * (f_next - f)
        + face * (f_own - f)
    )
    outer = factor * moved + jnp.where(iota((depth, 1), 0) == 0, frame, 0.0)
    sources = [factor * (face * f - half * f_own), jnp.where(inside, outer, 0.0)]
    found = dot(pair_ref[...], right_three(jnp.concatenate(sources, axis=0)))
    e = found[0:depth]
    outer = found[depth:]
    change = (
        (1.0 - (w_next + w_prev) - (half_own + inner)) * e
        + w_next * shift_next(e, 1)
        + w_prev * shift_prev(e, 1, 0.0)
        + face * outer
        - half * (e + edge_ref[n])
    )
    return right_three(jnp.concatenate([change, inner * e], axis=0)), e[0:1, :]


def add_segments(total, contribution, picked_rows, map_ref):
    owners, _, lanes = total.shape
    shape = (owners, 128)
    lane = iota(shape, 1)
    segment = jnp.where(lane < lanes, iota(shape, 0) * lanes + lane, -1)
    found = jnp.zeros(shape, F32)
    for block in range(contribution.shape[1] // 128):
        part = contribution[:, block * 128 : (block + 1) * 128]
        sums = jnp.sum(part, axis=1, keepdims=True)
        for n, row in enumerate(picked_rows):
            found += jnp.where(segment == map_ref[block, row], sums[n : n + 1, :], 0.0)
    return total + found[:, None, :lanes]


def near_kernel(
    scale,
    d_ref,
    excess_ref,
    edge_ref,
    pair_ref,
    map_vmem,
    place_ref,
    base_ref,
    contribution_ref,
    own_ref,
    got_ref,
    adj_hbm,
    part_ref,
    adj_ref,
    map_ref,
    sems,
):
    map_copy = pltpu.make_async_copy(map_vmem, map_ref, sems.at[0])
    map_copy.start()
    depth, rows, cols = adj_ref.shape
    size = depth * rows
    sources, surface = correction(0, got_ref, own_ref, d_ref, edge_ref, pair_ref)
    found = dot(place_ref[...], sources)
    adj_ref[...] = (chunked(base_ref, 0, size, size) + found).reshape(depth, rows, cols)
    adj_copy = pltpu.make_async_copy(adj_ref, adj_hbm, sems.at[1])
    adj_copy.start()
    row = jnp.where(sides()[0][0], rows - 1, 0)
    surface = jnp.where(iota((rows, cols), 0) == row, surface, 0.0)
    contribution = contribution_ref[...] + scale * (
        surface * excess_ref[1] + found[0:rows, :] * excess_ref[0]
    )
    map_copy.wait()
    part_ref[...] = add_segments(
        jnp.zeros(part_ref.shape, F32), contribution, range(rows), map_ref
    )
    adj_copy.wait()


def far_kernel(
    scale,
    own_ref,
    got_ref,
    d_ref,
    excess_ref,
    edge_ref,
    pair_ref,
    map_vmem,
    two_ref,
    part_in_ref,
    out_ref,
    part_ref,
    map_ref,
    map_sem,
):
    map_copy = pltpu.make_async_copy(map_vmem, map_ref, map_sem)
    map_copy.start()
    depth = two_ref.shape[1]
    rows = excess_ref.shape[1]
    sources, surface = correction(1, got_ref, own_ref, d_ref, edge_ref, pair_ref)
    found = dot(pair_ref[...], sources)
    edge, second = far_rows(rows)
    contribution = scale * jnp.concatenate(
        [
            surface * excess_ref[1, pl.ds(edge, 1), :]
            + found[0:1] * excess_ref[0, pl.ds(edge, 1), :],
            found[depth : depth + 1] * excess_ref[0, pl.ds(second, 1), :],
        ],
        axis=0,
    )
    map_copy.wait()
    part_ref[...] = add_segments(part_in_ref[...], contribution, (edge, second), map_ref)
    out_ref[...] = two_ref[...] + found.reshape(two_ref.shape)


def finish_kernel(_, two_ref, got_ref, adj_hbm, out_hbm, out_ref, sems):
    copies = []
    for n, row in enumerate(far_rows(adj_hbm.shape[1])):
        copies.append(pltpu.make_async_copy(two_ref.at[n], adj_hbm.at[:, row, :], sems.at[n]))
        copies[-1].start()
    out_ref[...] = jnp.sum(got_ref[:, 0, :], axis=0)
    copies.append(pltpu.make_async_copy(out_ref, out_hbm, sems.at[2]))
    copies[-1].start()
    for copy in copies:
        copy.wait()


def in_hbm(x):
    return pltpu.with_memory_space_constraint(x, pltpu.HBM)


def per_device(
    conductance, depth_inverse, surface_residual, surface_excess, segment_map, frame_index
):
    _, depth, rows, cols = conductance.shape
    frames = surface_residual.shape[1]
    blocks = segment_map.shape[1]
    size = depth * rows
    spans = lax.axis_size("span")
    devices = spans * lax.axis_size("blade")
    lanes = SEGS // devices
    field = pltpu.VMEM((depth, rows, cols), F32)
    chunks = cols // 128
    packed_far = pltpu.VMEM(((2 * depth + 4) * chunks, 128), F32)
    packed_near = pltpu.VMEM(((2 * depth + 3) * chunks, 128), F32)
    own_far, own_near, picked, inverse = pl.pallas_call(
        load_kernel,
        out_shape=(
            packed_far,
            packed_near,
            pltpu.VMEM((STEPS, rows, cols), F32),
            pltpu.VMEM((depth, depth), F32),
        ),
        in_specs=[HBM] * 4,
        out_specs=(VMEM,) * 4,
        scratch_shapes=[
            pltpu.SMEM((STEPS,), jnp.int32),
            pltpu.VMEM((frames, rows, cols), F32),
            pltpu.VMEM((2, depth, 8, cols), F32),
            pltpu.SemaphoreType.DMA((5,)),
        ],
        compiler_params=GRANT,
        name="load",
    )(
        in_hbm(frame_index),
        in_hbm(conductance[0]),
        in_hbm(surface_residual[0]),
        in_hbm(depth_inverse[0]),
    )
    across = [(i, i + 1) for i in range(1, spans - 1, 2)]
    within = [(i, i + 1) for i in range(0, spans - 1, 2)]
    near = lax.ppermute(own_near, "span", within + [(b, a) for a, b in within])
    far = lax.ppermute(own_far, "span", across + [(b, a) for a, b in across])
    scale = 1.0 / math.sqrt(128.0 * STEPS)
    line = pltpu.VMEM((rows, cols), F32)
    base, two, excess, ids, edge, contribution, pair, place = pl.pallas_call(
        functools.partial(base_kernel, scale),
        out_shape=(
            pltpu.VMEM((chunks * size, 128), F32),
            pltpu.VMEM((2, depth, cols), F32),
            pltpu.VMEM((STEPS, rows, cols), F32),
            pltpu.VMEM((blocks, rows), jnp.int32),
            pltpu.VMEM((2, depth, cols), F32),
            line,
            pltpu.VMEM((2 * depth, 6 * depth), BF16),
            pltpu.VMEM((size, 6 * depth), BF16),
        ),
        in_specs=[VMEM] * 3 + [HBM] * 2,
        out_specs=(VMEM,) * 8,
        scratch_shapes=[
            pltpu.VMEM((size, 3 * size), BF16),
            pltpu.VMEM((3, size, cols), BF16),
            pltpu.VMEM((chunks * size, 128), F32),
            field,
            field,
            pltpu.VMEM((depth, 128), F32),
            pltpu.SemaphoreType.DMA((2,)),
        ],
        compiler_params=GRANT,
        name="base",
    )(conductance[0], picked, inverse, in_hbm(surface_excess[0]), in_hbm(segment_map.T))
    fixed = (inverse, excess, edge, pair, ids)
    sums = pltpu.VMEM((devices, 1, lanes), F32)
    adjoint, partial = pl.pallas_call(
        functools.partial(near_kernel, scale),
        out_shape=(pltpu.HBM((depth, rows, cols), F32), sums),
        in_specs=[VMEM] * 10,
        out_specs=(HBM, VMEM),
        scratch_shapes=[
            field,
            pltpu.SMEM((blocks, rows), jnp.int32),
            pltpu.SemaphoreType.DMA((2,)),
        ],
        compiler_params=GRANT,
        name="near",
    )(*fixed, place, base, contribution, own_near, near)
    two, partial = pl.pallas_call(
        functools.partial(far_kernel, scale),
        out_shape=(pltpu.VMEM((2, depth, cols), F32), sums),
        in_specs=[VMEM] * 9,
        out_specs=(VMEM,) * 2,
        scratch_shapes=[pltpu.SMEM((blocks, rows), jnp.int32), pltpu.SemaphoreType.DMA],
        compiler_params=GRANT,
        name="far",
    )(own_far, far, *fixed, two, partial)
    pieces = lax.all_to_all(partial, ("blade", "span"), 0, 0, tiled=True)
    adjoint, owned = pl.pallas_call(
        finish_kernel,
        out_shape=(pltpu.HBM((depth, rows, cols), F32), pltpu.HBM((lanes,), F32)),
        in_specs=[HBM, VMEM, VMEM],
        out_specs=(HBM,) * 2,
        scratch_shapes=[pltpu.VMEM((lanes,), F32), pltpu.SemaphoreType.DMA((3,))],
        input_output_aliases={0: 0},
        compiler_params=GRANT,
        name="finish",
    )(in_hbm(adjoint), two, pltpu.with_memory_space_constraint(pieces, pltpu.VMEM))
    return (adjoint[None], owned)


def solution(mesh):
    placed = (
        P("blade", None, "span", None),
        P("blade", None, None),
        P("blade", None, "span", None),
        P("blade", None, "span", None),
        P("span", None),
        P(),
    )
    return jax.shard_map(
        per_device,
        mesh=mesh,
        in_specs=placed,
        out_specs=(P("blade", None, "span", None), P(("blade", "span"))),
        check_vma=False,
    )
```

```python
import functools
import math

import jax
import jax.numpy as jnp
from jax import lax
from jax.experimental import pallas as pl
from jax.experimental.pallas import tpu as pltpu
from jax.sharding import PartitionSpec as P

STEPS = 3
SEGS = 2048
GROUP = 2
F32 = jnp.float32
BF16 = jnp.bfloat16
VMEM = pl.BlockSpec(memory_space=pltpu.VMEM)
HBM = pl.BlockSpec(memory_space=pltpu.HBM)
GRANT = pltpu.CompilerParams(vmem_limit_bytes=16 * 2**20)


def split(x):
    high = x.astype(BF16)
    return high, (x - high.astype(F32)).astype(BF16)


def dot(a, b):
    return jnp.dot(a, b, preferred_element_type=F32)


def left_three(matrix):
    high, low = matrix
    return jnp.concatenate([high, low, high], axis=1)


def right_three(x):
    high, low = split(x)
    return jnp.concatenate([high, high, low], axis=0)


def iota(shape, dim):
    return lax.broadcasted_iota(jnp.int32, shape, dim)


def shift_next(x, axis):
    size = x.shape[axis]
    return jnp.where(iota(x.shape, axis) == size - 1, 0.0, pltpu.roll(x, size - 1, axis))


def shift_prev(x, axis, first):
    return jnp.where(iota(x.shape, axis) == 0, first, pltpu.roll(x, 1, axis))


def divergence(v, weight, half, axis):
    flux = weight * (shift_next(v, axis) - v)
    return flux - shift_prev(flux, axis, half * v)


def sides():
    span = lax.axis_index("span")
    count = lax.axis_size("span")
    even = lax.rem(span, 2) == 0
    has_next = span + 1 < count
    has_prev = span > 0
    return (
        (even, jnp.where(even, has_next, has_prev)),
        (jnp.logical_not(even), jnp.where(even, has_prev, has_next)),
    )


def chunked(ref, start, count, step):
    chunks = ref.shape[0] // step
    return jnp.concatenate(
        [ref[c * step + start : c * step + start + count, :] for c in range(chunks)], axis=1
    )


def packed_field(ref, depth, cols, n):
    chunks = cols // 128
    return chunked(ref.at[n * chunks * depth : (n + 1) * chunks * depth], 0, depth, depth)


def packed_line(ref, depth, cols, n):
    chunks = cols // 128
    base = (2 * depth + n) * chunks
    return chunked(ref.at[base : base + chunks], 0, 1, 1)


def row_of_each(ref, chunk, depth, rows, row):
    return ref[pl.ds(chunk * depth * rows + row, depth, stride=rows), :]


def far_rows(rows):
    after = sides()[1][0]
    return jnp.where(after, rows - 1, 0), jnp.where(after, rows - 2, 1)


def put_lines(ref, frames_ref, depth, rows, after):
    chunks = frames_ref.shape[2] // 128
    base = 2 * chunks * depth
    edge, second = jnp.where(after, rows - 1, 0), jnp.where(after, rows - 2, 1)
    for n, (frame, row) in enumerate(((2, edge), (1, edge), (2, second))):
        line = frames_ref[frame, pl.ds(row, 1), :]
        for c in range(chunks):
            spot = base + n * chunks + c
            ref[spot : spot + 1, :] = line[:, c * 128 : (c + 1) * 128]
    if ref.shape[0] > base + 3 * chunks:
        ref[base + 3 * chunks :, :] = jnp.zeros((ref.shape[0] - base - 3 * chunks, 128), F32)


def put_rows(ref, depth, items):
    for which, x in enumerate(items):
        for c in range(x.shape[1] // 128):
            spot = (which * (x.shape[1] // 128) + c) * depth
            ref[spot : spot + depth, :] = x[:, c * 128 : (c + 1) * 128]


def load_kernel(
    frame_hbm,
    k_hbm,
    res_hbm,
    d_hbm,
    far_ref,
    frames_ref,
    d_ref,
    frame_ref,
    res_ref,
    edge_ref,
    sems,
):
    depth, rows, cols = k_hbm.shape
    after = sides()[1][0]
    first = jnp.where(after, rows - 2, 0)
    pairs = (
        (frame_hbm, frame_ref),
        (res_hbm, res_ref),
        (k_hbm.at[:, pl.ds(first, 2), :], edge_ref.at[:, 0:2, :]),
        (d_hbm, d_ref),
    )
    copies = [pltpu.make_async_copy(a, b, sems.at[n]) for n, (a, b) in enumerate(pairs)]
    for copy in copies:
        copy.start()
    copies[0].wait()
    copies[1].wait()
    for n in range(STEPS):
        frames_ref[n] = res_ref[frame_ref[n]]
    put_lines(far_ref, frames_ref, depth, rows, after)
    copies[2].wait()
    low, high = edge_ref[:, 0, :], edge_ref[:, 1, :]
    put_rows(far_ref, depth, (jnp.where(after, high, low), jnp.where(after, low, high)))
    copies[3].wait()


def pack_kernel(k_ref, frames_ref, near_ref):
    depth, rows, _ = k_ref.shape
    after = sides()[0][0]
    put_lines(near_ref, frames_ref, depth, rows, after)
    items = []
    for first, last in ((0, rows - 1), (1, rows - 2)):
        items.append(jnp.where(after, k_ref[:, last, :], k_ref[:, first, :]))
    put_rows(near_ref, depth, items)


def base_kernel(
    scale,
    k_ref,
    frames_ref,
    d_ref,
    excess_hbm,
    map_hbm,
    adj_ref,
    two_ref,
    excess_ref,
    map_ref,
    edge_ref,
    contribution_ref,
    pair_ref,
    place_ref,
    mat_ref,
    right_ref,
    first_ref,
    chord_ref,
    span_ref,
    factor_ref,
    sems,
):
    copies = [
        pltpu.make_async_copy(excess_hbm, excess_ref, sems.at[0]),
        pltpu.make_async_copy(map_hbm, map_ref, sems.at[1]),
    ]
    for copy in copies:
        copy.start()
    depth, rows, cols = chord_ref.shape
    size = depth * rows
    factor_ref[...] = jnp.broadcast_to(d_ref[:, 0:1], factor_ref.shape)

    parts = split(d_ref[...])
    tall = (iota((size, depth), 0) // rows == iota((size, depth), 1)).astype(BF16)
    wide = (iota((depth, size), 0) == iota((depth, size), 1) // rows).astype(BF16)
    two = 2 * depth
    tile = (iota((depth, two), 0) == iota((depth, two), 1) % depth).astype(BF16)
    same = iota((size, size), 0) % rows == iota((size, size), 1) % rows
    pair_same = iota((two, two), 0) // depth == iota((two, two), 1) // depth
    row_of = iota((size, two), 0) % rows
    first_half = iota((size, two), 1) < depth
    after = sides()[0][0]
    edge = jnp.where(after, rows - 1, 0)
    second = jnp.where(after, rows - 2, 1)
    placed = row_of == jnp.where(first_half, edge, second)
    mats, pairs, places = [], [], []
    for part in parts:
        column = dot(tall, part).astype(BF16)
        row = dot(part, tile)
        mats.append(jnp.where(same, dot(column, wide), 0.0).astype(BF16))
        places.append(jnp.where(placed, dot(column, tile), 0.0).astype(BF16))
        pairs.append(
            jnp.where(pair_same, jnp.concatenate([row] * 2, axis=0), 0.0).astype(BF16)
        )
    mat_ref[...] = left_three(mats)
    pair_ref[...] = left_three(pairs)
    place_ref[...] = left_three(places)

    f = frames_ref[2]
    f_chord = shift_next(f, 1) - f
    f_span = shift_next(f, 0) - f

    def put(i, both):
        high, low = split(both)
        span = pl.ds(i * rows, 2 * rows)
        right_ref[0, span, :] = high
        right_ref[1, span, :] = high
        right_ref[2, span, :] = low

    def lines_of(ref, i):
        return [chunked(ref, j * rows, rows, size) for j in range(i, i + GROUP)]

    for i in range(0, depth, GROUP):
        halves = [0.5 * k_ref[i + n] for n in range(GROUP)]
        factors = [jnp.broadcast_to(factor_ref[j : j + 1, :], (rows, 128)) for j in range(i, i + GROUP)]
        chords = [half + shift_next(half, 1) for half in halves]
        spans = [half + shift_next(half, 0) for half in halves]
        found = []
        for half, factor, w_chord, w_span in zip(halves, factors, chords, spans):
            edge = half * f
            flux_chord = w_chord * f_chord
            flux_span = w_span * f_span
            moved = f + flux_chord - shift_prev(flux_chord, 1, edge)
            moved = moved + flux_span - shift_prev(flux_span, 0, edge)
            found.append(jnp.concatenate([factor] * (cols // 128), axis=1) * moved)
        if i == 0:
            found[0] = found[0] + frames_ref[1]
        for n in range(GROUP):
            chord_ref[i + n] = chords[n]
            span_ref[i + n] = spans[n]
        for n in range(0, GROUP, 2):
            put(i + n, jnp.concatenate(found[n : n + 2], axis=0))
    right = right_ref[...].reshape(3 * size, cols)
    first = dot(mat_ref[...], right)
    for c in range(cols // 128):
        first_ref[c * size : (c + 1) * size, :] = first[:, c * 128 : (c + 1) * 128]

    for i in range(0, depth, GROUP):
        halves = [0.5 * k_ref[i + n] for n in range(GROUP)]
        values = lines_of(first_ref, i)
        chords = [chord_ref[i + n] for n in range(GROUP)]
        spans = [span_ref[i + n] for n in range(GROUP)]
        found = [
            v + divergence(v, w_chord, half, 1) + divergence(v, w_span, half, 0)
            for v, w_chord, w_span, half in zip(values, chords, spans, halves)
        ]
        if i == 0:
            found[0] = found[0] + frames_ref[0]
        for n in range(0, GROUP, 2):
            put(i + n, jnp.concatenate(found[n : n + 2], axis=0))
    right = right_ref[...].reshape(3 * size, cols)
    adj = dot(mat_ref[...], right)
    for c in range(cols // 128):
        adj_ref[c * size : (c + 1) * size, :] = adj[:, c * 128 : (c + 1) * 128]

    for n, (after, _) in enumerate(sides()):
        row = jnp.where(after, rows - 1, 0)
        for c in range(cols // 128):
            edge_ref[n, :, c * 128 : (c + 1) * 128] = row_of_each(first_ref, c, depth, rows, row)
    for n, row in enumerate(far_rows(rows)):
        for c in range(cols // 128):
            two_ref[n, :, c * 128 : (c + 1) * 128] = row_of_each(adj_ref, c, depth, rows, row)
    for copy in copies:
        copy.wait()
    contribution_ref[...] = scale * (
        d_ref[0:1, 0:1] * f * excess_ref[2]
        + chunked(first_ref, 0, rows, size) * excess_ref[1]
        + chunked(adj_ref, 0, rows, size) * excess_ref[0]
    )


def correction(n, got, own, d_ref, edge_ref, pair_ref):
    _, depth, cols = edge_ref.shape
    _, inside = sides()[n]
    factor = d_ref[:, 0:1]
    half = 0.5 * packed_field(got, depth, cols, 0)
    half_next = 0.5 * packed_field(got, depth, cols, 1)
    f = packed_line(got, depth, cols, 0)
    frame = packed_line(got, depth, cols, 1)
    f_next = packed_line(got, depth, cols, 2)
    f_own = packed_line(own, depth, cols, 0)
    half_own = 0.5 * packed_field(own, depth, cols, 0)
    inner = half_own + 0.5 * packed_field(own, depth, cols, 1)
    w_next = half_own + shift_next(half_own, 1)
    w_prev = half_own + shift_prev(half_own, 1, 0.0)
    face = half + half_own
    moved = (
        f
        + (half + shift_next(half, 1)) * (shift_next(f, 1) - f)
        + (half + shift_prev(half, 1, 0.0)) * (shift_prev(f, 1, 0.0) - f)
        + (half + half_next) * (f_next - f)
        + face * (f_own - f)
    )
    outer = factor * moved + jnp.where(iota((depth, 1), 0) == 0, frame, 0.0)
    sources = [factor * (face * f - half * f_own), jnp.where(inside, outer, 0.0)]
    found = dot(pair_ref[...], right_three(jnp.concatenate(sources, axis=0)))
    e = found[0:depth]
    outer = found[depth:]
    change = (
        (1.0 - (w_next + w_prev) - (half_own + inner)) * e
        + w_next * shift_next(e, 1)
        + w_prev * shift_prev(e, 1, 0.0)
        + face * outer
        - half * (e + edge_ref[n])
    )
    return right_three(jnp.concatenate([change, inner * e], axis=0)), e[0:1, :]


def add_segments(total, contribution, picked_rows, map_ref):
    owners, _, lanes = total.shape
    shape = (owners, 128)
    lane = iota(shape, 1)
    segment = jnp.where(lane < lanes, iota(shape, 0) * lanes + lane, -1)
    found = jnp.zeros(shape, F32)
    for block in range(contribution.shape[1] // 128):
        part = contribution[:, block * 128 : (block + 1) * 128]
        sums = jnp.sum(part, axis=1, keepdims=True)
        for n, row in enumerate(picked_rows):
            found += jnp.where(segment == map_ref[block, row], sums[n : n + 1, :], 0.0)
    return total + found[:, None, :lanes]


def near_kernel(
    scale,
    d_ref,
    excess_ref,
    edge_ref,
    pair_ref,
    map_vmem,
    place_ref,
    base_ref,
    contribution_ref,
    own_ref,
    got_ref,
    adj_hbm,
    part_ref,
    adj_ref,
    map_ref,
    sems,
):
    map_copy = pltpu.make_async_copy(map_vmem, map_ref, sems.at[0])
    map_copy.start()
    depth, rows, cols = adj_ref.shape
    size = depth * rows
    sources, surface = correction(0, got_ref, own_ref, d_ref, edge_ref, pair_ref)
    found = dot(place_ref[...], sources)
    adj_ref[...] = (chunked(base_ref, 0, size, size) + found).reshape(depth, rows, cols)
    adj_copy = pltpu.make_async_copy(adj_ref, adj_hbm, sems.at[1])
    adj_copy.start()
    row = jnp.where(sides()[0][0], rows - 1, 0)
    surface = jnp.where(iota((rows, cols), 0) == row, surface, 0.0)
    contribution = contribution_ref[...] + scale * (
        surface * excess_ref[1] + found[0:rows, :] * excess_ref[0]
    )
    map_copy.wait()
    part_ref[...] = add_segments(
        jnp.zeros(part_ref.shape, F32), contribution, range(rows), map_ref
    )
    adj_copy.wait()


def far_kernel(
    scale,
    own_ref,
    got_ref,
    d_ref,
    excess_ref,
    edge_ref,
    pair_ref,
    map_vmem,
    two_ref,
    part_in_ref,
    out_ref,
    part_ref,
    map_ref,
    map_sem,
):
    map_copy = pltpu.make_async_copy(map_vmem, map_ref, map_sem)
    map_copy.start()
    depth = two_ref.shape[1]
    rows = excess_ref.shape[1]
    sources, surface = correction(1, got_ref, own_ref, d_ref, edge_ref, pair_ref)
    found = dot(pair_ref[...], sources)
    edge, second = far_rows(rows)
    contribution = scale * jnp.concatenate(
        [
            surface * excess_ref[1, pl.ds(edge, 1), :]
            + found[0:1] * excess_ref[0, pl.ds(edge, 1), :],
            found[depth : depth + 1] * excess_ref[0, pl.ds(second, 1), :],
        ],
        axis=0,
    )
    map_copy.wait()
    part_ref[...] = add_segments(part_in_ref[...], contribution, (edge, second), map_ref)
    out_ref[...] = two_ref[...] + found.reshape(two_ref.shape)


def finish_kernel(_, two_ref, got_ref, adj_hbm, out_hbm, out_ref, sems):
    copies = []
    for n, row in enumerate(far_rows(adj_hbm.shape[1])):
        copies.append(pltpu.make_async_copy(two_ref.at[n], adj_hbm.at[:, row, :], sems.at[n]))
        copies[-1].start()
    out_ref[...] = jnp.sum(got_ref[:, 0, :], axis=0)
    copies.append(pltpu.make_async_copy(out_ref, out_hbm, sems.at[2]))
    copies[-1].start()
    for copy in copies:
        copy.wait()


def in_hbm(x):
    return pltpu.with_memory_space_constraint(x, pltpu.HBM)


def per_device(
    conductance, depth_inverse, surface_residual, surface_excess, segment_map, frame_index
):
    _, depth, rows, cols = conductance.shape
    frames = surface_residual.shape[1]
    blocks = segment_map.shape[1]
    size = depth * rows
    spans = lax.axis_size("span")
    devices = spans * lax.axis_size("blade")
    lanes = SEGS // devices
    field = pltpu.VMEM((depth, rows, cols), F32)
    chunks = cols // 128
    packed_far = pltpu.VMEM(((2 * depth + 4) * chunks, 128), F32)
    packed_near = pltpu.VMEM(((2 * depth + 3) * chunks, 128), F32)
    own_far, picked, inverse = pl.pallas_call(
        load_kernel,
        out_shape=(
            packed_far,
            pltpu.VMEM((STEPS, rows, cols), F32),
            pltpu.VMEM((depth, depth), F32),
        ),
        in_specs=[HBM] * 4,
        out_specs=(VMEM,) * 3,
        scratch_shapes=[
            pltpu.SMEM((STEPS,), jnp.int32),
            pltpu.VMEM((frames, rows, cols), F32),
            pltpu.VMEM((depth, 8, cols), F32),
            pltpu.SemaphoreType.DMA((4,)),
        ],
        compiler_params=GRANT,
        name="load",
    )(
        in_hbm(frame_index),
        in_hbm(conductance[0]),
        in_hbm(surface_residual[0]),
        in_hbm(depth_inverse[0]),
    )
    k = conductance[0]
    own_near = pl.pallas_call(
        pack_kernel,
        out_shape=packed_near,
        in_specs=[VMEM] * 2,
        out_specs=VMEM,
        compiler_params=GRANT,
        name="pack",
    )(k, picked)
    across = [(i, i + 1) for i in range(1, spans - 1, 2)]
    within = [(i, i + 1) for i in range(0, spans - 1, 2)]
    near = lax.ppermute(own_near, "span", within + [(b, a) for a, b in within])
    far = lax.ppermute(own_far, "span", across + [(b, a) for a, b in across])
    scale = 1.0 / math.sqrt(128.0 * STEPS)
    line = pltpu.VMEM((rows, cols), F32)
    base, two, excess, ids, edge, contribution, pair, place = pl.pallas_call(
        functools.partial(base_kernel, scale),
        out_shape=(
            pltpu.VMEM((chunks * size, 128), F32),
            pltpu.VMEM((2, depth, cols), F32),
            pltpu.VMEM((STEPS, rows, cols), F32),
            pltpu.VMEM((blocks, rows), jnp.int32),
            pltpu.VMEM((2, depth, cols), F32),
            line,
            pltpu.VMEM((2 * depth, 6 * depth), BF16),
            pltpu.VMEM((size, 6 * depth), BF16),
        ),
        in_specs=[VMEM] * 3 + [HBM] * 2,
        out_specs=(VMEM,) * 8,
        scratch_shapes=[
            pltpu.VMEM((size, 3 * size), BF16),
            pltpu.VMEM((3, size, cols), BF16),
            pltpu.VMEM((chunks * size, 128), F32),
            field,
            field,
            pltpu.VMEM((depth, 128), F32),
            pltpu.SemaphoreType.DMA((2,)),
        ],
        compiler_params=GRANT,
        name="base",
    )(k, picked, inverse, in_hbm(surface_excess[0]), in_hbm(segment_map.T))
    fixed = (inverse, excess, edge, pair, ids)
    sums = pltpu.VMEM((devices, 1, lanes), F32)
    adjoint, partial = pl.pallas_call(
        functools.partial(near_kernel, scale),
        out_shape=(pltpu.HBM((depth, rows, cols), F32), sums),
        in_specs=[VMEM] * 10,
        out_specs=(HBM, VMEM),
        scratch_shapes=[
            field,
            pltpu.SMEM((blocks, rows), jnp.int32),
            pltpu.SemaphoreType.DMA((2,)),
        ],
        compiler_params=GRANT,
        name="near",
    )(*fixed, place, base, contribution, own_near, near)
    two, partial = pl.pallas_call(
        functools.partial(far_kernel, scale),
        out_shape=(pltpu.VMEM((2, depth, cols), F32), sums),
        in_specs=[VMEM] * 9,
        out_specs=(VMEM,) * 2,
        scratch_shapes=[pltpu.SMEM((blocks, rows), jnp.int32), pltpu.SemaphoreType.DMA],
        compiler_params=GRANT,
        name="far",
    )(own_far, far, *fixed, two, partial)
    pieces = lax.all_to_all(partial, ("blade", "span"), 0, 0, tiled=True)
    adjoint, owned = pl.pallas_call(
        finish_kernel,
        out_shape=(pltpu.HBM((depth, rows, cols), F32), pltpu.HBM((lanes,), F32)),
        in_specs=[HBM, VMEM, VMEM],
        out_specs=(HBM,) * 2,
        scratch_shapes=[pltpu.VMEM((lanes,), F32), pltpu.SemaphoreType.DMA((3,))],
        input_output_aliases={0: 0},
        compiler_params=GRANT,
        name="finish",
    )(in_hbm(adjoint), two, pltpu.with_memory_space_constraint(pieces, pltpu.VMEM))
    return (adjoint[None], owned)


def solution(mesh):
    placed = (
        P("blade", None, "span", None),
        P("blade", None, None),
        P("blade", None, "span", None),
        P("blade", None, "span", None),
        P("span", None),
        P(),
    )
    return jax.shard_map(
        per_device,
        mesh=mesh,
        in_specs=placed,
        out_specs=(P("blade", None, "span", None), P(("blade", "span"))),
        check_vma=False,
    )
```

```python
import functools
import math

import jax
import jax.numpy as jnp
from jax import lax
from jax.experimental import pallas as pl
from jax.experimental.pallas import tpu as pltpu
from jax.sharding import PartitionSpec as P

STEPS = 3
SEGS = 2048
GROUP = 2
F32 = jnp.float32
BF16 = jnp.bfloat16
VMEM = pl.BlockSpec(memory_space=pltpu.VMEM)
HBM = pl.BlockSpec(memory_space=pltpu.HBM)
GRANT = pltpu.CompilerParams(vmem_limit_bytes=16 * 2**20)


def split(x):
    high = x.astype(BF16)
    return high, (x - high.astype(F32)).astype(BF16)


def dot(a, b):
    return jnp.dot(a, b, preferred_element_type=F32)


def left_three(matrix):
    high, low = matrix
    return jnp.concatenate([high, low, high], axis=1)


def right_three(x):
    high, low = split(x)
    return jnp.concatenate([high, high, low], axis=0)


def iota(shape, dim):
    return lax.broadcasted_iota(jnp.int32, shape, dim)


def shift_next(x, axis):
    size = x.shape[axis]
    return jnp.where(iota(x.shape, axis) == size - 1, 0.0, pltpu.roll(x, size - 1, axis))


def shift_prev(x, axis, first):
    return jnp.where(iota(x.shape, axis) == 0, first, pltpu.roll(x, 1, axis))


def divergence(v, weight, half, axis):
    flux = weight * (shift_next(v, axis) - v)
    return flux - shift_prev(flux, axis, half * v)


def sides():
    span = lax.axis_index("span")
    count = lax.axis_size("span")
    even = lax.rem(span, 2) == 0
    has_next = span + 1 < count
    has_prev = span > 0
    return (
        (even, jnp.where(even, has_next, has_prev)),
        (jnp.logical_not(even), jnp.where(even, has_prev, has_next)),
    )


def chunked(ref, start, count, step):
    chunks = ref.shape[0] // step
    return jnp.concatenate(
        [ref[c * step + start : c * step + start + count, :] for c in range(chunks)], axis=1
    )


def packed_field(ref, depth, cols, n):
    chunks = cols // 128
    return chunked(ref.at[n * chunks * depth : (n + 1) * chunks * depth], 0, depth, depth)


def packed_line(ref, depth, cols, n):
    chunks = cols // 128
    base = (2 * depth + n) * chunks
    return chunked(ref.at[base : base + chunks], 0, 1, 1)


def row_of_each(ref, chunk, depth, rows, row):
    return ref[pl.ds(chunk * depth * rows + row, depth, stride=rows), :]


def far_rows(rows):
    after = sides()[1][0]
    return jnp.where(after, rows - 1, 0), jnp.where(after, rows - 2, 1)


def put_lines(ref, depth, lines):
    chunks = lines[0].shape[1] // 128
    base = 2 * chunks * depth
    for n, line in enumerate(lines):
        for c in range(chunks):
            spot = base + n * chunks + c
            ref[spot : spot + 1, :] = line[:, c * 128 : (c + 1) * 128]
    if ref.shape[0] > base + 3 * chunks:
        ref[base + 3 * chunks :, :] = jnp.zeros((ref.shape[0] - base - 3 * chunks, 128), F32)


def put_rows(ref, depth, items):
    for which, x in enumerate(items):
        for c in range(x.shape[1] // 128):
            spot = (which * (x.shape[1] // 128) + c) * depth
            ref[spot : spot + depth, :] = x[:, c * 128 : (c + 1) * 128]


def load_kernel(
    frame_hbm,
    k_hbm,
    res_hbm,
    d_hbm,
    far_ref,
    index_ref,
    d_ref,
    frame_ref,
    res_ref,
    edge_ref,
    sems,
):
    depth, rows, cols = k_hbm.shape
    after = sides()[1][0]
    first = jnp.where(after, rows - 2, 0)
    pairs = (
        (frame_hbm, frame_ref),
        (res_hbm.at[:, pl.ds(first, 2), :], res_ref.at[:, 0:2, :]),
        (k_hbm.at[:, pl.ds(first, 2), :], edge_ref.at[:, 0:2, :]),
        (d_hbm, d_ref),
    )
    copies = [pltpu.make_async_copy(a, b, sems.at[n]) for n, (a, b) in enumerate(pairs)]
    for copy in copies:
        copy.start()
    copies[0].wait()
    copies[1].wait()
    for n in range(STEPS):
        index_ref[n : n + 1, :] = jnp.full((1, 128), frame_ref[n], jnp.int32)
    lines = []
    for step, near in ((2, True), (1, True), (2, False)):
        low, high = res_ref[frame_ref[step], 0:1, :], res_ref[frame_ref[step], 1:2, :]
        lines.append(jnp.where(after, high, low) if near else jnp.where(after, low, high))
    put_lines(far_ref, depth, lines)
    copies[2].wait()
    low, high = edge_ref[:, 0, :], edge_ref[:, 1, :]
    put_rows(far_ref, depth, (jnp.where(after, high, low), jnp.where(after, low, high)))
    copies[3].wait()


def pack_kernel(k_ref, res_ref, index_ref, near_ref, frames_ref):
    depth, rows, cols = k_ref.shape
    after = sides()[0][0]
    for n in range(STEPS):
        wanted = jnp.concatenate(
            [jnp.broadcast_to(index_ref[n : n + 1, :], (rows, 128))] * (cols // 128), axis=1
        )
        picked = res_ref[0]
        for frame in range(1, res_ref.shape[0]):
            picked = jnp.where(wanted == frame, res_ref[frame], picked)
        frames_ref[n] = picked
    edge, second = jnp.where(after, rows - 1, 0), jnp.where(after, rows - 2, 1)
    lines = [frames_ref[n, pl.ds(row, 1), :] for n, row in ((2, edge), (1, edge), (2, second))]
    put_lines(near_ref, depth, lines)
    items = []
    for first, last in ((0, rows - 1), (1, rows - 2)):
        items.append(jnp.where(after, k_ref[:, last, :], k_ref[:, first, :]))
    put_rows(near_ref, depth, items)


def base_kernel(
    scale,
    k_ref,
    frames_ref,
    d_ref,
    excess_hbm,
    map_hbm,
    adj_ref,
    two_ref,
    excess_ref,
    map_ref,
    edge_ref,
    contribution_ref,
    pair_ref,
    place_ref,
    mat_ref,
    right_ref,
    first_ref,
    chord_ref,
    span_ref,
    factor_ref,
    sems,
):
    copies = [
        pltpu.make_async_copy(excess_hbm, excess_ref, sems.at[0]),
        pltpu.make_async_copy(map_hbm, map_ref, sems.at[1]),
    ]
    for copy in copies:
        copy.start()
    depth, rows, cols = chord_ref.shape
    size = depth * rows
    factor_ref[...] = jnp.broadcast_to(d_ref[:, 0:1], factor_ref.shape)

    parts = split(d_ref[...])
    tall = (iota((size, depth), 0) // rows == iota((size, depth), 1)).astype(BF16)
    wide = (iota((depth, size), 0) == iota((depth, size), 1) // rows).astype(BF16)
    two = 2 * depth
    tile = (iota((depth, two), 0) == iota((depth, two), 1) % depth).astype(BF16)
    same = iota((size, size), 0) % rows == iota((size, size), 1) % rows
    pair_same = iota((two, two), 0) // depth == iota((two, two), 1) // depth
    row_of = iota((size, two), 0) % rows
    first_half = iota((size, two), 1) < depth
    after = sides()[0][0]
    edge = jnp.where(after, rows - 1, 0)
    second = jnp.where(after, rows - 2, 1)
    placed = row_of == jnp.where(first_half, edge, second)
    mats, pairs, places = [], [], []
    for part in parts:
        column = dot(tall, part).astype(BF16)
        row = dot(part, tile)
        mats.append(jnp.where(same, dot(column, wide), 0.0).astype(BF16))
        places.append(jnp.where(placed, dot(column, tile), 0.0).astype(BF16))
        pairs.append(
            jnp.where(pair_same, jnp.concatenate([row] * 2, axis=0), 0.0).astype(BF16)
        )
    mat_ref[...] = left_three(mats)
    pair_ref[...] = left_three(pairs)
    place_ref[...] = left_three(places)

    f = frames_ref[2]
    f_chord = shift_next(f, 1) - f
    f_span = shift_next(f, 0) - f

    def put(i, both):
        high, low = split(both)
        span = pl.ds(i * rows, 2 * rows)
        right_ref[0, span, :] = high
        right_ref[1, span, :] = high
        right_ref[2, span, :] = low

    def lines_of(ref, i):
        return [chunked(ref, j * rows, rows, size) for j in range(i, i + GROUP)]

    for i in range(0, depth, GROUP):
        halves = [0.5 * k_ref[i + n] for n in range(GROUP)]
        factors = [jnp.broadcast_to(factor_ref[j : j + 1, :], (rows, 128)) for j in range(i, i + GROUP)]
        chords = [half + shift_next(half, 1) for half in halves]
        spans = [half + shift_next(half, 0) for half in halves]
        found = []
        for half, factor, w_chord, w_span in zip(halves, factors, chords, spans):
            edge = half * f
            flux_chord = w_chord * f_chord
            flux_span = w_span * f_span
            moved = f + flux_chord - shift_prev(flux_chord, 1, edge)
            moved = moved + flux_span - shift_prev(flux_span, 0, edge)
            found.append(jnp.concatenate([factor] * (cols // 128), axis=1) * moved)
        if i == 0:
            found[0] = found[0] + frames_ref[1]
        for n in range(GROUP):
            chord_ref[i + n] = chords[n]
            span_ref[i + n] = spans[n]
        for n in range(0, GROUP, 2):
            put(i + n, jnp.concatenate(found[n : n + 2], axis=0))
    right = right_ref[...].reshape(3 * size, cols)
    first = dot(mat_ref[...], right)
    for c in range(cols // 128):
        first_ref[c * size : (c + 1) * size, :] = first[:, c * 128 : (c + 1) * 128]

    for i in range(0, depth, GROUP):
        halves = [0.5 * k_ref[i + n] for n in range(GROUP)]
        values = lines_of(first_ref, i)
        chords = [chord_ref[i + n] for n in range(GROUP)]
        spans = [span_ref[i + n] for n in range(GROUP)]
        found = [
            v + divergence(v, w_chord, half, 1) + divergence(v, w_span, half, 0)
            for v, w_chord, w_span, half in zip(values, chords, spans, halves)
        ]
        if i == 0:
            found[0] = found[0] + frames_ref[0]
        for n in range(0, GROUP, 2):
            put(i + n, jnp.concatenate(found[n : n + 2], axis=0))
    right = right_ref[...].reshape(3 * size, cols)
    adj = dot(mat_ref[...], right)
    for c in range(cols // 128):
        adj_ref[c * size : (c + 1) * size, :] = adj[:, c * 128 : (c + 1) * 128]

    for n, (after, _) in enumerate(sides()):
        row = jnp.where(after, rows - 1, 0)
        for c in range(cols // 128):
            edge_ref[n, :, c * 128 : (c + 1) * 128] = row_of_each(first_ref, c, depth, rows, row)
    for n, row in enumerate(far_rows(rows)):
        for c in range(cols // 128):
            two_ref[n, :, c * 128 : (c + 1) * 128] = row_of_each(adj_ref, c, depth, rows, row)
    for copy in copies:
        copy.wait()
    contribution_ref[...] = scale * (
        d_ref[0:1, 0:1] * f * excess_ref[2]
        + chunked(first_ref, 0, rows, size) * excess_ref[1]
        + chunked(adj_ref, 0, rows, size) * excess_ref[0]
    )


def correction(n, got, own, d_ref, edge_ref, pair_ref):
    _, depth, cols = edge_ref.shape
    _, inside = sides()[n]
    factor = d_ref[:, 0:1]
    half = 0.5 * packed_field(got, depth, cols, 0)
    half_next = 0.5 * packed_field(got, depth, cols, 1)
    f = packed_line(got, depth, cols, 0)
    frame = packed_line(got, depth, cols, 1)
    f_next = packed_line(got, depth, cols, 2)
    f_own = packed_line(own, depth, cols, 0)
    half_own = 0.5 * packed_field(own, depth, cols, 0)
    inner = half_own + 0.5 * packed_field(own, depth, cols, 1)
    w_next = half_own + shift_next(half_own, 1)
    w_prev = half_own + shift_prev(half_own, 1, 0.0)
    face = half + half_own
    moved = (
        f
        + (half + shift_next(half, 1)) * (shift_next(f, 1) - f)
        + (half + shift_prev(half, 1, 0.0)) * (shift_prev(f, 1, 0.0) - f)
        + (half + half_next) * (f_next - f)
        + face * (f_own - f)
    )
    outer = factor * moved + jnp.where(iota((depth, 1), 0) == 0, frame, 0.0)
    sources = [factor * (face * f - half * f_own), jnp.where(inside, outer, 0.0)]
    found = dot(pair_ref[...], right_three(jnp.concatenate(sources, axis=0)))
    e = found[0:depth]
    outer = found[depth:]
    change = (
        (1.0 - (w_next + w_prev) - (half_own + inner)) * e
        + w_next * shift_next(e, 1)
        + w_prev * shift_prev(e, 1, 0.0)
        + face * outer
        - half * (e + edge_ref[n])
    )
    return right_three(jnp.concatenate([change, inner * e], axis=0)), e[0:1, :]


def add_segments(total, contribution, picked_rows, map_ref):
    owners, _, lanes = total.shape
    shape = (owners, 128)
    lane = iota(shape, 1)
    segment = jnp.where(lane < lanes, iota(shape, 0) * lanes + lane, -1)
    found = jnp.zeros(shape, F32)
    for block in range(contribution.shape[1] // 128):
        part = contribution[:, block * 128 : (block + 1) * 128]
        sums = jnp.sum(part, axis=1, keepdims=True)
        for n, row in enumerate(picked_rows):
            found += jnp.where(segment == map_ref[block, row], sums[n : n + 1, :], 0.0)
    return total + found[:, None, :lanes]


def near_kernel(
    scale,
    d_ref,
    excess_ref,
    edge_ref,
    pair_ref,
    map_vmem,
    place_ref,
    base_ref,
    contribution_ref,
    own_ref,
    got_ref,
    adj_hbm,
    part_ref,
    adj_ref,
    map_ref,
    sems,
):
    map_copy = pltpu.make_async_copy(map_vmem, map_ref, sems.at[0])
    map_copy.start()
    depth, rows, cols = adj_ref.shape
    size = depth * rows
    sources, surface = correction(0, got_ref, own_ref, d_ref, edge_ref, pair_ref)
    found = dot(place_ref[...], sources)
    adj_ref[...] = (chunked(base_ref, 0, size, size) + found).reshape(depth, rows, cols)
    adj_copy = pltpu.make_async_copy(adj_ref, adj_hbm, sems.at[1])
    adj_copy.start()
    row = jnp.where(sides()[0][0], rows - 1, 0)
    surface = jnp.where(iota((rows, cols), 0) == row, surface, 0.0)
    contribution = contribution_ref[...] + scale * (
        surface * excess_ref[1] + found[0:rows, :] * excess_ref[0]
    )
    map_copy.wait()
    part_ref[...] = add_segments(
        jnp.zeros(part_ref.shape, F32), contribution, range(rows), map_ref
    )
    adj_copy.wait()


def far_kernel(
    scale,
    own_ref,
    got_ref,
    d_ref,
    excess_ref,
    edge_ref,
    pair_ref,
    map_vmem,
    two_ref,
    part_in_ref,
    out_ref,
    part_ref,
    map_ref,
    map_sem,
):
    map_copy = pltpu.make_async_copy(map_vmem, map_ref, map_sem)
    map_copy.start()
    depth = two_ref.shape[1]
    rows = excess_ref.shape[1]
    sources, surface = correction(1, got_ref, own_ref, d_ref, edge_ref, pair_ref)
    found = dot(pair_ref[...], sources)
    edge, second = far_rows(rows)
    contribution = scale * jnp.concatenate(
        [
            surface * excess_ref[1, pl.ds(edge, 1), :]
            + found[0:1] * excess_ref[0, pl.ds(edge, 1), :],
            found[depth : depth + 1] * excess_ref[0, pl.ds(second, 1), :],
        ],
        axis=0,
    )
    map_copy.wait()
    part_ref[...] = add_segments(part_in_ref[...], contribution, (edge, second), map_ref)
    out_ref[...] = two_ref[...] + found.reshape(two_ref.shape)


def finish_kernel(_, two_ref, got_ref, adj_hbm, out_hbm, out_ref, sems):
    copies = []
    for n, row in enumerate(far_rows(adj_hbm.shape[1])):
        copies.append(pltpu.make_async_copy(two_ref.at[n], adj_hbm.at[:, row, :], sems.at[n]))
        copies[-1].start()
    out_ref[...] = jnp.sum(got_ref[:, 0, :], axis=0)
    copies.append(pltpu.make_async_copy(out_ref, out_hbm, sems.at[2]))
    copies[-1].start()
    for copy in copies:
        copy.wait()


def in_hbm(x):
    return pltpu.with_memory_space_constraint(x, pltpu.HBM)


def per_device(
    conductance, depth_inverse, surface_residual, surface_excess, segment_map, frame_index
):
    _, depth, rows, cols = conductance.shape
    frames = surface_residual.shape[1]
    blocks = segment_map.shape[1]
    size = depth * rows
    spans = lax.axis_size("span")
    devices = spans * lax.axis_size("blade")
    lanes = SEGS // devices
    field = pltpu.VMEM((depth, rows, cols), F32)
    chunks = cols // 128
    packed_far = pltpu.VMEM(((2 * depth + 4) * chunks, 128), F32)
    packed_near = pltpu.VMEM(((2 * depth + 3) * chunks, 128), F32)
    own_far, index, inverse = pl.pallas_call(
        load_kernel,
        out_shape=(
            packed_far,
            pltpu.VMEM((STEPS, 128), jnp.int32),
            pltpu.VMEM((depth, depth), F32),
        ),
        in_specs=[HBM] * 4,
        out_specs=(VMEM,) * 3,
        scratch_shapes=[
            pltpu.SMEM((STEPS,), jnp.int32),
            pltpu.VMEM((frames, rows, cols), F32),
            pltpu.VMEM((depth, 8, cols), F32),
            pltpu.SemaphoreType.DMA((4,)),
        ],
        compiler_params=GRANT,
        name="load",
    )(
        in_hbm(frame_index),
        in_hbm(conductance[0]),
        in_hbm(surface_residual[0]),
        in_hbm(depth_inverse[0]),
    )
    k = conductance[0]
    own_near, picked = pl.pallas_call(
        pack_kernel,
        out_shape=(packed_near, pltpu.VMEM((STEPS, rows, cols), F32)),
        in_specs=[VMEM] * 3,
        out_specs=(VMEM,) * 2,
        compiler_params=GRANT,
        name="pack",
    )(k, surface_residual[0], index)
    across = [(i, i + 1) for i in range(1, spans - 1, 2)]
    within = [(i, i + 1) for i in range(0, spans - 1, 2)]
    near = lax.ppermute(own_near, "span", within + [(b, a) for a, b in within])
    far = lax.ppermute(own_far, "span", across + [(b, a) for a, b in across])
    scale = 1.0 / math.sqrt(128.0 * STEPS)
    line = pltpu.VMEM((rows, cols), F32)
    base, two, excess, ids, edge, contribution, pair, place = pl.pallas_call(
        functools.partial(base_kernel, scale),
        out_shape=(
            pltpu.VMEM((chunks * size, 128), F32),
            pltpu.VMEM((2, depth, cols), F32),
            pltpu.VMEM((STEPS, rows, cols), F32),
            pltpu.VMEM((blocks, rows), jnp.int32),
            pltpu.VMEM((2, depth, cols), F32),
            line,
            pltpu.VMEM((2 * depth, 6 * depth), BF16),
            pltpu.VMEM((size, 6 * depth), BF16),
        ),
        in_specs=[VMEM] * 3 + [HBM] * 2,
        out_specs=(VMEM,) * 8,
        scratch_shapes=[
            pltpu.VMEM((size, 3 * size), BF16),
            pltpu.VMEM((3, size, cols), BF16),
            pltpu.VMEM((chunks * size, 128), F32),
            field,
            field,
            pltpu.VMEM((depth, 128), F32),
            pltpu.SemaphoreType.DMA((2,)),
        ],
        compiler_params=GRANT,
        name="base",
    )(k, picked, inverse, in_hbm(surface_excess[0]), in_hbm(segment_map.T))
    fixed = (inverse, excess, edge, pair, ids)
    sums = pltpu.VMEM((devices, 1, lanes), F32)
    adjoint, partial = pl.pallas_call(
        functools.partial(near_kernel, scale),
        out_shape=(pltpu.HBM((depth, rows, cols), F32), sums),
        in_specs=[VMEM] * 10,
        out_specs=(HBM, VMEM),
        scratch_shapes=[
            field,
            pltpu.SMEM((blocks, rows), jnp.int32),
            pltpu.SemaphoreType.DMA((2,)),
        ],
        compiler_params=GRANT,
        name="near",
    )(*fixed, place, base, contribution, own_near, near)
    two, partial = pl.pallas_call(
        functools.partial(far_kernel, scale),
        out_shape=(pltpu.VMEM((2, depth, cols), F32), sums),
        in_specs=[VMEM] * 9,
        out_specs=(VMEM,) * 2,
        scratch_shapes=[pltpu.SMEM((blocks, rows), jnp.int32), pltpu.SemaphoreType.DMA],
        compiler_params=GRANT,
        name="far",
    )(own_far, far, *fixed, two, partial)
    pieces = lax.all_to_all(partial, ("blade", "span"), 0, 0, tiled=True)
    adjoint, owned = pl.pallas_call(
        finish_kernel,
        out_shape=(pltpu.HBM((depth, rows, cols), F32), pltpu.HBM((lanes,), F32)),
        in_specs=[HBM, VMEM, VMEM],
        out_specs=(HBM,) * 2,
        scratch_shapes=[pltpu.VMEM((lanes,), F32), pltpu.SemaphoreType.DMA((3,))],
        input_output_aliases={0: 0},
        compiler_params=GRANT,
        name="finish",
    )(in_hbm(adjoint), two, pltpu.with_memory_space_constraint(pieces, pltpu.VMEM))
    return (adjoint[None], owned)


def solution(mesh):
    placed = (
        P("blade", None, "span", None),
        P("blade", None, None),
        P("blade", None, "span", None),
        P("blade", None, "span", None),
        P("span", None),
        P(),
    )
    return jax.shard_map(
        per_device,
        mesh=mesh,
        in_specs=placed,
        out_specs=(P("blade", None, "span", None), P(("blade", "span"))),
        check_vma=False,
    )
```

```python
import functools
import math

import jax
import jax.numpy as jnp
from jax import lax
from jax.experimental import pallas as pl
from jax.experimental.pallas import tpu as pltpu
from jax.sharding import PartitionSpec as P

STEPS = 3
SEGS = 2048
GROUP = 2
F32 = jnp.float32
BF16 = jnp.bfloat16
VMEM = pl.BlockSpec(memory_space=pltpu.VMEM)
HBM = pl.BlockSpec(memory_space=pltpu.HBM)
GRANT = pltpu.CompilerParams(vmem_limit_bytes=16 * 2**20)


def split(x):
    high = x.astype(BF16)
    return high, (x - high.astype(F32)).astype(BF16)


def dot(a, b):
    return jnp.dot(a, b, preferred_element_type=F32)


def left_three(matrix):
    high, low = matrix
    return jnp.concatenate([high, low, high], axis=1)


def right_three(x):
    high, low = split(x)
    return jnp.concatenate([high, high, low], axis=0)


def iota(shape, dim):
    return lax.broadcasted_iota(jnp.int32, shape, dim)


def shift_next(x, axis):
    size = x.shape[axis]
    return jnp.where(iota(x.shape, axis) == size - 1, 0.0, pltpu.roll(x, size - 1, axis))


def shift_prev(x, axis, first):
    return jnp.where(iota(x.shape, axis) == 0, first, pltpu.roll(x, 1, axis))


def divergence(v, weight, half, axis):
    flux = weight * (shift_next(v, axis) - v)
    return flux - shift_prev(flux, axis, half * v)


def sides():
    span = lax.axis_index("span")
    count = lax.axis_size("span")
    even = lax.rem(span, 2) == 0
    has_next = span + 1 < count
    has_prev = span > 0
    return (
        (even, jnp.where(even, has_next, has_prev)),
        (jnp.logical_not(even), jnp.where(even, has_prev, has_next)),
    )


def chunked(ref, start, count, step):
    chunks = ref.shape[0] // step
    return jnp.concatenate(
        [ref[c * step + start : c * step + start + count, :] for c in range(chunks)], axis=1
    )


def packed_field(ref, depth, cols, n):
    chunks = cols // 128
    return chunked(ref.at[n * chunks * depth : (n + 1) * chunks * depth], 0, depth, depth)


def packed_line(ref, depth, cols, n):
    chunks = cols // 128
    base = (2 * depth + n) * chunks
    return chunked(ref.at[base : base + chunks], 0, 1, 1)


def row_of_each(ref, chunk, depth, rows, row):
    return ref[pl.ds(chunk * depth * rows + row, depth, stride=rows), :]


def far_rows(rows):
    after = sides()[1][0]
    return jnp.where(after, rows - 1, 0), jnp.where(after, rows - 2, 1)


def put_lines(ref, frames_ref, depth, rows, after):
    chunks = frames_ref.shape[2] // 128
    base = 2 * chunks * depth
    edge, second = jnp.where(after, rows - 1, 0), jnp.where(after, rows - 2, 1)
    for n, (frame, row) in enumerate(((2, edge), (1, edge), (2, second))):
        line = frames_ref[frame, pl.ds(row, 1), :]
        for c in range(chunks):
            spot = base + n * chunks + c
            ref[spot : spot + 1, :] = line[:, c * 128 : (c + 1) * 128]
    if ref.shape[0] > base + 3 * chunks:
        ref[base + 3 * chunks :, :] = jnp.zeros((ref.shape[0] - base - 3 * chunks, 128), F32)


def put_rows(ref, depth, items):
    for which, x in enumerate(items):
        for c in range(x.shape[1] // 128):
            spot = (which * (x.shape[1] // 128) + c) * depth
            ref[spot : spot + depth, :] = x[:, c * 128 : (c + 1) * 128]


def load_kernel(
    frame_hbm,
    k_hbm,
    res_hbm,
    d_hbm,
    far_ref,
    frames_ref,
    d_ref,
    frame_ref,
    res_ref,
    edge_ref,
    sems,
):
    depth, rows, cols = k_hbm.shape
    after = sides()[1][0]
    first = jnp.where(after, rows - 2, 0)
    pairs = (
        (frame_hbm, frame_ref),
        (res_hbm, res_ref),
        (k_hbm.at[:, pl.ds(first, 2), :], edge_ref.at[:, 0:2, :]),
        (d_hbm, d_ref),
    )
    copies = [pltpu.make_async_copy(a, b, sems.at[n]) for n, (a, b) in enumerate(pairs)]
    for copy in copies:
        copy.start()
    copies[0].wait()
    copies[1].wait()
    for n in range(STEPS):
        frames_ref[n] = res_ref[frame_ref[n]]
    put_lines(far_ref, frames_ref, depth, rows, after)
    copies[2].wait()
    low, high = edge_ref[:, 0, :], edge_ref[:, 1, :]
    put_rows(far_ref, depth, (jnp.where(after, high, low), jnp.where(after, low, high)))
    copies[3].wait()


def pack_kernel(k_ref, frames_ref, near_ref):
    depth, rows, _ = k_ref.shape
    after = sides()[0][0]
    put_lines(near_ref, frames_ref, depth, rows, after)
    items = []
    for first, last in ((0, rows - 1), (1, rows - 2)):
        items.append(jnp.where(after, k_ref[:, last, :], k_ref[:, first, :]))
    put_rows(near_ref, depth, items)


def base_kernel(
    scale,
    k_ref,
    frames_ref,
    d_ref,
    excess_hbm,
    map_hbm,
    adj_ref,
    two_ref,
    excess_ref,
    map_ref,
    edge_ref,
    contribution_ref,
    pair_ref,
    place_ref,
    mat_ref,
    right_ref,
    first_ref,
    chord_ref,
    span_ref,
    factor_ref,
    sems,
):
    copies = [
        pltpu.make_async_copy(excess_hbm, excess_ref, sems.at[0]),
        pltpu.make_async_copy(map_hbm, map_ref, sems.at[1]),
    ]
    for copy in copies:
        copy.start()
    depth, rows, cols = chord_ref.shape
    size = depth * rows
    factor_ref[...] = jnp.broadcast_to(d_ref[:, 0:1], factor_ref.shape)

    parts = split(d_ref[...])
    tall = (iota((size, depth), 0) // rows == iota((size, depth), 1)).astype(BF16)
    wide = (iota((depth, size), 0) == iota((depth, size), 1) // rows).astype(BF16)
    two = 2 * depth
    tile = (iota((depth, two), 0) == iota((depth, two), 1) % depth).astype(BF16)
    same = iota((size, size), 0) % rows == iota((size, size), 1) % rows
    pair_same = iota((two, two), 0) // depth == iota((two, two), 1) // depth
    row_of = iota((size, two), 0) % rows
    first_half = iota((size, two), 1) < depth
    after = sides()[0][0]
    edge = jnp.where(after, rows - 1, 0)
    second = jnp.where(after, rows - 2, 1)
    placed = row_of == jnp.where(first_half, edge, second)
    mats, pairs, places = [], [], []
    for part in parts:
        column = dot(tall, part).astype(BF16)
        row = dot(part, tile)
        mats.append(jnp.where(same, dot(column, wide), 0.0).astype(BF16))
        places.append(jnp.where(placed, dot(column, tile), 0.0).astype(BF16))
        pairs.append(
            jnp.where(pair_same, jnp.concatenate([row] * 2, axis=0), 0.0).astype(BF16)
        )
    mat_ref[...] = left_three(mats)
    pair_ref[...] = left_three(pairs)
    place_ref[...] = left_three(places)

    f = frames_ref[2]
    f_chord = shift_next(f, 1) - f
    f_span = shift_next(f, 0) - f

    def put(i, both):
        high, low = split(both)
        span = pl.ds(i * rows, 2 * rows)
        right_ref[0, span, :] = high
        right_ref[1, span, :] = high
        right_ref[2, span, :] = low

    def lines_of(ref, i):
        return [chunked(ref, j * rows, rows, size) for j in range(i, i + GROUP)]

    for i in range(0, depth, GROUP):
        halves = [0.5 * k_ref[i + n] for n in range(GROUP)]
        factors = [jnp.broadcast_to(factor_ref[j : j + 1, :], (rows, 128)) for j in range(i, i + GROUP)]
        chords = [half + shift_next(half, 1) for half in halves]
        spans = [half + shift_next(half, 0) for half in halves]
        found = []
        for half, factor, w_chord, w_span in zip(halves, factors, chords, spans):
            edge = half * f
            flux_chord = w_chord * f_chord
            flux_span = w_span * f_span
            moved = f + flux_chord - shift_prev(flux_chord, 1, edge)
            moved = moved + flux_span - shift_prev(flux_span, 0, edge)
            found.append(jnp.concatenate([factor] * (cols // 128), axis=1) * moved)
        if i == 0:
            found[0] = found[0] + frames_ref[1]
        for n in range(GROUP):
            chord_ref[i + n] = chords[n]
            span_ref[i + n] = spans[n]
        for n in range(0, GROUP, 2):
            put(i + n, jnp.concatenate(found[n : n + 2], axis=0))
    right = right_ref[...].reshape(3 * size, cols)
    first = dot(mat_ref[...], right)
    for c in range(cols // 128):
        first_ref[c * size : (c + 1) * size, :] = first[:, c * 128 : (c + 1) * 128]

    for i in range(0, depth, GROUP):
        halves = [0.5 * k_ref[i + n] for n in range(GROUP)]
        values = lines_of(first_ref, i)
        chords = [chord_ref[i + n] for n in range(GROUP)]
        spans = [span_ref[i + n] for n in range(GROUP)]
        found = [
            v + divergence(v, w_chord, half, 1) + divergence(v, w_span, half, 0)
            for v, w_chord, w_span, half in zip(values, chords, spans, halves)
        ]
        if i == 0:
            found[0] = found[0] + frames_ref[0]
        for n in range(0, GROUP, 2):
            put(i + n, jnp.concatenate(found[n : n + 2], axis=0))
    right = right_ref[...].reshape(3 * size, cols)
    adj = dot(mat_ref[...], right)
    for c in range(cols // 128):
        adj_ref[c * size : (c + 1) * size, :] = adj[:, c * 128 : (c + 1) * 128]

    for n, (after, _) in enumerate(sides()):
        row = jnp.where(after, rows - 1, 0)
        for c in range(cols // 128):
            edge_ref[n, :, c * 128 : (c + 1) * 128] = row_of_each(first_ref, c, depth, rows, row)
    for n, row in enumerate(far_rows(rows)):
        for c in range(cols // 128):
            two_ref[n, :, c * 128 : (c + 1) * 128] = row_of_each(adj_ref, c, depth, rows, row)
    for copy in copies:
        copy.wait()
    contribution_ref[...] = scale * (
        d_ref[0:1, 0:1] * f * excess_ref[2]
        + chunked(first_ref, 0, rows, size) * excess_ref[1]
        + chunked(adj_ref, 0, rows, size) * excess_ref[0]
    )


def own_weights(own, depth, cols):
    half = 0.5 * packed_field(own, depth, cols, 0)
    inner = half + 0.5 * packed_field(own, depth, cols, 1)
    w_next = half + shift_next(half, 1)
    w_prev = half + shift_prev(half, 1, 0.0)
    return half, inner, w_next, w_prev, 1.0 - (w_next + w_prev) - (half + inner)


def correction(n, got, own, weights, d_ref, edge_ref, pair_ref):
    _, depth, cols = edge_ref.shape
    _, inside = sides()[n]
    factor = d_ref[:, 0:1]
    half = 0.5 * packed_field(got, depth, cols, 0)
    half_next = 0.5 * packed_field(got, depth, cols, 1)
    f = packed_line(got, depth, cols, 0)
    frame = packed_line(got, depth, cols, 1)
    f_next = packed_line(got, depth, cols, 2)
    f_own = packed_line(own, depth, cols, 0)
    half_own, inner, w_next, w_prev, centre = weights
    face = half + half_own
    moved = (
        f
        + (half + shift_next(half, 1)) * (shift_next(f, 1) - f)
        + (half + shift_prev(half, 1, 0.0)) * (shift_prev(f, 1, 0.0) - f)
        + (half + half_next) * (f_next - f)
        + face * (f_own - f)
    )
    outer = factor * moved + jnp.where(iota((depth, 1), 0) == 0, frame, 0.0)
    sources = [factor * (face * f - half * f_own), jnp.where(inside, outer, 0.0)]
    found = dot(pair_ref[...], right_three(jnp.concatenate(sources, axis=0)))
    e = found[0:depth]
    outer = found[depth:]
    change = (
        centre * e
        + w_next * shift_next(e, 1)
        + w_prev * shift_prev(e, 1, 0.0)
        + face * outer
        - half * (e + edge_ref[n])
    )
    return right_three(jnp.concatenate([change, inner * e], axis=0)), e[0:1, :]


def add_segments(total, contribution, picked_rows, map_ref):
    owners, _, lanes = total.shape
    shape = (owners, 128)
    lane = iota(shape, 1)
    segment = jnp.where(lane < lanes, iota(shape, 0) * lanes + lane, -1)
    found = jnp.zeros(shape, F32)
    for block in range(contribution.shape[1] // 128):
        part = contribution[:, block * 128 : (block + 1) * 128]
        sums = jnp.sum(part, axis=1, keepdims=True)
        for n, row in enumerate(picked_rows):
            found += jnp.where(segment == map_ref[block, row], sums[n : n + 1, :], 0.0)
    return total + found[:, None, :lanes]


def near_kernel(
    scale,
    d_ref,
    excess_ref,
    edge_ref,
    pair_ref,
    map_vmem,
    place_ref,
    base_ref,
    contribution_ref,
    own_far_ref,
    own_ref,
    got_ref,
    adj_hbm,
    part_ref,
    far_weights_ref,
    adj_ref,
    map_ref,
    sems,
):
    map_copy = pltpu.make_async_copy(map_vmem, map_ref, sems.at[0])
    map_copy.start()
    depth, rows, cols = adj_ref.shape
    size = depth * rows
    sources, surface = correction(
        0, got_ref, own_ref, own_weights(own_ref, depth, cols), d_ref, edge_ref, pair_ref
    )
    found = dot(place_ref[...], sources)
    adj_ref[...] = (chunked(base_ref, 0, size, size) + found).reshape(depth, rows, cols)
    adj_copy = pltpu.make_async_copy(adj_ref, adj_hbm, sems.at[1])
    adj_copy.start()
    row = jnp.where(sides()[0][0], rows - 1, 0)
    surface = jnp.where(iota((rows, cols), 0) == row, surface, 0.0)
    contribution = contribution_ref[...] + scale * (
        surface * excess_ref[1] + found[0:rows, :] * excess_ref[0]
    )
    for n, x in enumerate(own_weights(own_far_ref, depth, cols)):
        far_weights_ref[n] = x
    map_copy.wait()
    part_ref[...] = add_segments(
        jnp.zeros(part_ref.shape, F32), contribution, range(rows), map_ref
    )
    adj_copy.wait()


def far_kernel(
    scale,
    own_ref,
    got_ref,
    d_ref,
    excess_ref,
    edge_ref,
    pair_ref,
    map_vmem,
    far_weights_ref,
    two_ref,
    part_in_ref,
    out_ref,
    part_ref,
    map_ref,
    map_sem,
):
    map_copy = pltpu.make_async_copy(map_vmem, map_ref, map_sem)
    map_copy.start()
    depth = two_ref.shape[1]
    rows = excess_ref.shape[1]
    sources, surface = correction(
        1, got_ref, own_ref, [far_weights_ref[n] for n in range(5)], d_ref, edge_ref, pair_ref
    )
    found = dot(pair_ref[...], sources)
    edge, second = far_rows(rows)
    contribution = scale * jnp.concatenate(
        [
            surface * excess_ref[1, pl.ds(edge, 1), :]
            + found[0:1] * excess_ref[0, pl.ds(edge, 1), :],
            found[depth : depth + 1] * excess_ref[0, pl.ds(second, 1), :],
        ],
        axis=0,
    )
    map_copy.wait()
    part_ref[...] = add_segments(part_in_ref[...], contribution, (edge, second), map_ref)
    after = sides()[1][0]
    new_edge = two_ref[0] + found[0:depth]
    new_second = two_ref[1] + found[depth:]
    out_ref[:, 0, :] = jnp.where(after, new_second, new_edge)
    out_ref[:, 1, :] = jnp.where(after, new_edge, new_second)


def finish_kernel(_, two_ref, got_ref, adj_hbm, out_hbm, out_ref, sems):
    first = jnp.where(sides()[1][0], adj_hbm.shape[1] - 2, 0)
    copies = [
        pltpu.make_async_copy(
            two_ref.at[:, 0:2, :], adj_hbm.at[:, pl.ds(first, 2), :], sems.at[0]
        )
    ]
    copies[0].start()
    out_ref[...] = jnp.sum(got_ref[:, 0, :], axis=0)
    copies.append(pltpu.make_async_copy(out_ref, out_hbm, sems.at[1]))
    copies[-1].start()
    for copy in copies:
        copy.wait()


def in_hbm(x):
    return pltpu.with_memory_space_constraint(x, pltpu.HBM)


def per_device(
    conductance, depth_inverse, surface_residual, surface_excess, segment_map, frame_index
):
    _, depth, rows, cols = conductance.shape
    frames = surface_residual.shape[1]
    blocks = segment_map.shape[1]
    size = depth * rows
    spans = lax.axis_size("span")
    devices = spans * lax.axis_size("blade")
    lanes = SEGS // devices
    field = pltpu.VMEM((depth, rows, cols), F32)
    chunks = cols // 128
    packed_far = pltpu.VMEM(((2 * depth + 4) * chunks, 128), F32)
    packed_near = pltpu.VMEM(((2 * depth + 3) * chunks, 128), F32)
    own_far, picked, inverse = pl.pallas_call(
        load_kernel,
        out_shape=(
            packed_far,
            pltpu.VMEM((STEPS, rows, cols), F32),
            pltpu.VMEM((depth, depth), F32),
        ),
        in_specs=[HBM] * 4,
        out_specs=(VMEM,) * 3,
        scratch_shapes=[
            pltpu.SMEM((STEPS,), jnp.int32),
            pltpu.VMEM((frames, rows, cols), F32),
            pltpu.VMEM((depth, 8, cols), F32),
            pltpu.SemaphoreType.DMA((4,)),
        ],
        compiler_params=GRANT,
        name="load",
    )(
        in_hbm(frame_index),
        in_hbm(conductance[0]),
        in_hbm(surface_residual[0]),
        in_hbm(depth_inverse[0]),
    )
    k = conductance[0]
    own_near = pl.pallas_call(
        pack_kernel,
        out_shape=packed_near,
        in_specs=[VMEM] * 2,
        out_specs=VMEM,
        compiler_params=GRANT,
        name="pack",
    )(k, picked)
    across = [(i, i + 1) for i in range(1, spans - 1, 2)]
    within = [(i, i + 1) for i in range(0, spans - 1, 2)]
    near = lax.ppermute(own_near, "span", within + [(b, a) for a, b in within])
    far = lax.ppermute(own_far, "span", across + [(b, a) for a, b in across])
    scale = 1.0 / math.sqrt(128.0 * STEPS)
    line = pltpu.VMEM((rows, cols), F32)
    base, two, excess, ids, edge, contribution, pair, place = pl.pallas_call(
        functools.partial(base_kernel, scale),
        out_shape=(
            pltpu.VMEM((chunks * size, 128), F32),
            pltpu.VMEM((2, depth, cols), F32),
            pltpu.VMEM((STEPS, rows, cols), F32),
            pltpu.VMEM((blocks, rows), jnp.int32),
            pltpu.VMEM((2, depth, cols), F32),
            line,
            pltpu.VMEM((2 * depth, 6 * depth), BF16),
            pltpu.VMEM((size, 6 * depth), BF16),
        ),
        in_specs=[VMEM] * 3 + [HBM] * 2,
        out_specs=(VMEM,) * 8,
        scratch_shapes=[
            pltpu.VMEM((size, 3 * size), BF16),
            pltpu.VMEM((3, size, cols), BF16),
            pltpu.VMEM((chunks * size, 128), F32),
            field,
            field,
            pltpu.VMEM((depth, 128), F32),
            pltpu.SemaphoreType.DMA((2,)),
        ],
        compiler_params=GRANT,
        name="base",
    )(k, picked, inverse, in_hbm(surface_excess[0]), in_hbm(segment_map.T))
    fixed = (inverse, excess, edge, pair, ids)
    sums = pltpu.VMEM((devices, 1, lanes), F32)
    adjoint, partial, far_weights = pl.pallas_call(
        functools.partial(near_kernel, scale),
        out_shape=(
            pltpu.HBM((depth, rows, cols), F32),
            sums,
            pltpu.VMEM((5, depth, cols), F32),
        ),
        in_specs=[VMEM] * 11,
        out_specs=(HBM, VMEM, VMEM),
        scratch_shapes=[
            field,
            pltpu.SMEM((blocks, rows), jnp.int32),
            pltpu.SemaphoreType.DMA((2,)),
        ],
        compiler_params=GRANT,
        name="near",
    )(*fixed, place, base, contribution, own_far, own_near, near)
    two, partial = pl.pallas_call(
        functools.partial(far_kernel, scale),
        out_shape=(field, sums),
        in_specs=[VMEM] * 10,
        out_specs=(VMEM,) * 2,
        scratch_shapes=[pltpu.SMEM((blocks, rows), jnp.int32), pltpu.SemaphoreType.DMA],
        compiler_params=GRANT,
        name="far",
    )(own_far, far, *fixed, far_weights, two, partial)
    pieces = lax.all_to_all(partial, ("blade", "span"), 0, 0, tiled=True)
    adjoint, owned = pl.pallas_call(
        finish_kernel,
        out_shape=(pltpu.HBM((depth, rows, cols), F32), pltpu.HBM((lanes,), F32)),
        in_specs=[HBM, VMEM, VMEM],
        out_specs=(HBM,) * 2,
        scratch_shapes=[pltpu.VMEM((lanes,), F32), pltpu.SemaphoreType.DMA((2,))],
        input_output_aliases={0: 0},
        compiler_params=GRANT,
        name="finish",
    )(in_hbm(adjoint), two, pltpu.with_memory_space_constraint(pieces, pltpu.VMEM))
    return (adjoint[None], owned)


def solution(mesh):
    placed = (
        P("blade", None, "span", None),
        P("blade", None, None),
        P("blade", None, "span", None),
        P("blade", None, "span", None),
        P("span", None),
        P(),
    )
    return jax.shard_map(
        per_device,
        mesh=mesh,
        in_specs=placed,
        out_specs=(P("blade", None, "span", None), P(("blade", "span"))),
        check_vma=False,
    )
```

```python
import functools
import math

import jax
import jax.numpy as jnp
from jax import lax
from jax.experimental import pallas as pl
from jax.experimental.pallas import tpu as pltpu
from jax.sharding import PartitionSpec as P

STEPS = 3
SEGS = 2048
GROUP = 2
F32 = jnp.float32
BF16 = jnp.bfloat16
VMEM = pl.BlockSpec(memory_space=pltpu.VMEM)
HBM = pl.BlockSpec(memory_space=pltpu.HBM)
GRANT = pltpu.CompilerParams(vmem_limit_bytes=16 * 2**20)


def split(x):
    high = x.astype(BF16)
    return high, (x - high.astype(F32)).astype(BF16)


def dot(a, b):
    return jnp.dot(a, b, preferred_element_type=F32)


def left_three(matrix):
    high, low = matrix
    return jnp.concatenate([high, low, high], axis=1)


def right_three(x):
    high, low = split(x)
    return jnp.concatenate([high, high, low], axis=0)


def iota(shape, dim):
    return lax.broadcasted_iota(jnp.int32, shape, dim)


def shift_next(x, axis):
    size = x.shape[axis]
    return jnp.where(iota(x.shape, axis) == size - 1, 0.0, pltpu.roll(x, size - 1, axis))


def shift_prev(x, axis, first):
    return jnp.where(iota(x.shape, axis) == 0, first, pltpu.roll(x, 1, axis))


def divergence(v, weight, half, axis):
    flux = weight * (shift_next(v, axis) - v)
    return flux - shift_prev(flux, axis, half * v)


def sides():
    span = lax.axis_index("span")
    count = lax.axis_size("span")
    even = lax.rem(span, 2) == 0
    has_next = span + 1 < count
    has_prev = span > 0
    return (
        (even, jnp.where(even, has_next, has_prev)),
        (jnp.logical_not(even), jnp.where(even, has_prev, has_next)),
    )


def chunked(ref, start, count, step):
    chunks = ref.shape[0] // step
    return jnp.concatenate(
        [ref[c * step + start : c * step + start + count, :] for c in range(chunks)], axis=1
    )


def packed_field(ref, depth, cols, n):
    chunks = cols // 128
    return chunked(ref.at[n * chunks * depth : (n + 1) * chunks * depth], 0, depth, depth)


def packed_line(ref, depth, cols, n):
    chunks = cols // 128
    base = (2 * depth + n) * chunks
    return chunked(ref.at[base : base + chunks], 0, 1, 1)


def row_of_each(ref, chunk, depth, rows, row):
    return ref[pl.ds(chunk * depth * rows + row, depth, stride=rows), :]


def far_rows(rows):
    after = sides()[1][0]
    return jnp.where(after, rows - 1, 0), jnp.where(after, rows - 2, 1)


def put_lines(ref, frames_ref, depth, rows, after):
    chunks = frames_ref.shape[2] // 128
    base = 2 * chunks * depth
    edge, second = jnp.where(after, rows - 1, 0), jnp.where(after, rows - 2, 1)
    for n, (frame, row) in enumerate(((2, edge), (1, edge), (2, second))):
        line = frames_ref[frame, pl.ds(row, 1), :]
        for c in range(chunks):
            spot = base + n * chunks + c
            ref[spot : spot + 1, :] = line[:, c * 128 : (c + 1) * 128]
    if ref.shape[0] > base + 3 * chunks:
        ref[base + 3 * chunks :, :] = jnp.zeros((ref.shape[0] - base - 3 * chunks, 128), F32)


def put_rows(ref, depth, items):
    for which, x in enumerate(items):
        for c in range(x.shape[1] // 128):
            spot = (which * (x.shape[1] // 128) + c) * depth
            ref[spot : spot + depth, :] = x[:, c * 128 : (c + 1) * 128]


def load_kernel(
    frame_hbm,
    k_hbm,
    res_hbm,
    d_hbm,
    far_ref,
    frames_ref,
    d_ref,
    frame_ref,
    res_ref,
    edge_ref,
    sems,
):
    depth, rows, cols = k_hbm.shape
    after = sides()[1][0]
    first = jnp.where(after, rows - 2, 0)
    pairs = (
        (frame_hbm, frame_ref),
        (res_hbm, res_ref),
        (k_hbm.at[:, pl.ds(first, 2), :], edge_ref.at[:, 0:2, :]),
        (d_hbm, d_ref),
    )
    copies = [pltpu.make_async_copy(a, b, sems.at[n]) for n, (a, b) in enumerate(pairs)]
    for copy in copies:
        copy.start()
    copies[0].wait()
    copies[1].wait()
    for n in range(STEPS):
        frames_ref[n] = res_ref[frame_ref[n]]
    put_lines(far_ref, frames_ref, depth, rows, after)
    copies[2].wait()
    low, high = edge_ref[:, 0, :], edge_ref[:, 1, :]
    put_rows(far_ref, depth, (jnp.where(after, high, low), jnp.where(after, low, high)))
    copies[3].wait()


def pack_kernel(k_ref, frames_ref, near_ref):
    depth, rows, _ = k_ref.shape
    after = sides()[0][0]
    put_lines(near_ref, frames_ref, depth, rows, after)
    items = []
    for first, last in ((0, rows - 1), (1, rows - 2)):
        items.append(jnp.where(after, k_ref[:, last, :], k_ref[:, first, :]))
    put_rows(near_ref, depth, items)


def base_kernel(
    scale,
    k_ref,
    frames_ref,
    d_ref,
    excess_hbm,
    map_hbm,
    adj_ref,
    two_ref,
    excess_ref,
    map_ref,
    edge_ref,
    contribution_ref,
    pair_ref,
    place_ref,
    mat_ref,
    right_ref,
    first_ref,
    chord_ref,
    span_ref,
    factor_ref,
    sems,
):
    copies = [
        pltpu.make_async_copy(excess_hbm, excess_ref, sems.at[0]),
        pltpu.make_async_copy(map_hbm, map_ref, sems.at[1]),
    ]
    for copy in copies:
        copy.start()
    depth, rows, cols = chord_ref.shape
    size = depth * rows
    factor_ref[...] = jnp.broadcast_to(d_ref[:, 0:1], factor_ref.shape)

    parts = split(d_ref[...])
    tall = (iota((size, depth), 0) // rows == iota((size, depth), 1)).astype(BF16)
    wide = (iota((depth, size), 0) == iota((depth, size), 1) // rows).astype(BF16)
    two = 2 * depth
    tile = (iota((depth, two), 0) == iota((depth, two), 1) % depth).astype(BF16)
    same = iota((size, size), 0) % rows == iota((size, size), 1) % rows
    pair_same = iota((two, two), 0) // depth == iota((two, two), 1) // depth
    row_of = iota((size, two), 0) % rows
    first_half = iota((size, two), 1) < depth
    after = sides()[0][0]
    edge = jnp.where(after, rows - 1, 0)
    second = jnp.where(after, rows - 2, 1)
    placed = row_of == jnp.where(first_half, edge, second)
    mats, pairs, places = [], [], []
    for part in parts:
        column = dot(tall, part).astype(BF16)
        row = dot(part, tile)
        mats.append(jnp.where(same, dot(column, wide), 0.0).astype(BF16))
        places.append(jnp.where(placed, dot(column, tile), 0.0).astype(BF16))
        pairs.append(
            jnp.where(pair_same, jnp.concatenate([row] * 2, axis=0), 0.0).astype(BF16)
        )
    mat_ref[...] = left_three(mats)
    pair_ref[...] = left_three(pairs)
    place_ref[...] = left_three(places)

    f = frames_ref[2]
    f_chord = shift_next(f, 1) - f
    f_span = shift_next(f, 0) - f

    def put(i, both):
        high, low = split(both)
        span = pl.ds(i * rows, 2 * rows)
        right_ref[0, span, :] = high
        right_ref[1, span, :] = high
        right_ref[2, span, :] = low

    def lines_of(ref, i):
        return [chunked(ref, j * rows, rows, size) for j in range(i, i + GROUP)]

    for i in range(0, depth, GROUP):
        halves = [0.5 * k_ref[i + n] for n in range(GROUP)]
        factors = [jnp.broadcast_to(factor_ref[j : j + 1, :], (rows, 128)) for j in range(i, i + GROUP)]
        chords = [half + shift_next(half, 1) for half in halves]
        spans = [half + shift_next(half, 0) for half in halves]
        found = []
        for half, factor, w_chord, w_span in zip(halves, factors, chords, spans):
            edge = half * f
            flux_chord = w_chord * f_chord
            flux_span = w_span * f_span
            moved = f + flux_chord - shift_prev(flux_chord, 1, edge)
            moved = moved + flux_span - shift_prev(flux_span, 0, edge)
            found.append(jnp.concatenate([factor] * (cols // 128), axis=1) * moved)
        if i == 0:
            found[0] = found[0] + frames_ref[1]
        for n in range(GROUP):
            chord_ref[i + n] = chords[n]
            span_ref[i + n] = spans[n]
        for n in range(0, GROUP, 2):
            put(i + n, jnp.concatenate(found[n : n + 2], axis=0))
    right = right_ref[...].reshape(3 * size, cols)
    first = dot(mat_ref[...], right)
    for c in range(cols // 128):
        first_ref[c * size : (c + 1) * size, :] = first[:, c * 128 : (c + 1) * 128]

    for i in range(0, depth, GROUP):
        halves = [0.5 * k_ref[i + n] for n in range(GROUP)]
        values = lines_of(first_ref, i)
        chords = [chord_ref[i + n] for n in range(GROUP)]
        spans = [span_ref[i + n] for n in range(GROUP)]
        found = [
            v + divergence(v, w_chord, half, 1) + divergence(v, w_span, half, 0)
            for v, w_chord, w_span, half in zip(values, chords, spans, halves)
        ]
        if i == 0:
            found[0] = found[0] + frames_ref[0]
        for n in range(0, GROUP, 2):
            put(i + n, jnp.concatenate(found[n : n + 2], axis=0))
    right = right_ref[...].reshape(3 * size, cols)
    adj = dot(mat_ref[...], right)
    for c in range(cols // 128):
        adj_ref[c * size : (c + 1) * size, :] = adj[:, c * 128 : (c + 1) * 128]

    for n, (after, _) in enumerate(sides()):
        row = jnp.where(after, rows - 1, 0)
        for c in range(cols // 128):
            edge_ref[n, :, c * 128 : (c + 1) * 128] = row_of_each(first_ref, c, depth, rows, row)
    for n, row in enumerate(far_rows(rows)):
        for c in range(cols // 128):
            two_ref[n, :, c * 128 : (c + 1) * 128] = row_of_each(adj_ref, c, depth, rows, row)
    for copy in copies:
        copy.wait()
    contribution_ref[...] = scale * (
        d_ref[0:1, 0:1] * f * excess_ref[2]
        + chunked(first_ref, 0, rows, size) * excess_ref[1]
        + chunked(adj_ref, 0, rows, size) * excess_ref[0]
    )


def correction(n, got, own, d_ref, edge_ref, pair_ref):
    _, depth, cols = edge_ref.shape
    _, inside = sides()[n]
    factor = d_ref[:, 0:1]
    half = 0.5 * packed_field(got, depth, cols, 0)
    half_next = 0.5 * packed_field(got, depth, cols, 1)
    f = packed_line(got, depth, cols, 0)
    frame = packed_line(got, depth, cols, 1)
    f_next = packed_line(got, depth, cols, 2)
    f_own = packed_line(own, depth, cols, 0)
    half_own = 0.5 * packed_field(own, depth, cols, 0)
    inner = half_own + 0.5 * packed_field(own, depth, cols, 1)
    w_next = half_own + shift_next(half_own, 1)
    w_prev = half_own + shift_prev(half_own, 1, 0.0)
    face = half + half_own
    moved = (
        f
        + (half + shift_next(half, 1)) * (shift_next(f, 1) - f)
        + (half + shift_prev(half, 1, 0.0)) * (shift_prev(f, 1, 0.0) - f)
        + (half + half_next) * (f_next - f)
        + face * (f_own - f)
    )
    outer = factor * moved + jnp.where(iota((depth, 1), 0) == 0, frame, 0.0)
    sources = [factor * (face * f - half * f_own), jnp.where(inside, outer, 0.0)]
    found = dot(pair_ref[...], right_three(jnp.concatenate(sources, axis=0)))
    e = found[0:depth]
    outer = found[depth:]
    change = (
        (1.0 - (w_next + w_prev) - (half_own + inner)) * e
        + w_next * shift_next(e, 1)
        + w_prev * shift_prev(e, 1, 0.0)
        + face * outer
        - half * (e + edge_ref[n])
    )
    return right_three(jnp.concatenate([change, inner * e], axis=0)), e[0:1, :]


def add_segments(lanes, total, contribution, picked_rows, map_ref):
    shape = (total.shape[0], 128)
    lane = iota(shape, 1)
    segment = jnp.where(lane < lanes, iota(shape, 0) * lanes + lane, -1)
    found = jnp.zeros(shape, F32)
    for block in range(contribution.shape[1] // 128):
        part = contribution[:, block * 128 : (block + 1) * 128]
        sums = jnp.sum(part, axis=1, keepdims=True)
        for n, row in enumerate(picked_rows):
            found += jnp.where(segment == map_ref[block, row], sums[n : n + 1, :], 0.0)
    return total + found[:, None, :]


def near_kernel(
    lanes,
    scale,
    d_ref,
    excess_ref,
    edge_ref,
    pair_ref,
    map_vmem,
    place_ref,
    base_ref,
    contribution_ref,
    own_ref,
    got_ref,
    adj_hbm,
    part_ref,
    adj_ref,
    map_ref,
    sems,
):
    map_copy = pltpu.make_async_copy(map_vmem, map_ref, sems.at[0])
    map_copy.start()
    depth, rows, cols = adj_ref.shape
    size = depth * rows
    sources, surface = correction(0, got_ref, own_ref, d_ref, edge_ref, pair_ref)
    found = dot(place_ref[...], sources)
    adj_ref[...] = (chunked(base_ref, 0, size, size) + found).reshape(depth, rows, cols)
    adj_copy = pltpu.make_async_copy(adj_ref, adj_hbm, sems.at[1])
    adj_copy.start()
    row = jnp.where(sides()[0][0], rows - 1, 0)
    surface = jnp.where(iota((rows, cols), 0) == row, surface, 0.0)
    contribution = contribution_ref[...] + scale * (
        surface * excess_ref[1] + found[0:rows, :] * excess_ref[0]
    )
    map_copy.wait()
    part_ref[...] = add_segments(
        lanes, jnp.zeros(part_ref.shape, F32), contribution, range(rows), map_ref
    )
    adj_copy.wait()


def far_kernel(
    lanes,
    scale,
    own_ref,
    got_ref,
    d_ref,
    excess_ref,
    edge_ref,
    pair_ref,
    map_vmem,
    two_ref,
    part_in_ref,
    out_ref,
    part_ref,
    map_ref,
    map_sem,
):
    map_copy = pltpu.make_async_copy(map_vmem, map_ref, map_sem)
    map_copy.start()
    depth = two_ref.shape[1]
    rows = excess_ref.shape[1]
    sources, surface = correction(1, got_ref, own_ref, d_ref, edge_ref, pair_ref)
    found = dot(pair_ref[...], sources)
    edge, second = far_rows(rows)
    contribution = scale * jnp.concatenate(
        [
            surface * excess_ref[1, pl.ds(edge, 1), :]
            + found[0:1] * excess_ref[0, pl.ds(edge, 1), :],
            found[depth : depth + 1] * excess_ref[0, pl.ds(second, 1), :],
        ],
        axis=0,
    )
    map_copy.wait()
    part_ref[...] = add_segments(lanes, part_in_ref[...], contribution, (edge, second), map_ref)
    out_ref[...] = two_ref[...] + found.reshape(two_ref.shape)


def finish_kernel(_, two_ref, got_ref, adj_hbm, out_hbm, out_ref, sems):
    copies = []
    for n, row in enumerate(far_rows(adj_hbm.shape[1])):
        copies.append(pltpu.make_async_copy(two_ref.at[n], adj_hbm.at[:, row, :], sems.at[n]))
        copies[-1].start()
    out_ref[...] = jnp.sum(got_ref[:, 0, : out_ref.shape[0]], axis=0)
    copies.append(pltpu.make_async_copy(out_ref, out_hbm, sems.at[2]))
    copies[-1].start()
    for copy in copies:
        copy.wait()


def in_hbm(x):
    return pltpu.with_memory_space_constraint(x, pltpu.HBM)


def per_device(
    conductance, depth_inverse, surface_residual, surface_excess, segment_map, frame_index
):
    _, depth, rows, cols = conductance.shape
    frames = surface_residual.shape[1]
    blocks = segment_map.shape[1]
    size = depth * rows
    spans = lax.axis_size("span")
    devices = spans * lax.axis_size("blade")
    lanes = SEGS // devices
    field = pltpu.VMEM((depth, rows, cols), F32)
    chunks = cols // 128
    packed_far = pltpu.VMEM(((2 * depth + 4) * chunks, 128), F32)
    packed_near = pltpu.VMEM(((2 * depth + 3) * chunks, 128), F32)
    own_far, picked, inverse = pl.pallas_call(
        load_kernel,
        out_shape=(
            packed_far,
            pltpu.VMEM((STEPS, rows, cols), F32),
            pltpu.VMEM((depth, depth), F32),
        ),
        in_specs=[HBM] * 4,
        out_specs=(VMEM,) * 3,
        scratch_shapes=[
            pltpu.SMEM((STEPS,), jnp.int32),
            pltpu.VMEM((frames, rows, cols), F32),
            pltpu.VMEM((depth, 8, cols), F32),
            pltpu.SemaphoreType.DMA((4,)),
        ],
        compiler_params=GRANT,
        name="load",
    )(
        in_hbm(frame_index),
        in_hbm(conductance[0]),
        in_hbm(surface_residual[0]),
        in_hbm(depth_inverse[0]),
    )
    k = conductance[0]
    own_near = pl.pallas_call(
        pack_kernel,
        out_shape=packed_near,
        in_specs=[VMEM] * 2,
        out_specs=VMEM,
        compiler_params=GRANT,
        name="pack",
    )(k, picked)
    across = [(i, i + 1) for i in range(1, spans - 1, 2)]
    within = [(i, i + 1) for i in range(0, spans - 1, 2)]
    near = lax.ppermute(own_near, "span", within + [(b, a) for a, b in within])
    far = lax.ppermute(own_far, "span", across + [(b, a) for a, b in across])
    scale = 1.0 / math.sqrt(128.0 * STEPS)
    line = pltpu.VMEM((rows, cols), F32)
    base, two, excess, ids, edge, contribution, pair, place = pl.pallas_call(
        functools.partial(base_kernel, scale),
        out_shape=(
            pltpu.VMEM((chunks * size, 128), F32),
            pltpu.VMEM((2, depth, cols), F32),
            pltpu.VMEM((STEPS, rows, cols), F32),
            pltpu.VMEM((blocks, rows), jnp.int32),
            pltpu.VMEM((2, depth, cols), F32),
            line,
            pltpu.VMEM((2 * depth, 6 * depth), BF16),
            pltpu.VMEM((size, 6 * depth), BF16),
        ),
        in_specs=[VMEM] * 3 + [HBM] * 2,
        out_specs=(VMEM,) * 8,
        scratch_shapes=[
            pltpu.VMEM((size, 3 * size), BF16),
            pltpu.VMEM((3, size, cols), BF16),
            pltpu.VMEM((chunks * size, 128), F32),
            field,
            field,
            pltpu.VMEM((depth, 128), F32),
            pltpu.SemaphoreType.DMA((2,)),
        ],
        compiler_params=GRANT,
        name="base",
    )(k, picked, inverse, in_hbm(surface_excess[0]), in_hbm(segment_map.T))
    fixed = (inverse, excess, edge, pair, ids)
    sums = pltpu.VMEM((devices, 1, 128), F32)
    adjoint, partial = pl.pallas_call(
        functools.partial(near_kernel, lanes, scale),
        out_shape=(pltpu.HBM((depth, rows, cols), F32), sums),
        in_specs=[VMEM] * 10,
        out_specs=(HBM, VMEM),
        scratch_shapes=[
            field,
            pltpu.SMEM((blocks, rows), jnp.int32),
            pltpu.SemaphoreType.DMA((2,)),
        ],
        compiler_params=GRANT,
        name="near",
    )(*fixed, place, base, contribution, own_near, near)
    two, partial = pl.pallas_call(
        functools.partial(far_kernel, lanes, scale),
        out_shape=(pltpu.VMEM((2, depth, cols), F32), sums),
        in_specs=[VMEM] * 9,
        out_specs=(VMEM,) * 2,
        scratch_shapes=[pltpu.SMEM((blocks, rows), jnp.int32), pltpu.SemaphoreType.DMA],
        compiler_params=GRANT,
        name="far",
    )(own_far, far, *fixed, two, partial)
    pieces = lax.all_to_all(partial, ("blade", "span"), 0, 0, tiled=True)
    adjoint, owned = pl.pallas_call(
        finish_kernel,
        out_shape=(pltpu.HBM((depth, rows, cols), F32), pltpu.HBM((lanes,), F32)),
        in_specs=[HBM, VMEM, VMEM],
        out_specs=(HBM,) * 2,
        scratch_shapes=[pltpu.VMEM((lanes,), F32), pltpu.SemaphoreType.DMA((3,))],
        input_output_aliases={0: 0},
        compiler_params=GRANT,
        name="finish",
    )(in_hbm(adjoint), two, pltpu.with_memory_space_constraint(pieces, pltpu.VMEM))
    return (adjoint[None], owned)


def solution(mesh):
    placed = (
        P("blade", None, "span", None),
        P("blade", None, None),
        P("blade", None, "span", None),
        P("blade", None, "span", None),
        P("span", None),
        P(),
    )
    return jax.shard_map(
        per_device,
        mesh=mesh,
        in_specs=placed,
        out_specs=(P("blade", None, "span", None), P(("blade", "span"))),
        check_vma=False,
    )
```

```python
import functools
import math

import jax
import jax.numpy as jnp
from jax import lax
from jax.experimental import pallas as pl
from jax.experimental.pallas import tpu as pltpu
from jax.sharding import PartitionSpec as P

STEPS = 3
SEGS = 2048
GROUP = 2
F32 = jnp.float32
BF16 = jnp.bfloat16
VMEM = pl.BlockSpec(memory_space=pltpu.VMEM)
HBM = pl.BlockSpec(memory_space=pltpu.HBM)
GRANT = pltpu.CompilerParams(vmem_limit_bytes=16 * 2**20)


def split(x):
    high = x.astype(BF16)
    return high, (x - high.astype(F32)).astype(BF16)


def dot(a, b):
    return jnp.dot(a, b, preferred_element_type=F32)


def left_three(matrix):
    high, low = matrix
    return jnp.concatenate([high, low, high], axis=1)


def right_three(x):
    high, low = split(x)
    return jnp.concatenate([high, high, low], axis=0)


def iota(shape, dim):
    return lax.broadcasted_iota(jnp.int32, shape, dim)


def shift_next(x, axis):
    size = x.shape[axis]
    return jnp.where(iota(x.shape, axis) == size - 1, 0.0, pltpu.roll(x, size - 1, axis))


def shift_prev(x, axis, first):
    return jnp.where(iota(x.shape, axis) == 0, first, pltpu.roll(x, 1, axis))


def divergence(v, weight, half, axis):
    flux = weight * (shift_next(v, axis) - v)
    return flux - shift_prev(flux, axis, half * v)


def sides():
    span = lax.axis_index("span")
    count = lax.axis_size("span")
    even = lax.rem(span, 2) == 0
    has_next = span + 1 < count
    has_prev = span > 0
    return (
        (even, jnp.where(even, has_next, has_prev)),
        (jnp.logical_not(even), jnp.where(even, has_prev, has_next)),
    )


def chunked(ref, start, count, step):
    chunks = ref.shape[0] // step
    return jnp.concatenate(
        [ref[c * step + start : c * step + start + count, :] for c in range(chunks)], axis=1
    )


def packed_field(ref, depth, cols, n):
    chunks = cols // 128
    return chunked(ref.at[n * chunks * depth : (n + 1) * chunks * depth], 0, depth, depth)


def packed_line(ref, depth, cols, n):
    chunks = cols // 128
    base = (2 * depth + n) * chunks
    return chunked(ref.at[base : base + chunks], 0, 1, 1)


def row_of_each(ref, chunk, depth, rows, row):
    return ref[pl.ds(chunk * depth * rows + row, depth, stride=rows), :]


def far_rows(rows):
    after = sides()[1][0]
    return jnp.where(after, rows - 1, 0), jnp.where(after, rows - 2, 1)


def put_lines(ref, depth, lines):
    chunks = lines[0].shape[1] // 128
    base = 2 * chunks * depth
    for n, line in enumerate(lines):
        for c in range(chunks):
            spot = base + n * chunks + c
            ref[spot : spot + 1, :] = line[:, c * 128 : (c + 1) * 128]
    if ref.shape[0] > base + 3 * chunks:
        ref[base + 3 * chunks :, :] = jnp.zeros((ref.shape[0] - base - 3 * chunks, 128), F32)


def put_rows(ref, depth, items):
    for which, x in enumerate(items):
        for c in range(x.shape[1] // 128):
            spot = (which * (x.shape[1] // 128) + c) * depth
            ref[spot : spot + depth, :] = x[:, c * 128 : (c + 1) * 128]


def load_kernel(
    frame_hbm,
    k_hbm,
    res_hbm,
    d_hbm,
    far_ref,
    index_ref,
    d_ref,
    frame_ref,
    res_ref,
    edge_ref,
    sems,
):
    depth, rows, cols = k_hbm.shape
    after = sides()[1][0]
    first = jnp.where(after, rows - 2, 0)
    pairs = (
        (k_hbm.at[:, pl.ds(first, 2), :], edge_ref.at[:, 0:2, :]),
        (frame_hbm, frame_ref),
        (res_hbm.at[:, pl.ds(first, 2), :], res_ref.at[:, 0:2, :]),
        (d_hbm, d_ref),
    )
    copies = [pltpu.make_async_copy(a, b, sems.at[n]) for n, (a, b) in enumerate(pairs)]
    for copy in copies:
        copy.start()
    copies[1].wait()
    copies[2].wait()
    for n in range(STEPS):
        index_ref[n : n + 1, :] = jnp.full((1, 128), frame_ref[n], jnp.int32)
    lines = []
    for step, near in ((2, True), (1, True), (2, False)):
        low, high = res_ref[frame_ref[step], 0:1, :], res_ref[frame_ref[step], 1:2, :]
        lines.append(jnp.where(after, high, low) if near else jnp.where(after, low, high))
    put_lines(far_ref, depth, lines)
    copies[0].wait()
    low, high = edge_ref[:, 0, :], edge_ref[:, 1, :]
    put_rows(far_ref, depth, (jnp.where(after, high, low), jnp.where(after, low, high)))
    copies[3].wait()


def pack_kernel(k_ref, res_ref, index_ref, near_ref, frames_ref):
    depth, rows, cols = k_ref.shape
    after = sides()[0][0]
    for n in range(STEPS):
        wanted = jnp.concatenate(
            [jnp.broadcast_to(index_ref[n : n + 1, :], (rows, 128))] * (cols // 128), axis=1
        )
        picked = res_ref[0]
        for frame in range(1, res_ref.shape[0]):
            picked = jnp.where(wanted == frame, res_ref[frame], picked)
        frames_ref[n] = picked
    edge, second = jnp.where(after, rows - 1, 0), jnp.where(after, rows - 2, 1)
    lines = [frames_ref[n, pl.ds(row, 1), :] for n, row in ((2, edge), (1, edge), (2, second))]
    put_lines(near_ref, depth, lines)
    items = []
    for first, last in ((0, rows - 1), (1, rows - 2)):
        items.append(jnp.where(after, k_ref[:, last, :], k_ref[:, first, :]))
    put_rows(near_ref, depth, items)


def base_kernel(
    scale,
    k_ref,
    frames_ref,
    d_ref,
    excess_hbm,
    map_hbm,
    adj_ref,
    two_ref,
    excess_ref,
    map_ref,
    edge_ref,
    contribution_ref,
    pair_ref,
    place_ref,
    mat_ref,
    right_ref,
    first_ref,
    chord_ref,
    span_ref,
    factor_ref,
    sems,
):
    copies = [
        pltpu.make_async_copy(excess_hbm, excess_ref, sems.at[0]),
        pltpu.make_async_copy(map_hbm, map_ref, sems.at[1]),
    ]
    for copy in copies:
        copy.start()
    depth, rows, cols = chord_ref.shape
    size = depth * rows
    factor_ref[...] = jnp.broadcast_to(d_ref[:, 0:1], factor_ref.shape)

    parts = split(d_ref[...])
    tall = (iota((size, depth), 0) // rows == iota((size, depth), 1)).astype(BF16)
    wide = (iota((depth, size), 0) == iota((depth, size), 1) // rows).astype(BF16)
    two = 2 * depth
    tile = (iota((depth, two), 0) == iota((depth, two), 1) % depth).astype(BF16)
    same = iota((size, size), 0) % rows == iota((size, size), 1) % rows
    pair_same = iota((two, two), 0) // depth == iota((two, two), 1) // depth
    row_of = iota((size, two), 0) % rows
    first_half = iota((size, two), 1) < depth
    after = sides()[0][0]
    edge = jnp.where(after, rows - 1, 0)
    second = jnp.where(after, rows - 2, 1)
    placed = row_of == jnp.where(first_half, edge, second)
    mats, pairs, places = [], [], []
    for part in parts:
        column = dot(tall, part).astype(BF16)
        row = dot(part, tile)
        mats.append(jnp.where(same, dot(column, wide), 0.0).astype(BF16))
        places.append(jnp.where(placed, dot(column, tile), 0.0).astype(BF16))
        pairs.append(
            jnp.where(pair_same, jnp.concatenate([row] * 2, axis=0), 0.0).astype(BF16)
        )
    mat_ref[...] = left_three(mats)
    pair_ref[...] = left_three(pairs)
    place_ref[...] = left_three(places)

    f = frames_ref[2]
    f_chord = shift_next(f, 1) - f
    f_span = shift_next(f, 0) - f

    def put(i, both):
        high, low = split(both)
        span = pl.ds(i * rows, 2 * rows)
        right_ref[0, span, :] = high
        right_ref[1, span, :] = high
        right_ref[2, span, :] = low

    def lines_of(ref, i):
        return [chunked(ref, j * rows, rows, size) for j in range(i, i + GROUP)]

    for i in range(0, depth, GROUP):
        halves = [0.5 * k_ref[i + n] for n in range(GROUP)]
        factors = [jnp.broadcast_to(factor_ref[j : j + 1, :], (rows, 128)) for j in range(i, i + GROUP)]
        chords = [half + shift_next(half, 1) for half in halves]
        spans = [half + shift_next(half, 0) for half in halves]
        found = []
        for half, factor, w_chord, w_span in zip(halves, factors, chords, spans):
            edge = half * f
            flux_chord = w_chord * f_chord
            flux_span = w_span * f_span
            moved = f + flux_chord - shift_prev(flux_chord, 1, edge)
            moved = moved + flux_span - shift_prev(flux_span, 0, edge)
            found.append(jnp.concatenate([factor] * (cols // 128), axis=1) * moved)
        if i == 0:
            found[0] = found[0] + frames_ref[1]
        for n in range(GROUP):
            chord_ref[i + n] = chords[n]
            span_ref[i + n] = spans[n]
        for n in range(0, GROUP, 2):
            put(i + n, jnp.concatenate(found[n : n + 2], axis=0))
    right = right_ref[...].reshape(3 * size, cols)
    first = dot(mat_ref[...], right)
    for c in range(cols // 128):
        first_ref[c * size : (c + 1) * size, :] = first[:, c * 128 : (c + 1) * 128]

    for i in range(0, depth, GROUP):
        halves = [0.5 * k_ref[i + n] for n in range(GROUP)]
        values = lines_of(first_ref, i)
        chords = [chord_ref[i + n] for n in range(GROUP)]
        spans = [span_ref[i + n] for n in range(GROUP)]
        found = [
            v + divergence(v, w_chord, half, 1) + divergence(v, w_span, half, 0)
            for v, w_chord, w_span, half in zip(values, chords, spans, halves)
        ]
        if i == 0:
            found[0] = found[0] + frames_ref[0]
        for n in range(0, GROUP, 2):
            put(i + n, jnp.concatenate(found[n : n + 2], axis=0))
    right = right_ref[...].reshape(3 * size, cols)
    adj = dot(mat_ref[...], right)
    for c in range(cols // 128):
        adj_ref[c * size : (c + 1) * size, :] = adj[:, c * 128 : (c + 1) * 128]

    for n, (after, _) in enumerate(sides()):
        row = jnp.where(after, rows - 1, 0)
        for c in range(cols // 128):
            edge_ref[n, :, c * 128 : (c + 1) * 128] = row_of_each(first_ref, c, depth, rows, row)
    for n, row in enumerate(far_rows(rows)):
        for c in range(cols // 128):
            two_ref[n, :, c * 128 : (c + 1) * 128] = row_of_each(adj_ref, c, depth, rows, row)
    for copy in copies:
        copy.wait()
    contribution_ref[...] = scale * (
        d_ref[0:1, 0:1] * f * excess_ref[2]
        + chunked(first_ref, 0, rows, size) * excess_ref[1]
        + chunked(adj_ref, 0, rows, size) * excess_ref[0]
    )


def correction(n, got, own, d_ref, edge_ref, pair_ref):
    _, depth, cols = edge_ref.shape
    _, inside = sides()[n]
    factor = d_ref[:, 0:1]
    half = 0.5 * packed_field(got, depth, cols, 0)
    half_next = 0.5 * packed_field(got, depth, cols, 1)
    f = packed_line(got, depth, cols, 0)
    frame = packed_line(got, depth, cols, 1)
    f_next = packed_line(got, depth, cols, 2)
    f_own = packed_line(own, depth, cols, 0)
    half_own = 0.5 * packed_field(own, depth, cols, 0)
    inner = half_own + 0.5 * packed_field(own, depth, cols, 1)
    w_next = half_own + shift_next(half_own, 1)
    w_prev = half_own + shift_prev(half_own, 1, 0.0)
    face = half + half_own
    moved = (
        f
        + (half + shift_next(half, 1)) * (shift_next(f, 1) - f)
        + (half + shift_prev(half, 1, 0.0)) * (shift_prev(f, 1, 0.0) - f)
        + (half + half_next) * (f_next - f)
        + face * (f_own - f)
    )
    outer = factor * moved + jnp.where(iota((depth, 1), 0) == 0, frame, 0.0)
    sources = [factor * (face * f - half * f_own), jnp.where(inside, outer, 0.0)]
    found = dot(pair_ref[...], right_three(jnp.concatenate(sources, axis=0)))
    e = found[0:depth]
    outer = found[depth:]
    change = (
        (1.0 - (w_next + w_prev) - (half_own + inner)) * e
        + w_next * shift_next(e, 1)
        + w_prev * shift_prev(e, 1, 0.0)
        + face * outer
        - half * (e + edge_ref[n])
    )
    return right_three(jnp.concatenate([change, inner * e], axis=0)), e[0:1, :]


def add_segments(total, contribution, picked_rows, map_ref):
    owners, _, lanes = total.shape
    shape = (owners, 128)
    lane = iota(shape, 1)
    segment = jnp.where(lane < lanes, iota(shape, 0) * lanes + lane, -1)
    found = jnp.zeros(shape, F32)
    for block in range(contribution.shape[1] // 128):
        part = contribution[:, block * 128 : (block + 1) * 128]
        sums = jnp.sum(part, axis=1, keepdims=True)
        for n, row in enumerate(picked_rows):
            found += jnp.where(segment == map_ref[block, row], sums[n : n + 1, :], 0.0)
    return total + found[:, None, :lanes]


def near_kernel(
    scale,
    d_ref,
    excess_ref,
    edge_ref,
    pair_ref,
    map_vmem,
    place_ref,
    base_ref,
    contribution_ref,
    own_ref,
    got_ref,
    adj_hbm,
    part_ref,
    adj_ref,
    map_ref,
    sems,
):
    map_copy = pltpu.make_async_copy(map_vmem, map_ref, sems.at[0])
    map_copy.start()
    depth, rows, cols = adj_ref.shape
    size = depth * rows
    sources, surface = correction(0, got_ref, own_ref, d_ref, edge_ref, pair_ref)
    found = dot(place_ref[...], sources)
    adj_ref[...] = (chunked(base_ref, 0, size, size) + found).reshape(depth, rows, cols)
    adj_copy = pltpu.make_async_copy(adj_ref, adj_hbm, sems.at[1])
    adj_copy.start()
    row = jnp.where(sides()[0][0], rows - 1, 0)
    surface = jnp.where(iota((rows, cols), 0) == row, surface, 0.0)
    contribution = contribution_ref[...] + scale * (
        surface * excess_ref[1] + found[0:rows, :] * excess_ref[0]
    )
    map_copy.wait()
    part_ref[...] = add_segments(
        jnp.zeros(part_ref.shape, F32), contribution, range(rows), map_ref
    )
    adj_copy.wait()


def far_kernel(
    scale,
    own_ref,
    got_ref,
    d_ref,
    excess_ref,
    edge_ref,
    pair_ref,
    map_vmem,
    two_ref,
    part_in_ref,
    out_ref,
    part_ref,
    map_ref,
    map_sem,
):
    map_copy = pltpu.make_async_copy(map_vmem, map_ref, map_sem)
    map_copy.start()
    depth = two_ref.shape[1]
    rows = excess_ref.shape[1]
    sources, surface = correction(1, got_ref, own_ref, d_ref, edge_ref, pair_ref)
    found = dot(pair_ref[...], sources)
    edge, second = far_rows(rows)
    contribution = scale * jnp.concatenate(
        [
            surface * excess_ref[1, pl.ds(edge, 1), :]
            + found[0:1] * excess_ref[0, pl.ds(edge, 1), :],
            found[depth : depth + 1] * excess_ref[0, pl.ds(second, 1), :],
        ],
        axis=0,
    )
    map_copy.wait()
    part_ref[...] = add_segments(part_in_ref[...], contribution, (edge, second), map_ref)
    out_ref[...] = two_ref[...] + found.reshape(two_ref.shape)


def finish_kernel(_, two_ref, got_ref, adj_hbm, out_hbm, out_ref, sems):
    copies = []
    for n, row in enumerate(far_rows(adj_hbm.shape[1])):
        copies.append(pltpu.make_async_copy(two_ref.at[n], adj_hbm.at[:, row, :], sems.at[n]))
        copies[-1].start()
    out_ref[...] = jnp.sum(got_ref[:, 0, :], axis=0)
    copies.append(pltpu.make_async_copy(out_ref, out_hbm, sems.at[2]))
    copies[-1].start()
    for copy in copies:
        copy.wait()


def in_hbm(x):
    return pltpu.with_memory_space_constraint(x, pltpu.HBM)


def per_device(
    conductance, depth_inverse, surface_residual, surface_excess, segment_map, frame_index
):
    _, depth, rows, cols = conductance.shape
    frames = surface_residual.shape[1]
    blocks = segment_map.shape[1]
    size = depth * rows
    spans = lax.axis_size("span")
    devices = spans * lax.axis_size("blade")
    lanes = SEGS // devices
    field = pltpu.VMEM((depth, rows, cols), F32)
    chunks = cols // 128
    packed_far = pltpu.VMEM(((2 * depth + 4) * chunks, 128), F32)
    packed_near = pltpu.VMEM(((2 * depth + 3) * chunks, 128), F32)
    own_far, index, inverse = pl.pallas_call(
        load_kernel,
        out_shape=(
            packed_far,
            pltpu.VMEM((STEPS, 128), jnp.int32),
            pltpu.VMEM((depth, depth), F32),
        ),
        in_specs=[HBM] * 4,
        out_specs=(VMEM,) * 3,
        scratch_shapes=[
            pltpu.SMEM((STEPS,), jnp.int32),
            pltpu.VMEM((frames, rows, cols), F32),
            pltpu.VMEM((depth, 8, cols), F32),
            pltpu.SemaphoreType.DMA((4,)),
        ],
        compiler_params=GRANT,
        name="load",
    )(
        in_hbm(frame_index),
        in_hbm(conductance[0]),
        in_hbm(surface_residual[0]),
        in_hbm(depth_inverse[0]),
    )
    k = conductance[0]
    own_near, picked = pl.pallas_call(
        pack_kernel,
        out_shape=(packed_near, pltpu.VMEM((STEPS, rows, cols), F32)),
        in_specs=[VMEM] * 3,
        out_specs=(VMEM,) * 2,
        compiler_params=GRANT,
        name="pack",
    )(k, surface_residual[0], index)
    across = [(i, i + 1) for i in range(1, spans - 1, 2)]
    within = [(i, i + 1) for i in range(0, spans - 1, 2)]
    near = lax.ppermute(own_near, "span", within + [(b, a) for a, b in within])
    far = lax.ppermute(own_far, "span", across + [(b, a) for a, b in across])
    scale = 1.0 / math.sqrt(128.0 * STEPS)
    line = pltpu.VMEM((rows, cols), F32)
    base, two, excess, ids, edge, contribution, pair, place = pl.pallas_call(
        functools.partial(base_kernel, scale),
        out_shape=(
            pltpu.VMEM((chunks * size, 128), F32),
            pltpu.VMEM((2, depth, cols), F32),
            pltpu.VMEM((STEPS, rows, cols), F32),
            pltpu.VMEM((blocks, rows), jnp.int32),
            pltpu.VMEM((2, depth, cols), F32),
            line,
            pltpu.VMEM((2 * depth, 6 * depth), BF16),
            pltpu.VMEM((size, 6 * depth), BF16),
        ),
        in_specs=[VMEM] * 3 + [HBM] * 2,
        out_specs=(VMEM,) * 8,
        scratch_shapes=[
            pltpu.VMEM((size, 3 * size), BF16),
            pltpu.VMEM((3, size, cols), BF16),
            pltpu.VMEM((chunks * size, 128), F32),
            field,
            field,
            pltpu.VMEM((depth, 128), F32),
            pltpu.SemaphoreType.DMA((2,)),
        ],
        compiler_params=GRANT,
        name="base",
    )(k, picked, inverse, in_hbm(surface_excess[0]), in_hbm(segment_map.T))
    fixed = (inverse, excess, edge, pair, ids)
    sums = pltpu.VMEM((devices, 1, lanes), F32)
    adjoint, partial = pl.pallas_call(
        functools.partial(near_kernel, scale),
        out_shape=(pltpu.HBM((depth, rows, cols), F32), sums),
        in_specs=[VMEM] * 10,
        out_specs=(HBM, VMEM),
        scratch_shapes=[
            field,
            pltpu.SMEM((blocks, rows), jnp.int32),
            pltpu.SemaphoreType.DMA((2,)),
        ],
        compiler_params=GRANT,
        name="near",
    )(*fixed, place, base, contribution, own_near, near)
    two, partial = pl.pallas_call(
        functools.partial(far_kernel, scale),
        out_shape=(pltpu.VMEM((2, depth, cols), F32), sums),
        in_specs=[VMEM] * 9,
        out_specs=(VMEM,) * 2,
        scratch_shapes=[pltpu.SMEM((blocks, rows), jnp.int32), pltpu.SemaphoreType.DMA],
        compiler_params=GRANT,
        name="far",
    )(own_far, far, *fixed, two, partial)
    pieces = lax.all_to_all(partial, ("blade", "span"), 0, 0, tiled=True)
    adjoint, owned = pl.pallas_call(
        finish_kernel,
        out_shape=(pltpu.HBM((depth, rows, cols), F32), pltpu.HBM((lanes,), F32)),
        in_specs=[HBM, VMEM, VMEM],
        out_specs=(HBM,) * 2,
        scratch_shapes=[pltpu.VMEM((lanes,), F32), pltpu.SemaphoreType.DMA((3,))],
        input_output_aliases={0: 0},
        compiler_params=GRANT,
        name="finish",
    )(in_hbm(adjoint), two, pltpu.with_memory_space_constraint(pieces, pltpu.VMEM))
    return (adjoint[None], owned)


def solution(mesh):
    placed = (
        P("blade", None, "span", None),
        P("blade", None, None),
        P("blade", None, "span", None),
        P("blade", None, "span", None),
        P("span", None),
        P(),
    )
    return jax.shard_map(
        per_device,
        mesh=mesh,
        in_specs=placed,
        out_specs=(P("blade", None, "span", None), P(("blade", "span"))),
        check_vma=False,
    )
```

```python
import functools
import math

import jax
import jax.numpy as jnp
from jax import lax
from jax.experimental import pallas as pl
from jax.experimental.pallas import tpu as pltpu
from jax.sharding import PartitionSpec as P

STEPS = 3
SEGS = 2048
GROUP = 4
F32 = jnp.float32
BF16 = jnp.bfloat16
VMEM = pl.BlockSpec(memory_space=pltpu.VMEM)
HBM = pl.BlockSpec(memory_space=pltpu.HBM)
GRANT = pltpu.CompilerParams(vmem_limit_bytes=16 * 2**20)


def split(x):
    high = x.astype(BF16)
    return high, (x - high.astype(F32)).astype(BF16)


def dot(a, b):
    return jnp.dot(a, b, preferred_element_type=F32)


def left_three(matrix):
    high, low = matrix
    return jnp.concatenate([high, low, high], axis=1)


def right_three(x):
    high, low = split(x)
    return jnp.concatenate([high, high, low], axis=0)


def iota(shape, dim):
    return lax.broadcasted_iota(jnp.int32, shape, dim)


def shift_next(x, axis):
    size = x.shape[axis]
    return jnp.where(iota(x.shape, axis) == size - 1, 0.0, pltpu.roll(x, size - 1, axis))


def shift_prev(x, axis, first):
    return jnp.where(iota(x.shape, axis) == 0, first, pltpu.roll(x, 1, axis))


def divergence(v, weight, half, axis):
    flux = weight * (shift_next(v, axis) - v)
    return flux - shift_prev(flux, axis, half * v)


def sides():
    span = lax.axis_index("span")
    count = lax.axis_size("span")
    even = lax.rem(span, 2) == 0
    has_next = span + 1 < count
    has_prev = span > 0
    return (
        (even, jnp.where(even, has_next, has_prev)),
        (jnp.logical_not(even), jnp.where(even, has_prev, has_next)),
    )


def chunked(ref, start, count, step):
    chunks = ref.shape[0] // step
    return jnp.concatenate(
        [ref[c * step + start : c * step + start + count, :] for c in range(chunks)], axis=1
    )


def packed_field(ref, depth, cols, n):
    chunks = cols // 128
    return chunked(ref.at[n * chunks * depth : (n + 1) * chunks * depth], 0, depth, depth)


def packed_line(ref, depth, cols, n):
    chunks = cols // 128
    base = (2 * depth + n) * chunks
    return chunked(ref.at[base : base + chunks], 0, 1, 1)


def row_of_each(ref, chunk, depth, rows, row):
    return ref[pl.ds(chunk * depth * rows + row, depth, stride=rows), :]


def far_rows(rows):
    after = sides()[1][0]
    return jnp.where(after, rows - 1, 0), jnp.where(after, rows - 2, 1)


def put_lines(ref, frames_ref, depth, rows, after):
    chunks = frames_ref.shape[2] // 128
    base = 2 * chunks * depth
    edge, second = jnp.where(after, rows - 1, 0), jnp.where(after, rows - 2, 1)
    for n, (frame, row) in enumerate(((2, edge), (1, edge), (2, second))):
        line = frames_ref[frame, pl.ds(row, 1), :]
        for c in range(chunks):
            spot = base + n * chunks + c
            ref[spot : spot + 1, :] = line[:, c * 128 : (c + 1) * 128]
    if ref.shape[0] > base + 3 * chunks:
        ref[base + 3 * chunks :, :] = jnp.zeros((ref.shape[0] - base - 3 * chunks, 128), F32)


def put_rows(ref, depth, items):
    for which, x in enumerate(items):
        for c in range(x.shape[1] // 128):
            spot = (which * (x.shape[1] // 128) + c) * depth
            ref[spot : spot + depth, :] = x[:, c * 128 : (c + 1) * 128]


def load_kernel(
    frame_hbm,
    k_hbm,
    res_hbm,
    d_hbm,
    far_ref,
    frames_ref,
    d_ref,
    frame_ref,
    res_ref,
    edge_ref,
    sems,
):
    depth, rows, cols = k_hbm.shape
    after = sides()[1][0]
    first = jnp.where(after, rows - 2, 0)
    pairs = (
        (frame_hbm, frame_ref),
        (res_hbm, res_ref),
        (k_hbm.at[:, pl.ds(first, 2), :], edge_ref.at[:, 0:2, :]),
        (d_hbm, d_ref),
    )
    copies = [pltpu.make_async_copy(a, b, sems.at[n]) for n, (a, b) in enumerate(pairs)]
    for copy in copies:
        copy.start()
    copies[0].wait()
    copies[1].wait()
    for n in range(STEPS):
        frames_ref[n] = res_ref[frame_ref[n]]
    put_lines(far_ref, frames_ref, depth, rows, after)
    copies[2].wait()
    low, high = edge_ref[:, 0, :], edge_ref[:, 1, :]
    put_rows(far_ref, depth, (jnp.where(after, high, low), jnp.where(after, low, high)))
    copies[3].wait()


def pack_kernel(k_ref, frames_ref, near_ref):
    depth, rows, _ = k_ref.shape
    after = sides()[0][0]
    put_lines(near_ref, frames_ref, depth, rows, after)
    items = []
    for first, last in ((0, rows - 1), (1, rows - 2)):
        items.append(jnp.where(after, k_ref[:, last, :], k_ref[:, first, :]))
    put_rows(near_ref, depth, items)


def base_kernel(
    scale,
    k_ref,
    frames_ref,
    d_ref,
    excess_hbm,
    map_hbm,
    adj_ref,
    two_ref,
    excess_ref,
    map_ref,
    edge_ref,
    contribution_ref,
    pair_ref,
    place_ref,
    mat_ref,
    right_ref,
    first_ref,
    chord_ref,
    span_ref,
    factor_ref,
    sems,
):
    copies = [
        pltpu.make_async_copy(excess_hbm, excess_ref, sems.at[0]),
        pltpu.make_async_copy(map_hbm, map_ref, sems.at[1]),
    ]
    for copy in copies:
        copy.start()
    depth, rows, cols = chord_ref.shape
    size = depth * rows
    factor_ref[...] = jnp.broadcast_to(d_ref[:, 0:1], factor_ref.shape)

    parts = split(d_ref[...])
    tall = (iota((size, depth), 0) // rows == iota((size, depth), 1)).astype(BF16)
    wide = (iota((depth, size), 0) == iota((depth, size), 1) // rows).astype(BF16)
    two = 2 * depth
    tile = (iota((depth, two), 0) == iota((depth, two), 1) % depth).astype(BF16)
    same = iota((size, size), 0) % rows == iota((size, size), 1) % rows
    pair_same = iota((two, two), 0) // depth == iota((two, two), 1) // depth
    row_of = iota((size, two), 0) % rows
    first_half = iota((size, two), 1) < depth
    after = sides()[0][0]
    edge = jnp.where(after, rows - 1, 0)
    second = jnp.where(after, rows - 2, 1)
    placed = row_of == jnp.where(first_half, edge, second)
    mats, pairs, places = [], [], []
    for part in parts:
        column = dot(tall, part).astype(BF16)
        row = dot(part, tile)
        mats.append(jnp.where(same, dot(column, wide), 0.0).astype(BF16))
        places.append(jnp.where(placed, dot(column, tile), 0.0).astype(BF16))
        pairs.append(
            jnp.where(pair_same, jnp.concatenate([row] * 2, axis=0), 0.0).astype(BF16)
        )
    mat_ref[...] = left_three(mats)
    pair_ref[...] = left_three(pairs)
    place_ref[...] = left_three(places)

    f = frames_ref[2]
    f_chord = shift_next(f, 1) - f
    f_span = shift_next(f, 0) - f

    def put(i, both):
        high, low = split(both)
        span = pl.ds(i * rows, 2 * rows)
        right_ref[0, span, :] = high
        right_ref[1, span, :] = high
        right_ref[2, span, :] = low

    def lines_of(ref, i):
        return [chunked(ref, j * rows, rows, size) for j in range(i, i + GROUP)]

    for i in range(0, depth, GROUP):
        halves = [0.5 * k_ref[i + n] for n in range(GROUP)]
        factors = [jnp.broadcast_to(factor_ref[j : j + 1, :], (rows, 128)) for j in range(i, i + GROUP)]
        chords = [half + shift_next(half, 1) for half in halves]
        spans = [half + shift_next(half, 0) for half in halves]
        found = []
        for half, factor, w_chord, w_span in zip(halves, factors, chords, spans):
            edge = half * f
            flux_chord = w_chord * f_chord
            flux_span = w_span * f_span
            moved = f + flux_chord - shift_prev(flux_chord, 1, edge)
            moved = moved + flux_span - shift_prev(flux_span, 0, edge)
            found.append(jnp.concatenate([factor] * (cols // 128), axis=1) * moved)
        if i == 0:
            found[0] = found[0] + frames_ref[1]
        for n in range(GROUP):
            chord_ref[i + n] = chords[n]
            span_ref[i + n] = spans[n]
        for n in range(0, GROUP, 2):
            put(i + n, jnp.concatenate(found[n : n + 2], axis=0))
    right = right_ref[...].reshape(3 * size, cols)
    first = dot(mat_ref[...], right)
    for c in range(cols // 128):
        first_ref[c * size : (c + 1) * size, :] = first[:, c * 128 : (c + 1) * 128]

    for i in range(0, depth, GROUP):
        halves = [0.5 * k_ref[i + n] for n in range(GROUP)]
        values = lines_of(first_ref, i)
        chords = [chord_ref[i + n] for n in range(GROUP)]
        spans = [span_ref[i + n] for n in range(GROUP)]
        found = [
            v + divergence(v, w_chord, half, 1) + divergence(v, w_span, half, 0)
            for v, w_chord, w_span, half in zip(values, chords, spans, halves)
        ]
        if i == 0:
            found[0] = found[0] + frames_ref[0]
        for n in range(0, GROUP, 2):
            put(i + n, jnp.concatenate(found[n : n + 2], axis=0))
    right = right_ref[...].reshape(3 * size, cols)
    adj = dot(mat_ref[...], right)
    for c in range(cols // 128):
        adj_ref[c * size : (c + 1) * size, :] = adj[:, c * 128 : (c + 1) * 128]

    for n, (after, _) in enumerate(sides()):
        row = jnp.where(after, rows - 1, 0)
        for c in range(cols // 128):
            edge_ref[n, :, c * 128 : (c + 1) * 128] = row_of_each(first_ref, c, depth, rows, row)
    for n, row in enumerate(far_rows(rows)):
        for c in range(cols // 128):
            two_ref[n, :, c * 128 : (c + 1) * 128] = row_of_each(adj_ref, c, depth, rows, row)
    for copy in copies:
        copy.wait()
    contribution_ref[...] = scale * (
        d_ref[0:1, 0:1] * f * excess_ref[2]
        + chunked(first_ref, 0, rows, size) * excess_ref[1]
        + chunked(adj_ref, 0, rows, size) * excess_ref[0]
    )


def correction(n, got, own, d_ref, edge_ref, pair_ref):
    _, depth, cols = edge_ref.shape
    _, inside = sides()[n]
    factor = d_ref[:, 0:1]
    half = 0.5 * packed_field(got, depth, cols, 0)
    half_next = 0.5 * packed_field(got, depth, cols, 1)
    f = packed_line(got, depth, cols, 0)
    frame = packed_line(got, depth, cols, 1)
    f_next = packed_line(got, depth, cols, 2)
    f_own = packed_line(own, depth, cols, 0)
    half_own = 0.5 * packed_field(own, depth, cols, 0)
    inner = half_own + 0.5 * packed_field(own, depth, cols, 1)
    w_next = half_own + shift_next(half_own, 1)
    w_prev = half_own + shift_prev(half_own, 1, 0.0)
    face = half + half_own
    moved = (
        f
        + (half + shift_next(half, 1)) * (shift_next(f, 1) - f)
        + (half + shift_prev(half, 1, 0.0)) * (shift_prev(f, 1, 0.0) - f)
        + (half + half_next) * (f_next - f)
        + face * (f_own - f)
    )
    outer = factor * moved + jnp.where(iota((depth, 1), 0) == 0, frame, 0.0)
    sources = [factor * (face * f - half * f_own), jnp.where(inside, outer, 0.0)]
    found = dot(pair_ref[...], right_three(jnp.concatenate(sources, axis=0)))
    e = found[0:depth]
    outer = found[depth:]
    change = (
        (1.0 - (w_next + w_prev) - (half_own + inner)) * e
        + w_next * shift_next(e, 1)
        + w_prev * shift_prev(e, 1, 0.0)
        + face * outer
        - half * (e + edge_ref[n])
    )
    return right_three(jnp.concatenate([change, inner * e], axis=0)), e[0:1, :]


def add_segments(total, contribution, picked_rows, map_ref):
    owners, _, lanes = total.shape
    shape = (owners, 128)
    lane = iota(shape, 1)
    segment = jnp.where(lane < lanes, iota(shape, 0) * lanes + lane, -1)
    found = jnp.zeros(shape, F32)
    for block in range(contribution.shape[1] // 128):
        part = contribution[:, block * 128 : (block + 1) * 128]
        sums = jnp.sum(part, axis=1, keepdims=True)
        for n, row in enumerate(picked_rows):
            found += jnp.where(segment == map_ref[block, row], sums[n : n + 1, :], 0.0)
    return total + found[:, None, :lanes]


def near_kernel(
    scale,
    d_ref,
    excess_ref,
    edge_ref,
    pair_ref,
    map_vmem,
    place_ref,
    base_ref,
    contribution_ref,
    own_ref,
    got_ref,
    adj_hbm,
    part_ref,
    adj_ref,
    map_ref,
    sems,
):
    map_copy = pltpu.make_async_copy(map_vmem, map_ref, sems.at[0])
    map_copy.start()
    depth, rows, cols = adj_ref.shape
    size = depth * rows
    sources, surface = correction(0, got_ref, own_ref, d_ref, edge_ref, pair_ref)
    found = dot(place_ref[...], sources)
    adj_ref[...] = (chunked(base_ref, 0, size, size) + found).reshape(depth, rows, cols)
    adj_copy = pltpu.make_async_copy(adj_ref, adj_hbm, sems.at[1])
    adj_copy.start()
    row = jnp.where(sides()[0][0], rows - 1, 0)
    surface = jnp.where(iota((rows, cols), 0) == row, surface, 0.0)
    contribution = contribution_ref[...] + scale * (
        surface * excess_ref[1] + found[0:rows, :] * excess_ref[0]
    )
    map_copy.wait()
    part_ref[...] = add_segments(
        jnp.zeros(part_ref.shape, F32), contribution, range(rows), map_ref
    )
    adj_copy.wait()


def far_kernel(
    scale,
    own_ref,
    got_ref,
    d_ref,
    excess_ref,
    edge_ref,
    pair_ref,
    map_vmem,
    two_ref,
    part_in_ref,
    out_ref,
    part_ref,
    map_ref,
    map_sem,
):
    map_copy = pltpu.make_async_copy(map_vmem, map_ref, map_sem)
    map_copy.start()
    depth = two_ref.shape[1]
    rows = excess_ref.shape[1]
    sources, surface = correction(1, got_ref, own_ref, d_ref, edge_ref, pair_ref)
    found = dot(pair_ref[...], sources)
    edge, second = far_rows(rows)
    contribution = scale * jnp.concatenate(
        [
            surface * excess_ref[1, pl.ds(edge, 1), :]
            + found[0:1] * excess_ref[0, pl.ds(edge, 1), :],
            found[depth : depth + 1] * excess_ref[0, pl.ds(second, 1), :],
        ],
        axis=0,
    )
    map_copy.wait()
    part_ref[...] = add_segments(part_in_ref[...], contribution, (edge, second), map_ref)
    out_ref[...] = two_ref[...] + found.reshape(two_ref.shape)


def finish_kernel(_, two_ref, got_ref, adj_hbm, out_hbm, out_ref, sems):
    copies = []
    for n, row in enumerate(far_rows(adj_hbm.shape[1])):
        copies.append(pltpu.make_async_copy(two_ref.at[n], adj_hbm.at[:, row, :], sems.at[n]))
        copies[-1].start()
    out_ref[...] = jnp.sum(got_ref[:, 0, :], axis=0)
    copies.append(pltpu.make_async_copy(out_ref, out_hbm, sems.at[2]))
    copies[-1].start()
    for copy in copies:
        copy.wait()


def in_hbm(x):
    return pltpu.with_memory_space_constraint(x, pltpu.HBM)


def per_device(
    conductance, depth_inverse, surface_residual, surface_excess, segment_map, frame_index
):
    _, depth, rows, cols = conductance.shape
    frames = surface_residual.shape[1]
    blocks = segment_map.shape[1]
    size = depth * rows
    spans = lax.axis_size("span")
    devices = spans * lax.axis_size("blade")
    lanes = SEGS // devices
    field = pltpu.VMEM((depth, rows, cols), F32)
    chunks = cols // 128
    packed_far = pltpu.VMEM(((2 * depth + 4) * chunks, 128), F32)
    packed_near = pltpu.VMEM(((2 * depth + 3) * chunks, 128), F32)
    own_far, picked, inverse = pl.pallas_call(
        load_kernel,
        out_shape=(
            packed_far,
            pltpu.VMEM((STEPS, rows, cols), F32),
            pltpu.VMEM((depth, depth), F32),
        ),
        in_specs=[HBM] * 4,
        out_specs=(VMEM,) * 3,
        scratch_shapes=[
            pltpu.SMEM((STEPS,), jnp.int32),
            pltpu.VMEM((frames, rows, cols), F32),
            pltpu.VMEM((depth, 8, cols), F32),
            pltpu.SemaphoreType.DMA((4,)),
        ],
        compiler_params=GRANT,
        name="load",
    )(
        in_hbm(frame_index),
        in_hbm(conductance[0]),
        in_hbm(surface_residual[0]),
        in_hbm(depth_inverse[0]),
    )
    k = conductance[0]
    own_near = pl.pallas_call(
        pack_kernel,
        out_shape=packed_near,
        in_specs=[VMEM] * 2,
        out_specs=VMEM,
        compiler_params=GRANT,
        name="pack",
    )(k, picked)
    across = [(i, i + 1) for i in range(1, spans - 1, 2)]
    within = [(i, i + 1) for i in range(0, spans - 1, 2)]
    near = lax.ppermute(own_near, "span", within + [(b, a) for a, b in within])
    far = lax.ppermute(own_far, "span", across + [(b, a) for a, b in across])
    scale = 1.0 / math.sqrt(128.0 * STEPS)
    line = pltpu.VMEM((rows, cols), F32)
    base, two, excess, ids, edge, contribution, pair, place = pl.pallas_call(
        functools.partial(base_kernel, scale),
        out_shape=(
            pltpu.VMEM((chunks * size, 128), F32),
            pltpu.VMEM((2, depth, cols), F32),
            pltpu.VMEM((STEPS, rows, cols), F32),
            pltpu.VMEM((blocks, rows), jnp.int32),
            pltpu.VMEM((2, depth, cols), F32),
            line,
            pltpu.VMEM((2 * depth, 6 * depth), BF16),
            pltpu.VMEM((size, 6 * depth), BF16),
        ),
        in_specs=[VMEM] * 3 + [HBM] * 2,
        out_specs=(VMEM,) * 8,
        scratch_shapes=[
            pltpu.VMEM((size, 3 * size), BF16),
            pltpu.VMEM((3, size, cols), BF16),
            pltpu.VMEM((chunks * size, 128), F32),
            field,
            field,
            pltpu.VMEM((depth, 128), F32),
            pltpu.SemaphoreType.DMA((2,)),
        ],
        compiler_params=GRANT,
        name="base",
    )(k, picked, inverse, in_hbm(surface_excess[0]), in_hbm(segment_map.T))
    fixed = (inverse, excess, edge, pair, ids)
    sums = pltpu.VMEM((devices, 1, lanes), F32)
    adjoint, partial = pl.pallas_call(
        functools.partial(near_kernel, scale),
        out_shape=(pltpu.HBM((depth, rows, cols), F32), sums),
        in_specs=[VMEM] * 10,
        out_specs=(HBM, VMEM),
        scratch_shapes=[
            field,
            pltpu.SMEM((blocks, rows), jnp.int32),
            pltpu.SemaphoreType.DMA((2,)),
        ],
        compiler_params=GRANT,
        name="near",
    )(*fixed, place, base, contribution, own_near, near)
    two, partial = pl.pallas_call(
        functools.partial(far_kernel, scale),
        out_shape=(pltpu.VMEM((2, depth, cols), F32), sums),
        in_specs=[VMEM] * 9,
        out_specs=(VMEM,) * 2,
        scratch_shapes=[pltpu.SMEM((blocks, rows), jnp.int32), pltpu.SemaphoreType.DMA],
        compiler_params=GRANT,
        name="far",
    )(own_far, far, *fixed, two, partial)
    pieces = lax.all_to_all(partial, ("blade", "span"), 0, 0, tiled=True)
    adjoint, owned = pl.pallas_call(
        finish_kernel,
        out_shape=(pltpu.HBM((depth, rows, cols), F32), pltpu.HBM((lanes,), F32)),
        in_specs=[HBM, VMEM, VMEM],
        out_specs=(HBM,) * 2,
        scratch_shapes=[pltpu.VMEM((lanes,), F32), pltpu.SemaphoreType.DMA((3,))],
        input_output_aliases={0: 0},
        compiler_params=GRANT,
        name="finish",
    )(in_hbm(adjoint), two, pltpu.with_memory_space_constraint(pieces, pltpu.VMEM))
    return (adjoint[None], owned)


def solution(mesh):
    placed = (
        P("blade", None, "span", None),
        P("blade", None, None),
        P("blade", None, "span", None),
        P("blade", None, "span", None),
        P("span", None),
        P(),
    )
    return jax.shard_map(
        per_device,
        mesh=mesh,
        in_specs=placed,
        out_specs=(P("blade", None, "span", None), P(("blade", "span"))),
        check_vma=False,
    )
```
